32 devices in a mesh: dp: 4 (over z), ctx: 8 (over y, x, core).
Axes of the slice: x: 2, y: 2, z: 4, core: 2. Of those that a mesh axis runs over, the one named last changes fastest.
Arguments:
- block_in: bfloat16 [8192, 2048], P(('dp', 'ctx')), may hold values from -6 to 6
- gain_attn: bfloat16 [2048], P(('dp', 'ctx')), may hold values from 0.5 to 1.5
- qkv_weight: bfloat16 [2048, 2560], P(('dp', 'ctx')), may hold values from -0.125 to 0.125
- out_weight: bfloat16 [2048, 2048], P(('dp', 'ctx')), may hold values from -0.5 to 0.5
- gain_ffn: bfloat16 [2048], P(('dp', 'ctx')), may hold values from 0.5 to 1.5
- gate_up_weight: bfloat16 [2048, 11264], P(('dp', 'ctx')), may hold values from -0.125 to 0.125
- down_weight: bfloat16 [5632, 2048], P(('dp', 'ctx')), may hold values from -0.078125 to 0.078125
- doc_lengths: int32 [4, 4], P('dp'), may hold values from 1 to 2045, as said below
- out_grad: bfloat16 [8192, 2048], P(('dp', 'ctx')), may hold values from -6 to 6
Outputs:
- block_out: bfloat16 [8192, 2048], P(('dp', 'ctx'))
- input_grad: float32 [8192, 2048], P(('dp', 'ctx'))
- gain_attn_grad: float32 [2048], P(('dp', 'ctx'))
- qkv_weight_grad: float32 [2048, 2560], P(('dp', 'ctx'))
- out_weight_grad: float32 [2048, 2048], P(('dp', 'ctx'))
- gain_ffn_grad: float32 [2048], P(('dp', 'ctx'))
- gate_up_weight_grad: float32 [2048, 11264], P(('dp', 'ctx'))
- down_weight_grad: float32 [5632, 2048], P(('dp', 'ctx'))
The draws below stay inside these ranges and needn't reach their ends.
Inputs may be any that keep to these rules, and one draw needn't show every extreme that they name: `doc_lengths`: each sequence holds 4 documents; the second starts within the sequence's first 256 tokens and ends within its last 256; the others have 1 to 127 tokens each, and the lengths of a sequence add up to 2048; in one sequence the others have 1 token each.
All inputs are finite; a program needn't handle non-finite values.
Results may differ from the reference program's by a relative error of at most 0.015.
Values may be sent and summed in bfloat16 or wider, within the bound.
No kernel may reach another device: no remote copies, remote signals or barrier semaphores. Data moves between devices by JAX's collectives and lax.ppermute only.
A program may use at most 384 MiB of HBM per device.

```python
import math
import jax
import jax.numpy as jnp
from jax import lax

D = 2048
H = 32
KVH = 4
HD = 64
FF = 5632
QKV = 2560
TOK_DEV = 256
DOCS = 4
SEQ = 2048
SEQS = 4
TOKENS = 8192


def draw_doc_lengths(key, part):
    key = jax.random.fold_in(key, 7)
    half_rows = max(TOK_DEV // 2, 2)
    shorter = jax.random.randint(key, (SEQS, DOCS - 1), 1, half_rows).astype(jnp.int32)
    chosen = jax.random.randint(jax.random.fold_in(key, 1), (), 0, SEQS).astype(jnp.int32)
    rows = jnp.arange(SEQS, dtype=jnp.int32)[:, None]
    shorter = jnp.where(rows == chosen, jnp.ones_like(shorter), shorter).astype(jnp.int32)
    longest = SEQ - jnp.sum(shorter, axis=1, keepdims=True)
    return jnp.concatenate([shorter[:, :1], longest, shorter[:, 1:]], axis=1).astype(jnp.int32)


def shard_levels(stream_key, dims, cuts, least, largest):
    factor_of, own = 1.0, jax.random.fold_in(stream_key, 6)
    for dim, blocks in cuts:
        heights = jnp.exp(jax.random.uniform(jax.random.fold_in(own, dim), (blocks,), jnp.float32, least / len(cuts), largest / len(cuts)))
        factor_of = factor_of * jnp.repeat(heights, dims[dim] // blocks).reshape([-1 if axis == dim else 1 for axis in range(len(dims))])
    return factor_of


def normal_values(own_key, shape, deviation, most, split=(), kind=jnp.bfloat16):
    values = jax.random.normal(own_key, shape, jnp.float32) * deviation
    if len(split) > 0:
        values = shard_levels(own_key, shape, split, -0.22, 0.18) * values
    return jnp.clip(values, min=-most, max=most).astype(kind)


def setup_inputs(seed: int = 0) -> dict:
    splits = jax.random.split(jax.random.key(seed), 10)
    block_in = normal_values(splits[0], (TOKENS, D), 1.0, 6.0, ((0, 32),))
    gain_attn = jnp.clip(1.0 + 0.1 * jax.random.normal(splits[1], (D,), jnp.float32), 0.5, 1.5).astype(jnp.bfloat16)
    qkv_weight = normal_values(splits[2], (D, QKV), D ** -0.5, 0.125, ((0, 32),))
    out_weight = normal_values(splits[3], (H * HD, D), (H * HD // 16) ** -0.5, 0.5, ((0, 32),))
    gain_ffn = jnp.clip(1.0 + 0.1 * jax.random.normal(splits[4], (D,), jnp.float32), 0.5, 1.5).astype(jnp.bfloat16)
    gate_up_weight = normal_values(splits[5], (D, 2 * FF), D ** -0.5, 0.125, ((0, 32),))
    down_weight = normal_values(splits[6], (FF, D), FF ** -0.5, 0.078125, ((0, 32),))
    doc_lengths = draw_doc_lengths(jax.random.fold_in(splits[9], 71), 0)
    out_grad = normal_values(splits[8], (TOKENS, D), 1.0, 6.0, ((0, 32),))
    return {"block_in": block_in, "gain_attn": gain_attn, "qkv_weight": qkv_weight, "out_weight": out_weight, "gain_ffn": gain_ffn, "gate_up_weight": gate_up_weight, "down_weight": down_weight, "doc_lengths": doc_lengths, "out_grad": out_grad}


@jax.custom_vjp
def low(v):
    return lax.optimization_barrier(v.astype(jnp.bfloat16)).astype(jnp.float32)

@jax.custom_vjp
def low_back(v):
    return v

def low_keep(v):
    return (low(v), None)

def low_pass(kept, grad):
    return (grad,)

def back_keep(v):
    return (v, None)

def back_low(kept, grad):
    return (low(grad),)
low.defvjp(low_keep, low_pass)
low_back.defvjp(back_keep, back_low)
EPS = 1e-05
MASKED = -1e+30
HIGHEST = lax.Precision.HIGHEST

def documents(lengths):
    doc_ends = jnp.cumsum(lengths).astype(jnp.int32)
    positions = jnp.arange(SEQ, dtype=jnp.int32)
    passed = (positions[:, None] >= doc_ends[None, :]).astype(jnp.int32)
    segment = lax.optimization_barrier(jnp.sum(passed, axis=1)).astype(jnp.int32)
    starts = lax.optimization_barrier(jnp.sum(passed * lengths[None, :], axis=1)).astype(jnp.int32)
    return (segment, positions - starts)

def rotate(values, places, direction):
    half_width = values.shape[-1] // 2
    frequency = 10000.0 ** (-jnp.arange(half_width, dtype=jnp.float32) * 2.0 / values.shape[-1])
    angles = places.astype(jnp.float32)[:, None] * frequency[None, :]
    cosine = jnp.cos(angles)[:, None, :]
    sine_term = direction * jnp.sin(angles)[:, None, :]
    lower_half = values[..., :half_width]
    upper_half = values[..., half_width:]
    return jnp.concatenate([lower_half * cosine - upper_half * sine_term, upper_half * cosine + lower_half * sine_term], axis=-1)

def attend(queries, keys, values, segment):
    block_size = math.gcd(256, SEQ)
    places = jnp.arange(SEQ, dtype=jnp.int32)
    group_size = H // KVH
    query_blocks = queries.reshape(SEQ // block_size, block_size, KVH, group_size, HD)

    def one_block(inputs):
        query_block, seg_block, place_block = inputs
        scores = jnp.einsum('tkgd,skd->kgts', query_block, keys, precision=HIGHEST)
        scores = low_back(scores * HD ** (-0.5))
        visible = (seg_block[:, None] == segment[None, :]) & (places[None, :] <= place_block[:, None])
        scores = jnp.where(visible[None, None], scores, MASKED)
        probs = jax.nn.softmax(scores, axis=-1)
        return jnp.einsum('kgts,skd->tkgd', low(probs), values, precision=HIGHEST)
    result = lax.map(jax.checkpoint(one_block), (query_blocks, segment.reshape(-1, block_size), places.reshape(-1, block_size)))
    return result.reshape(SEQ, H * HD)

def layer_one(hidden_in, segment, places, gain_attn, qkv_weight, out_weight, gain_ffn, gate_up_weight, down_weight):
    norm_one = hidden_in * lax.rsqrt(lax.optimization_barrier(jnp.mean(hidden_in * hidden_in, axis=-1, keepdims=True)) + EPS)
    xn_one = low(norm_one * gain_attn)
    mixed = low_back(jnp.dot(xn_one, qkv_weight, precision=HIGHEST))
    queries = low(rotate(mixed[:, :H * HD].reshape(SEQ, H, HD), places, 1.0))
    keys = low(rotate(mixed[:, H * HD:(H + KVH) * HD].reshape(SEQ, KVH, HD), places, 1.0))
    values = low(mixed[:, (H + KVH) * HD:].reshape(SEQ, KVH, HD))
    attended = attend(queries, keys, values, segment)
    attn = low_back(low(attended))
    state = hidden_in + low_back(jnp.dot(attn, out_weight, precision=HIGHEST))
    norm_two = state * lax.rsqrt(lax.optimization_barrier(jnp.mean(state * state, axis=-1, keepdims=True)) + EPS)
    xn_two = low(norm_two * gain_ffn)
    gate_up = low_back(jnp.dot(xn_two, gate_up_weight, precision=HIGHEST))
    hidden = low(jax.nn.silu(gate_up[:, :FF]) * gate_up[:, FF:])
    return state + low_back(jnp.dot(hidden, down_weight, precision=HIGHEST))

def reference(block_in, gain_attn, qkv_weight, out_weight, gain_ffn, gate_up_weight, down_weight, doc_lengths, out_grad):
    segment, places = jax.vmap(documents)(doc_lengths)
    weights = tuple((weight.astype(jnp.float32) for weight in (gain_attn, qkv_weight, out_weight, gain_ffn, gate_up_weight, down_weight)))
    hidden_in = block_in.astype(jnp.float32).reshape(SEQS, SEQ, D)

    def forward(inputs, w_one, w_two, w_three, w_four, w_five, w_six):

        def one_seq(args):
            return layer_one(args[0], args[1], args[2], w_one, w_two, w_three, w_four, w_five, w_six)
        return lax.map(jax.checkpoint(one_seq), (inputs, segment, places))
    result, pull = jax.vjp(forward, hidden_in, *weights)
    grads = pull(out_grad.astype(jnp.float32).reshape(SEQS, SEQ, D))
    return (result.reshape(TOKENS, D).astype(jnp.bfloat16), grads[0].reshape(TOKENS, D), grads[1], grads[2], grads[3], grads[4], grads[5], grads[6])
```

```python
import jax
import jax.numpy as jnp
import numpy as np
from jax import lax
from jax.experimental import pallas as pl
from jax.experimental.pallas import tpu as pltpu
from jax.sharding import PartitionSpec as P

D = 2048
H = 32
KVH = 4
HD = 64
FF = 5632
HALF = HD // 2

EPS = 1e-05
MASKED = -1e30
BF = jnp.bfloat16
F32 = jnp.float32


def walk(n_ctx, parity):
    bits = []
    bit = 2
    while bit < n_ctx:
        bits.append(bit)
        bit *= 2
    return bits if parity == 0 else bits[::-1]


def swap_stage(x, n_ctx, stage):
    pairs = [(c, c ^ walk(n_ctx, c % 2)[stage]) for c in range(n_ctx)]
    return lax.ppermute(x, "ctx", pairs)


def swap_core(x, n_ctx):
    return lax.ppermute(x, "ctx", [(c, c ^ 1) for c in range(n_ctx)])


def slot_table(n_ctx):
    lists = []
    for parity in (0, 1):
        row = [0]
        for bit in walk(n_ctx, parity):
            row = row + [v ^ bit for v in row]
        lists.append(row)
    return np.array(
        [lists[p] + [v ^ 1 for v in lists[1 - p]] for p in (0, 1)], dtype=np.int32
    )


def gather_slots(x, n_ctx):
    have = [x]
    for stage in range(len(walk(n_ctx, 0))):
        have = have + [swap_stage(block, n_ctx, stage) for block in have]
    have = have + [swap_core(block, n_ctx) for block in have]
    return jnp.concatenate(have, axis=0)


def scatter_slots(keep, send, n_ctx, rows):
    total = keep + swap_core(send, n_ctx).astype(F32)
    for stage in reversed(range(len(walk(n_ctx, 0)))):
        half = total.shape[0] // 2
        arrived = swap_stage(total[half:].astype(BF), n_ctx, stage)
        total = total[:half] + arrived.astype(F32)
    return total


def lane_heads(rows, width):
    lane = lax.broadcasted_iota(jnp.int32, (rows, width), 1)
    return (lane % (width // 2)) // HALF


def nt(a, b):
    return lax.dot_general(a, b, (((1,), (1,)), ((), ())), preferred_element_type=F32)


def nn(a, b):
    return jnp.dot(a, b, preferred_element_type=F32)


def attend_forward(order, slot_of, starts, queries, keys, values_t, heads, tok):
    seq, width = queries.shape
    blocks = seq // tok

    def kernel(order_ref, slot_ref, start_ref, q_ref, k_ref, v_ref, attn_ref, full_ref, lse_ref, scores):
        block = order_ref[pl.program_id(0)]
        start = start_ref[...]
        here = block * tok + lax.broadcasted_iota(jnp.int32, (1, tok), 1)
        head_of = lane_heads(tok, width)
        q = q_ref[...]
        q_heads = [jnp.where(head_of == h, q, jnp.zeros_like(q)) for h in range(heads)]

        def score(i, peaks):
            k = k_ref[pl.ds(pl.multiple_of(slot_ref[i] * tok, tok), tok), :]
            there = i * tok + lax.broadcasted_iota(jnp.int32, (tok, tok), 0)
            visible = (there >= start) & (there <= here)
            out = []
            for h in range(heads):
                s = jnp.where(visible, nt(k, q_heads[h]), MASKED)
                scores[h, pl.ds(pl.multiple_of(i * tok, tok), tok), :] = s
                out.append(jnp.maximum(peaks[h], jnp.max(s.reshape(tok // 8, 8, tok), axis=0)))
            return tuple(out)

        peaks = lax.fori_loop(
            0, block + 1, score, tuple(jnp.full((8, tok), MASKED, F32) for _ in range(heads))
        )
        peaks = [jnp.max(peak, axis=0, keepdims=True) for peak in peaks]

        def weigh(i, running):
            v = v_ref[:, pl.ds(pl.multiple_of(slot_ref[i] * tok, tok), tok)]
            out = []
            for h in range(heads):
                total, acc = running[h]
                p = jnp.exp(scores[h, pl.ds(pl.multiple_of(i * tok, tok), tok), :] - peaks[h])
                total = total + jnp.sum(p.reshape(tok // 8, 8, tok), axis=0)
                out.append((total, acc + nn(v, p.astype(BF))))
            return tuple(out)

        result = lax.fori_loop(
            0,
            block + 1,
            weigh,
            tuple((jnp.zeros((8, tok), F32), jnp.zeros((HD, tok), F32)) for _ in range(heads)),
        )
        rows = []
        for h in range(heads):
            total, acc = result[h]
            total = jnp.sum(total, axis=0, keepdims=True)
            rows.append(acc / total)
            lse_ref[0, h : h + 1, :] = peaks[h] + jnp.log(total)
        full = jnp.concatenate(rows, axis=0).T
        full_ref[...] = full
        attn_ref[...] = full.astype(BF)

    return pl.pallas_call(
        kernel,
        grid_spec=pltpu.PrefetchScalarGridSpec(
            num_scalar_prefetch=2,
            grid=(blocks,),
            in_specs=[
                pl.BlockSpec((1, tok), lambda j, *_: (0, j)),
                pl.BlockSpec((tok, width), lambda j, *_: (j, 0)),
                pl.BlockSpec((seq, width), lambda j, *_: (0, 0)),
                pl.BlockSpec((HD, seq), lambda j, *_: (0, 0)),
            ],
            out_specs=[
                pl.BlockSpec((tok, width), lambda j, *_: (j, 0)),
                pl.BlockSpec((tok, width), lambda j, *_: (j, 0)),
                pl.BlockSpec((1, heads, tok), lambda j, *_: (j, 0, 0)),
            ],
            scratch_shapes=[pltpu.VMEM((heads, seq, tok), F32)],
        ),
        out_shape=[
            jax.ShapeDtypeStruct((seq, width), BF),
            jax.ShapeDtypeStruct((seq, width), F32),
            jax.ShapeDtypeStruct((blocks, heads, tok), F32),
        ],
        compiler_params=pltpu.CompilerParams(vmem_limit_bytes=40 << 20),
        cost_estimate=pl.CostEstimate(
            flops=2 * seq * seq * width * heads,
            bytes_accessed=12 * seq * width,
            transcendentals=seq * seq * heads // 2,
        ),
        name="attend_forward",
    )(order, slot_of, starts, queries, keys, values_t)


def attend_backward(
    order, slot_of, starts, queries, keys, keys_t, values, grads, full, lse, heads, tok
):
    seq, width = queries.shape
    blocks = seq // tok
    half = width // 2

    def kernel(
        order_ref, slot_ref, start_ref, q_ref, k_ref, kt_ref, v_ref, g_ref, full_ref, lse_ref,
        dq_ref, dkv_ref, dk, dv,
    ):
        j = pl.program_id(0)
        block = order_ref[j]

        @pl.when(j == 0)
        def _():
            dk[...] = jnp.zeros_like(dk)
            dv[...] = jnp.zeros_like(dv)

        start = start_ref[...]
        here = block * tok + lax.broadcasted_iota(jnp.int32, (1, tok), 1)
        head_of = lane_heads(tok, width)
        wide = lax.broadcasted_iota(jnp.int32, (tok, width), 1) // HD
        q = q_ref[...]
        g = g_ref[...]
        q_heads = [jnp.where(head_of == h, q, jnp.zeros_like(q)) for h in range(heads)]
        g_heads = [jnp.where(wide == h, g, jnp.zeros_like(g)) for h in range(heads)]
        q_stack = jnp.concatenate(q_heads, axis=0)
        g_stack = jnp.concatenate(g_heads, axis=0)
        picks = (
            lax.broadcasted_iota(jnp.int32, (8, width), 1) // HD
            == lax.broadcasted_iota(jnp.int32, (8, width), 0)
        ).astype(F32)
        deltas = lax.dot_general(
            picks,
            g.astype(F32) * full_ref[...],
            (((1,), (1,)), ((), ())),
            preferred_element_type=F32,
            precision=lax.Precision.HIGHEST,
        )

        def step(i, dq):
            rows = pl.ds(pl.multiple_of(slot_ref[i] * tok, tok), tok)
            k = k_ref[rows, :]
            v = v_ref[rows, :]
            kt = kt_ref[:, rows]
            there = i * tok + lax.broadcasted_iota(jnp.int32, (tok, tok), 0)
            visible = (there >= start) & (there <= here)
            probs, grad_scores, out = [], [], []
            for h in range(heads):
                s = jnp.where(visible, nt(k, q_heads[h]), MASKED)
                p = jnp.exp(s - lse_ref[0, h : h + 1, :])
                ds = (p * (nt(v, g_heads[h]) - deltas[h : h + 1, :])).astype(BF)
                probs.append(p.astype(BF))
                grad_scores.append(ds)
                out.append(dq[h] + nn(kt, ds))
            dv[rows, :] += nn(jnp.concatenate(probs, axis=1), g_stack)
            dk[rows, :] += nn(jnp.concatenate(grad_scores, axis=1), q_stack)
            return tuple(out)

        dq = lax.fori_loop(
            0, block + 1, step, tuple(jnp.zeros((HD, tok), F32) for _ in range(heads))
        )
        dq_ref[...] = jnp.concatenate([x[:HALF] for x in dq] + [x[HALF:] for x in dq], axis=0).T

        @pl.when(j == blocks - 1)
        def _():
            lane = lax.broadcasted_iota(jnp.int32, (width, 128), 0)
            column = lax.broadcasted_iota(jnp.int32, (width, 128), 1)
            fold_k = ((lane // half) * HALF + lane % HALF == column).astype(BF)
            fold_v = (lane % HD + HD == column).astype(BF)

            def fold(i, unused):
                rows = pl.ds(pl.multiple_of(i * tok, tok), tok)
                a = dk[rows, :]
                b = dv[rows, :]
                a_high = a.astype(BF)
                b_high = b.astype(BF)
                dkv_ref[rows, :] = (
                    nn(a_high, fold_k)
                    + nn((a - a_high.astype(F32)).astype(BF), fold_k)
                    + nn(b_high, fold_v)
                    + nn((b - b_high.astype(F32)).astype(BF), fold_v)
                )
                return unused

            lax.fori_loop(0, blocks, fold, 0)

    return pl.pallas_call(
        kernel,
        grid_spec=pltpu.PrefetchScalarGridSpec(
            num_scalar_prefetch=2,
            grid=(blocks,),
            in_specs=[
                pl.BlockSpec((1, tok), lambda j, *_: (0, j)),
                pl.BlockSpec((tok, width), lambda j, *_: (j, 0)),
                pl.BlockSpec((seq, width), lambda j, *_: (0, 0)),
                pl.BlockSpec((HD, seq), lambda j, *_: (0, 0)),
                pl.BlockSpec((seq, width), lambda j, *_: (0, 0)),
                pl.BlockSpec((tok, width), lambda j, *_: (j, 0)),
                pl.BlockSpec((tok, width), lambda j, *_: (j, 0)),
                pl.BlockSpec((1, heads, tok), lambda j, *_: (j, 0, 0)),
            ],
            out_specs=[
                pl.BlockSpec((tok, width), lambda j, *_: (j, 0)),
                pl.BlockSpec((seq, 128), lambda j, *_: (0, 0)),
            ],
            scratch_shapes=[pltpu.VMEM((seq, width), F32), pltpu.VMEM((seq, width), F32)],
        ),
        out_shape=[
            jax.ShapeDtypeStruct((seq, width), F32),
            jax.ShapeDtypeStruct((seq, 128), F32),
        ],
        compiler_params=pltpu.CompilerParams(vmem_limit_bytes=40 << 20),
        cost_estimate=pl.CostEstimate(
            flops=5 * seq * seq * width * heads,
            bytes_accessed=16 * seq * width,
            transcendentals=seq * seq * heads // 2,
        ),
        name="attend_backward",
    )(order, slot_of, starts, queries, keys, keys_t, values, grads, full, lse)


def normalize(values):
    inverse_rms = lax.rsqrt(jnp.mean(values * values, axis=-1, keepdims=True) + EPS)
    return (values * inverse_rms, inverse_rms)


def norm_back(grad_normed, normed, inverse_rms):
    return inverse_rms * (
        grad_normed - normed * jnp.mean(grad_normed * normed, axis=-1, keepdims=True)
    )


def outer_rows(activations, gradients):
    return lax.dot_general(
        activations, gradients, (((0,), (0,)), ((), ())), preferred_element_type=F32
    ).astype(BF)


def exchange(x):
    return lax.all_to_all(x, "ctx", split_axis=0, concat_axis=0, tiled=False)


def gather_dp(x):
    return lax.all_gather(x, "dp", axis=0, tiled=True)


def scatter_dp(x):
    return lax.psum_scatter(x, "dp", scatter_dimension=0, tiled=True)


def on_device(
    block_in,
    gain_attn,
    qkv_weight,
    out_weight,
    gain_ffn,
    gate_up_weight,
    down_weight,
    doc_lengths,
    out_grad,
):
    n_ctx = lax.axis_size("ctx")
    n_dp = lax.axis_size("dp")
    me = lax.axis_index("ctx")
    tok = block_in.shape[0]
    seq = tok * n_ctx
    heads = H // n_ctx
    width = heads * HD
    sharers = n_ctx // KVH
    rows = qkv_weight.shape[0]
    ff_rows = down_weight.shape[0]
    ff = ff_rows * n_dp

    order = me ^ jnp.where(me % 2 == 0, *[jnp.asarray(t) for t in slot_table(n_ctx)])
    slot_of = jnp.sum(
        jnp.where(
            order[None, :] == jnp.arange(n_ctx, dtype=jnp.int32)[:, None],
            jnp.arange(n_ctx, dtype=jnp.int32)[None, :],
            0,
        ),
        axis=1,
    )
    index = (order[:, None] * tok + jnp.arange(tok, dtype=jnp.int32)[None, :]).reshape(seq)
    lengths = doc_lengths[0]
    ends = jnp.cumsum(lengths)
    starts = jnp.sum((index[:, None] >= ends[None, :]).astype(jnp.int32) * lengths[None, :], axis=1)
    lane = jnp.arange(width // 2, dtype=F32) % HALF
    frequency = 10000.0 ** (-lane * 2.0 / HD)
    angles = (index - starts).astype(F32)[:, None] * frequency[None, :]
    cosine = jnp.cos(angles)
    sine = jnp.sin(angles)
    starts_row = starts[None, :]

    gain_one = gain_attn.astype(F32)[:, None]
    gain_two = gain_ffn.astype(F32)[:, None]
    qkv = (qkv_weight.astype(F32) * gain_one).astype(BF)
    q_cols = (
        qkv[:, : H * HD]
        .reshape(rows, n_ctx, heads, 2, HALF)
        .transpose(1, 0, 3, 2, 4)
        .reshape(n_ctx, rows, width)
    )
    k_cols = qkv[:, H * HD : (H + KVH) * HD].reshape(rows, KVH, HD).transpose(1, 0, 2)
    v_cols = qkv[:, (H + KVH) * HD :].reshape(rows, KVH, HD).transpose(1, 0, 2)
    kv_cols = jnp.repeat(jnp.concatenate([k_cols, v_cols], axis=2), sharers, axis=0)
    qkv_part = gather_dp(
        exchange(jnp.concatenate([q_cols, kv_cols], axis=2)).reshape(n_ctx * rows, width + 2 * HD)
    )

    hidden_in = block_in.astype(F32)
    norm_one, rms_one = normalize(hidden_in)
    all_one = gather_slots(norm_one.astype(BF), n_ctx)

    owner_pairs = [
        (b, (b % n_dp) * n_ctx + b // n_dp) for b in range(n_dp * n_ctx)
    ]
    out_part = gather_dp(lax.ppermute(out_weight, ("dp", "ctx"), owner_pairs))
    gate_up = (gate_up_weight.astype(F32) * gain_two).astype(BF)
    gate_up_cols = (
        gate_up.reshape(rows, 2, n_dp, n_ctx, ff_rows)
        .transpose(3, 0, 1, 2, 4)
        .reshape(n_ctx, rows, 2 * ff)
    )
    gate_up_part = gather_dp(exchange(gate_up_cols).reshape(n_ctx * rows, 2 * ff))
    down_part = gather_dp(down_weight)

    mixed = nn(all_one, qkv_part)
    q_low, q_high = mixed[:, : width // 2], mixed[:, width // 2 : width]
    queries = (
        jnp.concatenate(
            [q_low * cosine - q_high * sine, q_high * cosine + q_low * sine], axis=1
        )
        * HD**-0.5
    ).astype(BF)
    k_low, k_high = mixed[:, width : width + HALF], mixed[:, width + HALF : width + HD]
    cos_k, sin_k = cosine[:, :HALF], sine[:, :HALF]
    keys_low = (k_low * cos_k - k_high * sin_k).astype(BF)
    keys_high = (k_high * cos_k + k_low * sin_k).astype(BF)
    values = mixed[:, width + HD :].astype(BF)
    keys_wide = jnp.concatenate([keys_low] * heads + [keys_high] * heads, axis=1)
    values_wide = jnp.concatenate([values] * heads, axis=1)
    keys_t = jnp.concatenate([keys_low, keys_high], axis=1).T
    attn, attended, lse = attend_forward(
        order, slot_of, starts_row, queries, keys_wide, values.T, heads, tok
    )
    mid = seq // 2
    state = hidden_in + scatter_slots(
        nn(attn[:mid], out_part), nn(attn[mid:], out_part).astype(BF), n_ctx, tok
    )
    norm_two, rms_two = normalize(state)
    all_two = gather_slots(norm_two.astype(BF), n_ctx)
    all_grad = gather_slots(out_grad, n_ctx)

    both = nn(all_two, gate_up_part)
    gate, up = both[:, :ff], both[:, ff:]
    sigmoid_gate = jax.nn.sigmoid(gate)
    silu_gate = gate * sigmoid_gate
    hidden = (silu_gate * up).astype(BF)
    grad_hidden = nt(all_grad, down_part)
    grad_gate_up = jnp.concatenate(
        [grad_hidden * up * sigmoid_gate * (1.0 + gate * (1.0 - sigmoid_gate)), grad_hidden * silu_gate],
        axis=1,
    ).astype(BF)
    d_two = scatter_slots(
        nt(grad_gate_up[:mid], gate_up_part),
        nt(grad_gate_up[mid:], gate_up_part).astype(BF),
        n_ctx,
        tok,
    )
    block_out = (
        state
        + scatter_slots(
            nn(hidden[:mid], down_part), nn(hidden[mid:], down_part).astype(BF), n_ctx, tok
        )
    ).astype(BF)
    down_weight_grad = scatter_dp(outer_rows(hidden, all_grad)).astype(F32)
    gate_up_sums = scatter_dp(outer_rows(all_two, grad_gate_up))

    grad_state = out_grad.astype(F32) + norm_back(d_two, norm_two, rms_two)
    all_branch = gather_slots(grad_state.astype(BF), n_ctx)
    grad_attn = nt(all_branch, out_part).astype(BF)
    out_sums = scatter_dp(outer_rows(attn, all_branch))
    grad_queries, grad_kv = attend_backward(
        order,
        slot_of,
        starts_row,
        queries,
        keys_wide,
        keys_t,
        values_wide,
        grad_attn,
        attended,
        lse,
        heads,
        tok,
    )
    g_low, g_high = grad_queries[:, : width // 2], grad_queries[:, width // 2 :]
    gk_low, gk_high = grad_kv[:, :HALF], grad_kv[:, HALF:HD]
    scale = HD**-0.5
    grad_mixed = jnp.concatenate(
        [
            (g_low * cosine + g_high * sine) * scale,
            (g_high * cosine - g_low * sine) * scale,
            gk_low * cos_k + gk_high * sin_k,
            gk_high * cos_k - gk_low * sin_k,
            grad_kv[:, HD:],
        ],
        axis=1,
    ).astype(BF)
    d_one = scatter_slots(
        nt(grad_mixed[:mid], qkv_part), nt(grad_mixed[mid:], qkv_part).astype(BF), n_ctx, tok
    )
    input_grad = grad_state + norm_back(d_one, norm_one, rms_one)
    qkv_sums = scatter_dp(outer_rows(all_one, grad_mixed))

    back_pairs = [(b, a) for a, b in owner_pairs]
    out_weight_grad = lax.ppermute(out_sums, ("dp", "ctx"), back_pairs).astype(F32)
    gate_up_back = (
        exchange(gate_up_sums.reshape(n_ctx, rows, 2 * ff))
        .reshape(n_ctx, rows, 2, n_dp, ff_rows)
        .transpose(1, 2, 3, 0, 4)
        .reshape(rows, 2 * FF)
        .astype(F32)
    )
    gate_up_weight_grad = gate_up_back * gain_two
    gain_ffn_grad = jnp.sum(gate_up_back * gate_up_weight.astype(F32), axis=1)
    qkv_back = exchange(qkv_sums.reshape(n_ctx, rows, width + 2 * HD)).astype(F32)
    q_back = (
        qkv_back[:, :, :width]
        .reshape(n_ctx, rows, 2, heads, HALF)
        .transpose(1, 0, 3, 2, 4)
        .reshape(rows, H * HD)
    )
    kv_back = jnp.sum(qkv_back[:, :, width:].reshape(KVH, sharers, rows, 2 * HD), axis=1)
    k_back = kv_back[:, :, :HD].transpose(1, 0, 2).reshape(rows, KVH * HD)
    v_back = kv_back[:, :, HD:].transpose(1, 0, 2).reshape(rows, KVH * HD)
    qkv_back = jnp.concatenate([q_back, k_back, v_back], axis=1)
    qkv_weight_grad = qkv_back * gain_one
    gain_attn_grad = jnp.sum(qkv_back * qkv_weight.astype(F32), axis=1)
    return (
        block_out,
        input_grad,
        gain_attn_grad,
        qkv_weight_grad,
        out_weight_grad,
        gain_ffn_grad,
        gate_up_weight_grad,
        down_weight_grad,
    )


def solution(mesh):
    rows = P(("dp", "ctx"), None)
    entries = P(("dp", "ctx"))
    return jax.shard_map(
        on_device,
        mesh=mesh,
        in_specs=(rows, entries, rows, rows, entries, rows, rows, P("dp", None), rows),
        out_specs=(rows, rows, entries, rows, rows, entries, rows, rows),
        check_vma=False,
    )
```

```python
import jax
import jax.numpy as jnp
import numpy as np
from jax import lax
from jax.experimental import pallas as pl
from jax.experimental.pallas import tpu as pltpu
from jax.sharding import PartitionSpec as P

D = 2048
H = 32
KVH = 4
HD = 64
FF = 5632
HALF = HD // 2

EPS = 1e-05
MASKED = -1e30
BF = jnp.bfloat16
F32 = jnp.float32
MIB = 1 << 20


def nt(a, b):
    return lax.dot_general(a, b, (((1,), (1,)), ((), ())), preferred_element_type=F32)


def nn(a, b):
    return jnp.dot(a, b, preferred_element_type=F32)


def after(x, *earlier):
    return lax.optimization_barrier((x, *earlier))[0]


def walk(n_ctx, parity):
    bits = []
    bit = 2
    while bit < n_ctx:
        bits.append(bit)
        bit *= 2
    return bits if parity == 0 else bits[::-1]


def swap_stage(x, n_ctx, stage):
    pairs = [(c, c ^ walk(n_ctx, c % 2)[stage]) for c in range(n_ctx)]
    return lax.ppermute(x, "ctx", pairs)


def swap_core(x, n_ctx):
    return lax.ppermute(x, "ctx", [(c, c ^ 1) for c in range(n_ctx)])


def slot_table(n_ctx):
    lists = []
    for parity in (0, 1):
        row = [0]
        for bit in walk(n_ctx, parity):
            row = row + [v ^ bit for v in row]
        lists.append(row)
    return np.array(
        [lists[p] + [v ^ 1 for v in lists[1 - p]] for p in (0, 1)], dtype=np.int32
    )


def gather_slots(x, n_ctx):
    have = [x]
    for stage in range(len(walk(n_ctx, 0))):
        have = have + [swap_stage(block, n_ctx, stage) for block in have]
    return have + [swap_core(block, n_ctx) for block in have]


def scatter_slots(send, keep, tok, n_ctx):
    mine = n_ctx // 2
    stages = len(walk(n_ctx, 0))
    totals = {}
    cut = mine // 2
    for lo, hi in ((cut, mine), (0, cut)):
        arrived = swap_core(send(mine + lo, mine + hi), n_ctx)
        totals[lo, hi] = keep(lo, hi) + arrived.astype(F32)
    upper, rest = totals[cut, mine], totals[0, cut]
    for stage in reversed(range(stages)):
        arrived = swap_stage(upper.astype(BF), n_ctx, stage).astype(F32)
        rest = rest + arrived
        half = rest.shape[0] // 2
        if stage:
            upper, rest = rest[half:], rest[:half]
    return rest


def exchange(x):
    return lax.all_to_all(x, "ctx", split_axis=0, concat_axis=0, tiled=False)


def gather_dp(x):
    return lax.all_gather(x, "dp", axis=0, tiled=True)


def scatter_dp(x):
    return lax.psum_scatter(x, "dp", scatter_dimension=0, tiled=True)


def fetch_piece(pieces, buffer, semaphores):
    step = pl.program_id(0)
    count = len(pieces)

    def start(k):
        for i, piece in enumerate(pieces):

            @pl.when(k == i)
            def _():
                pltpu.make_async_copy(piece, buffer.at[i % 2], semaphores.at[i % 2]).start()

    @pl.when(step == 0)
    def _():
        start(0)

    @pl.when(step + 1 < count)
    def _():
        start(step + 1)

    pltpu.make_async_copy(
        pieces[0], buffer.at[lax.rem(step, 2)], semaphores.at[lax.rem(step, 2)]
    ).wait()
    return buffer[lax.rem(step, 2)]


def swap_halves(x):
    return pltpu.roll(x, x.shape[1] // 2, axis=1)


def turn_tables(cosine, sine, width):
    times = width // 128
    cosine = jnp.concatenate([cosine] * times, axis=1) if times > 1 else cosine
    sine = jnp.concatenate([sine] * times, axis=1) if times > 1 else sine
    lane = lax.broadcasted_iota(jnp.int32, sine.shape, 1)
    return cosine, jnp.where(lane < width // 2, -sine, sine)


def any_specs(pieces):
    return [pl.BlockSpec(memory_space=pl.ANY) for _ in pieces]


def project_qkv(order, pieces, weight, spread, cosine, sine, width, tok):
    n = len(pieces)
    seq = n * tok

    def kernel(order_ref, *refs):
        parts = refs[:n]
        w_ref, spread_ref, cos_ref, sin_ref = refs[n : n + 4]
        q_ref, k_ref, v_ref, kt_ref, vt_ref, all_ref, wide, buffer, semaphores = refs[n + 4 :]

        @pl.when(pl.program_id(0) == 0)
        def _():
            wide[...] = nn(w_ref[...], spread_ref[...]).astype(BF)

        x = fetch_piece(parts, buffer, semaphores)
        all_ref[...] = x
        mixed = nn(x, wide[...])
        cos, sin = turn_tables(cos_ref[...], sin_ref[...], width)
        q = mixed[:, :width]
        k = mixed[:, width : 2 * width]
        v = mixed[:, 2 * width :].astype(BF)
        q_ref[...] = (q * cos + swap_halves(q) * sin).astype(BF) * (HD**-0.5)
        k = (k * cos + swap_halves(k) * sin).astype(BF)
        k_ref[...] = k
        v_ref[...] = v
        k_turned = k.T
        kt_ref[:HALF, :] = k_turned[:HALF]
        kt_ref[HALF:, :] = k_turned[width // 2 : width // 2 + HALF]
        vt_ref[...] = v.T[:HD]

    rows = lambda s, order: (order[s], 0)
    lanes = lambda s, order: (0, order[s])
    whole = lambda s, order: (0, 0)
    return pl.pallas_call(
        kernel,
        grid_spec=pltpu.PrefetchScalarGridSpec(
            num_scalar_prefetch=1,
            grid=(n,),
            in_specs=any_specs(pieces)
            + [
                pl.BlockSpec(weight.shape, whole),
                pl.BlockSpec(spread.shape, whole),
                pl.BlockSpec((tok, 128), rows),
                pl.BlockSpec((tok, 128), rows),
            ],
            out_specs=[
                pl.BlockSpec((tok, width), rows),
                pl.BlockSpec((tok, width), rows),
                pl.BlockSpec((tok, width), rows),
                pl.BlockSpec((HD, tok), lanes),
                pl.BlockSpec((HD, tok), lanes),
                pl.BlockSpec((tok, D), rows),
            ],
            scratch_shapes=[
                pltpu.VMEM((D, 3 * width), BF),
                pltpu.VMEM((2, tok, D), BF),
                pltpu.SemaphoreType.DMA((2,)),
            ],
        ),
        out_shape=[
            jax.ShapeDtypeStruct((seq, width), BF),
            jax.ShapeDtypeStruct((seq, width), BF),
            jax.ShapeDtypeStruct((seq, width), BF),
            jax.ShapeDtypeStruct((HD, seq), BF),
            jax.ShapeDtypeStruct((HD, seq), BF),
            jax.ShapeDtypeStruct((seq, D), BF),
        ],
        compiler_params=pltpu.CompilerParams(vmem_limit_bytes=40 * MIB),
        cost_estimate=pl.CostEstimate(
            flops=6 * seq * D * width, bytes_accessed=4 * seq * D, transcendentals=0
        ),
        name="project_qkv",
    )(order, *pieces, weight, spread, cosine, sine)


def project_out(order, heads_in, pieces, residual):
    n, tok, width = heads_in.shape

    def kernel(order_ref, a_ref, *refs):
        parts = refs[:n]
        x_ref, state_ref, norm_ref, buffer, semaphores = refs[n:]
        step = pl.program_id(0)
        w = fetch_piece(parts, buffer, semaphores)

        @pl.when(step == 0)
        def _():
            state_ref[...] = x_ref[...].astype(F32)

        state_ref[...] += nn(a_ref[0], w)

        @pl.when(step == n - 1)
        def _():
            state = state_ref[...]
            scale = lax.rsqrt(jnp.mean(state * state, axis=-1, keepdims=True) + EPS)
            norm_ref[...] = (state * scale).astype(BF)

    whole = lambda s, order: (0, 0)
    return pl.pallas_call(
        kernel,
        grid_spec=pltpu.PrefetchScalarGridSpec(
            num_scalar_prefetch=1,
            grid=(n,),
            in_specs=[pl.BlockSpec((1, tok, width), lambda s, order: (order[s], 0, 0))]
            + any_specs(pieces)
            + [pl.BlockSpec((tok, D), whole)],
            out_specs=[pl.BlockSpec((tok, D), whole), pl.BlockSpec((tok, D), whole)],
            scratch_shapes=[
                pltpu.VMEM((2, width, D), BF),
                pltpu.SemaphoreType.DMA((2,)),
            ],
        ),
        out_shape=[
            jax.ShapeDtypeStruct((tok, D), F32),
            jax.ShapeDtypeStruct((tok, D), BF),
        ],
        compiler_params=pltpu.CompilerParams(vmem_limit_bytes=32 * MIB),
        cost_estimate=pl.CostEstimate(
            flops=2 * tok * D * width * n, bytes_accessed=2 * D * width * n, transcendentals=0
        ),
        name="project_out",
    )(order, heads_in, *pieces, residual)


def feed_forward(pieces, weight):
    n = len(pieces)
    tok = pieces[0].shape[0]
    seq = n * tok
    ff = weight.shape[1] // 2

    def kernel(*refs):
        parts = refs[:n]
        w_ref, both_ref, hidden_ref, all_ref, buffer, semaphores = refs[n:]
        x = fetch_piece(parts, buffer, semaphores)
        all_ref[...] = x
        both = nn(x, w_ref[...])
        both_ref[...] = both
        gate = both[:, :ff]
        up = both[:, ff:]
        hidden_ref[...] = (gate * jax.nn.sigmoid(gate) * up).astype(BF)

    rows = lambda s: (s, 0)
    return pl.pallas_call(
        kernel,
        grid=(n,),
        in_specs=any_specs(pieces) + [pl.BlockSpec(weight.shape, lambda s: (0, 0))],
        out_specs=[
            pl.BlockSpec((tok, 2 * ff), rows),
            pl.BlockSpec((tok, ff), rows),
            pl.BlockSpec((tok, D), rows),
        ],
        scratch_shapes=[pltpu.VMEM((2, tok, D), BF), pltpu.SemaphoreType.DMA((2,))],
        out_shape=[
            jax.ShapeDtypeStruct((seq, 2 * ff), F32),
            jax.ShapeDtypeStruct((seq, ff), BF),
            jax.ShapeDtypeStruct((seq, D), BF),
        ],
        compiler_params=pltpu.CompilerParams(vmem_limit_bytes=44 * MIB),
        cost_estimate=pl.CostEstimate(
            flops=4 * seq * D * ff, bytes_accessed=10 * seq * ff + 4 * seq * D, transcendentals=seq * ff
        ),
        name="feed_forward",
    )(*pieces, weight)


def feed_backward(both, grads, weight):
    seq = both.shape[0]
    ff = weight.shape[0]
    tok = 256

    def kernel(both_ref, g_ref, w_ref, out_ref):
        grad_hidden = nt(g_ref[...], w_ref[...])
        both = both_ref[...]
        gate = both[:, :ff]
        up = both[:, ff:]
        sig = jax.nn.sigmoid(gate)
        out_ref[:, :ff] = (grad_hidden * up * sig * (1.0 + gate * (1.0 - sig))).astype(BF)
        out_ref[:, ff:] = (grad_hidden * (gate * sig)).astype(BF)

    rows = lambda s: (s, 0)
    return pl.pallas_call(
        kernel,
        grid=(seq // tok,),
        in_specs=[
            pl.BlockSpec((tok, 2 * ff), rows),
            pl.BlockSpec((tok, D), rows),
            pl.BlockSpec(weight.shape, lambda s: (0, 0)),
        ],
        out_specs=pl.BlockSpec((tok, 2 * ff), rows),
        out_shape=jax.ShapeDtypeStruct((seq, 2 * ff), BF),
        compiler_params=pltpu.CompilerParams(vmem_limit_bytes=40 * MIB),
        cost_estimate=pl.CostEstimate(
            flops=2 * seq * D * ff, bytes_accessed=12 * seq * ff + 2 * seq * D, transcendentals=seq * ff
        ),
        name="feed_backward",
    )(both, grads, weight)


def branch_back(order, d_two, state, out_grad, pieces):
    n = len(pieces)
    tok = d_two.shape[0]
    width = pieces[0].shape[0]

    def kernel(order_ref, d_ref, state_ref, g_ref, *refs):
        parts = refs[:n]
        grad_ref, branch_ref, heads_ref, buffer, semaphores = refs[n:]

        @pl.when(pl.program_id(0) == 0)
        def _():
            state = state_ref[...]
            scale = lax.rsqrt(jnp.mean(state * state, axis=-1, keepdims=True) + EPS)
            norm = state * scale
            d = d_ref[...]
            grad = g_ref[...].astype(F32) + scale * (
                d - norm * jnp.mean(d * norm, axis=-1, keepdims=True)
            )
            grad_ref[...] = grad
            branch_ref[...] = grad.astype(BF)

        w = fetch_piece(parts, buffer, semaphores)
        heads_ref[0] = nt(branch_ref[...], w).astype(BF)

    whole = lambda s, order: (0, 0)
    return pl.pallas_call(
        kernel,
        grid_spec=pltpu.PrefetchScalarGridSpec(
            num_scalar_prefetch=1,
            grid=(n,),
            in_specs=[
                pl.BlockSpec((tok, D), whole),
                pl.BlockSpec((tok, D), whole),
                pl.BlockSpec((tok, D), whole),
            ]
            + any_specs(pieces),
            out_specs=[
                pl.BlockSpec((tok, D), whole),
                pl.BlockSpec((tok, D), whole),
                pl.BlockSpec((1, tok, width), lambda s, order: (order[s], 0, 0)),
            ],
            scratch_shapes=[
                pltpu.VMEM((2, width, D), BF),
                pltpu.SemaphoreType.DMA((2,)),
            ],
        ),
        out_shape=[
            jax.ShapeDtypeStruct((tok, D), F32),
            jax.ShapeDtypeStruct((tok, D), BF),
            jax.ShapeDtypeStruct((n, tok, width), BF),
        ],
        compiler_params=pltpu.CompilerParams(vmem_limit_bytes=32 * MIB),
        cost_estimate=pl.CostEstimate(
            flops=2 * tok * D * width * n, bytes_accessed=2 * D * width * n, transcendentals=0
        ),
        name="branch_back",
    )(order, d_two, state, out_grad, *pieces)


def input_back(order, grad_mixed, pieces, block_in, grad_state):
    n, tok, columns = grad_mixed.shape

    def kernel(order_ref, gm_ref, *refs):
        parts = refs[:n]
        x_ref, grad_ref, out_ref, total, buffer, semaphores = refs[n:]
        step = pl.program_id(0)
        w = fetch_piece(parts, buffer, semaphores)
        term = nt(gm_ref[0], w)

        @pl.when(step == 0)
        def _():
            total[...] = term

        @pl.when(step > 0)
        def _():
            total[...] += term

        @pl.when(step == n - 1)
        def _():
            x = x_ref[...].astype(F32)
            scale = lax.rsqrt(jnp.mean(x * x, axis=-1, keepdims=True) + EPS)
            norm = x * scale
            d = total[...]
            out_ref[...] = grad_ref[...] + scale * (
                d - norm * jnp.mean(d * norm, axis=-1, keepdims=True)
            )

    whole = lambda s, order: (0, 0)
    return pl.pallas_call(
        kernel,
        grid_spec=pltpu.PrefetchScalarGridSpec(
            num_scalar_prefetch=1,
            grid=(n,),
            in_specs=[pl.BlockSpec((1, tok, columns), lambda s, order: (order[s], 0, 0))]
            + any_specs(pieces)
            + [pl.BlockSpec((tok, D), whole), pl.BlockSpec((tok, D), whole)],
            out_specs=pl.BlockSpec((tok, D), whole),
            scratch_shapes=[
                pltpu.VMEM((tok, D), F32),
                pltpu.VMEM((2, D, columns), BF),
                pltpu.SemaphoreType.DMA((2,)),
            ],
        ),
        out_shape=jax.ShapeDtypeStruct((tok, D), F32),
        compiler_params=pltpu.CompilerParams(vmem_limit_bytes=40 * MIB),
        cost_estimate=pl.CostEstimate(
            flops=2 * tok * D * columns * n, bytes_accessed=2 * D * columns * n, transcendentals=0
        ),
        name="input_back",
    )(order, grad_mixed, *pieces, block_in, grad_state)


def split_columns(weight, gain, n_ctx, n_dp, ff_rows):
    rows = weight.shape[0]
    ff = ff_rows * n_dp

    def kernel(w_ref, gain_ref, out_ref):
        gains = gain_ref[...]
        for part in range(2):
            for d in range(n_dp):
                for c in range(n_ctx):
                    at = part * FF + (d * n_ctx + c) * ff_rows
                    to = part * ff + d * ff_rows
                    values = w_ref[:, at : at + ff_rows].astype(F32) * gains
                    out_ref[c, :, to : to + ff_rows] = values.astype(BF)

    return pl.pallas_call(
        kernel,
        in_specs=[pl.BlockSpec(memory_space=pltpu.VMEM)] * 2,
        out_specs=pl.BlockSpec(memory_space=pltpu.VMEM),
        out_shape=jax.ShapeDtypeStruct((n_ctx, rows, 2 * ff), BF),
        compiler_params=pltpu.CompilerParams(vmem_limit_bytes=24 * MIB),
        cost_estimate=pl.CostEstimate(
            flops=weight.size, bytes_accessed=4 * weight.size, transcendentals=0
        ),
        name="split_columns",
    )(weight, gain)


def join_columns(sums, weight, gain, n_dp, ff_rows):
    n_ctx, rows, both = sums.shape
    ff = both // 2

    def kernel(s_ref, w_ref, gain_ref, out_ref, gain_out_ref):
        gains = gain_ref[...]
        total = jnp.zeros((rows, ff_rows), F32)
        for part in range(2):
            for d in range(n_dp):
                for c in range(n_ctx):
                    at = part * ff + d * ff_rows
                    to = part * FF + (d * n_ctx + c) * ff_rows
                    values = s_ref[c, :, at : at + ff_rows].astype(F32)
                    total = total + values * w_ref[:, to : to + ff_rows].astype(F32)
                    out_ref[:, to : to + ff_rows] = values * gains
        gain_out_ref[...] = jnp.sum(total, axis=1, keepdims=True)

    return pl.pallas_call(
        kernel,
        in_specs=[pl.BlockSpec(memory_space=pltpu.VMEM)] * 3,
        out_specs=[pl.BlockSpec(memory_space=pltpu.VMEM)] * 2,
        out_shape=[
            jax.ShapeDtypeStruct((rows, 2 * FF), F32),
            jax.ShapeDtypeStruct((rows, 1), F32),
        ],
        compiler_params=pltpu.CompilerParams(vmem_limit_bytes=24 * MIB),
        cost_estimate=pl.CostEstimate(
            flops=4 * weight.size, bytes_accessed=8 * weight.size, transcendentals=0
        ),
        name="join_columns",
    )(sums, weight, gain)


def lane_heads(rows, width):
    lane = lax.broadcasted_iota(jnp.int32, (rows, width), 1)
    return (lane % (width // 2)) // HALF


def attend_forward(starts, queries, keys, values_t, heads, tok):
    seq, width = queries.shape
    blocks = seq // tok

    def kernel(start_ref, q_ref, k_ref, v_ref, attn_ref, full_ref, lse_ref, scores):
        block = pl.program_id(0)
        start = start_ref[...]
        here = block * tok + lax.broadcasted_iota(jnp.int32, (1, tok), 1)
        head_of = lane_heads(tok, width)
        q = q_ref[...]
        q_heads = [jnp.where(head_of == h, q, jnp.zeros_like(q)) for h in range(heads)]

        def score(i, peaks):
            rows = pl.ds(pl.multiple_of(i * tok, tok), tok)
            k = k_ref[rows, :]
            there = i * tok + lax.broadcasted_iota(jnp.int32, (tok, tok), 0)
            visible = (there >= start) & (there <= here)
            out = []
            for h in range(heads):
                s = jnp.where(visible, nt(k, q_heads[h]), MASKED)
                scores[h, rows, :] = s
                out.append(jnp.maximum(peaks[h], jnp.max(s.reshape(tok // 8, 8, tok), axis=0)))
            return tuple(out)

        peaks = lax.fori_loop(
            0, block + 1, score, tuple(jnp.full((8, tok), MASKED, F32) for _ in range(heads))
        )
        peaks = [jnp.max(peak, axis=0, keepdims=True) for peak in peaks]

        def weigh(i, running):
            rows = pl.ds(pl.multiple_of(i * tok, tok), tok)
            v = v_ref[:, rows]
            out = []
            for h in range(heads):
                total, acc = running[h]
                p = jnp.exp(scores[h, rows, :] - peaks[h])
                total = total + jnp.sum(p.reshape(tok // 8, 8, tok), axis=0)
                out.append((total, acc + nn(v, p.astype(BF))))
            return tuple(out)

        result = lax.fori_loop(
            0,
            block + 1,
            weigh,
            tuple((jnp.zeros((8, tok), F32), jnp.zeros((HD, tok), F32)) for _ in range(heads)),
        )
        rows = []
        for h in range(heads):
            total, acc = result[h]
            total = jnp.sum(total, axis=0, keepdims=True)
            rows.append(acc / total)
            lse_ref[0, h : h + 1, :] = peaks[h] + jnp.log(total)
        full = jnp.concatenate(rows, axis=0).T
        full_ref[...] = full
        attn_ref[...] = full.astype(BF)

    return pl.pallas_call(
        kernel,
        grid=(blocks,),
        in_specs=[
            pl.BlockSpec((1, tok), lambda j: (0, j)),
            pl.BlockSpec((tok, width), lambda j: (j, 0)),
            pl.BlockSpec((seq, width), lambda j: (0, 0)),
            pl.BlockSpec((HD, seq), lambda j: (0, 0)),
        ],
        out_specs=[
            pl.BlockSpec((tok, width), lambda j: (j, 0)),
            pl.BlockSpec((tok, width), lambda j: (j, 0)),
            pl.BlockSpec((1, heads, tok), lambda j: (j, 0, 0)),
        ],
        scratch_shapes=[pltpu.VMEM((heads, seq, tok), F32)],
        out_shape=[
            jax.ShapeDtypeStruct((seq, width), BF),
            jax.ShapeDtypeStruct((seq, width), F32),
            jax.ShapeDtypeStruct((blocks, heads, tok), F32),
        ],
        compiler_params=pltpu.CompilerParams(vmem_limit_bytes=40 * MIB),
        cost_estimate=pl.CostEstimate(
            flops=2 * seq * seq * width * heads,
            bytes_accessed=12 * seq * width,
            transcendentals=seq * seq * heads // 2,
        ),
        name="attend_forward",
    )(starts, queries, keys, values_t)


def attend_backward(
    starts, queries, keys, keys_t, values, grads, full, lse, cosine, sine, unsplit, heads, tok
):
    seq, width = queries.shape
    blocks = seq // tok
    half = width // 2

    def kernel(
        start_ref, q_ref, k_ref, kt_ref, v_ref, g_ref, full_ref, lse_ref, cos_ref, sin_ref, unsplit_ref,
        out_ref, dk, dv,
    ):
        block = pl.program_id(0)

        @pl.when(block == 0)
        def _():
            dk[...] = jnp.zeros_like(dk)
            dv[...] = jnp.zeros_like(dv)

        start = start_ref[...]
        here = block * tok + lax.broadcasted_iota(jnp.int32, (1, tok), 1)
        head_of = lane_heads(tok, width)
        wide = lax.broadcasted_iota(jnp.int32, (tok, width), 1) // HD
        q = q_ref[...]
        g = g_ref[...]
        q_heads = [jnp.where(head_of == h, q, jnp.zeros_like(q)) for h in range(heads)]
        g_heads = [jnp.where(wide == h, g, jnp.zeros_like(g)) for h in range(heads)]
        q_stack = jnp.concatenate(q_heads, axis=0)
        g_stack = jnp.concatenate(g_heads, axis=0)
        picks = (
            lax.broadcasted_iota(jnp.int32, (8, width), 1) // HD
            == lax.broadcasted_iota(jnp.int32, (8, width), 0)
        ).astype(F32)
        deltas = lax.dot_general(
            picks,
            g.astype(F32) * full_ref[...],
            (((1,), (1,)), ((), ())),
            preferred_element_type=F32,
            precision=lax.Precision.HIGHEST,
        )

        def step(i, dq):
            rows = pl.ds(pl.multiple_of(i * tok, tok), tok)
            k = k_ref[rows, :]
            v = v_ref[rows, :]
            kt = kt_ref[:, rows]
            there = i * tok + lax.broadcasted_iota(jnp.int32, (tok, tok), 0)
            visible = (there >= start) & (there <= here)
            probs, grad_scores, out = [], [], []
            for h in range(heads):
                s = jnp.where(visible, nt(k, q_heads[h]), MASKED)
                p = jnp.exp(s - lse_ref[0, h : h + 1, :])
                ds = (p * (nt(v, g_heads[h]) - deltas[h : h + 1, :])).astype(BF)
                probs.append(p.astype(BF))
                grad_scores.append(ds)
                out.append(dq[h] + nn(kt, ds))
            dv[rows, :] += nn(jnp.concatenate(probs, axis=1), g_stack)
            dk[rows, :] += nn(jnp.concatenate(grad_scores, axis=1), q_stack)
            return tuple(out)

        dq = lax.fori_loop(
            0, block + 1, step, tuple(jnp.zeros((HD, tok), F32) for _ in range(heads))
        )
        dq = jnp.concatenate([x[:HALF] for x in dq] + [x[HALF:] for x in dq], axis=0).T
        here_rows = pl.ds(pl.multiple_of(block * tok, tok), tok)
        cos, sin = turn_tables(cos_ref[here_rows, :], sin_ref[here_rows, :], width)
        dq = (dq * cos - swap_halves(dq) * sin) * (HD**-0.5)
        out_ref[here_rows, :width] = nn(dq.astype(BF), unsplit_ref[...]).astype(BF)

        @pl.when(block == blocks - 1)
        def _():
            lane = lax.broadcasted_iota(jnp.int32, (width, 128), 0)
            column = lax.broadcasted_iota(jnp.int32, (width, 128), 1)
            fold_k = ((lane // half) * HALF + lane % HALF == column).astype(BF)
            fold_v = (lane % HD + HD == column).astype(BF)

            def fold(i, unused):
                rows = pl.ds(pl.multiple_of(i * tok, tok), tok)
                cos, sin = turn_tables(cos_ref[rows, :], sin_ref[rows, :], width)
                a = dk[rows, :]
                a = a * cos - swap_halves(a) * sin
                b = dv[rows, :]
                a_high = a.astype(BF)
                b_high = b.astype(BF)
                out_ref[rows, width:] = (
                    nn(a_high, fold_k)
                    + nn((a - a_high.astype(F32)).astype(BF), fold_k)
                    + nn(b_high, fold_v)
                    + nn((b - b_high.astype(F32)).astype(BF), fold_v)
                ).astype(BF)
                return unused

            lax.fori_loop(0, blocks, fold, 0)

    return pl.pallas_call(
        kernel,
        grid=(blocks,),
        in_specs=[
            pl.BlockSpec((1, tok), lambda j: (0, j)),
            pl.BlockSpec((tok, width), lambda j: (j, 0)),
            pl.BlockSpec((seq, width), lambda j: (0, 0)),
            pl.BlockSpec((HD, seq), lambda j: (0, 0)),
            pl.BlockSpec((seq, width), lambda j: (0, 0)),
            pl.BlockSpec((tok, width), lambda j: (j, 0)),
            pl.BlockSpec((tok, width), lambda j: (j, 0)),
            pl.BlockSpec((1, heads, tok), lambda j: (j, 0, 0)),
            pl.BlockSpec((seq, 128), lambda j: (0, 0)),
            pl.BlockSpec((seq, 128), lambda j: (0, 0)),
            pl.BlockSpec((width, width), lambda j: (0, 0)),
        ],
        out_specs=pl.BlockSpec((seq, width + 128), lambda j: (0, 0)),
        scratch_shapes=[pltpu.VMEM((seq, width), F32), pltpu.VMEM((seq, width), F32)],
        out_shape=jax.ShapeDtypeStruct((seq, width + 128), BF),
        compiler_params=pltpu.CompilerParams(vmem_limit_bytes=40 * MIB),
        cost_estimate=pl.CostEstimate(
            flops=5 * seq * seq * width * heads,
            bytes_accessed=16 * seq * width,
            transcendentals=seq * seq * heads // 2,
        ),
        name="attend_backward",
    )(starts, queries, keys, keys_t, values, grads, full, lse, cosine, sine, unsplit)


def outer_rows(activations, gradients):
    return lax.dot_general(
        activations, gradients, (((0,), (0,)), ((), ())), preferred_element_type=F32
    ).astype(BF)


def split_source(width):
    lane = np.arange(width)
    half = lane // (width // 2)
    head = (lane % (width // 2)) // HALF
    return head * HD + half * HALF + lane % HALF


def spread_matrix(width):
    matrix = np.zeros((width + 2 * HD, 3 * width), np.float32)
    lane = np.arange(width)
    matrix[split_source(width), lane] = 1
    matrix[width + (lane // (width // 2)) * HALF + lane % HALF, width + lane] = 1
    matrix[width + HD + lane % HD, 2 * width + lane] = 1
    return jnp.asarray(matrix, BF)


def unsplit_matrix(width):
    matrix = np.zeros((width, width), np.float32)
    matrix[np.arange(width), split_source(width)] = 1
    return jnp.asarray(matrix, BF)


def on_device(
    block_in,
    gain_attn,
    qkv_weight,
    out_weight,
    gain_ffn,
    gate_up_weight,
    down_weight,
    doc_lengths,
    out_grad,
):
    n_ctx = lax.axis_size("ctx")
    n_dp = lax.axis_size("dp")
    me = lax.axis_index("ctx")
    tok = block_in.shape[0]
    seq = tok * n_ctx
    heads = H // n_ctx
    width = heads * HD
    sharers = n_ctx // KVH
    rows = qkv_weight.shape[0]
    ff_rows = down_weight.shape[0]
    ff = ff_rows * n_dp
    columns = width + 2 * HD

    order = me ^ jnp.where(me % 2 == 0, *[jnp.asarray(t) for t in slot_table(n_ctx)])
    index = jnp.arange(seq, dtype=jnp.int32)
    lengths = doc_lengths[0]
    ends = jnp.cumsum(lengths)
    starts = jnp.sum((index[:, None] >= ends[None, :]).astype(jnp.int32) * lengths[None, :], axis=1)
    lane = jnp.arange(128, dtype=F32) % HALF
    frequency = 10000.0 ** (-lane * 2.0 / HD)
    angles = (index - starts).astype(F32)[:, None] * frequency[None, :]
    cosine = jnp.cos(angles)
    sine = jnp.sin(angles)
    starts_row = starts[None, :]

    gain_one = gain_attn.astype(F32)[:, None]
    gain_two = gain_ffn.astype(F32)[:, None]
    qkv = (qkv_weight.astype(F32) * gain_one).astype(BF)
    q_cols = qkv[:, : H * HD].reshape(rows, n_ctx, width).transpose(1, 0, 2)
    k_cols = qkv[:, H * HD : (H + KVH) * HD].reshape(rows, KVH, HD).transpose(1, 0, 2)
    v_cols = qkv[:, (H + KVH) * HD :].reshape(rows, KVH, HD).transpose(1, 0, 2)
    kv_cols = jnp.repeat(jnp.concatenate([k_cols, v_cols], axis=2), sharers, axis=0)
    qkv_own = exchange(jnp.concatenate([q_cols, kv_cols], axis=2)).reshape(n_ctx * rows, columns)
    qkv_part = gather_dp(qkv_own)

    hidden_in = block_in.astype(F32)
    rms_one = lax.rsqrt(jnp.mean(hidden_in * hidden_in, axis=-1, keepdims=True) + EPS)
    one_pieces = gather_slots((hidden_in * rms_one).astype(BF), n_ctx)

    owner_pairs = [(b, (b % n_dp) * n_ctx + b // n_dp) for b in range(n_dp * n_ctx)]
    out_part = gather_dp(lax.ppermute(out_weight, ("dp", "ctx"), owner_pairs))
    gate_up_cols = split_columns(gate_up_weight, gain_two, n_ctx, n_dp, ff_rows)
    gate_up_part = gather_dp(exchange(gate_up_cols).reshape(n_ctx * rows, 2 * ff))
    down_part = gather_dp(down_weight)

    queries, keys, values, keys_t, values_t, all_one = project_qkv(
        order, one_pieces, qkv_part, spread_matrix(width), cosine, sine, width, tok
    )
    grad_pieces = gather_slots(after(out_grad, one_pieces[-1]), n_ctx)
    out_pieces = gather_slots(out_part, n_ctx)
    attn, attended, lse = attend_forward(starts_row, queries, keys, values_t, heads, tok)
    state, norm_two = project_out(
        order, exchange(attn.reshape(n_ctx, tok, width)), out_pieces, block_in
    )

    two_pieces = gather_slots(norm_two, n_ctx)
    qkv_pieces = gather_slots(after(qkv_part, two_pieces[-1]), n_ctx)
    both, hidden, all_two = feed_forward(two_pieces, gate_up_part)
    all_grad = jnp.concatenate(grad_pieces, axis=0)
    down_sums = scatter_dp(outer_rows(hidden, all_grad))
    grad_gate_up = feed_backward(both, all_grad, down_part)

    def rows_of(x, lo, hi):
        return lax.slice_in_dim(x, lo * tok, hi * tok, axis=0)

    d_two = scatter_slots(
        lambda lo, hi: nt(rows_of(grad_gate_up, lo, hi), gate_up_part).astype(BF),
        lambda lo, hi: nt(rows_of(grad_gate_up, lo, hi), gate_up_part),
        tok,
        n_ctx,
    )
    gate_up_sums = scatter_dp(outer_rows(all_two, grad_gate_up))

    grad_state, grad_branch, grad_heads = branch_back(order, d_two, state, out_grad, out_pieces)
    grad_attn = exchange(grad_heads).reshape(seq, width)
    branch_pieces = gather_slots(after(grad_branch, grad_attn), n_ctx)
    grad_mixed = attend_backward(
        starts_row,
        queries,
        keys,
        keys_t,
        values,
        grad_attn,
        attended,
        lse,
        cosine,
        sine,
        unsplit_matrix(width),
        heads,
        tok,
    )
    all_branch = jnp.zeros((seq, D), BF)
    for slot, piece in enumerate(branch_pieces):
        all_branch = lax.dynamic_update_slice(all_branch, piece, (order[slot] * tok, 0))
    out_sums = scatter_dp(outer_rows(attn, all_branch))
    late_hidden = after(hidden, branch_pieces[-1])
    block_out = (
        state
        + scatter_slots(
            lambda lo, hi: nn(rows_of(late_hidden, lo, hi), down_part).astype(BF),
            lambda lo, hi: nn(rows_of(late_hidden, lo, hi), down_part),
            tok,
            n_ctx,
        )
    ).astype(BF)
    input_grad = input_back(
        order, exchange(grad_mixed.reshape(n_ctx, tok, columns)), qkv_pieces, block_in, grad_state
    )
    qkv_sums = scatter_dp(outer_rows(all_one, grad_mixed))

    down_weight_grad = down_sums.astype(F32)
    out_weight_grad = lax.ppermute(
        out_sums, ("dp", "ctx"), [(b, a) for a, b in owner_pairs]
    ).astype(F32)
    gate_up_weight_grad, gain_ffn_grad = join_columns(
        exchange(gate_up_sums.reshape(n_ctx, rows, 2 * ff)), gate_up_weight, gain_two, n_dp, ff_rows
    )
    qkv_back = exchange(qkv_sums.reshape(n_ctx, rows, columns)).astype(F32)
    q_back = qkv_back[:, :, :width].transpose(1, 0, 2).reshape(rows, H * HD)
    kv_back = jnp.sum(qkv_back[:, :, width:].reshape(KVH, sharers, rows, 2 * HD), axis=1)
    k_back = kv_back[:, :, :HD].transpose(1, 0, 2).reshape(rows, KVH * HD)
    v_back = kv_back[:, :, HD:].transpose(1, 0, 2).reshape(rows, KVH * HD)
    qkv_back = jnp.concatenate([q_back, k_back, v_back], axis=1)
    qkv_weight_grad = qkv_back * gain_one
    gain_attn_grad = jnp.sum(qkv_back * qkv_weight.astype(F32), axis=1)
    return (
        block_out,
        input_grad,
        gain_attn_grad,
        qkv_weight_grad,
        out_weight_grad,
        gain_ffn_grad[:, 0],
        gate_up_weight_grad,
        down_weight_grad,
    )


def solution(mesh):
    rows = P(("dp", "ctx"), None)
    entries = P(("dp", "ctx"))
    return jax.shard_map(
        on_device,
        mesh=mesh,
        in_specs=(rows, entries, rows, rows, entries, rows, rows, P("dp", None), rows),
        out_specs=(rows, rows, entries, rows, rows, entries, rows, rows),
        check_vma=False,
    )
```

```python
import jax
import jax.numpy as jnp
import numpy as np
from jax import lax
from jax.experimental import pallas as pl
from jax.experimental.pallas import tpu as pltpu
from jax.sharding import PartitionSpec as P

D = 2048
H = 32
KVH = 4
HD = 64
FF = 5632
HALF = HD // 2

EPS = 1e-05
MASKED = -1e30
BF = jnp.bfloat16
F32 = jnp.float32
VMEM_LIMIT = 60 << 20
LONG = pl.CostEstimate(flops=10**11, bytes_accessed=1 << 20, transcendentals=0)


def nt(a, b):
    return lax.dot_general(a, b, (((1,), (1,)), ((), ())), preferred_element_type=F32)


def nn(a, b):
    return jnp.dot(a, b, preferred_element_type=F32)


def after(x, *earlier):
    return lax.optimization_barrier((x, *earlier))[0]


def walk(n_ctx, parity):
    bits = []
    bit = 2
    while bit < n_ctx:
        bits.append(bit)
        bit *= 2
    return bits if parity == 0 else bits[::-1]


def swap_stage(x, n_ctx, stage):
    pairs = [(c, c ^ walk(n_ctx, c % 2)[stage]) for c in range(n_ctx)]
    return lax.ppermute(x, "ctx", pairs)


def swap_core(x, n_ctx):
    return lax.ppermute(x, "ctx", [(c, c ^ 1) for c in range(n_ctx)])


def slot_table(n_ctx):
    lists = []
    for parity in (0, 1):
        row = [0]
        for bit in walk(n_ctx, parity):
            row = row + [v ^ bit for v in row]
        lists.append(row)
    return np.array(
        [lists[p] + [v ^ 1 for v in lists[1 - p]] for p in (0, 1)], dtype=np.int32
    )


def gather_direct(x, n_ctx):
    return [x] + [swap_stage(x, n_ctx, stage) for stage in range(len(walk(n_ctx, 0)))]


def gather_rest(direct, n_ctx, *earlier):
    have = direct[:1]
    for stage in range(len(walk(n_ctx, 0))):
        passed = [after(block, *earlier) if earlier else block for block in have[1:]]
        have = have + [direct[stage + 1]] + [swap_stage(block, n_ctx, stage) for block in passed]
    return have + [swap_core(block, n_ctx) for block in have]


def gather_slots(x, n_ctx):
    return gather_rest(gather_direct(x, n_ctx), n_ctx)


def scatter_slots(send, keep, tok, n_ctx):
    mine = n_ctx // 2
    stages = len(walk(n_ctx, 0))
    totals = {}
    cut = mine // 2
    for lo, hi in ((cut, mine), (0, cut)):
        arrived = swap_core(send(mine + lo, mine + hi), n_ctx)
        totals[lo, hi] = keep(lo, hi) + arrived.astype(F32)
    upper, rest = pairs = totals[cut, mine], totals[0, cut]
    for stage in reversed(range(stages)):
        arrived = swap_stage(upper.astype(BF), n_ctx, stage).astype(F32)
        rest = rest + arrived
        half = rest.shape[0] // 2
        if stage:
            upper, rest = rest[half:], rest[:half]
    return rest, pairs


def exchange(x):
    return lax.all_to_all(x, "ctx", split_axis=0, concat_axis=0, tiled=False)


def gather_dp(x):
    return lax.all_gather(x, "dp", axis=0, tiled=True)


def scatter_dp(x):
    return lax.psum_scatter(x, "dp", scatter_dimension=0, tiled=True)


def deal_pairs(n_dp, n_ctx, turn):
    return [
        (b, (b + turn) % n_dp * n_ctx + b // n_dp) for b in range(n_dp * n_ctx)
    ]


def deal_out(x, n_dp, n_ctx):
    plane = lax.axis_index("dp")
    result = jnp.zeros((n_dp * x.shape[0], x.shape[1]), x.dtype)
    for turn in range(n_dp):
        block = lax.ppermute(x, ("dp", "ctx"), deal_pairs(n_dp, n_ctx, turn))
        at = (plane - turn) % n_dp * x.shape[0]
        result = lax.dynamic_update_slice(result, block, (at, 0))
    return result


def deal_back(x, n_dp, n_ctx):
    plane = lax.axis_index("dp")
    rows = x.shape[0] // n_dp
    total = 0.0
    for turn in range(n_dp):
        block = lax.dynamic_slice_in_dim(x, (plane - turn) % n_dp * rows, rows)
        pairs = [(b, a) for a, b in deal_pairs(n_dp, n_ctx, turn)]
        total = total + lax.ppermute(block, ("dp", "ctx"), pairs).astype(F32)
    return total


def sum_dp(x, n_dp, *earlier):
    plane = lax.axis_index("dp")
    rows = x.shape[0] // n_dp
    total = lax.dynamic_slice_in_dim(x, plane * rows, rows).astype(F32)
    for turn in range(1, n_dp):
        block = lax.dynamic_slice_in_dim(x, (plane + turn) % n_dp * rows, rows)
        pairs = [(d, (d + turn) % n_dp) for d in range(n_dp)]
        total = total + after(lax.ppermute(block, "dp", pairs), *earlier).astype(F32)
    return total


def fetch_piece(pieces, buffer, semaphores):
    step = pl.program_id(0)

    @pl.when(step == 0)
    def _():
        for i, piece in enumerate(pieces):
            pltpu.make_async_copy(piece, buffer.at[i], semaphores.at[i]).start()

    pltpu.make_async_copy(pieces[0], buffer.at[step], semaphores.at[step]).wait()
    return buffer[step]


def chunks(rows):
    return next(count for count in (8, 4, 2, 1) if rows % (16 * count) == 0)


def fetch_rows(source, buffer, semaphores):
    count = semaphores.shape[0]
    rows = source.shape[0] // count

    @pl.when(pl.program_id(0) == 0)
    def _():
        copies = [
            pltpu.make_async_copy(
                source.at[pl.ds(i * rows, rows)], buffer.at[pl.ds(i * rows, rows)], semaphores.at[i]
            )
            for i in range(count)
        ]
        for copy in copies:
            copy.start()
        for copy in copies:
            copy.wait()


def swap_halves(x):
    return pltpu.roll(x, x.shape[1] // 2, axis=1)


def turn_tables(cosine, sine, width):
    times = width // 128
    cosine = jnp.concatenate([cosine] * times, axis=1) if times > 1 else cosine
    sine = jnp.concatenate([sine] * times, axis=1) if times > 1 else sine
    lane = lax.broadcasted_iota(jnp.int32, sine.shape, 1)
    return cosine, jnp.where(lane < width // 2, -sine, sine)


def any_specs(pieces):
    return [pl.BlockSpec(memory_space=pltpu.HBM) for _ in pieces]


def project_qkv(order, pieces, weight, spread, cosine, sine, width, tok):
    n = len(pieces)
    seq = n * tok

    def kernel(order_ref, *refs):
        parts = refs[:n]
        w_hbm, spread_ref, cos_ref, sin_ref = refs[n : n + 4]
        q_ref, k_ref, v_ref, kt_ref, vt_ref, all_ref, wide, buffer, semaphores, w_ref, w_semaphores = refs[
            n + 4 :
        ]
        fetch_rows(w_hbm, w_ref, w_semaphores)

        @pl.when(pl.program_id(0) == 0)
        def _():
            wide[...] = nn(w_ref[...], spread_ref[...]).astype(BF)

        x = fetch_piece(parts, buffer, semaphores)
        all_ref[...] = x
        mixed = nn(x, wide[...])
        cos, sin = turn_tables(cos_ref[...], sin_ref[...], width)
        q = mixed[:, :width]
        k = mixed[:, width : 2 * width]
        v = mixed[:, 2 * width :].astype(BF)
        q_ref[...] = (q * cos + swap_halves(q) * sin).astype(BF) * (HD**-0.5)
        k = (k * cos + swap_halves(k) * sin).astype(BF)
        k_ref[...] = k
        v_ref[...] = v
        k_turned = k.T
        kt_ref[:HALF, :] = k_turned[:HALF]
        kt_ref[HALF:, :] = k_turned[width // 2 : width // 2 + HALF]
        vt_ref[...] = v.T[:HD]

    rows = lambda s, order: (order[s], 0)
    lanes = lambda s, order: (0, order[s])
    whole = lambda s, order: (0, 0)
    return pl.pallas_call(
        kernel,
        grid_spec=pltpu.PrefetchScalarGridSpec(
            num_scalar_prefetch=1,
            grid=(n,),
            in_specs=any_specs(pieces)
            + [
                pl.BlockSpec(memory_space=pltpu.HBM),
                pl.BlockSpec(spread.shape, whole),
                pl.BlockSpec((tok, 128), rows),
                pl.BlockSpec((tok, 128), rows),
            ],
            out_specs=[
                pl.BlockSpec((tok, width), rows),
                pl.BlockSpec((tok, width), rows),
                pl.BlockSpec((tok, width), rows),
                pl.BlockSpec((HD, tok), lanes),
                pl.BlockSpec((HD, tok), lanes),
                pl.BlockSpec((tok, D), rows),
            ],
            scratch_shapes=[
                pltpu.VMEM((D, 3 * width), BF),
                pltpu.VMEM((n, tok, D), BF),
                pltpu.SemaphoreType.DMA((n,)),
                pltpu.VMEM(weight.shape, BF),
                pltpu.SemaphoreType.DMA((chunks(D),)),
            ],
        ),
        out_shape=[
            jax.ShapeDtypeStruct((seq, width), BF),
            jax.ShapeDtypeStruct((seq, width), BF),
            jax.ShapeDtypeStruct((seq, width), BF),
            jax.ShapeDtypeStruct((HD, seq), BF),
            jax.ShapeDtypeStruct((HD, seq), BF),
            jax.ShapeDtypeStruct((seq, D), BF),
        ],
        compiler_params=pltpu.CompilerParams(vmem_limit_bytes=VMEM_LIMIT),
        cost_estimate=LONG,
        name="project_qkv",
    )(order, *pieces, weight, spread, cosine, sine)


def project_out(order, heads_in, pieces, residual):
    n, tok, width = heads_in.shape

    def kernel(order_ref, a_ref, *refs):
        parts = refs[:n]
        x_ref, state_ref, norm_ref, buffer, semaphores = refs[n:]
        step = pl.program_id(0)
        w = fetch_piece(parts, buffer, semaphores)

        @pl.when(step == 0)
        def _():
            state_ref[...] = x_ref[...].astype(F32)

        state_ref[...] += nn(a_ref[0], w)

        @pl.when(step == n - 1)
        def _():
            state = state_ref[...]
            scale = lax.rsqrt(jnp.mean(state * state, axis=-1, keepdims=True) + EPS)
            norm_ref[...] = (state * scale).astype(BF)

    whole = lambda s, order: (0, 0)
    return pl.pallas_call(
        kernel,
        grid_spec=pltpu.PrefetchScalarGridSpec(
            num_scalar_prefetch=1,
            grid=(n,),
            in_specs=[pl.BlockSpec((1, tok, width), lambda s, order: (order[s], 0, 0))]
            + any_specs(pieces)
            + [pl.BlockSpec((tok, D), whole)],
            out_specs=[pl.BlockSpec((tok, D), whole), pl.BlockSpec((tok, D), whole)],
            scratch_shapes=[
                pltpu.VMEM((n, width, D), BF),
                pltpu.SemaphoreType.DMA((n,)),
            ],
        ),
        out_shape=[
            jax.ShapeDtypeStruct((tok, D), F32),
            jax.ShapeDtypeStruct((tok, D), BF),
        ],
        compiler_params=pltpu.CompilerParams(vmem_limit_bytes=VMEM_LIMIT),
        cost_estimate=LONG,
        name="project_out",
    )(order, heads_in, *pieces, residual)


def feed_forward(pieces, weight):
    n = len(pieces)
    tok = pieces[0].shape[0]
    seq = n * tok
    ff = weight.shape[1] // 2

    def kernel(*refs):
        parts = refs[:n]
        w_hbm, both_ref, hidden_ref, all_ref, buffer, semaphores, w_ref, w_semaphores = refs[n:]
        fetch_rows(w_hbm, w_ref, w_semaphores)
        x = fetch_piece(parts, buffer, semaphores)
        all_ref[...] = x
        both = nn(x, w_ref[...])
        both_ref[...] = both
        gate = both[:, :ff]
        up = both[:, ff:]
        hidden_ref[...] = (gate * jax.nn.sigmoid(gate) * up).astype(BF)

    rows = lambda s: (s, 0)
    return pl.pallas_call(
        kernel,
        grid=(n,),
        in_specs=any_specs(pieces) + [pl.BlockSpec(memory_space=pltpu.HBM)],
        out_specs=[
            pl.BlockSpec((tok, 2 * ff), rows),
            pl.BlockSpec((tok, ff), rows),
            pl.BlockSpec((tok, D), rows),
        ],
        scratch_shapes=[
            pltpu.VMEM((n, tok, D), BF),
            pltpu.SemaphoreType.DMA((n,)),
            pltpu.VMEM(weight.shape, BF),
            pltpu.SemaphoreType.DMA((chunks(D),)),
        ],
        out_shape=[
            jax.ShapeDtypeStruct((seq, 2 * ff), F32),
            jax.ShapeDtypeStruct((seq, ff), BF),
            jax.ShapeDtypeStruct((seq, D), BF),
        ],
        compiler_params=pltpu.CompilerParams(vmem_limit_bytes=VMEM_LIMIT),
        cost_estimate=LONG,
        name="feed_forward",
    )(*pieces, weight)


def feed_backward(both, grads, weight):
    seq = both.shape[0]
    ff = weight.shape[0]
    tok = 256

    def kernel(both_ref, g_ref, w_hbm, out_ref, w_ref, w_semaphores):
        fetch_rows(w_hbm, w_ref, w_semaphores)
        grad_hidden = nt(g_ref[...], w_ref[...])
        both = both_ref[...]
        gate = both[:, :ff]
        up = both[:, ff:]
        sig = jax.nn.sigmoid(gate)
        out_ref[:, :ff] = (grad_hidden * up * sig * (1.0 + gate * (1.0 - sig))).astype(BF)
        out_ref[:, ff:] = (grad_hidden * (gate * sig)).astype(BF)

    rows = lambda s: (s, 0)
    return pl.pallas_call(
        kernel,
        grid=(seq // tok,),
        in_specs=[
            pl.BlockSpec((tok, 2 * ff), rows),
            pl.BlockSpec((tok, D), rows),
            pl.BlockSpec(memory_space=pltpu.HBM),
        ],
        out_specs=pl.BlockSpec((tok, 2 * ff), rows),
        scratch_shapes=[pltpu.VMEM(weight.shape, BF), pltpu.SemaphoreType.DMA((chunks(ff),))],
        out_shape=jax.ShapeDtypeStruct((seq, 2 * ff), BF),
        compiler_params=pltpu.CompilerParams(vmem_limit_bytes=VMEM_LIMIT),
        cost_estimate=LONG,
        name="feed_backward",
    )(both, grads, weight)


def branch_back(order, d_two, state, out_grad, pieces):
    n = len(pieces)
    tok = d_two.shape[0]
    width = pieces[0].shape[0]

    def kernel(order_ref, d_ref, state_ref, g_ref, *refs):
        parts = refs[:n]
        grad_ref, branch_ref, heads_ref, buffer, semaphores = refs[n:]

        @pl.when(pl.program_id(0) == 0)
        def _():
            state = state_ref[...]
            scale = lax.rsqrt(jnp.mean(state * state, axis=-1, keepdims=True) + EPS)
            norm = state * scale
            d = d_ref[...]
            grad = g_ref[...].astype(F32) + scale * (
                d - norm * jnp.mean(d * norm, axis=-1, keepdims=True)
            )
            grad_ref[...] = grad
            branch_ref[...] = grad.astype(BF)

        w = fetch_piece(parts, buffer, semaphores)
        heads_ref[0] = nt(branch_ref[...], w).astype(BF)

    whole = lambda s, order: (0, 0)
    return pl.pallas_call(
        kernel,
        grid_spec=pltpu.PrefetchScalarGridSpec(
            num_scalar_prefetch=1,
            grid=(n,),
            in_specs=[
                pl.BlockSpec((tok, D), whole),
                pl.BlockSpec((tok, D), whole),
                pl.BlockSpec((tok, D), whole),
            ]
            + any_specs(pieces),
            out_specs=[
                pl.BlockSpec((tok, D), whole),
                pl.BlockSpec((tok, D), whole),
                pl.BlockSpec((1, tok, width), lambda s, order: (order[s], 0, 0)),
            ],
            scratch_shapes=[
                pltpu.VMEM((n, width, D), BF),
                pltpu.SemaphoreType.DMA((n,)),
            ],
        ),
        out_shape=[
            jax.ShapeDtypeStruct((tok, D), F32),
            jax.ShapeDtypeStruct((tok, D), BF),
            jax.ShapeDtypeStruct((n, tok, width), BF),
        ],
        compiler_params=pltpu.CompilerParams(vmem_limit_bytes=VMEM_LIMIT),
        cost_estimate=LONG,
        name="branch_back",
    )(order, d_two, state, out_grad, *pieces)


def input_back(order, grad_mixed, pieces, block_in, grad_state):
    n, tok, columns = grad_mixed.shape

    def kernel(order_ref, gm_ref, *refs):
        parts = refs[:n]
        x_ref, grad_ref, out_ref, total, buffer, semaphores = refs[n:]
        step = pl.program_id(0)
        w = fetch_piece(parts, buffer, semaphores)
        term = nn(gm_ref[0], w)

        @pl.when(step == 0)
        def _():
            total[...] = term

        @pl.when(step > 0)
        def _():
            total[...] += term

        @pl.when(step == n - 1)
        def _():
            x = x_ref[...].astype(F32)
            scale = lax.rsqrt(jnp.mean(x * x, axis=-1, keepdims=True) + EPS)
            norm = x * scale
            d = total[...]
            out_ref[...] = grad_ref[...] + scale * (
                d - norm * jnp.mean(d * norm, axis=-1, keepdims=True)
            )

    whole = lambda s, order: (0, 0)
    return pl.pallas_call(
        kernel,
        grid_spec=pltpu.PrefetchScalarGridSpec(
            num_scalar_prefetch=1,
            grid=(n,),
            in_specs=[pl.BlockSpec((1, tok, columns), lambda s, order: (order[s], 0, 0))]
            + any_specs(pieces)
            + [pl.BlockSpec((tok, D), whole), pl.BlockSpec((tok, D), whole)],
            out_specs=pl.BlockSpec((tok, D), whole),
            scratch_shapes=[
                pltpu.VMEM((tok, D), F32),
                pltpu.VMEM((n, columns, D), BF),
                pltpu.SemaphoreType.DMA((n,)),
            ],
        ),
        out_shape=jax.ShapeDtypeStruct((tok, D), F32),
        compiler_params=pltpu.CompilerParams(vmem_limit_bytes=VMEM_LIMIT),
        cost_estimate=LONG,
        name="input_back",
    )(order, grad_mixed, *pieces, block_in, grad_state)


def split_columns(weight, gain, n_ctx, n_dp, ff_rows):
    rows = weight.shape[0]
    ff = ff_rows * n_dp

    def kernel(w_ref, gain_ref, out_ref):
        gains = gain_ref[...]
        for part in range(2):
            for d in range(n_dp):
                for c in range(n_ctx):
                    at = part * FF + (d * n_ctx + c) * ff_rows
                    to = part * ff + d * ff_rows
                    values = w_ref[:, at : at + ff_rows].astype(F32) * gains
                    out_ref[c, :, to : to + ff_rows] = values.astype(BF)

    return pl.pallas_call(
        kernel,
        in_specs=[pl.BlockSpec(memory_space=pltpu.VMEM)] * 2,
        out_specs=pl.BlockSpec(memory_space=pltpu.VMEM),
        out_shape=jax.ShapeDtypeStruct((n_ctx, rows, 2 * ff), BF),
        compiler_params=pltpu.CompilerParams(vmem_limit_bytes=VMEM_LIMIT),
        cost_estimate=LONG,
        name="split_columns",
    )(weight, gain)


def join_columns(sums, weight, gain, n_dp, ff_rows):
    n_ctx, rows, both = sums.shape
    ff = both // 2

    def kernel(s_ref, w_ref, gain_ref, out_ref, gain_out_ref):
        gains = gain_ref[...]
        total = jnp.zeros((rows, ff_rows), F32)
        for part in range(2):
            for d in range(n_dp):
                for c in range(n_ctx):
                    at = part * ff + d * ff_rows
                    to = part * FF + (d * n_ctx + c) * ff_rows
                    values = s_ref[c, :, at : at + ff_rows].astype(F32)
                    total = total + values * w_ref[:, to : to + ff_rows].astype(F32)
                    out_ref[:, to : to + ff_rows] = values * gains
        gain_out_ref[...] = jnp.sum(total, axis=1, keepdims=True)

    return pl.pallas_call(
        kernel,
        in_specs=[pl.BlockSpec(memory_space=pltpu.VMEM)] * 3,
        out_specs=[pl.BlockSpec(memory_space=pltpu.VMEM)] * 2,
        out_shape=[
            jax.ShapeDtypeStruct((rows, 2 * FF), F32),
            jax.ShapeDtypeStruct((rows, 1), F32),
        ],
        compiler_params=pltpu.CompilerParams(vmem_limit_bytes=VMEM_LIMIT),
        cost_estimate=LONG,
        name="join_columns",
    )(sums, weight, gain)


def lane_heads(rows, width):
    lane = lax.broadcasted_iota(jnp.int32, (rows, width), 1)
    return (lane % (width // 2)) // HALF


def attend_forward(starts, queries, keys, values_t, heads, tok):
    seq, width = queries.shape
    blocks = seq // tok

    def kernel(start_ref, q_ref, k_ref, v_ref, attn_ref, full_ref, lse_ref, scores):
        block = pl.program_id(0)
        start = start_ref[...]
        here = block * tok + lax.broadcasted_iota(jnp.int32, (1, tok), 1)
        head_of = lane_heads(tok, width)
        q = q_ref[...]
        q_heads = [jnp.where(head_of == h, q, jnp.zeros_like(q)) for h in range(heads)]

        def score(i, peaks):
            rows = pl.ds(pl.multiple_of(i * tok, tok), tok)
            k = k_ref[rows, :]
            there = i * tok + lax.broadcasted_iota(jnp.int32, (tok, tok), 0)
            visible = (there >= start) & (there <= here)
            out = []
            for h in range(heads):
                s = jnp.where(visible, nt(k, q_heads[h]), MASKED)
                scores[h, rows, :] = s
                out.append(jnp.maximum(peaks[h], jnp.max(s.reshape(tok // 8, 8, tok), axis=0)))
            return tuple(out)

        peaks = lax.fori_loop(
            0, block + 1, score, tuple(jnp.full((8, tok), MASKED, F32) for _ in range(heads))
        )
        peaks = [jnp.max(peak, axis=0, keepdims=True) for peak in peaks]

        def weigh(i, running):
            rows = pl.ds(pl.multiple_of(i * tok, tok), tok)
            v = v_ref[:, rows]
            out = []
            for h in range(heads):
                total, acc = running[h]
                p = jnp.exp(scores[h, rows, :] - peaks[h])
                total = total + jnp.sum(p.reshape(tok // 8, 8, tok), axis=0)
                out.append((total, acc + nn(v, p.astype(BF))))
            return tuple(out)

        result = lax.fori_loop(
            0,
            block + 1,
            weigh,
            tuple((jnp.zeros((8, tok), F32), jnp.zeros((HD, tok), F32)) for _ in range(heads)),
        )
        rows = []
        for h in range(heads):
            total, acc = result[h]
            total = jnp.sum(total, axis=0, keepdims=True)
            rows.append(acc / total)
            lse_ref[0, h : h + 1, :] = peaks[h] + jnp.log(total)
        full = jnp.concatenate(rows, axis=0).T
        full_ref[...] = full
        attn_ref[...] = full.astype(BF)

    return pl.pallas_call(
        kernel,
        grid=(blocks,),
        in_specs=[
            pl.BlockSpec((1, tok), lambda j: (0, j)),
            pl.BlockSpec((tok, width), lambda j: (j, 0)),
            pl.BlockSpec((seq, width), lambda j: (0, 0)),
            pl.BlockSpec((HD, seq), lambda j: (0, 0)),
        ],
        out_specs=[
            pl.BlockSpec((tok, width), lambda j: (j, 0)),
            pl.BlockSpec((tok, width), lambda j: (j, 0)),
            pl.BlockSpec((1, heads, tok), lambda j: (j, 0, 0)),
        ],
        scratch_shapes=[pltpu.VMEM((heads, seq, tok), F32)],
        out_shape=[
            jax.ShapeDtypeStruct((seq, width), BF),
            jax.ShapeDtypeStruct((seq, width), F32),
            jax.ShapeDtypeStruct((blocks, heads, tok), F32),
        ],
        compiler_params=pltpu.CompilerParams(vmem_limit_bytes=VMEM_LIMIT),
        cost_estimate=LONG,
        name="attend_forward",
    )(starts, queries, keys, values_t)


def attend_backward(
    starts, queries, keys, keys_t, values, grads, full, lse, cosine, sine, unsplit, heads, tok, first, count, carry
):
    seq, width = queries.shape
    blocks = seq // tok
    half = width // 2
    done = first * tok
    last = first + count == blocks

    def kernel(
        start_ref, q_ref, k_ref, kt_ref, v_ref, g_ref, full_ref, lse_ref, cos_ref, sin_ref, unsplit_ref, *refs
    ):
        if carry:
            old_q, old_dk, old_dv, out_ref, dk, dv = refs
        else:
            out_ref, dk, dv = refs
        block = first + pl.program_id(0)

        @pl.when(pl.program_id(0) == 0)
        def _():
            if carry:
                dk[:done, :] = old_dk[...]
                dv[:done, :] = old_dv[...]
                out_ref[:done, :width] = old_q[...]
            dk[done:, :] = jnp.zeros((dk.shape[0] - done, width), F32)
            dv[done:, :] = jnp.zeros((dk.shape[0] - done, width), F32)

        start = start_ref[...]
        here = block * tok + lax.broadcasted_iota(jnp.int32, (1, tok), 1)
        head_of = lane_heads(tok, width)
        wide = lax.broadcasted_iota(jnp.int32, (tok, width), 1) // HD
        q = q_ref[...]
        g = g_ref[...]
        q_heads = [jnp.where(head_of == h, q, jnp.zeros_like(q)) for h in range(heads)]
        g_heads = [jnp.where(wide == h, g, jnp.zeros_like(g)) for h in range(heads)]
        q_stack = jnp.concatenate(q_heads, axis=0)
        g_stack = jnp.concatenate(g_heads, axis=0)
        picks = (
            lax.broadcasted_iota(jnp.int32, (8, width), 1) // HD
            == lax.broadcasted_iota(jnp.int32, (8, width), 0)
        ).astype(F32)
        deltas = lax.dot_general(
            picks,
            g.astype(F32) * full_ref[...],
            (((1,), (1,)), ((), ())),
            preferred_element_type=F32,
            precision=lax.Precision.HIGHEST,
        )

        def step(i, dq):
            rows = pl.ds(pl.multiple_of(i * tok, tok), tok)
            k = k_ref[rows, :]
            v = v_ref[rows, :]
            kt = kt_ref[:, rows]
            there = i * tok + lax.broadcasted_iota(jnp.int32, (tok, tok), 0)
            visible = (there >= start) & (there <= here)
            probs, grad_scores, out = [], [], []
            for h in range(heads):
                s = jnp.where(visible, nt(k, q_heads[h]), MASKED)
                p = jnp.exp(s - lse_ref[0, h : h + 1, :])
                ds = (p * (nt(v, g_heads[h]) - deltas[h : h + 1, :])).astype(BF)
                probs.append(p.astype(BF))
                grad_scores.append(ds)
                out.append(dq[h] + nn(kt, ds))
            dv[rows, :] += nn(jnp.concatenate(probs, axis=1), g_stack)
            dk[rows, :] += nn(jnp.concatenate(grad_scores, axis=1), q_stack)
            return tuple(out)

        dq = lax.fori_loop(
            0, block + 1, step, tuple(jnp.zeros((HD, tok), F32) for _ in range(heads))
        )
        dq = jnp.concatenate([x[:HALF] for x in dq] + [x[HALF:] for x in dq], axis=0).T
        here_rows = pl.ds(pl.multiple_of(block * tok, tok), tok)
        cos, sin = turn_tables(cos_ref[here_rows, :], sin_ref[here_rows, :], width)
        dq = (dq * cos - swap_halves(dq) * sin) * (HD**-0.5)
        out_ref[here_rows, :width] = nn(dq.astype(BF), unsplit_ref[...]).astype(BF)

        if last:

            @pl.when(block == blocks - 1)
            def _():
                lane = lax.broadcasted_iota(jnp.int32, (width, 128), 0)
                column = lax.broadcasted_iota(jnp.int32, (width, 128), 1)
                fold_k = ((lane // half) * HALF + lane % HALF == column).astype(BF)
                fold_v = (lane % HD + HD == column).astype(BF)

                def fold(i, unused):
                    rows = pl.ds(pl.multiple_of(i * tok, tok), tok)
                    cos, sin = turn_tables(cos_ref[rows, :], sin_ref[rows, :], width)
                    a = dk[rows, :]
                    a = a * cos - swap_halves(a) * sin
                    b = dv[rows, :]
                    a_high = a.astype(BF)
                    b_high = b.astype(BF)
                    out_ref[rows, width:] = (
                        nn(a_high, fold_k)
                        + nn((a - a_high.astype(F32)).astype(BF), fold_k)
                        + nn(b_high, fold_v)
                        + nn((b - b_high.astype(F32)).astype(BF), fold_v)
                    ).astype(BF)
                    return unused

                lax.fori_loop(0, blocks, fold, 0)

    part = (first + count) * tok
    whole = lambda shape: pl.BlockSpec(shape, lambda j: (0, 0))
    if last:
        out_specs = whole((seq, width + 128))
        out_shape = jax.ShapeDtypeStruct((seq, width + 128), BF)
        scratch = [pltpu.VMEM((seq, width), F32), pltpu.VMEM((seq, width), F32)]
    else:
        out_specs = [whole((part, width))] * 3
        out_shape = [jax.ShapeDtypeStruct((part, width), t) for t in (BF, F32, F32)]
        scratch = []
    return pl.pallas_call(
        kernel,
        grid=(count,),
        in_specs=[
            pl.BlockSpec((1, tok), lambda j: (0, first + j)),
            pl.BlockSpec((tok, width), lambda j: (first + j, 0)),
            whole((seq, width)),
            whole((HD, seq)),
            whole((seq, width)),
            pl.BlockSpec((tok, width), lambda j: (first + j, 0)),
            pl.BlockSpec((tok, width), lambda j: (first + j, 0)),
            pl.BlockSpec((1, heads, tok), lambda j: (first + j, 0, 0)),
            whole((seq, 128)),
            whole((seq, 128)),
            whole((width, width)),
        ]
        + [whole((done, width))] * len(carry),
        out_specs=out_specs,
        scratch_shapes=scratch,
        out_shape=out_shape,
        compiler_params=pltpu.CompilerParams(vmem_limit_bytes=VMEM_LIMIT),
        cost_estimate=LONG,
        name="attend_backward",
    )(starts, queries, keys, keys_t, values, grads, full, lse, cosine, sine, unsplit, *carry)


def outer_rows(activations, gradients):
    return lax.dot_general(
        activations, gradients, (((0,), (0,)), ((), ())), preferred_element_type=F32
    ).astype(BF)


def split_source(width):
    lane = np.arange(width)
    half = lane // (width // 2)
    head = (lane % (width // 2)) // HALF
    return head * HD + half * HALF + lane % HALF


def spread_matrix(width):
    matrix = np.zeros((width + 2 * HD, 3 * width), np.float32)
    lane = np.arange(width)
    matrix[split_source(width), lane] = 1
    matrix[width + (lane // (width // 2)) * HALF + lane % HALF, width + lane] = 1
    matrix[width + HD + lane % HD, 2 * width + lane] = 1
    return jnp.asarray(matrix, BF)


def unsplit_matrix(width):
    matrix = np.zeros((width, width), np.float32)
    matrix[np.arange(width), split_source(width)] = 1
    return jnp.asarray(matrix, BF)


def on_device(
    block_in,
    gain_attn,
    qkv_weight,
    out_weight,
    gain_ffn,
    gate_up_weight,
    down_weight,
    doc_lengths,
    out_grad,
):
    n_ctx = lax.axis_size("ctx")
    n_dp = lax.axis_size("dp")
    me = lax.axis_index("ctx")
    tok = block_in.shape[0]
    seq = tok * n_ctx
    heads = H // n_ctx
    width = heads * HD
    sharers = n_ctx // KVH
    rows = qkv_weight.shape[0]
    ff_rows = down_weight.shape[0]
    ff = ff_rows * n_dp
    columns = width + 2 * HD

    order = me ^ jnp.where(me % 2 == 0, *[jnp.asarray(t) for t in slot_table(n_ctx)])
    index = jnp.arange(seq, dtype=jnp.int32)
    lengths = doc_lengths[0]
    ends = jnp.cumsum(lengths)
    starts = jnp.sum((index[:, None] >= ends[None, :]).astype(jnp.int32) * lengths[None, :], axis=1)
    lane = jnp.arange(128, dtype=F32) % HALF
    frequency = 10000.0 ** (-lane * 2.0 / HD)
    angles = (index - starts).astype(F32)[:, None] * frequency[None, :]
    cosine = jnp.cos(angles)
    sine = jnp.sin(angles)
    starts_row = starts[None, :]

    gain_one = gain_attn.astype(F32)[:, None]
    gain_two = gain_ffn.astype(F32)[:, None]
    qkv = (qkv_weight.astype(F32) * gain_one).astype(BF)
    q_cols = qkv[:, : H * HD].reshape(rows, n_ctx, width).transpose(1, 0, 2)
    k_cols = qkv[:, H * HD : (H + KVH) * HD].reshape(rows, KVH, HD).transpose(1, 0, 2)
    v_cols = qkv[:, (H + KVH) * HD :].reshape(rows, KVH, HD).transpose(1, 0, 2)
    kv_cols = jnp.repeat(jnp.concatenate([k_cols, v_cols], axis=2), sharers, axis=0)
    qkv_own = exchange(jnp.concatenate([q_cols, kv_cols], axis=2)).reshape(n_ctx * rows, columns)
    down_part = gather_dp(down_weight)
    qkv_part = gather_dp(after(qkv_own, down_part))

    hidden_in = block_in.astype(F32)
    rms_one = lax.rsqrt(jnp.mean(hidden_in * hidden_in, axis=-1, keepdims=True) + EPS)
    one_pieces = gather_slots(after((hidden_in * rms_one).astype(BF), qkv_own), n_ctx)

    out_part = deal_out(after(out_weight, one_pieces[1]), n_dp, n_ctx)
    gate_up_cols = split_columns(gate_up_weight, gain_two, n_ctx, n_dp, ff_rows)
    gate_up_own = exchange(after(gate_up_cols, *one_pieces[: n_ctx // 2])).reshape(
        n_ctx * rows, 2 * ff
    )
    gate_up_part = gather_dp(after(gate_up_own, qkv_part))
    grad_pieces = gather_slots(after(out_grad, *one_pieces[: n_ctx // 2]), n_ctx)

    queries, keys, values, keys_t, values_t, all_one = project_qkv(
        order, one_pieces, qkv_part, spread_matrix(width), after(cosine, *grad_pieces), sine, width, tok
    )
    out_pieces = gather_slots(out_part, n_ctx)
    attn, attended, lse = attend_forward(
        starts_row, after(queries, gate_up_own), keys, values_t, heads, tok
    )
    state, norm_two = project_out(
        order, exchange(attn.reshape(n_ctx, tok, width)), out_pieces, block_in
    )

    two_pieces = gather_slots(norm_two, n_ctx)
    both, hidden, all_two = feed_forward(two_pieces, gate_up_part)
    all_grad = jnp.concatenate(grad_pieces, axis=0)
    qkv_blocks = gather_direct(after(qkv_part.T, *two_pieces), n_ctx)
    down_terms = outer_rows(hidden, all_grad)
    down_sums = scatter_dp(down_terms)
    grad_gate_up = feed_backward(
        after(both, *qkv_blocks), all_grad, down_part
    )

    def rows_of(x, lo, hi):
        return lax.slice_in_dim(x, lo * tok, hi * tok, axis=0)

    d_two, _ = scatter_slots(
        lambda lo, hi: nt(rows_of(grad_gate_up, lo, hi), gate_up_part).astype(BF),
        lambda lo, hi: nt(rows_of(grad_gate_up, lo, hi), gate_up_part),
        tok,
        n_ctx,
    )
    gate_up_terms = outer_rows(all_two, grad_gate_up)
    gate_up_sums = scatter_dp(gate_up_terms)

    grad_state, grad_branch, grad_heads = branch_back(
        order, after(d_two, down_terms, gate_up_terms), state, out_grad, out_pieces
    )
    grad_attn = exchange(grad_heads).reshape(seq, width)
    branch_pieces = gather_slots(after(grad_branch, grad_attn), n_ctx)
    qkv_pieces = gather_rest(qkv_blocks, n_ctx, grad_attn)
    blocks = n_ctx
    early = blocks * 3 // 4

    def backward(grads, first, count, carry):
        return attend_backward(
            starts_row,
            queries,
            keys,
            keys_t,
            values,
            grads,
            attended,
            lse,
            cosine,
            sine,
            unsplit_matrix(width),
            heads,
            tok,
            first,
            count,
            carry,
        )

    carry = backward(grad_attn, 0, early, ())
    grad_mixed = backward(
        after(grad_attn, *branch_pieces[: n_ctx // 2 - 1]), early, blocks - early, tuple(carry)
    )
    all_branch = jnp.zeros((seq, D), BF)
    for slot, piece in enumerate(branch_pieces):
        all_branch = lax.dynamic_update_slice(all_branch, piece, (order[slot] * tok, 0))
    qkv_terms = outer_rows(all_one, grad_mixed)
    token_mixed = exchange(grad_mixed.reshape(n_ctx, tok, columns))
    out_terms = outer_rows(attn, after(all_branch, qkv_terms, token_mixed))
    late_hidden = after(hidden, out_terms)
    hidden_out, hidden_pairs = scatter_slots(
        lambda lo, hi: nn(rows_of(late_hidden, lo, hi), down_part).astype(BF),
        lambda lo, hi: nn(rows_of(late_hidden, lo, hi), down_part),
        tok,
        n_ctx,
    )
    block_out = (state + hidden_out).astype(BF)
    input_grad = input_back(order, token_mixed, qkv_pieces, block_in, grad_state)
    qkv_sums = sum_dp(qkv_terms, n_dp, input_grad, *hidden_pairs).astype(BF)

    down_weight_grad = after(down_sums, input_grad).astype(F32)
    out_weight_grad = deal_back(out_terms, n_dp, n_ctx)
    gate_up_weight_grad, gain_ffn_grad = join_columns(
        exchange(after(gate_up_sums, input_grad, *hidden_pairs).reshape(n_ctx, rows, 2 * ff)), gate_up_weight, gain_two, n_dp, ff_rows
    )
    qkv_back = exchange(qkv_sums.reshape(n_ctx, rows, columns)).astype(F32)
    q_back = qkv_back[:, :, :width].transpose(1, 0, 2).reshape(rows, H * HD)
    kv_back = jnp.sum(qkv_back[:, :, width:].reshape(KVH, sharers, rows, 2 * HD), axis=1)
    k_back = kv_back[:, :, :HD].transpose(1, 0, 2).reshape(rows, KVH * HD)
    v_back = kv_back[:, :, HD:].transpose(1, 0, 2).reshape(rows, KVH * HD)
    qkv_back = jnp.concatenate([q_back, k_back, v_back], axis=1)
    qkv_weight_grad = qkv_back * gain_one
    gain_attn_grad = jnp.sum(qkv_back * qkv_weight.astype(F32), axis=1)
    return (
        block_out,
        input_grad,
        gain_attn_grad,
        qkv_weight_grad,
        out_weight_grad,
        gain_ffn_grad[:, 0],
        gate_up_weight_grad,
        down_weight_grad,
    )


def solution(mesh):
    rows = P(("dp", "ctx"), None)
    entries = P(("dp", "ctx"))
    return jax.shard_map(
        on_device,
        mesh=mesh,
        in_specs=(rows, entries, rows, rows, entries, rows, rows, P("dp", None), rows),
        out_specs=(rows, rows, entries, rows, rows, entries, rows, rows),
        check_vma=False,
    )
```

```python
import jax
import jax.numpy as jnp
import numpy as np
from jax import lax
from jax.experimental import pallas as pl
from jax.experimental.pallas import tpu as pltpu
from jax.sharding import PartitionSpec as P

D = 2048
H = 32
KVH = 4
HD = 64
FF = 5632
HALF = HD // 2

EPS = 1e-05
MASKED = -1e30
BF = jnp.bfloat16
F32 = jnp.float32
VMEM_LIMIT = 60 << 20
LONG = pl.CostEstimate(flops=10**11, bytes_accessed=1 << 20, transcendentals=0)


def nt(a, b):
    return lax.dot_general(a, b, (((1,), (1,)), ((), ())), preferred_element_type=F32)


def nn(a, b):
    return jnp.dot(a, b, preferred_element_type=F32)


def after(x, *earlier):
    return lax.optimization_barrier((x, *earlier))[0]


def walk(n_ctx, parity):
    bits = []
    bit = 2
    while bit < n_ctx:
        bits.append(bit)
        bit *= 2
    return bits if parity == 0 else bits[::-1]


def swap_stage(x, n_ctx, stage):
    pairs = [(c, c ^ walk(n_ctx, c % 2)[stage]) for c in range(n_ctx)]
    return lax.ppermute(x, "ctx", pairs)


def swap_core(x, n_ctx):
    return lax.ppermute(x, "ctx", [(c, c ^ 1) for c in range(n_ctx)])


def slot_table(n_ctx):
    lists = []
    for parity in (0, 1):
        row = [0]
        for bit in walk(n_ctx, parity):
            row = row + [v ^ bit for v in row]
        lists.append(row)
    return np.array(
        [lists[p] + [v ^ 1 for v in lists[1 - p]] for p in (0, 1)], dtype=np.int32
    )


def gather_direct(x, n_ctx):
    return [x] + [swap_stage(x, n_ctx, stage) for stage in range(len(walk(n_ctx, 0)))]


def gather_rest(direct, n_ctx, *earlier):
    have = direct[:1]
    for stage in range(len(walk(n_ctx, 0))):
        passed = [after(block, *earlier) if earlier else block for block in have[1:]]
        have = have + [direct[stage + 1]] + [swap_stage(block, n_ctx, stage) for block in passed]
    return have + [swap_core(block, n_ctx) for block in have]


def gather_slots(x, n_ctx):
    return gather_rest(gather_direct(x, n_ctx), n_ctx)


def scatter_pairs(send, keep, n_ctx):
    return keep + swap_core(send, n_ctx).astype(F32)


def scatter_chips_first(total, n_ctx):
    half = total.shape[0] // 2
    last = len(walk(n_ctx, 0)) - 1
    return total[:half] + swap_stage(total[half:].astype(BF), n_ctx, last).astype(F32)


def scatter_chips(total, n_ctx, done=0):
    for stage in reversed(range(len(walk(n_ctx, 0)) - done)):
        half = total.shape[0] // 2
        total = total[:half] + swap_stage(total[half:].astype(BF), n_ctx, stage).astype(F32)
    return total


def exchange(x):
    return lax.all_to_all(x, "ctx", split_axis=0, concat_axis=0, tiled=False)


def gather_dp(x):
    return lax.all_gather(x, "dp", axis=0, tiled=True)


def scatter_dp(x):
    return lax.psum_scatter(x, "dp", scatter_dimension=0, tiled=True)


def deal_pairs(n_dp, n_ctx, turn):
    return [
        (b, (b + turn) % n_dp * n_ctx + b // n_dp) for b in range(n_dp * n_ctx)
    ]


def deal_out(x, n_dp, n_ctx):
    plane = lax.axis_index("dp")
    result = jnp.zeros((n_dp * x.shape[0], x.shape[1]), x.dtype)
    for turn in range(n_dp):
        block = lax.ppermute(x, ("dp", "ctx"), deal_pairs(n_dp, n_ctx, turn))
        at = (plane - turn) % n_dp * x.shape[0]
        result = lax.dynamic_update_slice(result, block, (at, 0))
    return result


def deal_back(x, n_dp, n_ctx):
    plane = lax.axis_index("dp")
    rows = x.shape[0] // n_dp
    total = 0.0
    for turn in range(n_dp):
        block = lax.dynamic_slice_in_dim(x, (plane - turn) % n_dp * rows, rows)
        pairs = [(b, a) for a, b in deal_pairs(n_dp, n_ctx, turn)]
        total = total + lax.ppermute(block, ("dp", "ctx"), pairs).astype(F32)
    return total


def sum_dp(x, n_dp, *earlier):
    plane = lax.axis_index("dp")
    rows = x.shape[0] // n_dp
    total = lax.dynamic_slice_in_dim(x, plane * rows, rows).astype(F32)
    for turn in range(1, n_dp):
        block = lax.dynamic_slice_in_dim(x, (plane + turn) % n_dp * rows, rows)
        pairs = [(d, (d + turn) % n_dp) for d in range(n_dp)]
        total = total + after(lax.ppermute(block, "dp", pairs), *earlier).astype(F32)
    return total


def fetch_piece(pieces, buffer, semaphores):
    step = pl.program_id(0)

    @pl.when(step == 0)
    def _():
        for i, piece in enumerate(pieces):
            pltpu.make_async_copy(piece, buffer.at[i], semaphores.at[i]).start()

    pltpu.make_async_copy(pieces[0], buffer.at[step], semaphores.at[step]).wait()
    return buffer[step]


def chunks(rows):
    return next(count for count in (8, 4, 2, 1) if rows % (16 * count) == 0)


def fetch_rows(source, buffer, semaphores):
    count = semaphores.shape[0]
    rows = source.shape[0] // count

    @pl.when(pl.program_id(0) == 0)
    def _():
        copies = [
            pltpu.make_async_copy(
                source.at[pl.ds(i * rows, rows)], buffer.at[pl.ds(i * rows, rows)], semaphores.at[i]
            )
            for i in range(count)
        ]
        for copy in copies:
            copy.start()
        for copy in copies:
            copy.wait()


def swap_halves(x):
    return pltpu.roll(x, x.shape[1] // 2, axis=1)


def turn_tables(cosine, sine, width):
    times = width // 128
    cosine = jnp.concatenate([cosine] * times, axis=1) if times > 1 else cosine
    sine = jnp.concatenate([sine] * times, axis=1) if times > 1 else sine
    lane = lax.broadcasted_iota(jnp.int32, sine.shape, 1)
    return cosine, jnp.where(lane < width // 2, -sine, sine)


def any_specs(pieces):
    return [pl.BlockSpec(memory_space=pltpu.HBM) for _ in pieces]


def project_qkv(order, pieces, weight, spread, cosine, sine, width, tok):
    n = len(pieces)
    seq = n * tok

    def kernel(order_ref, *refs):
        parts = refs[:n]
        w_hbm, spread_ref, cos_ref, sin_ref = refs[n : n + 4]
        q_ref, k_ref, v_ref, kt_ref, vt_ref, all_ref, wide, buffer, semaphores, w_ref, w_semaphores = refs[
            n + 4 :
        ]
        fetch_rows(w_hbm, w_ref, w_semaphores)

        @pl.when(pl.program_id(0) == 0)
        def _():
            wide[...] = nn(w_ref[...], spread_ref[...]).astype(BF)

        x = fetch_piece(parts, buffer, semaphores)
        all_ref[...] = x
        mixed = nn(x, wide[...])
        cos, sin = turn_tables(cos_ref[...], sin_ref[...], width)
        q = mixed[:, :width]
        k = mixed[:, width : 2 * width]
        v = mixed[:, 2 * width :].astype(BF)
        q_ref[...] = (q * cos + swap_halves(q) * sin).astype(BF) * (HD**-0.5)
        k = (k * cos + swap_halves(k) * sin).astype(BF)
        k_ref[...] = k
        v_ref[...] = v
        k_turned = k.T
        kt_ref[:HALF, :] = k_turned[:HALF]
        kt_ref[HALF:, :] = k_turned[width // 2 : width // 2 + HALF]
        vt_ref[...] = v.T[:HD]

    rows = lambda s, order: (order[s], 0)
    lanes = lambda s, order: (0, order[s])
    whole = lambda s, order: (0, 0)
    return pl.pallas_call(
        kernel,
        grid_spec=pltpu.PrefetchScalarGridSpec(
            num_scalar_prefetch=1,
            grid=(n,),
            in_specs=any_specs(pieces)
            + [
                pl.BlockSpec(memory_space=pltpu.HBM),
                pl.BlockSpec(spread.shape, whole),
                pl.BlockSpec((tok, 128), rows),
                pl.BlockSpec((tok, 128), rows),
            ],
            out_specs=[
                pl.BlockSpec((tok, width), rows),
                pl.BlockSpec((tok, width), rows),
                pl.BlockSpec((tok, width), rows),
                pl.BlockSpec((HD, tok), lanes),
                pl.BlockSpec((HD, tok), lanes),
                pl.BlockSpec((tok, D), lambda s, order: (s, 0)),
            ],
            scratch_shapes=[
                pltpu.VMEM((D, 3 * width), BF),
                pltpu.VMEM((n, tok, D), BF),
                pltpu.SemaphoreType.DMA((n,)),
                pltpu.VMEM(weight.shape, BF),
                pltpu.SemaphoreType.DMA((chunks(D),)),
            ],
        ),
        out_shape=[
            jax.ShapeDtypeStruct((seq, width), BF),
            jax.ShapeDtypeStruct((seq, width), BF),
            jax.ShapeDtypeStruct((seq, width), BF),
            jax.ShapeDtypeStruct((HD, seq), BF),
            jax.ShapeDtypeStruct((HD, seq), BF),
            jax.ShapeDtypeStruct((seq, D), BF),
        ],
        compiler_params=pltpu.CompilerParams(vmem_limit_bytes=VMEM_LIMIT),
        cost_estimate=LONG,
        name="project_qkv",
    )(order, *pieces, weight, spread, cosine, sine)


def project_out(order, heads_in, pieces, residual):
    n, tok, width = heads_in.shape

    def kernel(order_ref, a_ref, *refs):
        parts = refs[:n]
        x_ref, state_ref, norm_ref, buffer, semaphores = refs[n:]
        step = pl.program_id(0)
        w = fetch_piece(parts, buffer, semaphores)

        @pl.when(step == 0)
        def _():
            state_ref[...] = x_ref[...].astype(F32)

        state_ref[...] += nn(a_ref[0], w)

        @pl.when(step == n - 1)
        def _():
            state = state_ref[...]
            scale = lax.rsqrt(jnp.mean(state * state, axis=-1, keepdims=True) + EPS)
            norm_ref[...] = (state * scale).astype(BF)

    whole = lambda s, order: (0, 0)
    return pl.pallas_call(
        kernel,
        grid_spec=pltpu.PrefetchScalarGridSpec(
            num_scalar_prefetch=1,
            grid=(n,),
            in_specs=[pl.BlockSpec((1, tok, width), lambda s, order: (order[s], 0, 0))]
            + any_specs(pieces)
            + [pl.BlockSpec((tok, D), whole)],
            out_specs=[pl.BlockSpec((tok, D), whole), pl.BlockSpec((tok, D), whole)],
            scratch_shapes=[
                pltpu.VMEM((n, width, D), BF),
                pltpu.SemaphoreType.DMA((n,)),
            ],
        ),
        out_shape=[
            jax.ShapeDtypeStruct((tok, D), F32),
            jax.ShapeDtypeStruct((tok, D), BF),
        ],
        compiler_params=pltpu.CompilerParams(vmem_limit_bytes=VMEM_LIMIT),
        cost_estimate=LONG,
        name="project_out",
    )(order, heads_in, *pieces, residual)


def feed_both_ways(pieces, grad_pieces, weight, down, first, before):
    n = len(pieces)
    tok = pieces[0].shape[0]
    seq = 2 * n * tok
    ff = weight.shape[1] // 2
    term_type = F32 if before else BF

    def kernel(*refs):
        x_parts, g_parts = refs[:n], refs[n : 2 * n]
        w_hbm, down_hbm = refs[2 * n : 2 * n + 2]
        refs = refs[2 * n + 2 + len(before) :]
        term_ref, hidden_ref, both_ref, x_out, g_out = refs[:5]
        x_buffer, x_semaphores, g_buffer, g_semaphores, w_ref, w_semaphores, down_ref, down_semaphores = refs[5:]
        fetch_rows(w_hbm, w_ref, w_semaphores)
        x = fetch_piece(x_parts, x_buffer, x_semaphores)
        fetch_rows(down_hbm, down_ref, down_semaphores)
        g = fetch_piece(g_parts, g_buffer, g_semaphores)
        x_out[...] = x
        g_out[...] = g
        both = nn(x, w_ref[...])
        gate = both[:, :ff]
        up = both[:, ff:]
        sig = jax.nn.sigmoid(gate)
        silu = gate * sig
        hidden_ref[...] = (silu * up).astype(BF)
        grad_hidden = nt(g, down_ref[...])
        both_ref[:, :ff] = (grad_hidden * up * sig * (1.0 + gate * (1.0 - sig))).astype(BF)
        both_ref[:, ff:] = (grad_hidden * silu).astype(BF)
        term_ref[...] = nt(both_ref[...], w_ref[...]).astype(term_type)

    rows = lambda s: (first + s, 0)
    hbm = pl.BlockSpec(memory_space=pltpu.HBM)
    return pl.pallas_call(
        kernel,
        grid=(n,),
        in_specs=[hbm] * (2 * n + 2 + len(before)),
        out_specs=[
            pl.BlockSpec((tok, D), lambda s: (s, 0)),
            pl.BlockSpec((tok, ff), rows),
            pl.BlockSpec((tok, 2 * ff), rows),
            pl.BlockSpec((tok, D), rows),
            pl.BlockSpec((tok, D), rows),
        ],
        scratch_shapes=[
            pltpu.VMEM((n, tok, D), BF),
            pltpu.SemaphoreType.DMA((n,)),
            pltpu.VMEM((n, tok, D), BF),
            pltpu.SemaphoreType.DMA((n,)),
            pltpu.VMEM(weight.shape, BF),
            pltpu.SemaphoreType.DMA((chunks(D),)),
            pltpu.VMEM(down.shape, BF),
            pltpu.SemaphoreType.DMA((chunks(ff),)),
        ],
        out_shape=[
            jax.ShapeDtypeStruct((n * tok, D), term_type),
            jax.ShapeDtypeStruct((seq, ff), BF),
            jax.ShapeDtypeStruct((seq, 2 * ff), BF),
            jax.ShapeDtypeStruct((seq, D), BF),
            jax.ShapeDtypeStruct((seq, D), BF),
        ],
        input_output_aliases={2 * n + 2 + i: 1 + i for i in range(len(before))},
        compiler_params=pltpu.CompilerParams(vmem_limit_bytes=VMEM_LIMIT),
        cost_estimate=LONG,
        name="feed_both_ways",
    )(*pieces, *grad_pieces, weight, down, *before)


def branch_back(order, d_two, state, out_grad, pieces):
    n = len(pieces)
    tok = d_two.shape[0]
    width = pieces[0].shape[0]

    def kernel(order_ref, d_ref, state_ref, g_ref, *refs):
        parts = refs[:n]
        grad_ref, branch_ref, heads_ref, buffer, semaphores = refs[n:]

        @pl.when(pl.program_id(0) == 0)
        def _():
            state = state_ref[...]
            scale = lax.rsqrt(jnp.mean(state * state, axis=-1, keepdims=True) + EPS)
            norm = state * scale
            d = d_ref[...]
            grad = g_ref[...].astype(F32) + scale * (
                d - norm * jnp.mean(d * norm, axis=-1, keepdims=True)
            )
            grad_ref[...] = grad
            branch_ref[...] = grad.astype(BF)

        w = fetch_piece(parts, buffer, semaphores)
        heads_ref[0] = nt(branch_ref[...], w).astype(BF)

    whole = lambda s, order: (0, 0)
    return pl.pallas_call(
        kernel,
        grid_spec=pltpu.PrefetchScalarGridSpec(
            num_scalar_prefetch=1,
            grid=(n,),
            in_specs=[
                pl.BlockSpec((tok, D), whole),
                pl.BlockSpec((tok, D), whole),
                pl.BlockSpec((tok, D), whole),
            ]
            + any_specs(pieces),
            out_specs=[
                pl.BlockSpec((tok, D), whole),
                pl.BlockSpec((tok, D), whole),
                pl.BlockSpec((1, tok, width), lambda s, order: (order[s], 0, 0)),
            ],
            scratch_shapes=[
                pltpu.VMEM((n, width, D), BF),
                pltpu.SemaphoreType.DMA((n,)),
            ],
        ),
        out_shape=[
            jax.ShapeDtypeStruct((tok, D), F32),
            jax.ShapeDtypeStruct((tok, D), BF),
            jax.ShapeDtypeStruct((n, tok, width), BF),
        ],
        compiler_params=pltpu.CompilerParams(vmem_limit_bytes=VMEM_LIMIT),
        cost_estimate=LONG,
        name="branch_back",
    )(order, d_two, state, out_grad, *pieces)


def split_columns(weight, gain, n_ctx, n_dp, ff_rows):
    rows = weight.shape[0]
    ff = ff_rows * n_dp

    def kernel(w_ref, gain_ref, out_ref):
        gains = gain_ref[...]
        for part in range(2):
            for d in range(n_dp):
                for c in range(n_ctx):
                    at = part * FF + (d * n_ctx + c) * ff_rows
                    to = part * ff + d * ff_rows
                    values = w_ref[:, at : at + ff_rows].astype(F32) * gains
                    out_ref[c, :, to : to + ff_rows] = values.astype(BF)

    return pl.pallas_call(
        kernel,
        in_specs=[pl.BlockSpec(memory_space=pltpu.VMEM)] * 2,
        out_specs=pl.BlockSpec(memory_space=pltpu.VMEM),
        out_shape=jax.ShapeDtypeStruct((n_ctx, rows, 2 * ff), BF),
        compiler_params=pltpu.CompilerParams(vmem_limit_bytes=VMEM_LIMIT),
        cost_estimate=LONG,
        name="split_columns",
    )(weight, gain)


def join_columns(sums, weight, gain, n_dp, ff_rows):
    n_ctx, rows, both = sums.shape
    ff = both // 2

    def kernel(s_ref, w_ref, gain_ref, out_ref, gain_out_ref):
        gains = gain_ref[...]
        total = jnp.zeros((rows, ff_rows), F32)
        for part in range(2):
            for d in range(n_dp):
                for c in range(n_ctx):
                    at = part * ff + d * ff_rows
                    to = part * FF + (d * n_ctx + c) * ff_rows
                    values = s_ref[c, :, at : at + ff_rows].astype(F32)
                    total = total + values * w_ref[:, to : to + ff_rows].astype(F32)
                    out_ref[:, to : to + ff_rows] = values * gains
        gain_out_ref[...] = jnp.sum(total, axis=1, keepdims=True)

    return pl.pallas_call(
        kernel,
        in_specs=[pl.BlockSpec(memory_space=pltpu.VMEM)] * 3,
        out_specs=[pl.BlockSpec(memory_space=pltpu.VMEM)] * 2,
        out_shape=[
            jax.ShapeDtypeStruct((rows, 2 * FF), F32),
            jax.ShapeDtypeStruct((rows, 1), F32),
        ],
        compiler_params=pltpu.CompilerParams(vmem_limit_bytes=VMEM_LIMIT),
        cost_estimate=LONG,
        name="join_columns",
    )(sums, weight, gain)


def lane_heads(rows, width):
    lane = lax.broadcasted_iota(jnp.int32, (rows, width), 1)
    return (lane % (width // 2)) // HALF


def attend_forward(starts, queries, keys, values_t, heads, tok):
    seq, width = queries.shape
    blocks = seq // tok

    def kernel(start_ref, q_ref, k_ref, v_ref, attn_ref, full_ref, lse_ref, scores):
        block = pl.program_id(0)
        start = start_ref[...]
        here = block * tok + lax.broadcasted_iota(jnp.int32, (1, tok), 1)
        head_of = lane_heads(tok, width)
        q = q_ref[...]
        q_heads = [jnp.where(head_of == h, q, jnp.zeros_like(q)) for h in range(heads)]

        def score(i, peaks):
            rows = pl.ds(pl.multiple_of(i * tok, tok), tok)
            k = k_ref[rows, :]
            there = i * tok + lax.broadcasted_iota(jnp.int32, (tok, tok), 0)
            visible = (there >= start) & (there <= here)
            out = []
            for h in range(heads):
                s = jnp.where(visible, nt(k, q_heads[h]), MASKED)
                scores[h, rows, :] = s
                out.append(jnp.maximum(peaks[h], jnp.max(s.reshape(tok // 8, 8, tok), axis=0)))
            return tuple(out)

        peaks = lax.fori_loop(
            0, block + 1, score, tuple(jnp.full((8, tok), MASKED, F32) for _ in range(heads))
        )
        peaks = [jnp.max(peak, axis=0, keepdims=True) for peak in peaks]

        def weigh(i, running):
            rows = pl.ds(pl.multiple_of(i * tok, tok), tok)
            v = v_ref[:, rows]
            out = []
            for h in range(heads):
                total, acc = running[h]
                p = jnp.exp(scores[h, rows, :] - peaks[h])
                total = total + jnp.sum(p.reshape(tok // 8, 8, tok), axis=0)
                out.append((total, acc + nn(v, p.astype(BF))))
            return tuple(out)

        result = lax.fori_loop(
            0,
            block + 1,
            weigh,
            tuple((jnp.zeros((8, tok), F32), jnp.zeros((HD, tok), F32)) for _ in range(heads)),
        )
        rows = []
        for h in range(heads):
            total, acc = result[h]
            total = jnp.sum(total, axis=0, keepdims=True)
            rows.append(acc / total)
            lse_ref[0, h : h + 1, :] = peaks[h] + jnp.log(total)
        full = jnp.concatenate(rows, axis=0).T
        full_ref[...] = full
        attn_ref[...] = full.astype(BF)

    return pl.pallas_call(
        kernel,
        grid=(blocks,),
        in_specs=[
            pl.BlockSpec((1, tok), lambda j: (0, j)),
            pl.BlockSpec((tok, width), lambda j: (j, 0)),
            pl.BlockSpec((seq, width), lambda j: (0, 0)),
            pl.BlockSpec((HD, seq), lambda j: (0, 0)),
        ],
        out_specs=[
            pl.BlockSpec((tok, width), lambda j: (j, 0)),
            pl.BlockSpec((tok, width), lambda j: (j, 0)),
            pl.BlockSpec((1, heads, tok), lambda j: (j, 0, 0)),
        ],
        scratch_shapes=[pltpu.VMEM((heads, seq, tok), F32)],
        out_shape=[
            jax.ShapeDtypeStruct((seq, width), BF),
            jax.ShapeDtypeStruct((seq, width), F32),
            jax.ShapeDtypeStruct((blocks, heads, tok), F32),
        ],
        compiler_params=pltpu.CompilerParams(vmem_limit_bytes=VMEM_LIMIT),
        cost_estimate=LONG,
        name="attend_forward",
    )(starts, queries, keys, values_t)


def attend_backward(
    slot_of, starts, queries, keys, keys_t, values, grads, full, lse, cosine, sine, unsplit, heads, tok, mine, carry
):
    seq, width = queries.shape
    blocks = seq // tok
    half = width // 2

    def kernel(
        slot_ref, start_ref, q_ref, k_ref, kt_ref, v_ref, g_ref, full_ref, lse_ref, cos_ref, sin_ref, unsplit_ref, *refs
    ):
        if carry:
            old_q, old_kv, out_ref, dk, dv = refs
        else:
            out_ref, kv_ref, dk, dv = refs
        block = pl.program_id(0)

        @pl.when(block == 0)
        def _():
            dk[...] = jnp.zeros_like(dk)
            dv[...] = jnp.zeros_like(dv)

        start = start_ref[...]
        here = block * tok + lax.broadcasted_iota(jnp.int32, (1, tok), 1)
        head_of = lane_heads(tok, width)
        wide = lax.broadcasted_iota(jnp.int32, (tok, width), 1) // HD
        q = q_ref[...]
        g = g_ref[...]
        q_heads = [jnp.where(head_of == h, q, jnp.zeros_like(q)) for h in mine]
        g_heads = [jnp.where(wide == h, g, jnp.zeros_like(g)) for h in mine]
        q_stack = jnp.concatenate(q_heads, axis=0)
        g_stack = jnp.concatenate(g_heads, axis=0)
        picks = (
            lax.broadcasted_iota(jnp.int32, (8, width), 1) // HD
            == lax.broadcasted_iota(jnp.int32, (8, width), 0)
        ).astype(F32)
        deltas = lax.dot_general(
            picks,
            g.astype(F32) * full_ref[...],
            (((1,), (1,)), ((), ())),
            preferred_element_type=F32,
            precision=lax.Precision.HIGHEST,
        )

        def step(i, dq):
            rows = pl.ds(pl.multiple_of(i * tok, tok), tok)
            k = k_ref[rows, :]
            v = v_ref[rows, :]
            kt = kt_ref[:, rows]
            there = i * tok + lax.broadcasted_iota(jnp.int32, (tok, tok), 0)
            visible = (there >= start) & (there <= here)
            probs, grad_scores, out = [], [], []
            for at, h in enumerate(mine):
                s = jnp.where(visible, nt(k, q_heads[at]), MASKED)
                p = jnp.exp(s - lse_ref[0, h : h + 1, :])
                ds = (p * (nt(v, g_heads[at]) - deltas[h : h + 1, :])).astype(BF)
                probs.append(p.astype(BF))
                grad_scores.append(ds)
                out.append(dq[at] + nn(kt, ds))
            dv[rows, :] += nn(jnp.concatenate(probs, axis=1), g_stack)
            dk[rows, :] += nn(jnp.concatenate(grad_scores, axis=1), q_stack)
            return tuple(out)

        dq = lax.fori_loop(
            0, block + 1, step, tuple(jnp.zeros((HD, tok), F32) for _ in mine)
        )
        zero = jnp.zeros((HALF, tok), F32)
        lower = [dq[mine.index(h)][:HALF] if h in mine else zero for h in range(heads)]
        upper = [dq[mine.index(h)][HALF:] if h in mine else zero for h in range(heads)]
        dq = jnp.concatenate(lower + upper, axis=0).T
        here_rows = pl.ds(pl.multiple_of(block * tok, tok), tok)
        cos, sin = turn_tables(cos_ref[here_rows, :], sin_ref[here_rows, :], width)
        dq = (dq * cos - swap_halves(dq) * sin) * (HD**-0.5)
        dq = nn(dq.astype(BF), unsplit_ref[...]).astype(BF)
        if carry:
            slot_rows = pl.ds(pl.multiple_of(slot_ref[block] * tok, tok), tok)
            out_ref[slot_rows, :width] = old_q[here_rows, :] + dq
        else:
            out_ref[here_rows, :] = dq

        @pl.when(block == blocks - 1)
        def _():
            lane = lax.broadcasted_iota(jnp.int32, (width, 128), 0)
            column = lax.broadcasted_iota(jnp.int32, (width, 128), 1)
            fold_k = ((lane // half) * HALF + lane % HALF == column).astype(BF)
            fold_v = (lane % HD + HD == column).astype(BF)

            def fold(i, unused):
                rows = pl.ds(pl.multiple_of(i * tok, tok), tok)
                cos, sin = turn_tables(cos_ref[rows, :], sin_ref[rows, :], width)
                a = dk[rows, :]
                a = a * cos - swap_halves(a) * sin
                b = dv[rows, :]
                a_high = a.astype(BF)
                b_high = b.astype(BF)
                terms = (
                    nn(a_high, fold_k)
                    + nn((a - a_high.astype(F32)).astype(BF), fold_k)
                    + nn(b_high, fold_v)
                    + nn((b - b_high.astype(F32)).astype(BF), fold_v)
                )
                if carry:
                    slot_rows = pl.ds(pl.multiple_of(slot_ref[i] * tok, tok), tok)
                    out_ref[slot_rows, width:] = (old_kv[rows, :] + terms).astype(BF)
                else:
                    kv_ref[rows, :] = terms
                return unused

            lax.fori_loop(0, blocks, fold, 0)

    whole = lambda shape: pl.BlockSpec(shape, lambda j, *_: (0, 0))
    if carry:
        out_specs = whole((seq, width + 128))
        out_shape = jax.ShapeDtypeStruct((seq, width + 128), BF)
    else:
        out_specs = [whole((seq, width)), whole((seq, 128))]
        out_shape = [
            jax.ShapeDtypeStruct((seq, width), BF),
            jax.ShapeDtypeStruct((seq, 128), F32),
        ]
    return pl.pallas_call(
        kernel,
        grid_spec=pltpu.PrefetchScalarGridSpec(
            num_scalar_prefetch=1,
            grid=(blocks,),
            in_specs=[
            pl.BlockSpec((1, tok), lambda j, *_: (0, j)),
            pl.BlockSpec((tok, width), lambda j, *_: (j, 0)),
            whole((seq, width)),
            whole((HD, seq)),
            whole((seq, width)),
            pl.BlockSpec((tok, width), lambda j, *_: (j, 0)),
            pl.BlockSpec((tok, width), lambda j, *_: (j, 0)),
            pl.BlockSpec((1, heads, tok), lambda j, *_: (j, 0, 0)),
            whole((seq, 128)),
            whole((seq, 128)),
            whole((width, width)),
        ]
        + [whole((seq, width)), whole((seq, 128))][: len(carry)],
            out_specs=out_specs,
            scratch_shapes=[pltpu.VMEM((seq, width), F32), pltpu.VMEM((seq, width), F32)],
        ),
        out_shape=out_shape,
        compiler_params=pltpu.CompilerParams(vmem_limit_bytes=VMEM_LIMIT),
        cost_estimate=LONG,
        name="attend_backward",
    )(slot_of, starts, queries, keys, keys_t, values, grads, full, lse, cosine, sine, unsplit, *carry)


def outer_rows(activations, gradients):
    return lax.dot_general(
        activations, gradients, (((0,), (0,)), ((), ())), preferred_element_type=F32
    ).astype(BF)


def split_source(width):
    lane = np.arange(width)
    half = lane // (width // 2)
    head = (lane % (width // 2)) // HALF
    return head * HD + half * HALF + lane % HALF


def spread_matrix(width):
    matrix = np.zeros((width + 2 * HD, 3 * width), np.float32)
    lane = np.arange(width)
    matrix[split_source(width), lane] = 1
    matrix[width + (lane // (width // 2)) * HALF + lane % HALF, width + lane] = 1
    matrix[width + HD + lane % HD, 2 * width + lane] = 1
    return jnp.asarray(matrix, BF)


def unsplit_matrix(width):
    matrix = np.zeros((width, width), np.float32)
    matrix[np.arange(width), split_source(width)] = 1
    return jnp.asarray(matrix, BF)


def on_device(
    block_in,
    gain_attn,
    qkv_weight,
    out_weight,
    gain_ffn,
    gate_up_weight,
    down_weight,
    doc_lengths,
    out_grad,
):
    n_ctx = lax.axis_size("ctx")
    n_dp = lax.axis_size("dp")
    me = lax.axis_index("ctx")
    tok = block_in.shape[0]
    seq = tok * n_ctx
    heads = H // n_ctx
    width = heads * HD
    sharers = n_ctx // KVH
    rows = qkv_weight.shape[0]
    ff_rows = down_weight.shape[0]
    ff = ff_rows * n_dp
    columns = width + 2 * HD

    order = me ^ jnp.where(me % 2 == 0, *[jnp.asarray(t) for t in slot_table(n_ctx)])
    slots = jnp.arange(n_ctx, dtype=jnp.int32)
    slot_of = jnp.sum(jnp.where(order[None, :] == slots[:, None], slots[None, :], 0), axis=1)
    index = jnp.arange(seq, dtype=jnp.int32)
    lengths = doc_lengths[0]
    ends = jnp.cumsum(lengths)
    starts = jnp.sum((index[:, None] >= ends[None, :]).astype(jnp.int32) * lengths[None, :], axis=1)
    lane = jnp.arange(128, dtype=F32) % HALF
    frequency = 10000.0 ** (-lane * 2.0 / HD)
    angles = (index - starts).astype(F32)[:, None] * frequency[None, :]
    cosine = jnp.cos(angles)
    sine = jnp.sin(angles)
    starts_row = starts[None, :]

    gain_one = gain_attn.astype(F32)[:, None]
    gain_two = gain_ffn.astype(F32)[:, None]
    qkv = (qkv_weight.astype(F32) * gain_one).astype(BF)
    q_cols = qkv[:, : H * HD].reshape(rows, n_ctx, width).transpose(1, 0, 2)
    k_cols = qkv[:, H * HD : (H + KVH) * HD].reshape(rows, KVH, HD).transpose(1, 0, 2)
    v_cols = qkv[:, (H + KVH) * HD :].reshape(rows, KVH, HD).transpose(1, 0, 2)
    kv_cols = jnp.repeat(jnp.concatenate([k_cols, v_cols], axis=2), sharers, axis=0)
    qkv_own = exchange(jnp.concatenate([q_cols, kv_cols], axis=2)).reshape(n_ctx * rows, columns)
    qkv_part = gather_dp(qkv_own)
    down_part = gather_dp(after(down_weight, qkv_part))

    hidden_in = block_in.astype(F32)
    rms_one = lax.rsqrt(jnp.mean(hidden_in * hidden_in, axis=-1, keepdims=True) + EPS)
    one_pieces = gather_slots(after((hidden_in * rms_one).astype(BF), qkv_own), n_ctx)

    owner_pairs = deal_pairs(n_dp, n_ctx, 0)
    out_own = lax.ppermute(after(out_weight, one_pieces[1]), ("dp", "ctx"), owner_pairs)
    out_part = gather_dp(after(out_own, qkv_part))
    gate_up_cols = split_columns(gate_up_weight, gain_two, n_ctx, n_dp, ff_rows)
    gate_up_own = exchange(after(gate_up_cols, *one_pieces[: n_ctx // 2])).reshape(
        n_ctx * rows, 2 * ff
    )
    gate_up_part = gather_dp(gate_up_own)

    queries, keys, values, keys_t, values_t, all_one = project_qkv(
        order, one_pieces, qkv_part, spread_matrix(width), cosine, sine, width, tok
    )
    out_pieces = gather_slots(out_part, n_ctx)
    attn, attended, lse = attend_forward(
        starts_row, after(queries, gate_up_own), keys, values_t, heads, tok
    )
    state, norm_two = project_out(
        order, exchange(attn.reshape(n_ctx, tok, width)), out_pieces, block_in
    )

    two_pieces = gather_slots(norm_two, n_ctx)
    grad_pieces = gather_slots(after(out_grad, *two_pieces), n_ctx)
    half = n_ctx // 2
    send, *rest = feed_both_ways(
        two_pieces[half:], grad_pieces[half:], gate_up_part, down_part, half, ()
    )
    keep, hidden, grad_gate_up, all_two, all_grad = feed_both_ways(
        two_pieces[:half], grad_pieces[:half], gate_up_part, down_part, 0, tuple(rest)
    )
    d_two = scatter_chips(scatter_pairs(send, keep, n_ctx), n_ctx)
    down_terms = outer_rows(hidden, all_grad)
    down_sums = scatter_dp(down_terms)
    gate_up_terms = outer_rows(all_two, grad_gate_up)
    gate_up_sums = scatter_dp(gate_up_terms)
    mid = half * tok
    hidden_terms = scatter_pairs(
        nn(hidden[mid:], down_part).astype(BF), nn(hidden[:mid], down_part), n_ctx
    )

    grad_state, grad_branch, grad_heads = branch_back(
        order, after(d_two, down_terms, gate_up_terms, hidden_terms), state, out_grad, out_pieces
    )
    grad_attn = exchange(grad_heads).reshape(seq, width)
    branch_pieces = gather_slots(after(grad_branch, grad_attn), n_ctx)
    hidden_half = scatter_chips_first(after(hidden_terms, grad_attn), n_ctx)

    def backward(grads, mine, carry):
        return attend_backward(
            slot_of,
            starts_row,
            queries,
            keys,
            keys_t,
            values,
            grads,
            attended,
            lse,
            cosine,
            sine,
            unsplit_matrix(width),
            heads,
            tok,
            mine,
            carry,
        )

    carry = backward(grad_attn, range(heads // 2), ())
    grad_mixed = backward(
        after(grad_attn, *branch_pieces[:3], hidden_half), range(heads // 2, heads), tuple(carry)
    )
    block_out = (state + scatter_chips(hidden_half, n_ctx, 1)).astype(BF)
    qkv_terms = outer_rows(all_one, grad_mixed)
    qkv_sums = sum_dp(qkv_terms, n_dp).astype(BF)
    d_one = scatter_chips(
        scatter_pairs(
            nt(grad_mixed[mid:], qkv_part).astype(BF), nt(grad_mixed[:mid], qkv_part), n_ctx
        ),
        n_ctx,
    )
    all_branch = jnp.zeros((seq, D), BF)
    for slot, piece in enumerate(branch_pieces):
        all_branch = lax.dynamic_update_slice(all_branch, piece, (order[slot] * tok, 0))
    out_terms = outer_rows(attn, after(all_branch, qkv_sums))
    norm_one = hidden_in * rms_one
    input_grad = grad_state + rms_one * (
        d_one - norm_one * jnp.mean(d_one * norm_one, axis=-1, keepdims=True)
    )

    down_weight_grad = after(down_sums, grad_mixed).astype(F32)
    out_weight_grad = deal_back(out_terms, n_dp, n_ctx)
    gate_up_weight_grad, gain_ffn_grad = join_columns(
        exchange(after(gate_up_sums, grad_mixed).reshape(n_ctx, rows, 2 * ff)), gate_up_weight, gain_two, n_dp, ff_rows
    )
    qkv_back = exchange(qkv_sums.reshape(n_ctx, rows, columns)).astype(F32)
    q_back = qkv_back[:, :, :width].transpose(1, 0, 2).reshape(rows, H * HD)
    kv_back = jnp.sum(qkv_back[:, :, width:].reshape(KVH, sharers, rows, 2 * HD), axis=1)
    k_back = kv_back[:, :, :HD].transpose(1, 0, 2).reshape(rows, KVH * HD)
    v_back = kv_back[:, :, HD:].transpose(1, 0, 2).reshape(rows, KVH * HD)
    qkv_back = jnp.concatenate([q_back, k_back, v_back], axis=1)
    qkv_weight_grad = qkv_back * gain_one
    gain_attn_grad = jnp.sum(qkv_back * qkv_weight.astype(F32), axis=1)
    return (
        block_out,
        input_grad,
        gain_attn_grad,
        qkv_weight_grad,
        out_weight_grad,
        gain_ffn_grad[:, 0],
        gate_up_weight_grad,
        down_weight_grad,
    )


def solution(mesh):
    rows = P(("dp", "ctx"), None)
    entries = P(("dp", "ctx"))
    return jax.shard_map(
        on_device,
        mesh=mesh,
        in_specs=(rows, entries, rows, rows, entries, rows, rows, P("dp", None), rows),
        out_specs=(rows, rows, entries, rows, rows, entries, rows, rows),
        check_vma=False,
    )
```

```python
import jax
import jax.numpy as jnp
import numpy as np
from jax import lax
from jax.experimental import pallas as pl
from jax.experimental.pallas import tpu as pltpu
from jax.sharding import PartitionSpec as P

D = 2048
H = 32
KVH = 4
HD = 64
FF = 5632
HALF = HD // 2

EPS = 1e-05
MASKED = -1e30
BF = jnp.bfloat16
F32 = jnp.float32
VMEM_LIMIT = 60 << 20
SHORT = pl.CostEstimate(flops=1 << 20, bytes_accessed=1 << 20, transcendentals=0)
MEDIUM = pl.CostEstimate(flops=2 * 10**10, bytes_accessed=1 << 20, transcendentals=0)
LONG = pl.CostEstimate(flops=10**11, bytes_accessed=1 << 20, transcendentals=0)


def nt(a, b):
    return lax.dot_general(a, b, (((1,), (1,)), ((), ())), preferred_element_type=F32)


def nn(a, b):
    return jnp.dot(a, b, preferred_element_type=F32)


def after(x, *earlier):
    return lax.optimization_barrier((x, *earlier))[0]


def after_each(values, *earlier):
    count = len(values)
    return lax.optimization_barrier((*values, *earlier))[:count]


def walk(n_ctx, parity):
    bits = []
    bit = 2
    while bit < n_ctx:
        bits.append(bit)
        bit *= 2
    return bits if parity == 0 else bits[::-1]


def swap_stage(x, n_ctx, stage):
    pairs = [(c, c ^ walk(n_ctx, c % 2)[stage]) for c in range(n_ctx)]
    return lax.ppermute(x, "ctx", pairs)


def swap_core(x, n_ctx):
    return lax.ppermute(x, "ctx", [(c, c ^ 1) for c in range(n_ctx)])


def slot_table(n_ctx):
    lists = []
    for parity in (0, 1):
        row = [0]
        for bit in walk(n_ctx, parity):
            row = row + [v ^ bit for v in row]
        lists.append(row)
    return np.array(
        [lists[p] + [v ^ 1 for v in lists[1 - p]] for p in (0, 1)], dtype=np.int32
    )


def gather_direct(x, n_ctx):
    return [x] + [swap_stage(x, n_ctx, stage) for stage in range(len(walk(n_ctx, 0)))]


def gather_rest(direct, n_ctx, *earlier):
    have = direct[:1]
    for stage in range(len(walk(n_ctx, 0))):
        passed = [after(block, *earlier) if earlier else block for block in have[1:]]
        have = have + [direct[stage + 1]] + [swap_stage(block, n_ctx, stage) for block in passed]
    return have + [swap_core(block, n_ctx) for block in have]


def gather_slots(x, n_ctx):
    return gather_rest(gather_direct(x, n_ctx), n_ctx)


def scatter_pairs(term, tok, n_ctx):
    mine = n_ctx // 2
    cut = mine // 2
    sums = []
    for lo, hi in ((cut, mine), (0, cut)):
        arrived = swap_core(term(mine + lo, mine + hi).astype(BF), n_ctx)
        sums.append(term(lo, hi) + arrived.astype(F32))
    return sums


def scatter_chips(upper, lower, stages, n_ctx):
    for stage in stages:
        lower = lower + swap_stage(upper.astype(BF), n_ctx, stage).astype(F32)
        if stage:
            half = lower.shape[0] // 2
            upper, lower = lower[half:], lower[:half]
    return lower if stages[-1] == 0 else (upper, lower)


def exchange(x):
    return lax.all_to_all(x, "ctx", split_axis=0, concat_axis=0, tiled=False)


def gather_dp(x):
    return lax.all_gather(x, "dp", axis=0, tiled=True)


def scatter_dp(x):
    return lax.psum_scatter(x, "dp", scatter_dimension=0, tiled=True)


def fetch_piece(pieces, buffer, semaphores):
    step = pl.program_id(0)

    @pl.when(step == 0)
    def _():
        for i, piece in enumerate(pieces):
            pltpu.make_async_copy(piece, buffer.at[i], semaphores.at[i]).start()

    pltpu.make_async_copy(pieces[0], buffer.at[step], semaphores.at[step]).wait()
    return buffer[step]


def chunks(rows):
    return next(count for count in (8, 4, 2, 1) if rows % (16 * count) == 0)


def fetch_rows(source, buffer, semaphores):
    count = semaphores.shape[0]
    rows = source.shape[0] // count

    @pl.when(pl.program_id(0) == 0)
    def _():
        copies = [
            pltpu.make_async_copy(
                source.at[pl.ds(i * rows, rows)], buffer.at[pl.ds(i * rows, rows)], semaphores.at[i]
            )
            for i in range(count)
        ]
        for copy in copies:
            copy.start()
        for copy in copies:
            copy.wait()


def swap_halves(x):
    return pltpu.roll(x, x.shape[1] // 2, axis=1)


def turn_tables(cosine, sine, width):
    times = width // 128
    cosine = jnp.concatenate([cosine] * times, axis=1) if times > 1 else cosine
    sine = jnp.concatenate([sine] * times, axis=1) if times > 1 else sine
    lane = lax.broadcasted_iota(jnp.int32, sine.shape, 1)
    return cosine, jnp.where(lane < width // 2, -sine, sine)


def any_specs(pieces):
    return [pl.BlockSpec(memory_space=pltpu.HBM) for _ in pieces]


def project_qkv(order, pieces, weight, spread, cosine, sine, width, tok):
    n = len(pieces)
    seq = n * tok

    def kernel(order_ref, *refs):
        parts = refs[:n]
        w_hbm, spread_ref, cos_ref, sin_ref = refs[n : n + 4]
        q_ref, k_ref, v_ref, kt_ref, vt_ref, all_ref, wide, buffer, semaphores, w_ref, w_semaphores = refs[
            n + 4 :
        ]
        fetch_rows(w_hbm, w_ref, w_semaphores)

        @pl.when(pl.program_id(0) == 0)
        def _():
            wide[...] = nn(w_ref[...], spread_ref[...]).astype(BF)

        x = fetch_piece(parts, buffer, semaphores)
        all_ref[...] = x
        mixed = nn(x, wide[...])
        cos, sin = turn_tables(cos_ref[...], sin_ref[...], width)
        q = mixed[:, :width]
        k = mixed[:, width : 2 * width]
        v = mixed[:, 2 * width :].astype(BF)
        q_ref[...] = (q * cos + swap_halves(q) * sin).astype(BF) * (HD**-0.5)
        k = (k * cos + swap_halves(k) * sin).astype(BF)
        k_ref[...] = k
        v_ref[...] = v
        k_turned = k.T
        kt_ref[:HALF, :] = k_turned[:HALF]
        kt_ref[HALF:, :] = k_turned[width // 2 : width // 2 + HALF]
        vt_ref[...] = v.T[:HD]

    rows = lambda s, order: (order[s], 0)
    lanes = lambda s, order: (0, order[s])
    whole = lambda s, order: (0, 0)
    return pl.pallas_call(
        kernel,
        grid_spec=pltpu.PrefetchScalarGridSpec(
            num_scalar_prefetch=1,
            grid=(n,),
            in_specs=any_specs(pieces)
            + [
                pl.BlockSpec(memory_space=pltpu.HBM),
                pl.BlockSpec(spread.shape, whole),
                pl.BlockSpec((tok, 128), rows),
                pl.BlockSpec((tok, 128), rows),
            ],
            out_specs=[
                pl.BlockSpec((tok, width), rows),
                pl.BlockSpec((tok, width), rows),
                pl.BlockSpec((tok, width), rows),
                pl.BlockSpec((HD, tok), lanes),
                pl.BlockSpec((HD, tok), lanes),
                pl.BlockSpec((tok, D), lambda s, order: (s, 0)),
            ],
            scratch_shapes=[
                pltpu.VMEM((D, 3 * width), BF),
                pltpu.VMEM((n, tok, D), BF),
                pltpu.SemaphoreType.DMA((n,)),
                pltpu.VMEM(weight.shape, BF),
                pltpu.SemaphoreType.DMA((chunks(D),)),
            ],
        ),
        out_shape=[
            jax.ShapeDtypeStruct((seq, width), BF),
            jax.ShapeDtypeStruct((seq, width), BF),
            jax.ShapeDtypeStruct((seq, width), BF),
            jax.ShapeDtypeStruct((HD, seq), BF),
            jax.ShapeDtypeStruct((HD, seq), BF),
            jax.ShapeDtypeStruct((seq, D), BF),
        ],
        compiler_params=pltpu.CompilerParams(vmem_limit_bytes=VMEM_LIMIT),
        cost_estimate=LONG,
        name="project_qkv",
    )(order, *pieces, weight, spread, cosine, sine)


def project_out(order, heads_in, pieces, residual):
    n, tok, width = heads_in.shape

    def kernel(order_ref, a_ref, *refs):
        parts = refs[:n]
        x_ref, state_ref, norm_ref, buffer, semaphores = refs[n:]
        step = pl.program_id(0)
        w = fetch_piece(parts, buffer, semaphores)

        @pl.when(step == 0)
        def _():
            state_ref[...] = x_ref[...].astype(F32)

        state_ref[...] += nn(a_ref[0], w)

        @pl.when(step == n - 1)
        def _():
            state = state_ref[...]
            scale = lax.rsqrt(jnp.mean(state * state, axis=-1, keepdims=True) + EPS)
            norm_ref[...] = (state * scale).astype(BF)

    whole = lambda s, order: (0, 0)
    return pl.pallas_call(
        kernel,
        grid_spec=pltpu.PrefetchScalarGridSpec(
            num_scalar_prefetch=1,
            grid=(n,),
            in_specs=[pl.BlockSpec((1, tok, width), lambda s, order: (order[s], 0, 0))]
            + any_specs(pieces)
            + [pl.BlockSpec((tok, D), whole)],
            out_specs=[pl.BlockSpec((tok, D), whole), pl.BlockSpec((tok, D), whole)],
            scratch_shapes=[
                pltpu.VMEM((n, width, D), BF),
                pltpu.SemaphoreType.DMA((n,)),
            ],
        ),
        out_shape=[
            jax.ShapeDtypeStruct((tok, D), F32),
            jax.ShapeDtypeStruct((tok, D), BF),
        ],
        compiler_params=pltpu.CompilerParams(vmem_limit_bytes=VMEM_LIMIT),
        cost_estimate=SHORT,
        name="project_out",
    )(order, heads_in, *pieces, residual)


def feed_forward(pieces, weight):
    n = len(pieces)
    tok = pieces[0].shape[0]
    seq = n * tok
    ff = weight.shape[1] // 2

    def kernel(*refs):
        parts = refs[:n]
        w_hbm, hidden_ref, factor_ref, all_ref, buffer, semaphores, w_ref, w_semaphores = refs[n:]
        fetch_rows(w_hbm, w_ref, w_semaphores)
        x = fetch_piece(parts, buffer, semaphores)
        all_ref[...] = x
        both = nn(x, w_ref[...])
        gate = both[:, :ff]
        up = both[:, ff:]
        sig = jax.nn.sigmoid(gate)
        silu = gate * sig
        hidden_ref[...] = (silu * up).astype(BF)
        factor_ref[:, :ff] = (up * sig * (1.0 + gate * (1.0 - sig))).astype(BF)
        factor_ref[:, ff:] = silu.astype(BF)

    rows = lambda s: (s, 0)
    return pl.pallas_call(
        kernel,
        grid=(n,),
        in_specs=any_specs(pieces) + [pl.BlockSpec(memory_space=pltpu.HBM)],
        out_specs=[
            pl.BlockSpec((tok, ff), rows),
            pl.BlockSpec((tok, 2 * ff), rows),
            pl.BlockSpec((tok, D), rows),
        ],
        scratch_shapes=[
            pltpu.VMEM((n, tok, D), BF),
            pltpu.SemaphoreType.DMA((n,)),
            pltpu.VMEM(weight.shape, BF),
            pltpu.SemaphoreType.DMA((chunks(D),)),
        ],
        out_shape=[
            jax.ShapeDtypeStruct((seq, ff), BF),
            jax.ShapeDtypeStruct((seq, 2 * ff), BF),
            jax.ShapeDtypeStruct((seq, D), BF),
        ],
        compiler_params=pltpu.CompilerParams(vmem_limit_bytes=VMEM_LIMIT),
        cost_estimate=LONG,
        name="feed_forward",
    )(*pieces, weight)


def feed_backward(factors, grads, weight):
    seq = factors.shape[0]
    ff = weight.shape[0]
    tok = 256

    def kernel(factor_ref, g_ref, w_hbm, out_ref, w_ref, w_semaphores):
        fetch_rows(w_hbm, w_ref, w_semaphores)
        grad_hidden = nt(g_ref[...], w_ref[...])
        factor = factor_ref[...].astype(F32)
        out_ref[:, :ff] = (grad_hidden * factor[:, :ff]).astype(BF)
        out_ref[:, ff:] = (grad_hidden * factor[:, ff:]).astype(BF)

    rows = lambda s: (s, 0)
    return pl.pallas_call(
        kernel,
        grid=(seq // tok,),
        in_specs=[
            pl.BlockSpec((tok, 2 * ff), rows),
            pl.BlockSpec((tok, D), rows),
            pl.BlockSpec(memory_space=pltpu.HBM),
        ],
        out_specs=pl.BlockSpec((tok, 2 * ff), rows),
        scratch_shapes=[pltpu.VMEM(weight.shape, BF), pltpu.SemaphoreType.DMA((chunks(ff),))],
        out_shape=jax.ShapeDtypeStruct((seq, 2 * ff), BF),
        compiler_params=pltpu.CompilerParams(vmem_limit_bytes=VMEM_LIMIT),
        cost_estimate=LONG,
        name="feed_backward",
    )(factors, grads, weight)


def lay_out(pieces):
    n = len(pieces)
    tok = pieces[0].shape[0]
    cuts = 2

    def kernel(*refs):
        parts = refs[:n]
        out_ref, semaphores = refs[n:]
        copies = []
        for i, part in enumerate(parts):
            for cut in range(cuts):
                rows = tok // cuts
                copies.append(
                    pltpu.make_async_copy(
                        part.at[pl.ds(cut * rows, rows)],
                        out_ref.at[pl.ds(i * tok + cut * rows, rows)],
                        semaphores.at[i * cuts + cut],
                    )
                )
        for copy in copies:
            copy.start()
        for copy in copies:
            copy.wait()

    return pl.pallas_call(
        kernel,
        in_specs=any_specs(pieces),
        out_specs=pl.BlockSpec(memory_space=pltpu.HBM),
        scratch_shapes=[pltpu.SemaphoreType.DMA((n * cuts,))],
        out_shape=jax.ShapeDtypeStruct((n * tok, pieces[0].shape[1]), BF),
        cost_estimate=SHORT,
        name="lay_out",
    )(*pieces)


def branch_back(order, d_two, state, out_grad, pieces):
    n = len(pieces)
    tok = d_two.shape[0]
    width = pieces[0].shape[0]

    def kernel(order_ref, d_ref, state_ref, g_ref, *refs):
        parts = refs[:n]
        grad_ref, branch_ref, heads_ref, buffer, semaphores = refs[n:]

        @pl.when(pl.program_id(0) == 0)
        def _():
            state = state_ref[...]
            scale = lax.rsqrt(jnp.mean(state * state, axis=-1, keepdims=True) + EPS)
            norm = state * scale
            d = d_ref[...]
            grad = g_ref[...].astype(F32) + scale * (
                d - norm * jnp.mean(d * norm, axis=-1, keepdims=True)
            )
            grad_ref[...] = grad
            branch_ref[...] = grad.astype(BF)

        w = fetch_piece(parts, buffer, semaphores)
        heads_ref[0] = nt(branch_ref[...], w).astype(BF)

    whole = lambda s, order: (0, 0)
    return pl.pallas_call(
        kernel,
        grid_spec=pltpu.PrefetchScalarGridSpec(
            num_scalar_prefetch=1,
            grid=(n,),
            in_specs=[
                pl.BlockSpec((tok, D), whole),
                pl.BlockSpec((tok, D), whole),
                pl.BlockSpec((tok, D), whole),
            ]
            + any_specs(pieces),
            out_specs=[
                pl.BlockSpec((tok, D), whole),
                pl.BlockSpec((tok, D), whole),
                pl.BlockSpec((1, tok, width), lambda s, order: (order[s], 0, 0)),
            ],
            scratch_shapes=[
                pltpu.VMEM((n, width, D), BF),
                pltpu.SemaphoreType.DMA((n,)),
            ],
        ),
        out_shape=[
            jax.ShapeDtypeStruct((tok, D), F32),
            jax.ShapeDtypeStruct((tok, D), BF),
            jax.ShapeDtypeStruct((n, tok, width), BF),
        ],
        compiler_params=pltpu.CompilerParams(vmem_limit_bytes=VMEM_LIMIT),
        cost_estimate=SHORT,
        name="branch_back",
    )(order, d_two, state, out_grad, *pieces)


def split_columns(weight, gain, n_ctx, n_dp, ff_rows):
    rows = weight.shape[0]
    ff = ff_rows * n_dp

    def kernel(w_ref, gain_ref, out_ref):
        gains = gain_ref[...]
        for part in range(2):
            for d in range(n_dp):
                for c in range(n_ctx):
                    at = part * FF + (d * n_ctx + c) * ff_rows
                    to = part * ff + d * ff_rows
                    values = w_ref[:, at : at + ff_rows].astype(F32) * gains
                    out_ref[c, :, to : to + ff_rows] = values.astype(BF)

    return pl.pallas_call(
        kernel,
        in_specs=[pl.BlockSpec(memory_space=pltpu.VMEM)] * 2,
        out_specs=pl.BlockSpec(memory_space=pltpu.VMEM),
        out_shape=jax.ShapeDtypeStruct((n_ctx, rows, 2 * ff), BF),
        compiler_params=pltpu.CompilerParams(vmem_limit_bytes=VMEM_LIMIT),
        cost_estimate=LONG,
        name="split_columns",
    )(weight, gain)


def join_columns(sums, weight, gain, n_dp, ff_rows):
    n_ctx, rows, both = sums.shape
    ff = both // 2

    def kernel(s_ref, w_ref, gain_ref, out_ref, gain_out_ref):
        gains = gain_ref[...]
        total = jnp.zeros((rows, ff_rows), F32)
        for part in range(2):
            for d in range(n_dp):
                for c in range(n_ctx):
                    at = part * ff + d * ff_rows
                    to = part * FF + (d * n_ctx + c) * ff_rows
                    values = s_ref[c, :, at : at + ff_rows].astype(F32)
                    total = total + values * w_ref[:, to : to + ff_rows].astype(F32)
                    out_ref[:, to : to + ff_rows] = values * gains
        gain_out_ref[...] = jnp.sum(total, axis=1, keepdims=True)

    return pl.pallas_call(
        kernel,
        in_specs=[pl.BlockSpec(memory_space=pltpu.VMEM)] * 3,
        out_specs=[pl.BlockSpec(memory_space=pltpu.VMEM)] * 2,
        out_shape=[
            jax.ShapeDtypeStruct((rows, 2 * FF), F32),
            jax.ShapeDtypeStruct((rows, 1), F32),
        ],
        compiler_params=pltpu.CompilerParams(vmem_limit_bytes=VMEM_LIMIT),
        cost_estimate=LONG,
        name="join_columns",
    )(sums, weight, gain)


def lane_heads(rows, width):
    lane = lax.broadcasted_iota(jnp.int32, (rows, width), 1)
    return (lane % (width // 2)) // HALF


def attend_forward(slot_of, starts, queries, keys, values_t, heads, tok):
    seq, width = queries.shape
    blocks = seq // tok

    def kernel(slot_ref, start_ref, q_ref, k_ref, v_ref, attn_ref, slot_attn_ref, full_ref, lse_ref, scores):
        block = pl.program_id(0)
        start = start_ref[...]
        here = block * tok + lax.broadcasted_iota(jnp.int32, (1, tok), 1)
        head_of = lane_heads(tok, width)
        q = q_ref[...]
        q_heads = [jnp.where(head_of == h, q, jnp.zeros_like(q)) for h in range(heads)]

        def score(i, peaks):
            rows = pl.ds(pl.multiple_of(i * tok, tok), tok)
            k = k_ref[rows, :]
            there = i * tok + lax.broadcasted_iota(jnp.int32, (tok, tok), 0)
            visible = (there >= start) & (there <= here)
            out = []
            for h in range(heads):
                s = jnp.where(visible, nt(k, q_heads[h]), MASKED)
                scores[h, rows, :] = s
                out.append(jnp.maximum(peaks[h], jnp.max(s.reshape(tok // 8, 8, tok), axis=0)))
            return tuple(out)

        peaks = lax.fori_loop(
            0, block + 1, score, tuple(jnp.full((8, tok), MASKED, F32) for _ in range(heads))
        )
        peaks = [jnp.max(peak, axis=0, keepdims=True) for peak in peaks]

        def weigh(i, running):
            rows = pl.ds(pl.multiple_of(i * tok, tok), tok)
            v = v_ref[:, rows]
            out = []
            for h in range(heads):
                total, acc = running[h]
                p = jnp.exp(scores[h, rows, :] - peaks[h])
                total = total + jnp.sum(p.reshape(tok // 8, 8, tok), axis=0)
                out.append((total, acc + nn(v, p.astype(BF))))
            return tuple(out)

        result = lax.fori_loop(
            0,
            block + 1,
            weigh,
            tuple((jnp.zeros((8, tok), F32), jnp.zeros((HD, tok), F32)) for _ in range(heads)),
        )
        rows = []
        for h in range(heads):
            total, acc = result[h]
            total = jnp.sum(total, axis=0, keepdims=True)
            rows.append(acc / total)
            lse_ref[0, h : h + 1, :] = peaks[h] + jnp.log(total)
        full = jnp.concatenate(rows, axis=0).T
        full_ref[...] = full
        attn_ref[...] = full.astype(BF)
        slot_attn_ref[...] = full.astype(BF)

    return pl.pallas_call(
        kernel,
        grid_spec=pltpu.PrefetchScalarGridSpec(
            num_scalar_prefetch=1,
            grid=(blocks,),
            in_specs=[
                pl.BlockSpec((1, tok), lambda j, slot: (0, j)),
                pl.BlockSpec((tok, width), lambda j, slot: (j, 0)),
                pl.BlockSpec((seq, width), lambda j, slot: (0, 0)),
                pl.BlockSpec((HD, seq), lambda j, slot: (0, 0)),
            ],
            out_specs=[
                pl.BlockSpec((tok, width), lambda j, slot: (j, 0)),
                pl.BlockSpec((tok, width), lambda j, slot: (slot[j], 0)),
                pl.BlockSpec((tok, width), lambda j, slot: (j, 0)),
                pl.BlockSpec((1, heads, tok), lambda j, slot: (j, 0, 0)),
            ],
            scratch_shapes=[pltpu.VMEM((heads, seq, tok), F32)],
        ),
        out_shape=[
            jax.ShapeDtypeStruct((seq, width), BF),
            jax.ShapeDtypeStruct((seq, width), BF),
            jax.ShapeDtypeStruct((seq, width), F32),
            jax.ShapeDtypeStruct((blocks, heads, tok), F32),
        ],
        compiler_params=pltpu.CompilerParams(vmem_limit_bytes=VMEM_LIMIT),
        cost_estimate=LONG,
        name="attend_forward",
    )(slot_of, starts, queries, keys, values_t)


def attend_backward(
    slot_of, starts, queries, keys, keys_t, values, grads, full, lse, cosine, sine, unsplit, heads, tok
):
    seq, width = queries.shape
    blocks = seq // tok
    half = width // 2

    def kernel(
        slot_ref, start_ref, q_ref, k_ref, kt_ref, v_ref, g_ref, full_ref, lse_ref, cos_ref, sin_ref, unsplit_ref,
        out_ref, dk, dv,
    ):
        block = pl.program_id(0)

        @pl.when(block == 0)
        def _():
            dk[...] = jnp.zeros_like(dk)
            dv[...] = jnp.zeros_like(dv)

        start = start_ref[...]
        here = block * tok + lax.broadcasted_iota(jnp.int32, (1, tok), 1)
        head_of = lane_heads(tok, width)
        wide = lax.broadcasted_iota(jnp.int32, (tok, width), 1) // HD
        q = q_ref[...]
        g = g_ref[...]
        q_heads = [jnp.where(head_of == h, q, jnp.zeros_like(q)) for h in range(heads)]
        g_heads = [jnp.where(wide == h, g, jnp.zeros_like(g)) for h in range(heads)]
        q_stack = jnp.concatenate(q_heads, axis=0)
        g_stack = jnp.concatenate(g_heads, axis=0)
        picks = (
            lax.broadcasted_iota(jnp.int32, (8, width), 1) // HD
            == lax.broadcasted_iota(jnp.int32, (8, width), 0)
        ).astype(F32)
        deltas = lax.dot_general(
            picks,
            g.astype(F32) * full_ref[...],
            (((1,), (1,)), ((), ())),
            preferred_element_type=F32,
            precision=lax.Precision.HIGHEST,
        )

        def step(i, dq):
            rows = pl.ds(pl.multiple_of(i * tok, tok), tok)
            k = k_ref[rows, :]
            v = v_ref[rows, :]
            kt = kt_ref[:, rows]
            there = i * tok + lax.broadcasted_iota(jnp.int32, (tok, tok), 0)
            visible = (there >= start) & (there <= here)
            probs, grad_scores, out = [], [], []
            for h in range(heads):
                s = jnp.where(visible, nt(k, q_heads[h]), MASKED)
                p = jnp.exp(s - lse_ref[0, h : h + 1, :])
                ds = (p * (nt(v, g_heads[h]) - deltas[h : h + 1, :])).astype(BF)
                probs.append(p.astype(BF))
                grad_scores.append(ds)
                out.append(dq[h] + nn(kt, ds))
            dv[rows, :] += nn(jnp.concatenate(probs, axis=1), g_stack)
            dk[rows, :] += nn(jnp.concatenate(grad_scores, axis=1), q_stack)
            return tuple(out)

        dq = lax.fori_loop(
            0, block + 1, step, tuple(jnp.zeros((HD, tok), F32) for _ in range(heads))
        )
        dq = jnp.concatenate([x[:HALF] for x in dq] + [x[HALF:] for x in dq], axis=0).T
        here_rows = pl.ds(pl.multiple_of(block * tok, tok), tok)
        cos, sin = turn_tables(cos_ref[here_rows, :], sin_ref[here_rows, :], width)
        dq = (dq * cos - swap_halves(dq) * sin) * (HD**-0.5)
        slot_rows = pl.ds(pl.multiple_of(slot_ref[block] * tok, tok), tok)
        out_ref[slot_rows, :width] = nn(dq.astype(BF), unsplit_ref[...]).astype(BF)

        @pl.when(block == blocks - 1)
        def _():
            lane = lax.broadcasted_iota(jnp.int32, (width, 128), 0)
            column = lax.broadcasted_iota(jnp.int32, (width, 128), 1)
            fold_k = ((lane // half) * HALF + lane % HALF == column).astype(BF)
            fold_v = (lane % HD + HD == column).astype(BF)

            def fold(i, unused):
                rows = pl.ds(pl.multiple_of(i * tok, tok), tok)
                cos, sin = turn_tables(cos_ref[rows, :], sin_ref[rows, :], width)
                a = dk[rows, :]
                a = a * cos - swap_halves(a) * sin
                b = dv[rows, :]
                a_high = a.astype(BF)
                b_high = b.astype(BF)
                terms = (
                    nn(a_high, fold_k)
                    + nn((a - a_high.astype(F32)).astype(BF), fold_k)
                    + nn(b_high, fold_v)
                    + nn((b - b_high.astype(F32)).astype(BF), fold_v)
                )
                slot_rows = pl.ds(pl.multiple_of(slot_ref[i] * tok, tok), tok)
                out_ref[slot_rows, width:] = terms.astype(BF)
                return unused

            lax.fori_loop(0, blocks, fold, 0)

    whole = lambda shape: pl.BlockSpec(shape, lambda j, *_: (0, 0))
    return pl.pallas_call(
        kernel,
        grid_spec=pltpu.PrefetchScalarGridSpec(
            num_scalar_prefetch=1,
            grid=(blocks,),
            in_specs=[
                pl.BlockSpec((1, tok), lambda j, *_: (0, j)),
                pl.BlockSpec((tok, width), lambda j, *_: (j, 0)),
                whole((seq, width)),
                whole((HD, seq)),
                whole((seq, width)),
                pl.BlockSpec((tok, width), lambda j, *_: (j, 0)),
                pl.BlockSpec((tok, width), lambda j, *_: (j, 0)),
                pl.BlockSpec((1, heads, tok), lambda j, *_: (j, 0, 0)),
                whole((seq, 128)),
                whole((seq, 128)),
                whole((width, width)),
            ],
            out_specs=whole((seq, width + 128)),
            scratch_shapes=[pltpu.VMEM((seq, width), F32), pltpu.VMEM((seq, width), F32)],
        ),
        out_shape=jax.ShapeDtypeStruct((seq, width + 128), BF),
        compiler_params=pltpu.CompilerParams(vmem_limit_bytes=VMEM_LIMIT),
        cost_estimate=MEDIUM,
        name="attend_backward",
    )(slot_of, starts, queries, keys, keys_t, values, grads, full, lse, cosine, sine, unsplit)


def outer_rows(activations, gradients):
    return lax.dot_general(
        activations, gradients, (((0,), (0,)), ((), ())), preferred_element_type=F32
    ).astype(BF)


def split_source(width):
    lane = np.arange(width)
    half = lane // (width // 2)
    head = (lane % (width // 2)) // HALF
    return head * HD + half * HALF + lane % HALF


def spread_matrix(width):
    matrix = np.zeros((width + 2 * HD, 3 * width), np.float32)
    lane = np.arange(width)
    matrix[split_source(width), lane] = 1
    matrix[width + (lane // (width // 2)) * HALF + lane % HALF, width + lane] = 1
    matrix[width + HD + lane % HD, 2 * width + lane] = 1
    return jnp.asarray(matrix, BF)


def unsplit_matrix(width):
    matrix = np.zeros((width, width), np.float32)
    matrix[np.arange(width), split_source(width)] = 1
    return jnp.asarray(matrix, BF)


def on_device(
    block_in,
    gain_attn,
    qkv_weight,
    out_weight,
    gain_ffn,
    gate_up_weight,
    down_weight,
    doc_lengths,
    out_grad,
):
    n_ctx = lax.axis_size("ctx")
    n_dp = lax.axis_size("dp")
    me = lax.axis_index("ctx")
    tok = block_in.shape[0]
    seq = tok * n_ctx
    heads = H // n_ctx
    width = heads * HD
    sharers = n_ctx // KVH
    rows = qkv_weight.shape[0]
    ff_rows = down_weight.shape[0]
    ff = ff_rows * n_dp
    columns = width + 2 * HD

    order = me ^ jnp.where(me % 2 == 0, *[jnp.asarray(t) for t in slot_table(n_ctx)])
    slots = jnp.arange(n_ctx, dtype=jnp.int32)
    slot_of = jnp.sum(jnp.where(order[None, :] == slots[:, None], slots[None, :], 0), axis=1)
    index = jnp.arange(seq, dtype=jnp.int32)
    lengths = doc_lengths[0]
    ends = jnp.cumsum(lengths)
    starts = jnp.sum((index[:, None] >= ends[None, :]).astype(jnp.int32) * lengths[None, :], axis=1)
    lane = jnp.arange(128, dtype=F32) % HALF
    frequency = 10000.0 ** (-lane * 2.0 / HD)
    angles = (index - starts).astype(F32)[:, None] * frequency[None, :]
    cosine = jnp.cos(angles)
    sine = jnp.sin(angles)
    starts_row = starts[None, :]

    gain_one = gain_attn.astype(F32)[:, None]
    gain_two = gain_ffn.astype(F32)[:, None]
    qkv = (qkv_weight.astype(F32) * gain_one).astype(BF)
    q_cols = qkv[:, : H * HD].reshape(rows, n_ctx, width).transpose(1, 0, 2)
    k_cols = qkv[:, H * HD : (H + KVH) * HD].reshape(rows, KVH, HD).transpose(1, 0, 2)
    v_cols = qkv[:, (H + KVH) * HD :].reshape(rows, KVH, HD).transpose(1, 0, 2)
    kv_cols = jnp.repeat(jnp.concatenate([k_cols, v_cols], axis=2), sharers, axis=0)
    qkv_own = exchange(jnp.concatenate([q_cols, kv_cols], axis=2)).reshape(n_ctx * rows, columns)
    qkv_part = gather_dp(qkv_own)

    hidden_in = block_in.astype(F32)
    rms_one = lax.rsqrt(jnp.mean(hidden_in * hidden_in, axis=-1, keepdims=True) + EPS)
    one_pieces = gather_slots(after((hidden_in * rms_one).astype(BF), qkv_own), n_ctx)

    owner_pairs = [(b, b % n_dp * n_ctx + b // n_dp) for b in range(n_dp * n_ctx)]
    out_part = gather_dp(lax.ppermute(out_weight, ("dp", "ctx"), owner_pairs))
    gate_up_cols = split_columns(gate_up_weight, gain_two, n_ctx, n_dp, ff_rows)
    gate_up_own = exchange(after(gate_up_cols, *one_pieces[: n_ctx // 2])).reshape(
        n_ctx * rows, 2 * ff
    )
    gate_up_part = gather_dp(gate_up_own)
    down_part = gather_dp(after(down_weight, gate_up_part))

    queries, keys, values, keys_t, values_t, all_one = project_qkv(
        order, one_pieces, qkv_part, spread_matrix(width), cosine, sine, width, tok
    )
    out_pieces = gather_slots(out_part, n_ctx)
    attn, slot_attn, attended, lse = attend_forward(
        slot_of, starts_row, after(queries, gate_up_own), keys, values_t, heads, tok
    )
    state, norm_two = project_out(
        order, exchange(attn.reshape(n_ctx, tok, width)), out_pieces, block_in
    )

    two_pieces = gather_slots(norm_two, n_ctx)
    grad_direct = gather_direct(after(out_grad, *two_pieces), n_ctx)
    hidden, factors, all_two = feed_forward(two_pieces, gate_up_part)
    grad_pieces = gather_rest(grad_direct, n_ctx, hidden)
    all_grad = lay_out(grad_pieces)
    down_terms = outer_rows(hidden, all_grad)
    down_sums = scatter_dp(down_terms)
    grad_gate_up = feed_backward(after(factors, down_terms), all_grad, down_part)

    def rows_of(x, lo, hi):
        return lax.slice_in_dim(x, lo * tok, hi * tok, axis=0)

    d_pairs = scatter_pairs(
        lambda lo, hi: nt(rows_of(grad_gate_up, lo, hi), gate_up_part), tok, n_ctx
    )
    stages = tuple(reversed(range(len(walk(n_ctx, 0)))))
    d_two = scatter_chips(*d_pairs, stages, n_ctx)
    gate_up_terms = outer_rows(after(all_two, *d_pairs), grad_gate_up)
    gate_up_sums = scatter_dp(gate_up_terms)
    hidden_pairs = scatter_pairs(
        lambda lo, hi: nn(rows_of(after(hidden, *d_pairs), lo, hi), down_part), tok, n_ctx
    )

    grad_state, grad_branch, grad_heads = branch_back(
        order, after(d_two, gate_up_terms, *hidden_pairs), state, out_grad, out_pieces
    )
    grad_attn = exchange(grad_heads).reshape(seq, width)
    branch_pieces = gather_slots(after(grad_branch, grad_attn), n_ctx)
    hidden_rest = scatter_chips(*after_each(hidden_pairs, grad_attn), stages[:1], n_ctx)
    grad_mixed = attend_backward(
        slot_of,
        starts_row,
        queries,
        keys,
        keys_t,
        values,
        grad_attn,
        attended,
        lse,
        cosine,
        sine,
        unsplit_matrix(width),
        heads,
        tok,
    )
    grad_mixed = after(grad_mixed, *branch_pieces[:3], *hidden_rest)
    qkv_terms = outer_rows(all_one, grad_mixed)
    qkv_sums = scatter_dp(after(qkv_terms, gate_up_sums))
    d_one = scatter_chips(
        *scatter_pairs(lambda lo, hi: nt(rows_of(grad_mixed, lo, hi), qkv_part), tok, n_ctx),
        stages,
        n_ctx,
    )
    block_out = (state + scatter_chips(*hidden_rest, stages[1:], n_ctx)).astype(BF)
    out_terms = outer_rows(slot_attn, after(lay_out(branch_pieces), qkv_terms))
    out_sums = scatter_dp(after(out_terms, qkv_sums))
    norm_one = hidden_in * rms_one
    input_grad = grad_state + rms_one * (
        d_one - norm_one * jnp.mean(d_one * norm_one, axis=-1, keepdims=True)
    )

    down_weight_grad = after(down_sums, grad_mixed).astype(F32)
    out_weight_grad = lax.ppermute(
        out_sums, ("dp", "ctx"), [(b, a) for a, b in owner_pairs]
    ).astype(F32)
    gate_up_weight_grad, gain_ffn_grad = join_columns(
        exchange(after(gate_up_sums, grad_mixed).reshape(n_ctx, rows, 2 * ff)), gate_up_weight, gain_two, n_dp, ff_rows
    )
    qkv_back = exchange(qkv_sums.reshape(n_ctx, rows, columns)).astype(F32)
    q_back = qkv_back[:, :, :width].transpose(1, 0, 2).reshape(rows, H * HD)
    kv_back = jnp.sum(qkv_back[:, :, width:].reshape(KVH, sharers, rows, 2 * HD), axis=1)
    k_back = kv_back[:, :, :HD].transpose(1, 0, 2).reshape(rows, KVH * HD)
    v_back = kv_back[:, :, HD:].transpose(1, 0, 2).reshape(rows, KVH * HD)
    qkv_back = jnp.concatenate([q_back, k_back, v_back], axis=1)
    qkv_weight_grad = qkv_back * gain_one
    gain_attn_grad = jnp.sum(qkv_back * qkv_weight.astype(F32), axis=1)
    return (
        block_out,
        input_grad,
        gain_attn_grad,
        qkv_weight_grad,
        out_weight_grad,
        gain_ffn_grad[:, 0],
        gate_up_weight_grad,
        down_weight_grad,
    )


def solution(mesh):
    rows = P(("dp", "ctx"), None)
    entries = P(("dp", "ctx"))
    return jax.shard_map(
        on_device,
        mesh=mesh,
        in_specs=(rows, entries, rows, rows, entries, rows, rows, P("dp", None), rows),
        out_specs=(rows, rows, entries, rows, rows, entries, rows, rows),
        check_vma=False,
    )
```

```python
import jax
import jax.numpy as jnp
import numpy as np
from jax import lax
from jax.experimental import pallas as pl
from jax.experimental.pallas import tpu as pltpu
from jax.sharding import PartitionSpec as P

D = 2048
H = 32
KVH = 4
HD = 64
FF = 5632
HALF = HD // 2

EPS = 1e-05
MASKED = -1e30
BF = jnp.bfloat16
F32 = jnp.float32
VMEM_LIMIT = 60 << 20
SHORT = pl.CostEstimate(flops=1 << 20, bytes_accessed=1 << 20, transcendentals=0)
MEDIUM = pl.CostEstimate(flops=2 * 10**10, bytes_accessed=1 << 20, transcendentals=0)
LONG = pl.CostEstimate(flops=10**11, bytes_accessed=1 << 20, transcendentals=0)


def nt(a, b):
    return lax.dot_general(a, b, (((1,), (1,)), ((), ())), preferred_element_type=F32)


def nn(a, b):
    return jnp.dot(a, b, preferred_element_type=F32)


def after(x, *earlier):
    return lax.optimization_barrier((x, *earlier))[0]


def after_each(values, *earlier):
    count = len(values)
    return lax.optimization_barrier((*values, *earlier))[:count]


def walk(n_ctx, parity):
    bits = []
    bit = 2
    while bit < n_ctx:
        bits.append(bit)
        bit *= 2
    return bits if parity == 0 else bits[::-1]


def swap_stage(x, n_ctx, stage):
    pairs = [(c, c ^ walk(n_ctx, c % 2)[stage]) for c in range(n_ctx)]
    return lax.ppermute(x, "ctx", pairs)


def swap_core(x, n_ctx):
    return lax.ppermute(x, "ctx", [(c, c ^ 1) for c in range(n_ctx)])


def slot_table(n_ctx):
    lists = []
    for parity in (0, 1):
        row = [0]
        for bit in walk(n_ctx, parity):
            row = row + [v ^ bit for v in row]
        lists.append(row)
    return np.array(
        [lists[p] + [v ^ 1 for v in lists[1 - p]] for p in (0, 1)], dtype=np.int32
    )


def gather_direct(x, n_ctx):
    return [x] + [swap_stage(x, n_ctx, stage) for stage in range(len(walk(n_ctx, 0)))]


def gather_rest(direct, n_ctx, earlier=None, last=None):
    have = direct[:1]
    for stage in range(len(walk(n_ctx, 0))):
        passed = [block if earlier is None else after(block, earlier) for block in have[1:]]
        have = have + [direct[stage + 1]] + [swap_stage(block, n_ctx, stage) for block in passed]
    return have + [swap_core(block if last is None else after(block, last), n_ctx) for block in have]


def gather_slots(x, n_ctx):
    return gather_rest(gather_direct(x, n_ctx), n_ctx)


def scatter_pairs(term, tok, n_ctx):
    mine = n_ctx // 2
    cut = mine // 2
    sums = []
    for lo, hi in ((cut, mine), (0, cut)):
        arrived = swap_core(term(mine + lo, mine + hi).astype(BF), n_ctx)
        sums.append(term(lo, hi) + arrived.astype(F32))
    return sums


def scatter_chips(upper, lower, stages, n_ctx):
    for stage in stages:
        lower = lower + swap_stage(upper.astype(BF), n_ctx, stage).astype(F32)
        if stage:
            half = lower.shape[0] // 2
            upper, lower = lower[half:], lower[:half]
    return lower if stages[-1] == 0 else (upper, lower)


def exchange(x):
    return lax.all_to_all(x, "ctx", split_axis=0, concat_axis=0, tiled=False)


def gather_dp(x):
    return lax.all_gather(x, "dp", axis=0, tiled=True)


def scatter_dp(x):
    return lax.psum_scatter(x, "dp", scatter_dimension=0, tiled=True)


def fetch_piece(pieces, buffer, semaphores, count=1):
    step = pl.program_id(0)

    @pl.when(step == 0)
    def _():
        for i, piece in enumerate(pieces):
            pltpu.make_async_copy(piece, buffer.at[i], semaphores.at[i]).start()

    for i in range(count):
        at = step * count + i
        pltpu.make_async_copy(pieces[0], buffer.at[at], semaphores.at[at]).wait()
    if count == 1:
        return buffer[step]
    return buffer[pl.ds(step * count, count)].reshape(count * buffer.shape[1], buffer.shape[2])


def chunks(rows):
    return next(count for count in (8, 4, 2, 1) if rows % (16 * count) == 0)


def fetch_rows(source, buffer, semaphores):
    count = semaphores.shape[0]
    rows = source.shape[0] // count

    @pl.when(pl.program_id(0) == 0)
    def _():
        copies = [
            pltpu.make_async_copy(
                source.at[pl.ds(i * rows, rows)], buffer.at[pl.ds(i * rows, rows)], semaphores.at[i]
            )
            for i in range(count)
        ]
        for copy in copies:
            copy.start()
        for copy in copies:
            copy.wait()


def swap_halves(x):
    return pltpu.roll(x, x.shape[1] // 2, axis=1)


def turn_tables(cosine, sine, width):
    times = width // 128
    cosine = jnp.concatenate([cosine] * times, axis=1) if times > 1 else cosine
    sine = jnp.concatenate([sine] * times, axis=1) if times > 1 else sine
    lane = lax.broadcasted_iota(jnp.int32, sine.shape, 1)
    return cosine, jnp.where(lane < width // 2, -sine, sine)


def any_specs(pieces):
    return [pl.BlockSpec(memory_space=pltpu.HBM) for _ in pieces]


def project_qkv(order, pieces, weight, spread, cosine, sine, width, tok):
    n = len(pieces)
    seq = n * tok

    def kernel(order_ref, *refs):
        parts = refs[:n]
        w_hbm, spread_ref, cos_ref, sin_ref = refs[n : n + 4]
        q_ref, k_ref, v_ref, kt_ref, vt_ref, all_ref, wide, buffer, semaphores, w_ref, w_semaphores = refs[
            n + 4 :
        ]
        fetch_rows(w_hbm, w_ref, w_semaphores)

        @pl.when(pl.program_id(0) == 0)
        def _():
            wide[...] = nn(w_ref[...], spread_ref[...]).astype(BF)

        x = fetch_piece(parts, buffer, semaphores)
        all_ref[...] = x
        mixed = nn(x, wide[...])
        cos, sin = turn_tables(cos_ref[...], sin_ref[...], width)
        q = mixed[:, :width]
        k = mixed[:, width : 2 * width]
        v = mixed[:, 2 * width :].astype(BF)
        q_ref[...] = (q * cos + swap_halves(q) * sin).astype(BF) * (HD**-0.5)
        k = (k * cos + swap_halves(k) * sin).astype(BF)
        k_ref[...] = k
        v_ref[...] = v
        k_turned = k.T
        kt_ref[:HALF, :] = k_turned[:HALF]
        kt_ref[HALF:, :] = k_turned[width // 2 : width // 2 + HALF]
        vt_ref[...] = v.T[:HD]

    rows = lambda s, order: (order[s], 0)
    lanes = lambda s, order: (0, order[s])
    whole = lambda s, order: (0, 0)
    return pl.pallas_call(
        kernel,
        grid_spec=pltpu.PrefetchScalarGridSpec(
            num_scalar_prefetch=1,
            grid=(n,),
            in_specs=any_specs(pieces)
            + [
                pl.BlockSpec(memory_space=pltpu.HBM),
                pl.BlockSpec(spread.shape, whole),
                pl.BlockSpec((tok, 128), rows),
                pl.BlockSpec((tok, 128), rows),
            ],
            out_specs=[
                pl.BlockSpec((tok, width), rows),
                pl.BlockSpec((tok, width), rows),
                pl.BlockSpec((tok, width), rows),
                pl.BlockSpec((HD, tok), lanes),
                pl.BlockSpec((HD, tok), lanes),
                pl.BlockSpec((tok, D), lambda s, order: (s, 0)),
            ],
            scratch_shapes=[
                pltpu.VMEM((D, 3 * width), BF),
                pltpu.VMEM((n, tok, D), BF),
                pltpu.SemaphoreType.DMA((n,)),
                pltpu.VMEM(weight.shape, BF),
                pltpu.SemaphoreType.DMA((chunks(D),)),
            ],
        ),
        out_shape=[
            jax.ShapeDtypeStruct((seq, width), BF),
            jax.ShapeDtypeStruct((seq, width), BF),
            jax.ShapeDtypeStruct((seq, width), BF),
            jax.ShapeDtypeStruct((HD, seq), BF),
            jax.ShapeDtypeStruct((HD, seq), BF),
            jax.ShapeDtypeStruct((seq, D), BF),
        ],
        compiler_params=pltpu.CompilerParams(vmem_limit_bytes=VMEM_LIMIT),
        cost_estimate=LONG,
        name="project_qkv",
    )(order, *pieces, weight, spread, cosine, sine)


def project_out(order, heads_in, pieces, residual):
    n, tok, width = heads_in.shape

    def kernel(order_ref, a_ref, *refs):
        parts = refs[:n]
        x_ref, state_ref, norm_ref, buffer, semaphores = refs[n:]
        step = pl.program_id(0)
        w = fetch_piece(parts, buffer, semaphores)

        @pl.when(step == 0)
        def _():
            state_ref[...] = x_ref[...].astype(F32)

        state_ref[...] += nn(a_ref[0], w)

        @pl.when(step == n - 1)
        def _():
            state = state_ref[...]
            scale = lax.rsqrt(jnp.mean(state * state, axis=-1, keepdims=True) + EPS)
            norm_ref[...] = (state * scale).astype(BF)

    whole = lambda s, order: (0, 0)
    return pl.pallas_call(
        kernel,
        grid_spec=pltpu.PrefetchScalarGridSpec(
            num_scalar_prefetch=1,
            grid=(n,),
            in_specs=[pl.BlockSpec((1, tok, width), lambda s, order: (order[s], 0, 0))]
            + any_specs(pieces)
            + [pl.BlockSpec((tok, D), whole)],
            out_specs=[pl.BlockSpec((tok, D), whole), pl.BlockSpec((tok, D), whole)],
            scratch_shapes=[
                pltpu.VMEM((n, width, D), BF),
                pltpu.SemaphoreType.DMA((n,)),
            ],
        ),
        out_shape=[
            jax.ShapeDtypeStruct((tok, D), F32),
            jax.ShapeDtypeStruct((tok, D), BF),
        ],
        compiler_params=pltpu.CompilerParams(vmem_limit_bytes=VMEM_LIMIT),
        cost_estimate=SHORT,
        name="project_out",
    )(order, heads_in, *pieces, residual)


def feed_forward(pieces, weight):
    n = len(pieces)
    tok = 2 * pieces[0].shape[0]
    seq = n * tok // 2
    ff = weight.shape[1] // 2

    def kernel(*refs):
        parts = refs[:n]
        w_hbm, hidden_ref, factor_ref, all_ref, buffer, semaphores, w_ref, w_semaphores = refs[n:]
        fetch_rows(w_hbm, w_ref, w_semaphores)
        x = fetch_piece(parts, buffer, semaphores, 2)
        all_ref[...] = x
        both = nn(x, w_ref[...])
        gate = both[:, :ff]
        up = both[:, ff:]
        sig = jax.nn.sigmoid(gate)
        silu = gate * sig
        hidden_ref[...] = (silu * up).astype(BF)
        factor_ref[:, :ff] = (up * sig * (1.0 + gate * (1.0 - sig))).astype(BF)
        factor_ref[:, ff:] = silu.astype(BF)

    rows = lambda s: (s, 0)
    return pl.pallas_call(
        kernel,
        grid=(n // 2,),
        in_specs=any_specs(pieces) + [pl.BlockSpec(memory_space=pltpu.HBM)],
        out_specs=[
            pl.BlockSpec((tok, ff), rows),
            pl.BlockSpec((tok, 2 * ff), rows),
            pl.BlockSpec((tok, D), rows),
        ],
        scratch_shapes=[
            pltpu.VMEM((n, tok // 2, D), BF),
            pltpu.SemaphoreType.DMA((n,)),
            pltpu.VMEM(weight.shape, BF),
            pltpu.SemaphoreType.DMA((chunks(D),)),
        ],
        out_shape=[
            jax.ShapeDtypeStruct((seq, ff), BF),
            jax.ShapeDtypeStruct((seq, 2 * ff), BF),
            jax.ShapeDtypeStruct((seq, D), BF),
        ],
        compiler_params=pltpu.CompilerParams(vmem_limit_bytes=VMEM_LIMIT),
        cost_estimate=LONG,
        name="feed_forward",
    )(*pieces, weight)


def feed_backward(factors, grads, weight):
    seq = factors.shape[0]
    ff = weight.shape[0]
    tok = 512

    def kernel(factor_ref, g_ref, w_hbm, out_ref, w_ref, w_semaphores):
        fetch_rows(w_hbm, w_ref, w_semaphores)
        grad_hidden = nt(g_ref[...], w_ref[...])
        factor = factor_ref[...].astype(F32)
        out_ref[:, :ff] = (grad_hidden * factor[:, :ff]).astype(BF)
        out_ref[:, ff:] = (grad_hidden * factor[:, ff:]).astype(BF)

    rows = lambda s: (s, 0)
    return pl.pallas_call(
        kernel,
        grid=(seq // tok,),
        in_specs=[
            pl.BlockSpec((tok, 2 * ff), rows),
            pl.BlockSpec((tok, D), rows),
            pl.BlockSpec(memory_space=pltpu.HBM),
        ],
        out_specs=pl.BlockSpec((tok, 2 * ff), rows),
        scratch_shapes=[pltpu.VMEM(weight.shape, BF), pltpu.SemaphoreType.DMA((chunks(ff),))],
        out_shape=jax.ShapeDtypeStruct((seq, 2 * ff), BF),
        compiler_params=pltpu.CompilerParams(vmem_limit_bytes=VMEM_LIMIT),
        cost_estimate=LONG,
        name="feed_backward",
    )(factors, grads, weight)


def lay_out(pieces):
    n = len(pieces)
    tok = pieces[0].shape[0]

    def kernel(*refs):
        parts = refs[:n]
        out_ref, buffer, in_semaphores, out_semaphores = refs[n:]
        arrive = [
            pltpu.make_async_copy(part, buffer.at[i], in_semaphores.at[i])
            for i, part in enumerate(parts)
        ]
        leave = [
            pltpu.make_async_copy(buffer.at[i], out_ref.at[pl.ds(i * tok, tok)], out_semaphores.at[i])
            for i in range(n)
        ]
        for copy in arrive:
            copy.start()
        for i in range(n):
            arrive[i].wait()
            leave[i].start()
        for copy in leave:
            copy.wait()

    return pl.pallas_call(
        kernel,
        in_specs=any_specs(pieces),
        out_specs=pl.BlockSpec(memory_space=pltpu.HBM),
        scratch_shapes=[
            pltpu.VMEM((n, tok, D), BF),
            pltpu.SemaphoreType.DMA((n,)),
            pltpu.SemaphoreType.DMA((n,)),
        ],
        out_shape=jax.ShapeDtypeStruct((n * tok, D), BF),
        compiler_params=pltpu.CompilerParams(vmem_limit_bytes=VMEM_LIMIT),
        cost_estimate=SHORT,
        name="lay_out",
    )(*pieces)


def branch_back(order, d_two, state, out_grad, pieces):
    n = len(pieces)
    tok = d_two.shape[0]
    width = pieces[0].shape[0]

    def kernel(order_ref, d_ref, state_ref, g_ref, *refs):
        parts = refs[:n]
        grad_ref, branch_ref, heads_ref, buffer, semaphores = refs[n:]

        @pl.when(pl.program_id(0) == 0)
        def _():
            state = state_ref[...]
            scale = lax.rsqrt(jnp.mean(state * state, axis=-1, keepdims=True) + EPS)
            norm = state * scale
            d = d_ref[...]
            grad = g_ref[...].astype(F32) + scale * (
                d - norm * jnp.mean(d * norm, axis=-1, keepdims=True)
            )
            grad_ref[...] = grad
            branch_ref[...] = grad.astype(BF)

        w = fetch_piece(parts, buffer, semaphores)
        heads_ref[0] = nt(branch_ref[...], w).astype(BF)

    whole = lambda s, order: (0, 0)
    return pl.pallas_call(
        kernel,
        grid_spec=pltpu.PrefetchScalarGridSpec(
            num_scalar_prefetch=1,
            grid=(n,),
            in_specs=[
                pl.BlockSpec((tok, D), whole),
                pl.BlockSpec((tok, D), whole),
                pl.BlockSpec((tok, D), whole),
            ]
            + any_specs(pieces),
            out_specs=[
                pl.BlockSpec((tok, D), whole),
                pl.BlockSpec((tok, D), whole),
                pl.BlockSpec((1, tok, width), lambda s, order: (order[s], 0, 0)),
            ],
            scratch_shapes=[
                pltpu.VMEM((n, width, D), BF),
                pltpu.SemaphoreType.DMA((n,)),
            ],
        ),
        out_shape=[
            jax.ShapeDtypeStruct((tok, D), F32),
            jax.ShapeDtypeStruct((tok, D), BF),
            jax.ShapeDtypeStruct((n, tok, width), BF),
        ],
        compiler_params=pltpu.CompilerParams(vmem_limit_bytes=VMEM_LIMIT),
        cost_estimate=SHORT,
        name="branch_back",
    )(order, d_two, state, out_grad, *pieces)


def split_columns(weight, gain, n_ctx, n_dp, ff_rows):
    rows = weight.shape[0]
    ff = ff_rows * n_dp

    def kernel(w_ref, gain_ref, out_ref):
        gains = gain_ref[...]
        for part in range(2):
            for d in range(n_dp):
                for c in range(n_ctx):
                    at = part * FF + (d * n_ctx + c) * ff_rows
                    to = part * ff + d * ff_rows
                    values = w_ref[:, at : at + ff_rows].astype(F32) * gains
                    out_ref[c, :, to : to + ff_rows] = values.astype(BF)

    return pl.pallas_call(
        kernel,
        in_specs=[pl.BlockSpec(memory_space=pltpu.VMEM)] * 2,
        out_specs=pl.BlockSpec(memory_space=pltpu.VMEM),
        out_shape=jax.ShapeDtypeStruct((n_ctx, rows, 2 * ff), BF),
        compiler_params=pltpu.CompilerParams(vmem_limit_bytes=VMEM_LIMIT),
        cost_estimate=LONG,
        name="split_columns",
    )(weight, gain)


def join_columns(sums, weight, gain, n_dp, ff_rows):
    n_ctx, rows, both = sums.shape
    ff = both // 2

    def kernel(s_ref, w_ref, gain_ref, out_ref, gain_out_ref):
        gains = gain_ref[...]
        total = jnp.zeros((rows, ff_rows), F32)
        for part in range(2):
            for d in range(n_dp):
                for c in range(n_ctx):
                    at = part * ff + d * ff_rows
                    to = part * FF + (d * n_ctx + c) * ff_rows
                    values = s_ref[c, :, at : at + ff_rows].astype(F32)
                    total = total + values * w_ref[:, to : to + ff_rows].astype(F32)
                    out_ref[:, to : to + ff_rows] = values * gains
        gain_out_ref[...] = jnp.sum(total, axis=1, keepdims=True)

    return pl.pallas_call(
        kernel,
        in_specs=[pl.BlockSpec(memory_space=pltpu.VMEM)] * 3,
        out_specs=[pl.BlockSpec(memory_space=pltpu.VMEM)] * 2,
        out_shape=[
            jax.ShapeDtypeStruct((rows, 2 * FF), F32),
            jax.ShapeDtypeStruct((rows, 1), F32),
        ],
        compiler_params=pltpu.CompilerParams(vmem_limit_bytes=VMEM_LIMIT),
        cost_estimate=LONG,
        name="join_columns",
    )(sums, weight, gain)


def lane_heads(rows, width):
    lane = lax.broadcasted_iota(jnp.int32, (rows, width), 1)
    return (lane % (width // 2)) // HALF


def attend_forward(slot_of, starts, queries, keys, values_t, heads, tok):
    seq, width = queries.shape
    blocks = seq // tok
    span = 2 * tok

    def kernel(slot_ref, start_ref, q_ref, k_ref, v_ref, attn_ref, slot_attn_ref, full_ref, lse_ref, scores):
        block = pl.program_id(0)
        steps = (block + 2) // 2
        start = start_ref[...]
        here = block * tok + lax.broadcasted_iota(jnp.int32, (1, tok), 1)
        head_of = lane_heads(tok, width)
        q = q_ref[...]
        q_heads = [jnp.where(head_of == h, q, jnp.zeros_like(q)) for h in range(heads)]

        def score(i, peaks):
            rows = pl.ds(pl.multiple_of(i * span, span), span)
            k = k_ref[rows, :]
            there = i * span + lax.broadcasted_iota(jnp.int32, (span, tok), 0)
            visible = (there >= start) & (there <= here)
            out = []
            for h in range(heads):
                s = jnp.where(visible, nt(k, q_heads[h]), MASKED)
                scores[h, rows, :] = s
                out.append(jnp.maximum(peaks[h], jnp.max(s.reshape(span // 8, 8, tok), axis=0)))
            return tuple(out)

        peaks = lax.fori_loop(
            0, steps, score, tuple(jnp.full((8, tok), MASKED, F32) for _ in range(heads))
        )
        peaks = [jnp.max(peak, axis=0, keepdims=True) for peak in peaks]

        def weigh(i, running):
            rows = pl.ds(pl.multiple_of(i * span, span), span)
            v = v_ref[:, rows]
            out = []
            for h in range(heads):
                total, acc = running[h]
                p = jnp.exp(scores[h, rows, :] - peaks[h])
                total = total + jnp.sum(p.reshape(span // 8, 8, tok), axis=0)
                out.append((total, acc + nn(v, p.astype(BF))))
            return tuple(out)

        result = lax.fori_loop(
            0,
            steps,
            weigh,
            tuple((jnp.zeros((8, tok), F32), jnp.zeros((HD, tok), F32)) for _ in range(heads)),
        )
        rows = []
        for h in range(heads):
            total, acc = result[h]
            total = jnp.sum(total, axis=0, keepdims=True)
            rows.append(acc / total)
            lse_ref[0, h : h + 1, :] = peaks[h] + jnp.log(total)
        full = jnp.concatenate(rows, axis=0).T
        full_ref[...] = full
        attn_ref[...] = full.astype(BF)
        slot_attn_ref[...] = full.astype(BF)

    return pl.pallas_call(
        kernel,
        grid_spec=pltpu.PrefetchScalarGridSpec(
            num_scalar_prefetch=1,
            grid=(blocks,),
            in_specs=[
                pl.BlockSpec((1, tok), lambda j, slot: (0, j)),
                pl.BlockSpec((tok, width), lambda j, slot: (j, 0)),
                pl.BlockSpec((seq, width), lambda j, slot: (0, 0)),
                pl.BlockSpec((HD, seq), lambda j, slot: (0, 0)),
            ],
            out_specs=[
                pl.BlockSpec((tok, width), lambda j, slot: (j, 0)),
                pl.BlockSpec((tok, width), lambda j, slot: (slot[j], 0)),
                pl.BlockSpec((tok, width), lambda j, slot: (j, 0)),
                pl.BlockSpec((1, heads, tok), lambda j, slot: (j, 0, 0)),
            ],
            scratch_shapes=[pltpu.VMEM((heads, seq, tok), F32)],
        ),
        out_shape=[
            jax.ShapeDtypeStruct((seq, width), BF),
            jax.ShapeDtypeStruct((seq, width), BF),
            jax.ShapeDtypeStruct((seq, width), F32),
            jax.ShapeDtypeStruct((blocks, heads, tok), F32),
        ],
        compiler_params=pltpu.CompilerParams(vmem_limit_bytes=VMEM_LIMIT),
        cost_estimate=LONG,
        name="attend_forward",
    )(slot_of, starts, queries, keys, values_t)


def attend_backward(
    slot_of, starts, queries, keys, keys_t, values, grads, full, lse, cosine, sine, unsplit, heads, tok
):
    seq, width = queries.shape
    blocks = seq // tok
    span = 2 * tok
    half = width // 2

    def kernel(
        slot_ref, start_ref, q_ref, k_ref, kt_ref, v_ref, g_ref, full_ref, lse_ref, cos_ref, sin_ref, unsplit_ref,
        out_ref, dk, dv,
    ):
        block = pl.program_id(0)
        steps = (block + 2) // 2

        @pl.when(block == 0)
        def _():
            dk[...] = jnp.zeros_like(dk)
            dv[...] = jnp.zeros_like(dv)

        start = start_ref[...]
        here = block * tok + lax.broadcasted_iota(jnp.int32, (1, tok), 1)
        head_of = lane_heads(tok, width)
        wide = lax.broadcasted_iota(jnp.int32, (tok, width), 1) // HD
        q = q_ref[...]
        g = g_ref[...]
        q_heads = [jnp.where(head_of == h, q, jnp.zeros_like(q)) for h in range(heads)]
        g_heads = [jnp.where(wide == h, g, jnp.zeros_like(g)) for h in range(heads)]
        q_stack = jnp.concatenate(q_heads, axis=0)
        g_stack = jnp.concatenate(g_heads, axis=0)
        picks = (
            lax.broadcasted_iota(jnp.int32, (8, width), 1) // HD
            == lax.broadcasted_iota(jnp.int32, (8, width), 0)
        ).astype(F32)
        deltas = lax.dot_general(
            picks,
            g.astype(F32) * full_ref[...],
            (((1,), (1,)), ((), ())),
            preferred_element_type=F32,
            precision=lax.Precision.HIGHEST,
        )

        def step(i, dq):
            rows = pl.ds(pl.multiple_of(i * span, span), span)
            k = k_ref[rows, :]
            v = v_ref[rows, :]
            kt = kt_ref[:, rows]
            there = i * span + lax.broadcasted_iota(jnp.int32, (span, tok), 0)
            visible = (there >= start) & (there <= here)
            probs, grad_scores, out = [], [], []
            for h in range(heads):
                s = jnp.where(visible, nt(k, q_heads[h]), MASKED)
                p = jnp.exp(s - lse_ref[0, h : h + 1, :])
                ds = (p * (nt(v, g_heads[h]) - deltas[h : h + 1, :])).astype(BF)
                probs.append(p.astype(BF))
                grad_scores.append(ds)
                out.append(dq[h] + nn(kt, ds))
            dv[rows, :] += nn(jnp.concatenate(probs, axis=1), g_stack)
            dk[rows, :] += nn(jnp.concatenate(grad_scores, axis=1), q_stack)
            return tuple(out)

        dq = lax.fori_loop(
            0, steps, step, tuple(jnp.zeros((HD, tok), F32) for _ in range(heads))
        )
        dq = jnp.concatenate([x[:HALF] for x in dq] + [x[HALF:] for x in dq], axis=0).T
        here_rows = pl.ds(pl.multiple_of(block * tok, tok), tok)
        cos, sin = turn_tables(cos_ref[here_rows, :], sin_ref[here_rows, :], width)
        dq = (dq * cos - swap_halves(dq) * sin) * (HD**-0.5)
        slot_rows = pl.ds(pl.multiple_of(slot_ref[block] * tok, tok), tok)
        out_ref[slot_rows, :width] = nn(dq.astype(BF), unsplit_ref[...]).astype(BF)

        @pl.when(block == blocks - 1)
        def _():
            lane = lax.broadcasted_iota(jnp.int32, (width, 128), 0)
            column = lax.broadcasted_iota(jnp.int32, (width, 128), 1)
            fold_k = ((lane // half) * HALF + lane % HALF == column).astype(BF)
            fold_v = (lane % HD + HD == column).astype(BF)

            def fold(i, unused):
                rows = pl.ds(pl.multiple_of(i * tok, tok), tok)
                cos, sin = turn_tables(cos_ref[rows, :], sin_ref[rows, :], width)
                a = dk[rows, :]
                a = a * cos - swap_halves(a) * sin
                b = dv[rows, :]
                a_high = a.astype(BF)
                b_high = b.astype(BF)
                terms = (
                    nn(a_high, fold_k)
                    + nn((a - a_high.astype(F32)).astype(BF), fold_k)
                    + nn(b_high, fold_v)
                    + nn((b - b_high.astype(F32)).astype(BF), fold_v)
                )
                slot_rows = pl.ds(pl.multiple_of(slot_ref[i] * tok, tok), tok)
                out_ref[slot_rows, width:] = terms.astype(BF)
                return unused

            lax.fori_loop(0, blocks, fold, 0)

    whole = lambda shape: pl.BlockSpec(shape, lambda j, *_: (0, 0))
    return pl.pallas_call(
        kernel,
        grid_spec=pltpu.PrefetchScalarGridSpec(
            num_scalar_prefetch=1,
            grid=(blocks,),
            in_specs=[
                pl.BlockSpec((1, tok), lambda j, *_: (0, j)),
                pl.BlockSpec((tok, width), lambda j, *_: (j, 0)),
                whole((seq, width)),
                whole((HD, seq)),
                whole((seq, width)),
                pl.BlockSpec((tok, width), lambda j, *_: (j, 0)),
                pl.BlockSpec((tok, width), lambda j, *_: (j, 0)),
                pl.BlockSpec((1, heads, tok), lambda j, *_: (j, 0, 0)),
                whole((seq, 128)),
                whole((seq, 128)),
                whole((width, width)),
            ],
            out_specs=whole((seq, width + 128)),
            scratch_shapes=[pltpu.VMEM((seq, width), F32), pltpu.VMEM((seq, width), F32)],
        ),
        out_shape=jax.ShapeDtypeStruct((seq, width + 128), BF),
        compiler_params=pltpu.CompilerParams(vmem_limit_bytes=VMEM_LIMIT),
        cost_estimate=MEDIUM,
        name="attend_backward",
    )(slot_of, starts, queries, keys, keys_t, values, grads, full, lse, cosine, sine, unsplit)


def outer_rows(activations, gradients):
    return lax.dot_general(
        activations, gradients, (((0,), (0,)), ((), ())), preferred_element_type=F32
    ).astype(BF)


def split_source(width):
    lane = np.arange(width)
    half = lane // (width // 2)
    head = (lane % (width // 2)) // HALF
    return head * HD + half * HALF + lane % HALF


def spread_matrix(width):
    matrix = np.zeros((width + 2 * HD, 3 * width), np.float32)
    lane = np.arange(width)
    matrix[split_source(width), lane] = 1
    matrix[width + (lane // (width // 2)) * HALF + lane % HALF, width + lane] = 1
    matrix[width + HD + lane % HD, 2 * width + lane] = 1
    return jnp.asarray(matrix, BF)


def unsplit_matrix(width):
    matrix = np.zeros((width, width), np.float32)
    matrix[np.arange(width), split_source(width)] = 1
    return jnp.asarray(matrix, BF)


def on_device(
    block_in,
    gain_attn,
    qkv_weight,
    out_weight,
    gain_ffn,
    gate_up_weight,
    down_weight,
    doc_lengths,
    out_grad,
):
    n_ctx = lax.axis_size("ctx")
    n_dp = lax.axis_size("dp")
    me = lax.axis_index("ctx")
    tok = block_in.shape[0]
    seq = tok * n_ctx
    heads = H // n_ctx
    width = heads * HD
    sharers = n_ctx // KVH
    rows = qkv_weight.shape[0]
    ff_rows = down_weight.shape[0]
    ff = ff_rows * n_dp
    columns = width + 2 * HD

    order = me ^ jnp.where(me % 2 == 0, *[jnp.asarray(t) for t in slot_table(n_ctx)])
    slots = jnp.arange(n_ctx, dtype=jnp.int32)
    slot_of = jnp.sum(jnp.where(order[None, :] == slots[:, None], slots[None, :], 0), axis=1)
    index = jnp.arange(seq, dtype=jnp.int32)
    lengths = doc_lengths[0]
    ends = jnp.cumsum(lengths)
    starts = jnp.sum((index[:, None] >= ends[None, :]).astype(jnp.int32) * lengths[None, :], axis=1)
    lane = jnp.arange(128, dtype=F32) % HALF
    frequency = 10000.0 ** (-lane * 2.0 / HD)
    angles = (index - starts).astype(F32)[:, None] * frequency[None, :]
    cosine = jnp.cos(angles)
    sine = jnp.sin(angles)
    starts_row = starts[None, :]

    gain_one = gain_attn.astype(F32)[:, None]
    gain_two = gain_ffn.astype(F32)[:, None]
    qkv = (qkv_weight.astype(F32) * gain_one).astype(BF)
    q_cols = qkv[:, : H * HD].reshape(rows, n_ctx, width).transpose(1, 0, 2)
    k_cols = qkv[:, H * HD : (H + KVH) * HD].reshape(rows, KVH, HD).transpose(1, 0, 2)
    v_cols = qkv[:, (H + KVH) * HD :].reshape(rows, KVH, HD).transpose(1, 0, 2)
    kv_cols = jnp.repeat(jnp.concatenate([k_cols, v_cols], axis=2), sharers, axis=0)
    qkv_own = exchange(jnp.concatenate([q_cols, kv_cols], axis=2)).reshape(n_ctx * rows, columns)
    qkv_part = gather_dp(qkv_own)

    hidden_in = block_in.astype(F32)
    rms_one = lax.rsqrt(jnp.mean(hidden_in * hidden_in, axis=-1, keepdims=True) + EPS)
    one_pieces = gather_slots(after((hidden_in * rms_one).astype(BF), qkv_own), n_ctx)

    owner_pairs = [(b, b % n_dp * n_ctx + b // n_dp) for b in range(n_dp * n_ctx)]
    out_own = lax.ppermute(after(out_weight, one_pieces[1]), ("dp", "ctx"), owner_pairs)
    out_part = gather_dp(after(out_own, qkv_part))
    gate_up_cols = split_columns(gate_up_weight, gain_two, n_ctx, n_dp, ff_rows)
    gate_up_own = exchange(after(gate_up_cols, *one_pieces[: n_ctx // 2])).reshape(
        n_ctx * rows, 2 * ff
    )
    gate_up_part = gather_dp(gate_up_own)
    down_part = gather_dp(after(down_weight, gate_up_part))

    queries, keys, values, keys_t, values_t, all_one = project_qkv(
        order, one_pieces, qkv_part, spread_matrix(width), after(cosine, gate_up_own), sine, width, tok
    )
    out_direct = gather_direct(after(out_part, queries), n_ctx)
    attn, slot_attn, attended, lse = attend_forward(
        slot_of, starts_row, queries, keys, values_t, heads, tok
    )
    attn_tokens = exchange(after(attn, *out_direct).reshape(n_ctx, tok, width))
    out_pieces = gather_rest(out_direct, n_ctx, attn, attn_tokens)
    state, norm_two = project_out(order, attn_tokens, out_pieces, block_in)

    two_pieces = gather_slots(norm_two, n_ctx)
    grad_direct = gather_direct(after(out_grad, *two_pieces), n_ctx)
    hidden, factors, all_two = feed_forward(two_pieces, gate_up_part)
    grad_pieces = gather_rest(grad_direct, n_ctx, hidden)
    all_grad = lay_out(grad_pieces)
    down_terms = outer_rows(hidden, all_grad)
    down_sums = scatter_dp(down_terms)
    grad_gate_up = feed_backward(after(factors, down_terms), all_grad, down_part)

    def rows_of(x, lo, hi):
        return lax.slice_in_dim(x, lo * tok, hi * tok, axis=0)

    d_pairs = scatter_pairs(
        lambda lo, hi: nt(rows_of(grad_gate_up, lo, hi), gate_up_part), tok, n_ctx
    )
    stages = tuple(reversed(range(len(walk(n_ctx, 0)))))
    d_two = scatter_chips(*d_pairs, stages, n_ctx)
    gate_up_terms = outer_rows(after(all_two, *d_pairs), grad_gate_up)
    gate_up_sums = scatter_dp(gate_up_terms)
    hidden_pairs = scatter_pairs(
        lambda lo, hi: nn(rows_of(after(hidden, *d_pairs), lo, hi), down_part), tok, n_ctx
    )

    grad_state, grad_branch, grad_heads = branch_back(
        order, after(d_two, gate_up_terms, *hidden_pairs), state, out_grad, out_pieces
    )
    grad_attn = exchange(grad_heads).reshape(seq, width)
    branch_pieces = gather_slots(after(grad_branch, grad_attn), n_ctx)
    hidden_rest = scatter_chips(*after_each(hidden_pairs, grad_attn), stages[:1], n_ctx)
    grad_mixed = attend_backward(
        slot_of,
        starts_row,
        queries,
        keys,
        keys_t,
        values,
        grad_attn,
        attended,
        lse,
        cosine,
        sine,
        unsplit_matrix(width),
        heads,
        tok,
    )
    grad_mixed = after(grad_mixed, *branch_pieces[:3], *hidden_rest)
    qkv_terms = outer_rows(all_one, grad_mixed)
    qkv_sums = scatter_dp(after(qkv_terms, gate_up_sums))
    d_one = scatter_chips(
        *scatter_pairs(lambda lo, hi: nt(rows_of(grad_mixed, lo, hi), qkv_part), tok, n_ctx),
        stages,
        n_ctx,
    )
    block_out = (state + scatter_chips(*hidden_rest, stages[1:], n_ctx)).astype(BF)
    out_terms = outer_rows(slot_attn, after(lay_out(branch_pieces), qkv_terms))
    out_sums = scatter_dp(after(out_terms, qkv_sums))
    norm_one = hidden_in * rms_one
    input_grad = grad_state + rms_one * (
        d_one - norm_one * jnp.mean(d_one * norm_one, axis=-1, keepdims=True)
    )

    down_weight_grad = after(down_sums, grad_mixed).astype(F32)
    out_weight_grad = lax.ppermute(
        out_sums, ("dp", "ctx"), [(b, a) for a, b in owner_pairs]
    ).astype(F32)
    gate_up_weight_grad, gain_ffn_grad = join_columns(
        exchange(after(gate_up_sums, grad_mixed).reshape(n_ctx, rows, 2 * ff)), gate_up_weight, gain_two, n_dp, ff_rows
    )
    qkv_back = exchange(qkv_sums.reshape(n_ctx, rows, columns)).astype(F32)
    q_back = qkv_back[:, :, :width].transpose(1, 0, 2).reshape(rows, H * HD)
    kv_back = jnp.sum(qkv_back[:, :, width:].reshape(KVH, sharers, rows, 2 * HD), axis=1)
    k_back = kv_back[:, :, :HD].transpose(1, 0, 2).reshape(rows, KVH * HD)
    v_back = kv_back[:, :, HD:].transpose(1, 0, 2).reshape(rows, KVH * HD)
    qkv_back = jnp.concatenate([q_back, k_back, v_back], axis=1)
    qkv_weight_grad = qkv_back * gain_one
    gain_attn_grad = jnp.sum(qkv_back * qkv_weight.astype(F32), axis=1)
    return (
        block_out,
        input_grad,
        gain_attn_grad,
        qkv_weight_grad,
        out_weight_grad,
        gain_ffn_grad[:, 0],
        gate_up_weight_grad,
        down_weight_grad,
    )


def solution(mesh):
    rows = P(("dp", "ctx"), None)
    entries = P(("dp", "ctx"))
    return jax.shard_map(
        on_device,
        mesh=mesh,
        in_specs=(rows, entries, rows, rows, entries, rows, rows, P("dp", None), rows),
        out_specs=(rows, rows, entries, rows, rows, entries, rows, rows),
        check_vma=False,
    )
```

```python
import jax
import jax.numpy as jnp
import numpy as np
from jax import lax
from jax.experimental import pallas as pl
from jax.experimental.pallas import tpu as pltpu
from jax.sharding import PartitionSpec as P

D = 2048
H = 32
KVH = 4
HD = 64
FF = 5632
HALF = HD // 2

EPS = 1e-05
MASKED = -1e30
BF = jnp.bfloat16
F32 = jnp.float32
VMEM_LIMIT = 60 << 20
SHORT = pl.CostEstimate(flops=1 << 20, bytes_accessed=1 << 20, transcendentals=0)
MEDIUM = pl.CostEstimate(flops=2 * 10**10, bytes_accessed=1 << 20, transcendentals=0)
LONG = pl.CostEstimate(flops=10**11, bytes_accessed=1 << 20, transcendentals=0)


def nt(a, b):
    return lax.dot_general(a, b, (((1,), (1,)), ((), ())), preferred_element_type=F32)


def nn(a, b):
    return jnp.dot(a, b, preferred_element_type=F32)


def after(x, *earlier):
    return lax.optimization_barrier((x, *earlier))[0]


def after_each(values, *earlier):
    count = len(values)
    return lax.optimization_barrier((*values, *earlier))[:count]


def walk(n_ctx, parity):
    bits = []
    bit = 2
    while bit < n_ctx:
        bits.append(bit)
        bit *= 2
    return bits if parity == 0 else bits[::-1]


def swap_stage(x, n_ctx, stage):
    pairs = [(c, c ^ walk(n_ctx, c % 2)[stage]) for c in range(n_ctx)]
    return lax.ppermute(x, "ctx", pairs)


def swap_core(x, n_ctx):
    return lax.ppermute(x, "ctx", [(c, c ^ 1) for c in range(n_ctx)])


def slot_table(n_ctx):
    lists = []
    for parity in (0, 1):
        row = [0]
        for bit in walk(n_ctx, parity):
            row = row + [v ^ bit for v in row]
        lists.append(row)
    return np.array(
        [lists[p] + [v ^ 1 for v in lists[1 - p]] for p in (0, 1)], dtype=np.int32
    )


def gather_direct(x, n_ctx):
    return [x] + [swap_stage(x, n_ctx, stage) for stage in range(len(walk(n_ctx, 0)))]


def gather_rest(direct, n_ctx, earlier=None, last=None):
    have = direct[:1]
    for stage in range(len(walk(n_ctx, 0))):
        passed = [block if earlier is None else after(block, earlier) for block in have[1:]]
        have = have + [direct[stage + 1]] + [swap_stage(block, n_ctx, stage) for block in passed]
    return have + [swap_core(block if last is None else after(block, last), n_ctx) for block in have]


def gather_slots(x, n_ctx):
    return gather_rest(gather_direct(x, n_ctx), n_ctx)


def scatter_pairs(term, tok, n_ctx):
    mine = n_ctx // 2
    cut = mine // 2
    sums = []
    for lo, hi in ((cut, mine), (0, cut)):
        arrived = swap_core(term(mine + lo, mine + hi).astype(BF), n_ctx)
        sums.append(term(lo, hi) + arrived.astype(F32))
    return sums


def scatter_chips(upper, lower, stages, n_ctx):
    for stage in stages:
        lower = lower + swap_stage(upper.astype(BF), n_ctx, stage).astype(F32)
        if stage:
            half = lower.shape[0] // 2
            upper, lower = lower[half:], lower[:half]
    return lower if stages[-1] == 0 else (upper, lower)


def exchange(x):
    return lax.all_to_all(x, "ctx", split_axis=0, concat_axis=0, tiled=False)


def gather_dp(x):
    return lax.all_gather(x, "dp", axis=0, tiled=True)


def scatter_dp(x):
    return lax.psum_scatter(x, "dp", scatter_dimension=0, tiled=True)


def fetch_piece(pieces, buffer, semaphores, count=1):
    step = pl.program_id(0)

    @pl.when(step == 0)
    def _():
        for i, piece in enumerate(pieces):
            pltpu.make_async_copy(piece, buffer.at[i], semaphores.at[i]).start()

    for i in range(count):
        at = step * count + i
        pltpu.make_async_copy(pieces[0], buffer.at[at], semaphores.at[at]).wait()
    if count == 1:
        return buffer[step]
    return buffer[pl.ds(step * count, count)].reshape(count * buffer.shape[1], buffer.shape[2])


def chunks(rows):
    return next(count for count in (8, 4, 2, 1) if rows % (16 * count) == 0)


def fetch_rows(source, buffer, semaphores):
    count = semaphores.shape[0]
    rows = source.shape[0] // count

    @pl.when(pl.program_id(0) == 0)
    def _():
        copies = [
            pltpu.make_async_copy(
                source.at[pl.ds(i * rows, rows)], buffer.at[pl.ds(i * rows, rows)], semaphores.at[i]
            )
            for i in range(count)
        ]
        for copy in copies:
            copy.start()
        for copy in copies:
            copy.wait()


def swap_halves(x):
    return pltpu.roll(x, x.shape[1] // 2, axis=1)


def turn_tables(cosine, sine, width):
    times = width // 128
    cosine = jnp.concatenate([cosine] * times, axis=1) if times > 1 else cosine
    sine = jnp.concatenate([sine] * times, axis=1) if times > 1 else sine
    lane = lax.broadcasted_iota(jnp.int32, sine.shape, 1)
    return cosine, jnp.where(lane < width // 2, -sine, sine)


def any_specs(pieces):
    return [pl.BlockSpec(memory_space=pltpu.HBM) for _ in pieces]


def project_qkv(order, pieces, weight, spread, widen, cosine, sine, width, tok):
    n = len(pieces)
    seq = n * tok

    def kernel(order_ref, *refs):
        parts = refs[:n]
        w_hbm, spread_ref, widen_ref, cos_ref, sin_ref = refs[n : n + 5]
        q_ref, k_ref, v_ref, kt_ref, vt_ref, all_ref, wide, buffer, semaphores, w_ref, w_semaphores = refs[
            n + 5 :
        ]
        fetch_rows(w_hbm, w_ref, w_semaphores)

        @pl.when(pl.program_id(0) == 0)
        def _():
            wide[...] = nn(w_ref[...], spread_ref[...]).astype(BF)

        x = fetch_piece(parts, buffer, semaphores)
        all_ref[...] = x
        mixed = nn(x, wide[...])
        cos, sin = turn_tables(cos_ref[...], sin_ref[...], width)
        q = mixed[:, :width]
        q_ref[...] = (q * cos + swap_halves(q) * sin).astype(BF) * (HD**-0.5)
        lane = lax.broadcasted_iota(jnp.int32, (tok, 128), 1)
        key_sine = jnp.where(lane < HALF, -sin_ref[...], sin_ref[...])
        both = jnp.where(
            lane < HD,
            mixed[:, width : width + 128] * cos_ref[...] + mixed[:, width + 128 :] * key_sine,
            mixed[:, width : width + 128],
        ).astype(BF)
        repeated = nn(both, widen_ref[...]).astype(BF)
        k_ref[...] = repeated[:, :width]
        v_ref[...] = repeated[:, width:]
        turned = both.T
        kt_ref[...] = turned[:HD]
        vt_ref[...] = turned[HD:]

    rows = lambda s, order: (order[s], 0)
    lanes = lambda s, order: (0, order[s])
    whole = lambda s, order: (0, 0)
    return pl.pallas_call(
        kernel,
        grid_spec=pltpu.PrefetchScalarGridSpec(
            num_scalar_prefetch=1,
            grid=(n,),
            in_specs=any_specs(pieces)
            + [
                pl.BlockSpec(memory_space=pltpu.HBM),
                pl.BlockSpec(spread.shape, whole),
                pl.BlockSpec(widen.shape, whole),
                pl.BlockSpec((tok, 128), rows),
                pl.BlockSpec((tok, 128), rows),
            ],
            out_specs=[
                pl.BlockSpec((tok, width), rows),
                pl.BlockSpec((tok, width), rows),
                pl.BlockSpec((tok, width), rows),
                pl.BlockSpec((HD, tok), lanes),
                pl.BlockSpec((HD, tok), lanes),
                pl.BlockSpec((tok, D), lambda s, order: (s, 0)),
            ],
            scratch_shapes=[
                pltpu.VMEM((D, width + 256), BF),
                pltpu.VMEM((n, tok, D), BF),
                pltpu.SemaphoreType.DMA((n,)),
                pltpu.VMEM(weight.shape, BF),
                pltpu.SemaphoreType.DMA((chunks(D),)),
            ],
        ),
        out_shape=[
            jax.ShapeDtypeStruct((seq, width), BF),
            jax.ShapeDtypeStruct((seq, width), BF),
            jax.ShapeDtypeStruct((seq, width), BF),
            jax.ShapeDtypeStruct((HD, seq), BF),
            jax.ShapeDtypeStruct((HD, seq), BF),
            jax.ShapeDtypeStruct((seq, D), BF),
        ],
        compiler_params=pltpu.CompilerParams(vmem_limit_bytes=VMEM_LIMIT),
        cost_estimate=LONG,
        name="project_qkv",
    )(order, *pieces, weight, spread, widen, cosine, sine)


def project_out(order, heads_in, pieces, residual):
    n, tok, width = heads_in.shape

    def kernel(order_ref, a_ref, *refs):
        parts = refs[:n]
        x_ref, state_ref, norm_ref, buffer, semaphores = refs[n:]
        step = pl.program_id(0)
        w = fetch_piece(parts, buffer, semaphores)

        @pl.when(step == 0)
        def _():
            state_ref[...] = x_ref[...].astype(F32)

        state_ref[...] += nn(a_ref[0], w)

        @pl.when(step == n - 1)
        def _():
            state = state_ref[...]
            scale = lax.rsqrt(jnp.mean(state * state, axis=-1, keepdims=True) + EPS)
            norm_ref[...] = (state * scale).astype(BF)

    whole = lambda s, order: (0, 0)
    return pl.pallas_call(
        kernel,
        grid_spec=pltpu.PrefetchScalarGridSpec(
            num_scalar_prefetch=1,
            grid=(n,),
            in_specs=[pl.BlockSpec((1, tok, width), lambda s, order: (order[s], 0, 0))]
            + any_specs(pieces)
            + [pl.BlockSpec((tok, D), whole)],
            out_specs=[pl.BlockSpec((tok, D), whole), pl.BlockSpec((tok, D), whole)],
            scratch_shapes=[
                pltpu.VMEM((n, width, D), BF),
                pltpu.SemaphoreType.DMA((n,)),
            ],
        ),
        out_shape=[
            jax.ShapeDtypeStruct((tok, D), F32),
            jax.ShapeDtypeStruct((tok, D), BF),
        ],
        compiler_params=pltpu.CompilerParams(vmem_limit_bytes=VMEM_LIMIT),
        cost_estimate=SHORT,
        name="project_out",
    )(order, heads_in, *pieces, residual)


def feed_forward(pieces, weight):
    n = len(pieces)
    tok = 2 * pieces[0].shape[0]
    seq = n * tok // 2
    ff = weight.shape[1] // 2

    def kernel(*refs):
        parts = refs[:n]
        w_hbm, hidden_ref, factor_ref, all_ref, buffer, semaphores, w_ref, w_semaphores = refs[n:]
        fetch_rows(w_hbm, w_ref, w_semaphores)
        x = fetch_piece(parts, buffer, semaphores, 2)
        all_ref[...] = x
        both = nn(x, w_ref[...])
        gate = both[:, :ff]
        up = both[:, ff:]
        sig = jax.nn.sigmoid(gate)
        silu = gate * sig
        hidden_ref[...] = (silu * up).astype(BF)
        factor_ref[:, :ff] = (up * sig * (1.0 + gate * (1.0 - sig))).astype(BF)
        factor_ref[:, ff:] = silu.astype(BF)

    rows = lambda s: (s, 0)
    return pl.pallas_call(
        kernel,
        grid=(n // 2,),
        in_specs=any_specs(pieces) + [pl.BlockSpec(memory_space=pltpu.HBM)],
        out_specs=[
            pl.BlockSpec((tok, ff), rows),
            pl.BlockSpec((tok, 2 * ff), rows),
            pl.BlockSpec((tok, D), rows),
        ],
        scratch_shapes=[
            pltpu.VMEM((n, tok // 2, D), BF),
            pltpu.SemaphoreType.DMA((n,)),
            pltpu.VMEM(weight.shape, BF),
            pltpu.SemaphoreType.DMA((chunks(D),)),
        ],
        out_shape=[
            jax.ShapeDtypeStruct((seq, ff), BF),
            jax.ShapeDtypeStruct((seq, 2 * ff), BF),
            jax.ShapeDtypeStruct((seq, D), BF),
        ],
        compiler_params=pltpu.CompilerParams(vmem_limit_bytes=VMEM_LIMIT),
        cost_estimate=LONG,
        name="feed_forward",
    )(*pieces, weight)


def feed_backward(factors, grads, weight):
    seq = factors.shape[0]
    ff = weight.shape[0]
    tok = 512

    def kernel(factor_ref, g_ref, w_hbm, out_ref, w_ref, w_semaphores, turned):
        fetch_rows(w_hbm, w_ref, w_semaphores)

        @pl.when(pl.program_id(0) == 0)
        def _():
            turned[...] = w_ref[...].T

        grad_hidden = nn(g_ref[...], turned[...])
        factor = factor_ref[...].astype(F32)
        out_ref[:, :ff] = (grad_hidden * factor[:, :ff]).astype(BF)
        out_ref[:, ff:] = (grad_hidden * factor[:, ff:]).astype(BF)

    rows = lambda s: (s, 0)
    return pl.pallas_call(
        kernel,
        grid=(seq // tok,),
        in_specs=[
            pl.BlockSpec((tok, 2 * ff), rows),
            pl.BlockSpec((tok, D), rows),
            pl.BlockSpec(memory_space=pltpu.HBM),
        ],
        out_specs=pl.BlockSpec((tok, 2 * ff), rows),
        scratch_shapes=[
            pltpu.VMEM(weight.shape, BF),
            pltpu.SemaphoreType.DMA((chunks(ff),)),
            pltpu.VMEM((D, ff), BF),
        ],
        out_shape=jax.ShapeDtypeStruct((seq, 2 * ff), BF),
        compiler_params=pltpu.CompilerParams(vmem_limit_bytes=VMEM_LIMIT),
        cost_estimate=LONG,
        name="feed_backward",
    )(factors, grads, weight)


def lay_out(pieces):
    n = len(pieces)
    tok = pieces[0].shape[0]

    def kernel(*refs):
        parts = refs[:n]
        out_ref, buffer, in_semaphores, out_semaphores = refs[n:]
        arrive = [
            pltpu.make_async_copy(part, buffer.at[i], in_semaphores.at[i])
            for i, part in enumerate(parts)
        ]
        leave = [
            pltpu.make_async_copy(buffer.at[i], out_ref.at[pl.ds(i * tok, tok)], out_semaphores.at[i])
            for i in range(n)
        ]
        for copy in arrive:
            copy.start()
        for i in range(n):
            arrive[i].wait()
            leave[i].start()
        for copy in leave:
            copy.wait()

    return pl.pallas_call(
        kernel,
        in_specs=any_specs(pieces),
        out_specs=pl.BlockSpec(memory_space=pltpu.HBM),
        scratch_shapes=[
            pltpu.VMEM((n, tok, D), BF),
            pltpu.SemaphoreType.DMA((n,)),
            pltpu.SemaphoreType.DMA((n,)),
        ],
        out_shape=jax.ShapeDtypeStruct((n * tok, D), BF),
        compiler_params=pltpu.CompilerParams(vmem_limit_bytes=VMEM_LIMIT),
        cost_estimate=SHORT,
        name="lay_out",
    )(*pieces)


def branch_back(order, d_two, state, out_grad, pieces):
    n = len(pieces)
    tok = d_two.shape[0]
    width = pieces[0].shape[0]

    def kernel(order_ref, d_ref, state_ref, g_ref, *refs):
        parts = refs[:n]
        grad_ref, branch_ref, heads_ref, buffer, semaphores = refs[n:]

        @pl.when(pl.program_id(0) == 0)
        def _():
            state = state_ref[...]
            scale = lax.rsqrt(jnp.mean(state * state, axis=-1, keepdims=True) + EPS)
            norm = state * scale
            d = d_ref[...]
            grad = g_ref[...].astype(F32) + scale * (
                d - norm * jnp.mean(d * norm, axis=-1, keepdims=True)
            )
            grad_ref[...] = grad
            branch_ref[...] = grad.astype(BF)

        w = fetch_piece(parts, buffer, semaphores)
        heads_ref[0] = nt(branch_ref[...], w).astype(BF)

    whole = lambda s, order: (0, 0)
    return pl.pallas_call(
        kernel,
        grid_spec=pltpu.PrefetchScalarGridSpec(
            num_scalar_prefetch=1,
            grid=(n,),
            in_specs=[
                pl.BlockSpec((tok, D), whole),
                pl.BlockSpec((tok, D), whole),
                pl.BlockSpec((tok, D), whole),
            ]
            + any_specs(pieces),
            out_specs=[
                pl.BlockSpec((tok, D), whole),
                pl.BlockSpec((tok, D), whole),
                pl.BlockSpec((1, tok, width), lambda s, order: (order[s], 0, 0)),
            ],
            scratch_shapes=[
                pltpu.VMEM((n, width, D), BF),
                pltpu.SemaphoreType.DMA((n,)),
            ],
        ),
        out_shape=[
            jax.ShapeDtypeStruct((tok, D), F32),
            jax.ShapeDtypeStruct((tok, D), BF),
            jax.ShapeDtypeStruct((n, tok, width), BF),
        ],
        compiler_params=pltpu.CompilerParams(vmem_limit_bytes=VMEM_LIMIT),
        cost_estimate=SHORT,
        name="branch_back",
    )(order, d_two, state, out_grad, *pieces)


def split_columns(weight, gain, n_ctx, n_dp, ff_rows):
    rows = weight.shape[0]
    ff = ff_rows * n_dp

    def kernel(w_ref, gain_ref, out_ref):
        gains = gain_ref[...]
        for part in range(2):
            for d in range(n_dp):
                for c in range(n_ctx):
                    at = part * FF + (d * n_ctx + c) * ff_rows
                    to = part * ff + d * ff_rows
                    values = w_ref[:, at : at + ff_rows].astype(F32) * gains
                    out_ref[c, :, to : to + ff_rows] = values.astype(BF)

    return pl.pallas_call(
        kernel,
        in_specs=[pl.BlockSpec(memory_space=pltpu.VMEM)] * 2,
        out_specs=pl.BlockSpec(memory_space=pltpu.VMEM),
        out_shape=jax.ShapeDtypeStruct((n_ctx, rows, 2 * ff), BF),
        compiler_params=pltpu.CompilerParams(vmem_limit_bytes=VMEM_LIMIT),
        cost_estimate=LONG,
        name="split_columns",
    )(weight, gain)


def join_columns(sums, weight, gain, n_dp, ff_rows):
    n_ctx, rows, both = sums.shape
    ff = both // 2

    def kernel(s_ref, w_ref, gain_ref, out_ref, gain_out_ref):
        gains = gain_ref[...]
        total = jnp.zeros((rows, ff_rows), F32)
        for part in range(2):
            for d in range(n_dp):
                for c in range(n_ctx):
                    at = part * ff + d * ff_rows
                    to = part * FF + (d * n_ctx + c) * ff_rows
                    values = s_ref[c, :, at : at + ff_rows].astype(F32)
                    total = total + values * w_ref[:, to : to + ff_rows].astype(F32)
                    out_ref[:, to : to + ff_rows] = values * gains
        gain_out_ref[...] = jnp.sum(total, axis=1, keepdims=True)

    return pl.pallas_call(
        kernel,
        in_specs=[pl.BlockSpec(memory_space=pltpu.VMEM)] * 3,
        out_specs=[pl.BlockSpec(memory_space=pltpu.VMEM)] * 2,
        out_shape=[
            jax.ShapeDtypeStruct((rows, 2 * FF), F32),
            jax.ShapeDtypeStruct((rows, 1), F32),
        ],
        compiler_params=pltpu.CompilerParams(vmem_limit_bytes=VMEM_LIMIT),
        cost_estimate=LONG,
        name="join_columns",
    )(sums, weight, gain)


def lane_heads(rows, width):
    lane = lax.broadcasted_iota(jnp.int32, (rows, width), 1)
    return (lane % (width // 2)) // HALF


def attend_forward(slot_of, starts, queries, keys, values_t, heads, tok, first, count, before):
    seq, width = queries.shape
    blocks = seq // tok
    span = 2 * tok

    def kernel(slot_ref, start_ref, q_ref, k_ref, v_ref, *refs):
        attn_ref, slot_attn_ref, full_ref, lse_ref, scores = refs[len(before) :]
        block = first + pl.program_id(0)
        steps = (block + 2) // 2
        start = start_ref[...]
        here = block * tok + lax.broadcasted_iota(jnp.int32, (1, tok), 1)
        head_of = lane_heads(tok, width)
        q = q_ref[...]
        q_heads = [jnp.where(head_of == h, q, jnp.zeros_like(q)) for h in range(heads)]

        def score(i, peaks):
            rows = pl.ds(pl.multiple_of(i * span, span), span)
            k = k_ref[rows, :]
            there = i * span + lax.broadcasted_iota(jnp.int32, (span, tok), 0)
            visible = (there >= start) & (there <= here)
            out = []
            for h in range(heads):
                s = jnp.where(visible, nt(k, q_heads[h]), MASKED)
                scores[h, rows, :] = s
                out.append(jnp.maximum(peaks[h], jnp.max(s.reshape(span // 8, 8, tok), axis=0)))
            return tuple(out)

        peaks = lax.fori_loop(
            0, steps, score, tuple(jnp.full((8, tok), MASKED, F32) for _ in range(heads))
        )
        peaks = [jnp.max(peak, axis=0, keepdims=True) for peak in peaks]

        def weigh(i, running):
            rows = pl.ds(pl.multiple_of(i * span, span), span)
            v = v_ref[:, rows]
            out = []
            for h in range(heads):
                total, acc = running[h]
                p = jnp.exp(scores[h, rows, :] - peaks[h])
                total = total + jnp.sum(p.reshape(span // 8, 8, tok), axis=0)
                out.append((total, acc + nn(v, p.astype(BF))))
            return tuple(out)

        result = lax.fori_loop(
            0,
            steps,
            weigh,
            tuple((jnp.zeros((8, tok), F32), jnp.zeros((HD, tok), F32)) for _ in range(heads)),
        )
        rows = []
        for h in range(heads):
            total, acc = result[h]
            total = jnp.sum(total, axis=0, keepdims=True)
            rows.append(acc / total)
            lse_ref[0, h : h + 1, :] = peaks[h] + jnp.log(total)
        full = jnp.concatenate(rows, axis=0).T
        full_ref[...] = full
        attn_ref[...] = full.astype(BF)
        slot_attn_ref[...] = full.astype(BF)

    return pl.pallas_call(
        kernel,
        grid_spec=pltpu.PrefetchScalarGridSpec(
            num_scalar_prefetch=1,
            grid=(count,),
            in_specs=[
                pl.BlockSpec((1, tok), lambda j, slot: (0, first + j)),
                pl.BlockSpec((tok, width), lambda j, slot: (first + j, 0)),
                pl.BlockSpec((seq, width), lambda j, slot: (0, 0)),
                pl.BlockSpec((HD, seq), lambda j, slot: (0, 0)),
            ]
            + [pl.BlockSpec(memory_space=pltpu.HBM)] * len(before),
            out_specs=[
                pl.BlockSpec((tok, width), lambda j, slot: (first + j, 0)),
                pl.BlockSpec((tok, width), lambda j, slot: (slot[first + j], 0)),
                pl.BlockSpec((tok, width), lambda j, slot: (first + j, 0)),
                pl.BlockSpec((1, heads, tok), lambda j, slot: (first + j, 0, 0)),
            ],
            scratch_shapes=[pltpu.VMEM((heads, seq, tok), F32)],
        ),
        out_shape=[
            jax.ShapeDtypeStruct((seq, width), BF),
            jax.ShapeDtypeStruct((seq, width), BF),
            jax.ShapeDtypeStruct((seq, width), F32),
            jax.ShapeDtypeStruct((blocks, heads, tok), F32),
        ],
        input_output_aliases={5 + i: i for i in range(len(before))},
        compiler_params=pltpu.CompilerParams(vmem_limit_bytes=VMEM_LIMIT),
        cost_estimate=LONG,
        name="attend_forward",
    )(slot_of, starts, queries, keys, values_t, *before)


def attend_backward(
    slot_of, starts, queries, keys, keys_t, values, grads, full, lse, cosine, sine, unsplit, heads, tok
):
    seq, width = queries.shape
    blocks = seq // tok
    span = 2 * tok
    half = width // 2

    def kernel(
        slot_ref, start_ref, q_ref, k_ref, kt_ref, v_ref, g_ref, full_ref, lse_ref, cos_ref, sin_ref, unsplit_ref,
        out_ref, dk, dv,
    ):
        block = pl.program_id(0)
        steps = (block + 2) // 2

        @pl.when(block == 0)
        def _():
            dk[...] = jnp.zeros_like(dk)
            dv[...] = jnp.zeros_like(dv)

        start = start_ref[...]
        here = block * tok + lax.broadcasted_iota(jnp.int32, (1, tok), 1)
        head_of = lane_heads(tok, width)
        wide = lax.broadcasted_iota(jnp.int32, (tok, width), 1) // HD
        q = q_ref[...]
        g = g_ref[...]
        q_heads = [jnp.where(head_of == h, q, jnp.zeros_like(q)) for h in range(heads)]
        g_heads = [jnp.where(wide == h, g, jnp.zeros_like(g)) for h in range(heads)]
        q_stack = jnp.concatenate(q_heads, axis=0)
        g_stack = jnp.concatenate(g_heads, axis=0)
        picks = (
            lax.broadcasted_iota(jnp.int32, (8, width), 1) // HD
            == lax.broadcasted_iota(jnp.int32, (8, width), 0)
        ).astype(F32)
        deltas = lax.dot_general(
            picks,
            g.astype(F32) * full_ref[...],
            (((1,), (1,)), ((), ())),
            preferred_element_type=F32,
            precision=lax.Precision.HIGHEST,
        )

        def step(i, dq):
            rows = pl.ds(pl.multiple_of(i * span, span), span)
            k = k_ref[rows, :]
            v = v_ref[rows, :]
            kt = kt_ref[:, rows]
            there = i * span + lax.broadcasted_iota(jnp.int32, (span, tok), 0)
            visible = (there >= start) & (there <= here)
            probs, grad_scores, out = [], [], []
            for h in range(heads):
                s = jnp.where(visible, nt(k, q_heads[h]), MASKED)
                p = jnp.exp(s - lse_ref[0, h : h + 1, :])
                ds = (p * (nt(v, g_heads[h]) - deltas[h : h + 1, :])).astype(BF)
                probs.append(p.astype(BF))
                grad_scores.append(ds)
                out.append(dq[h] + nn(kt, ds))
            dv[rows, :] += nn(jnp.concatenate(probs, axis=1), g_stack)
            dk[rows, :] += nn(jnp.concatenate(grad_scores, axis=1), q_stack)
            return tuple(out)

        dq = lax.fori_loop(
            0, steps, step, tuple(jnp.zeros((HD, tok), F32) for _ in range(heads))
        )
        dq = jnp.concatenate([x[:HALF] for x in dq] + [x[HALF:] for x in dq], axis=0).T
        here_rows = pl.ds(pl.multiple_of(block * tok, tok), tok)
        cos, sin = turn_tables(cos_ref[here_rows, :], sin_ref[here_rows, :], width)
        dq = (dq * cos - swap_halves(dq) * sin) * (HD**-0.5)
        slot_rows = pl.ds(pl.multiple_of(slot_ref[block] * tok, tok), tok)
        out_ref[slot_rows, :width] = nn(dq.astype(BF), unsplit_ref[...]).astype(BF)

        @pl.when(block == blocks - 1)
        def _():
            lane = lax.broadcasted_iota(jnp.int32, (width, 128), 0)
            column = lax.broadcasted_iota(jnp.int32, (width, 128), 1)
            fold_k = ((lane // half) * HALF + lane % HALF == column).astype(BF)
            fold_v = (lane % HD + HD == column).astype(BF)

            def fold(i, unused):
                rows = pl.ds(pl.multiple_of(i * tok, tok), tok)
                cos, sin = turn_tables(cos_ref[rows, :], sin_ref[rows, :], width)
                a = dk[rows, :]
                a = a * cos - swap_halves(a) * sin
                b = dv[rows, :]
                a_high = a.astype(BF)
                b_high = b.astype(BF)
                terms = (
                    nn(a_high, fold_k)
                    + nn((a - a_high.astype(F32)).astype(BF), fold_k)
                    + nn(b_high, fold_v)
                    + nn((b - b_high.astype(F32)).astype(BF), fold_v)
                )
                slot_rows = pl.ds(pl.multiple_of(slot_ref[i] * tok, tok), tok)
                out_ref[slot_rows, width:] = terms.astype(BF)
                return unused

            lax.fori_loop(0, blocks, fold, 0)

    whole = lambda shape: pl.BlockSpec(shape, lambda j, *_: (0, 0))
    return pl.pallas_call(
        kernel,
        grid_spec=pltpu.PrefetchScalarGridSpec(
            num_scalar_prefetch=1,
            grid=(blocks,),
            in_specs=[
                pl.BlockSpec((1, tok), lambda j, *_: (0, j)),
                pl.BlockSpec((tok, width), lambda j, *_: (j, 0)),
                whole((seq, width)),
                whole((HD, seq)),
                whole((seq, width)),
                pl.BlockSpec((tok, width), lambda j, *_: (j, 0)),
                pl.BlockSpec((tok, width), lambda j, *_: (j, 0)),
                pl.BlockSpec((1, heads, tok), lambda j, *_: (j, 0, 0)),
                whole((seq, 128)),
                whole((seq, 128)),
                whole((width, width)),
            ],
            out_specs=whole((seq, width + 128)),
            scratch_shapes=[pltpu.VMEM((seq, width), F32), pltpu.VMEM((seq, width), F32)],
        ),
        out_shape=jax.ShapeDtypeStruct((seq, width + 128), BF),
        compiler_params=pltpu.CompilerParams(vmem_limit_bytes=VMEM_LIMIT),
        cost_estimate=MEDIUM,
        name="attend_backward",
    )(slot_of, starts, queries, keys, keys_t, values, grads, full, lse, cosine, sine, unsplit)


def outer_rows(activations, gradients):
    return lax.dot_general(
        activations, gradients, (((0,), (0,)), ((), ())), preferred_element_type=F32
    ).astype(BF)


def split_source(width):
    lane = np.arange(width)
    half = lane // (width // 2)
    head = (lane % (width // 2)) // HALF
    return head * HD + half * HALF + lane % HALF


def spread_matrix(width):
    matrix = np.zeros((width + 2 * HD, width + 256), np.float32)
    lane = np.arange(width)
    matrix[split_source(width), lane] = 1
    lane = np.arange(2 * HD)
    matrix[width + lane, width + lane] = 1
    lane = np.arange(HD)
    matrix[width + (lane + HALF) % HD, width + 128 + lane] = 1
    return jnp.asarray(matrix, BF)


def widen_matrix(width):
    matrix = np.zeros((2 * HD, 2 * width), np.float32)
    lane = np.arange(width)
    matrix[(lane // (width // 2)) * HALF + lane % HALF, lane] = 1
    matrix[HD + lane % HD, width + lane] = 1
    return jnp.asarray(matrix, BF)


def unsplit_matrix(width):
    matrix = np.zeros((width, width), np.float32)
    matrix[np.arange(width), split_source(width)] = 1
    return jnp.asarray(matrix, BF)


def on_device(
    block_in,
    gain_attn,
    qkv_weight,
    out_weight,
    gain_ffn,
    gate_up_weight,
    down_weight,
    doc_lengths,
    out_grad,
):
    n_ctx = lax.axis_size("ctx")
    n_dp = lax.axis_size("dp")
    me = lax.axis_index("ctx")
    tok = block_in.shape[0]
    seq = tok * n_ctx
    heads = H // n_ctx
    width = heads * HD
    sharers = n_ctx // KVH
    rows = qkv_weight.shape[0]
    ff_rows = down_weight.shape[0]
    ff = ff_rows * n_dp
    columns = width + 2 * HD

    order = me ^ jnp.where(me % 2 == 0, *[jnp.asarray(t) for t in slot_table(n_ctx)])
    slots = jnp.arange(n_ctx, dtype=jnp.int32)
    slot_of = jnp.sum(jnp.where(order[None, :] == slots[:, None], slots[None, :], 0), axis=1)
    index = jnp.arange(seq, dtype=jnp.int32)
    lengths = doc_lengths[0]
    ends = jnp.cumsum(lengths)
    starts = jnp.sum((index[:, None] >= ends[None, :]).astype(jnp.int32) * lengths[None, :], axis=1)
    lane = jnp.arange(128, dtype=F32) % HALF
    frequency = 10000.0 ** (-lane * 2.0 / HD)
    angles = (index - starts).astype(F32)[:, None] * frequency[None, :]
    cosine = jnp.cos(angles)
    sine = jnp.sin(angles)
    starts_row = starts[None, :]

    gain_one = gain_attn.astype(F32)[:, None]
    gain_two = gain_ffn.astype(F32)[:, None]
    qkv = (qkv_weight.astype(F32) * gain_one).astype(BF)
    q_cols = qkv[:, : H * HD].reshape(rows, n_ctx, width).transpose(1, 0, 2)
    k_cols = qkv[:, H * HD : (H + KVH) * HD].reshape(rows, KVH, HD).transpose(1, 0, 2)
    v_cols = qkv[:, (H + KVH) * HD :].reshape(rows, KVH, HD).transpose(1, 0, 2)
    kv_cols = jnp.repeat(jnp.concatenate([k_cols, v_cols], axis=2), sharers, axis=0)
    qkv_own = exchange(jnp.concatenate([q_cols, kv_cols], axis=2)).reshape(n_ctx * rows, columns)
    qkv_part = gather_dp(qkv_own)

    hidden_in = block_in.astype(F32)
    rms_one = lax.rsqrt(jnp.mean(hidden_in * hidden_in, axis=-1, keepdims=True) + EPS)
    one_pieces = gather_slots(after((hidden_in * rms_one).astype(BF), qkv_own), n_ctx)

    owner_pairs = [(b, b % n_dp * n_ctx + b // n_dp) for b in range(n_dp * n_ctx)]
    out_own = lax.ppermute(after(out_weight, one_pieces[1]), ("dp", "ctx"), owner_pairs)
    out_part = gather_dp(after(out_own, qkv_part))
    gate_up_cols = split_columns(gate_up_weight, gain_two, n_ctx, n_dp, ff_rows)
    gate_up_own = exchange(after(gate_up_cols, *one_pieces[: n_ctx // 2])).reshape(
        n_ctx * rows, 2 * ff
    )
    gate_up_part = gather_dp(gate_up_own)
    down_part = gather_dp(after(down_weight, gate_up_own))

    grad_direct = gather_direct(after(out_grad, *one_pieces[: n_ctx // 2]), n_ctx)

    queries, keys, values, keys_t, values_t, all_one = project_qkv(
        order, one_pieces, qkv_part, spread_matrix(width), widen_matrix(width), cosine, sine, width, tok
    )
    grad_pieces = gather_rest(grad_direct, n_ctx, queries)
    queries = after(queries, gate_up_own, *grad_direct)
    part = n_ctx * 5 // 8
    begun = attend_forward(slot_of, starts_row, queries, keys, values_t, heads, tok, 0, part, ())
    out_direct = gather_direct(after(out_part, begun[2]), n_ctx)
    attn, slot_attn, attended, lse = attend_forward(
        slot_of,
        starts_row,
        after(queries, *grad_pieces[: n_ctx // 2]),
        keys,
        values_t,
        heads,
        tok,
        part,
        n_ctx - part,
        tuple(begun),
    )
    attn_tokens = exchange(after(attn, *out_direct).reshape(n_ctx, tok, width))
    out_pieces = gather_rest(out_direct, n_ctx, attn, attn_tokens)
    state, norm_two = project_out(order, attn_tokens, out_pieces, block_in)

    two_pieces = gather_slots(norm_two, n_ctx)
    hidden, factors, all_two = feed_forward(two_pieces, gate_up_part)
    all_grad = lay_out(grad_pieces)
    down_terms = outer_rows(hidden, all_grad)
    down_sums = scatter_dp(down_terms)
    grad_gate_up = feed_backward(after(factors, down_terms), all_grad, down_part)

    def rows_of(x, lo, hi):
        return lax.slice_in_dim(x, lo * tok, hi * tok, axis=0)

    d_pairs = scatter_pairs(
        lambda lo, hi: nt(rows_of(grad_gate_up, lo, hi), gate_up_part), tok, n_ctx
    )
    stages = tuple(reversed(range(len(walk(n_ctx, 0)))))
    d_two = scatter_chips(*d_pairs, stages, n_ctx)
    gate_up_terms = outer_rows(after(all_two, *d_pairs), grad_gate_up)
    gate_up_sums = scatter_dp(gate_up_terms)
    hidden_pairs = scatter_pairs(
        lambda lo, hi: nn(rows_of(after(hidden, *d_pairs), lo, hi), down_part), tok, n_ctx
    )

    grad_state, grad_branch, grad_heads = branch_back(
        order, after(d_two, gate_up_terms, *hidden_pairs), state, out_grad, out_pieces
    )
    grad_attn = exchange(grad_heads).reshape(seq, width)
    branch_pieces = gather_slots(after(grad_branch, grad_attn), n_ctx)
    hidden_upper, hidden_lower = hidden_pairs
    hidden_arrived = swap_stage(after(hidden_upper.astype(BF), grad_attn), n_ctx, stages[0])
    grad_mixed = attend_backward(
        slot_of,
        starts_row,
        queries,
        keys,
        keys_t,
        values,
        grad_attn,
        attended,
        lse,
        cosine,
        sine,
        unsplit_matrix(width),
        heads,
        tok,
    )
    grad_mixed = after(grad_mixed, *branch_pieces[:3], hidden_arrived)
    qkv_terms = outer_rows(all_one, grad_mixed)
    qkv_sums = scatter_dp(after(qkv_terms, gate_up_sums))
    d_one = scatter_chips(
        *scatter_pairs(lambda lo, hi: nt(rows_of(grad_mixed, lo, hi), qkv_part), tok, n_ctx),
        stages,
        n_ctx,
    )
    hidden_sums = hidden_lower + hidden_arrived.astype(F32)
    if len(stages) > 1:
        cut = hidden_sums.shape[0] // 2
        hidden_sums = scatter_chips(hidden_sums[cut:], hidden_sums[:cut], stages[1:], n_ctx)
    block_out = (state + hidden_sums).astype(BF)
    out_terms = outer_rows(slot_attn, after(lay_out(branch_pieces), qkv_terms))
    out_sums = scatter_dp(after(out_terms, qkv_sums))
    norm_one = hidden_in * rms_one
    input_grad = grad_state + rms_one * (
        d_one - norm_one * jnp.mean(d_one * norm_one, axis=-1, keepdims=True)
    )

    down_weight_grad = after(down_sums, grad_mixed).astype(F32)
    out_weight_grad = lax.ppermute(
        out_sums, ("dp", "ctx"), [(b, a) for a, b in owner_pairs]
    ).astype(F32)
    gate_up_weight_grad, gain_ffn_grad = join_columns(
        exchange(after(gate_up_sums, grad_mixed).reshape(n_ctx, rows, 2 * ff)), gate_up_weight, gain_two, n_dp, ff_rows
    )
    qkv_back = exchange(qkv_sums.reshape(n_ctx, rows, columns)).astype(F32)
    q_back = qkv_back[:, :, :width].transpose(1, 0, 2).reshape(rows, H * HD)
    kv_back = jnp.sum(qkv_back[:, :, width:].reshape(KVH, sharers, rows, 2 * HD), axis=1)
    k_back = kv_back[:, :, :HD].transpose(1, 0, 2).reshape(rows, KVH * HD)
    v_back = kv_back[:, :, HD:].transpose(1, 0, 2).reshape(rows, KVH * HD)
    qkv_back = jnp.concatenate([q_back, k_back, v_back], axis=1)
    qkv_weight_grad = qkv_back * gain_one
    gain_attn_grad = jnp.sum(qkv_back * qkv_weight.astype(F32), axis=1)
    return (
        block_out,
        input_grad,
        gain_attn_grad,
        qkv_weight_grad,
        out_weight_grad,
        gain_ffn_grad[:, 0],
        gate_up_weight_grad,
        down_weight_grad,
    )


def solution(mesh):
    rows = P(("dp", "ctx"), None)
    entries = P(("dp", "ctx"))
    return jax.shard_map(
        on_device,
        mesh=mesh,
        in_specs=(rows, entries, rows, rows, entries, rows, rows, P("dp", None), rows),
        out_specs=(rows, rows, entries, rows, rows, entries, rows, rows),
        check_vma=False,
    )
```

```python
import jax
import jax.numpy as jnp
import numpy as np
from jax import lax
from jax.experimental import pallas as pl
from jax.experimental.pallas import tpu as pltpu
from jax.sharding import PartitionSpec as P

D = 2048
H = 32
KVH = 4
HD = 64
FF = 5632
HALF = HD // 2

EPS = 1e-05
MASKED = -1e30
BF = jnp.bfloat16
F32 = jnp.float32
VMEM_LIMIT = 60 << 20
SHORT = pl.CostEstimate(flops=1 << 20, bytes_accessed=1 << 20, transcendentals=0)
MEDIUM = pl.CostEstimate(flops=2 * 10**10, bytes_accessed=1 << 20, transcendentals=0)
LONG = pl.CostEstimate(flops=10**11, bytes_accessed=1 << 20, transcendentals=0)


def nt(a, b):
    return lax.dot_general(a, b, (((1,), (1,)), ((), ())), preferred_element_type=F32)


def nn(a, b):
    return jnp.dot(a, b, preferred_element_type=F32)


def after(x, *earlier):
    return lax.optimization_barrier((x, *earlier))[0]


def after_each(values, *earlier):
    count = len(values)
    return lax.optimization_barrier((*values, *earlier))[:count]


def walk(n_ctx, parity):
    bits = []
    bit = 2
    while bit < n_ctx:
        bits.append(bit)
        bit *= 2
    return bits if parity == 0 else bits[::-1]


def swap_stage(x, n_ctx, stage):
    pairs = [(c, c ^ walk(n_ctx, c % 2)[stage]) for c in range(n_ctx)]
    return lax.ppermute(x, "ctx", pairs)


def swap_core(x, n_ctx):
    return lax.ppermute(x, "ctx", [(c, c ^ 1) for c in range(n_ctx)])


def slot_table(n_ctx):
    lists = []
    for parity in (0, 1):
        row = [0]
        for bit in walk(n_ctx, parity):
            row = row + [v ^ bit for v in row]
        lists.append(row)
    return np.array(
        [lists[p] + [v ^ 1 for v in lists[1 - p]] for p in (0, 1)], dtype=np.int32
    )


def gather_direct(x, n_ctx):
    return [x] + [swap_stage(x, n_ctx, stage) for stage in range(len(walk(n_ctx, 0)))]


def gather_rest(direct, n_ctx, earlier=None, last=None):
    have = direct[:1]
    for stage in range(len(walk(n_ctx, 0))):
        passed = [block if earlier is None else after(block, earlier) for block in have[1:]]
        have = have + [direct[stage + 1]] + [swap_stage(block, n_ctx, stage) for block in passed]
    return have + [swap_core(block if last is None else after(block, last), n_ctx) for block in have]


def gather_at_once(x, n_ctx):
    have = [x]
    table = slot_table(n_ctx)
    for slot in range(1, n_ctx // 2):
        pairs = [(c, c ^ int(table[c % 2][slot])) for c in range(n_ctx)]
        have.append(lax.ppermute(x, "ctx", pairs))
    return have, [swap_core(block, n_ctx) for block in have]


def gather_slots(x, n_ctx):
    return gather_rest(gather_direct(x, n_ctx), n_ctx)


def scatter_pairs(term, tok, n_ctx):
    mine = n_ctx // 2
    cut = mine // 2
    sums = []
    for lo, hi in ((cut, mine), (0, cut)):
        arrived = swap_core(term(mine + lo, mine + hi).astype(BF), n_ctx)
        sums.append(term(lo, hi) + arrived.astype(F32))
    return sums


def scatter_chips(upper, lower, stages, n_ctx, *earlier):
    for stage in stages:
        if earlier and stage == 0:
            upper = after(upper.astype(BF), *earlier)
        lower = lower + swap_stage(upper.astype(BF), n_ctx, stage).astype(F32)
        if stage:
            half = lower.shape[0] // 2
            upper, lower = lower[half:], lower[:half]
    return lower if stages[-1] == 0 else (upper, lower)


def scatter_rest(lower, arrived, stages, n_ctx, follower=None):
    sums = lower + arrived.astype(F32)
    if len(stages) == 1:
        return sums, follower
    half = sums.shape[0] // 2
    upper = sums[half:].astype(BF)
    if follower is not None:
        upper, follower = lax.optimization_barrier((upper, follower))
    return scatter_chips(upper, sums[:half], stages[1:], n_ctx), follower


def exchange(x):
    return lax.all_to_all(x, "ctx", split_axis=0, concat_axis=0, tiled=False)


def gather_dp(x):
    return lax.all_gather(x, "dp", axis=0, tiled=True)


def scatter_dp(x):
    return lax.psum_scatter(x, "dp", scatter_dimension=0, tiled=True)


def fetch_piece(pieces, buffer, semaphores, count=1):
    step = pl.program_id(0)

    @pl.when(step == 0)
    def _():
        for i, piece in enumerate(pieces):
            pltpu.make_async_copy(piece, buffer.at[i], semaphores.at[i]).start()

    for i in range(count):
        at = step * count + i
        pltpu.make_async_copy(pieces[0], buffer.at[at], semaphores.at[at]).wait()
    if count == 1:
        return buffer[step]
    return buffer[pl.ds(step * count, count)].reshape(count * buffer.shape[1], buffer.shape[2])


def keep_pieces(buffer, target, semaphores, count=1):
    step = pl.program_id(0)
    total, tok = buffer.shape[0], buffer.shape[1]

    def copy(at):
        rows = pl.ds(pl.multiple_of(at * tok, tok), tok)
        return pltpu.make_async_copy(buffer.at[at], target.at[rows], semaphores.at[at])

    for i in range(count):
        copy(step * count + i).start()

    @pl.when(step == total // count - 1)
    def _():
        for i in range(total):
            copy(i).wait()


def store_rows(source, target, semaphores):
    count = semaphores.shape[0]
    rows = source.shape[0] // count
    copies = [
        pltpu.make_async_copy(
            source.at[pl.ds(i * rows, rows)], target.at[pl.ds(i * rows, rows)], semaphores.at[i]
        )
        for i in range(count)
    ]
    for copy in copies:
        copy.start()
    return copies


def chunks(rows):
    return next(count for count in (8, 4, 2, 1) if rows % (16 * count) == 0)


def fetch_rows(source, buffer, semaphores):
    count = semaphores.shape[0]
    rows = source.shape[0] // count

    @pl.when(pl.program_id(0) == 0)
    def _():
        copies = [
            pltpu.make_async_copy(
                source.at[pl.ds(i * rows, rows)], buffer.at[pl.ds(i * rows, rows)], semaphores.at[i]
            )
            for i in range(count)
        ]
        for copy in copies:
            copy.start()
        for copy in copies:
            copy.wait()


def swap_halves(x):
    return pltpu.roll(x, x.shape[1] // 2, axis=1)


def turn_tables(cosine, sine, width):
    times = width // 128
    cosine = jnp.concatenate([cosine] * times, axis=1) if times > 1 else cosine
    sine = jnp.concatenate([sine] * times, axis=1) if times > 1 else sine
    lane = lax.broadcasted_iota(jnp.int32, sine.shape, 1)
    return cosine, jnp.where(lane < width // 2, -sine, sine)


def any_specs(pieces):
    return [pl.BlockSpec(memory_space=pltpu.HBM) for _ in pieces]


def project_qkv(order, pieces, weight, spread, widen, cosine, sine, width, tok):
    n = len(pieces)
    seq = n * tok

    def kernel(order_ref, *refs):
        parts = refs[:n]
        w_hbm, spread_ref, widen_ref, cos_ref, sin_ref = refs[n : n + 5]
        (
            q_ref, k_ref, v_ref, kt_ref, vt_ref, all_hbm, wide, buffer, semaphores, keep_semaphores, w_ref, w_semaphores
        ) = refs[n + 5 :]
        fetch_rows(w_hbm, w_ref, w_semaphores)

        @pl.when(pl.program_id(0) == 0)
        def _():
            wide[...] = nn(w_ref[...], spread_ref[...]).astype(BF)

        x = fetch_piece(parts, buffer, semaphores)
        keep_pieces(buffer, all_hbm, keep_semaphores)
        mixed = nn(x, wide[...])
        cos, sin = turn_tables(cos_ref[...], sin_ref[...], width)
        q = mixed[:, :width]
        q_ref[...] = (q * cos + swap_halves(q) * sin).astype(BF) * (HD**-0.5)
        lane = lax.broadcasted_iota(jnp.int32, (tok, 128), 1)
        key_sine = jnp.where(lane < HALF, -sin_ref[...], sin_ref[...])
        both = jnp.where(
            lane < HD,
            mixed[:, width : width + 128] * cos_ref[...] + mixed[:, width + 128 :] * key_sine,
            mixed[:, width : width + 128],
        ).astype(BF)
        repeated = nn(both, widen_ref[...]).astype(BF)
        k_ref[...] = repeated[:, :width]
        v_ref[...] = repeated[:, width:]
        turned = both.T
        kt_ref[...] = turned[:HD]
        vt_ref[...] = turned[HD:]

    rows = lambda s, order: (order[s], 0)
    lanes = lambda s, order: (0, order[s])
    whole = lambda s, order: (0, 0)
    return pl.pallas_call(
        kernel,
        grid_spec=pltpu.PrefetchScalarGridSpec(
            num_scalar_prefetch=1,
            grid=(n,),
            in_specs=any_specs(pieces)
            + [
                pl.BlockSpec(memory_space=pltpu.HBM),
                pl.BlockSpec(spread.shape, whole),
                pl.BlockSpec(widen.shape, whole),
                pl.BlockSpec((tok, 128), rows),
                pl.BlockSpec((tok, 128), rows),
            ],
            out_specs=[
                pl.BlockSpec((tok, width), rows),
                pl.BlockSpec((tok, width), rows),
                pl.BlockSpec((tok, width), rows),
                pl.BlockSpec((HD, tok), lanes),
                pl.BlockSpec((HD, tok), lanes),
                pl.BlockSpec(memory_space=pltpu.HBM),
            ],
            scratch_shapes=[
                pltpu.VMEM((D, width + 256), BF),
                pltpu.VMEM((n, tok, D), BF),
                pltpu.SemaphoreType.DMA((n,)),
                pltpu.SemaphoreType.DMA((n,)),
                pltpu.VMEM(weight.shape, BF),
                pltpu.SemaphoreType.DMA((chunks(D),)),
            ],
        ),
        out_shape=[
            jax.ShapeDtypeStruct((seq, width), BF),
            jax.ShapeDtypeStruct((seq, width), BF),
            jax.ShapeDtypeStruct((seq, width), BF),
            jax.ShapeDtypeStruct((HD, seq), BF),
            jax.ShapeDtypeStruct((HD, seq), BF),
            jax.ShapeDtypeStruct((seq, D), BF),
        ],
        compiler_params=pltpu.CompilerParams(vmem_limit_bytes=VMEM_LIMIT),
        cost_estimate=LONG,
        name="project_qkv",
    )(order, *pieces, weight, spread, widen, cosine, sine)


def project_out(order, heads_in, pieces, residual):
    n, tok, width = heads_in.shape

    def kernel(order_ref, a_ref, *refs):
        parts = refs[:n]
        x_ref, state_hbm, norm_hbm, buffer, semaphores, state_ref, norm_ref, out_semaphores = refs[n:]
        step = pl.program_id(0)
        w = fetch_piece(parts, buffer, semaphores)

        @pl.when(step == 0)
        def _():
            state_ref[...] = x_ref[...].astype(F32)

        state_ref[...] += nn(a_ref[0], w)

        @pl.when(step == n - 1)
        def _():
            state = state_ref[...]
            scale = lax.rsqrt(jnp.mean(state * state, axis=-1, keepdims=True) + EPS)
            copies = store_rows(state_ref, state_hbm, out_semaphores.at[0])
            norm_ref[...] = (state * scale).astype(BF)
            copies += store_rows(norm_ref, norm_hbm, out_semaphores.at[1])
            for copy in copies:
                copy.wait()

    whole = lambda s, order: (0, 0)
    return pl.pallas_call(
        kernel,
        grid_spec=pltpu.PrefetchScalarGridSpec(
            num_scalar_prefetch=1,
            grid=(n,),
            in_specs=[pl.BlockSpec((1, tok, width), lambda s, order: (order[s], 0, 0))]
            + any_specs(pieces)
            + [pl.BlockSpec((tok, D), whole)],
            out_specs=[pl.BlockSpec(memory_space=pltpu.HBM)] * 2,
            scratch_shapes=[
                pltpu.VMEM((n, width, D), BF),
                pltpu.SemaphoreType.DMA((n,)),
                pltpu.VMEM((tok, D), F32),
                pltpu.VMEM((tok, D), BF),
                pltpu.SemaphoreType.DMA((2, 4)),
            ],
        ),
        out_shape=[
            jax.ShapeDtypeStruct((tok, D), F32),
            jax.ShapeDtypeStruct((tok, D), BF),
        ],
        compiler_params=pltpu.CompilerParams(vmem_limit_bytes=VMEM_LIMIT),
        cost_estimate=SHORT,
        name="project_out",
    )(order, heads_in, *pieces, residual)


def feed_forward(pieces, weight):
    n = len(pieces)
    tok = 2 * pieces[0].shape[0]
    seq = n * tok // 2
    ff = weight.shape[1] // 2

    def kernel(*refs):
        parts = refs[:n]
        w_hbm, hidden_ref, factor_ref, all_hbm, buffer, semaphores, keep_semaphores, w_ref, w_semaphores = refs[n:]
        fetch_rows(w_hbm, w_ref, w_semaphores)
        x = fetch_piece(parts, buffer, semaphores, 2)
        keep_pieces(buffer, all_hbm, keep_semaphores, 2)
        both = nn(x, w_ref[...])
        gate = both[:, :ff]
        up = both[:, ff:]
        sig = jax.nn.sigmoid(gate)
        silu = gate * sig
        hidden_ref[...] = (silu * up).astype(BF)
        factor_ref[:, :ff] = (up * sig * (1.0 + gate * (1.0 - sig))).astype(BF)
        factor_ref[:, ff:] = silu.astype(BF)

    rows = lambda s: (s, 0)
    return pl.pallas_call(
        kernel,
        grid=(n // 2,),
        in_specs=any_specs(pieces) + [pl.BlockSpec(memory_space=pltpu.HBM)],
        out_specs=[
            pl.BlockSpec((tok, ff), rows),
            pl.BlockSpec((tok, 2 * ff), rows),
            pl.BlockSpec(memory_space=pltpu.HBM),
        ],
        scratch_shapes=[
            pltpu.VMEM((n, tok // 2, D), BF),
            pltpu.SemaphoreType.DMA((n,)),
            pltpu.SemaphoreType.DMA((n,)),
            pltpu.VMEM(weight.shape, BF),
            pltpu.SemaphoreType.DMA((chunks(D),)),
        ],
        out_shape=[
            jax.ShapeDtypeStruct((seq, ff), BF),
            jax.ShapeDtypeStruct((seq, 2 * ff), BF),
            jax.ShapeDtypeStruct((seq, D), BF),
        ],
        compiler_params=pltpu.CompilerParams(vmem_limit_bytes=VMEM_LIMIT),
        cost_estimate=LONG,
        name="feed_forward",
    )(*pieces, weight)


def feed_backward(factors, grads, weight):
    seq = factors.shape[0]
    ff = weight.shape[0]
    tok = 512

    def kernel(factor_ref, g_ref, w_hbm, out_ref, w_ref, w_semaphores, turned):
        fetch_rows(w_hbm, w_ref, w_semaphores)

        @pl.when(pl.program_id(0) == 0)
        def _():
            turned[...] = w_ref[...].T

        grad_hidden = nn(g_ref[...], turned[...])
        factor = factor_ref[...].astype(F32)
        out_ref[:, :ff] = (grad_hidden * factor[:, :ff]).astype(BF)
        out_ref[:, ff:] = (grad_hidden * factor[:, ff:]).astype(BF)

    rows = lambda s: (s, 0)
    return pl.pallas_call(
        kernel,
        grid=(seq // tok,),
        in_specs=[
            pl.BlockSpec((tok, 2 * ff), rows),
            pl.BlockSpec((tok, D), rows),
            pl.BlockSpec(memory_space=pltpu.HBM),
        ],
        out_specs=pl.BlockSpec((tok, 2 * ff), rows),
        scratch_shapes=[
            pltpu.VMEM(weight.shape, BF),
            pltpu.SemaphoreType.DMA((chunks(ff),)),
            pltpu.VMEM((D, ff), BF),
        ],
        out_shape=jax.ShapeDtypeStruct((seq, 2 * ff), BF),
        compiler_params=pltpu.CompilerParams(vmem_limit_bytes=VMEM_LIMIT),
        cost_estimate=LONG,
        name="feed_backward",
    )(factors, grads, weight)


def lay_out(pieces):
    n = len(pieces)
    tok = pieces[0].shape[0]

    def kernel(*refs):
        parts = refs[:n]
        out_ref, buffer, in_semaphores, out_semaphores = refs[n:]
        arrive = [
            pltpu.make_async_copy(part, buffer.at[i], in_semaphores.at[i])
            for i, part in enumerate(parts)
        ]
        leave = [
            pltpu.make_async_copy(buffer.at[i], out_ref.at[pl.ds(i * tok, tok)], out_semaphores.at[i])
            for i in range(n)
        ]
        for copy in arrive:
            copy.start()
        for i in range(n):
            arrive[i].wait()
            leave[i].start()
        for copy in leave:
            copy.wait()

    return pl.pallas_call(
        kernel,
        in_specs=any_specs(pieces),
        out_specs=pl.BlockSpec(memory_space=pltpu.HBM),
        scratch_shapes=[
            pltpu.VMEM((n, tok, D), BF),
            pltpu.SemaphoreType.DMA((n,)),
            pltpu.SemaphoreType.DMA((n,)),
        ],
        out_shape=jax.ShapeDtypeStruct((n * tok, D), BF),
        compiler_params=pltpu.CompilerParams(vmem_limit_bytes=VMEM_LIMIT),
        cost_estimate=SHORT,
        name="lay_out",
    )(*pieces)


def branch_back(order, d_two, state, out_grad, pieces):
    n = len(pieces)
    tok = d_two.shape[0]
    width = pieces[0].shape[0]

    def kernel(order_ref, d_ref, state_ref, g_ref, *refs):
        parts = refs[:n]
        grad_hbm, branch_hbm, heads_ref, buffer, semaphores, grad_ref, branch_ref, out_semaphores = refs[n:]

        @pl.when(pl.program_id(0) == 0)
        def _():
            state = state_ref[...]
            scale = lax.rsqrt(jnp.mean(state * state, axis=-1, keepdims=True) + EPS)
            norm = state * scale
            d = d_ref[...]
            grad = g_ref[...].astype(F32) + scale * (
                d - norm * jnp.mean(d * norm, axis=-1, keepdims=True)
            )
            grad_ref[...] = grad
            branch_ref[...] = grad.astype(BF)
            store_rows(grad_ref, grad_hbm, out_semaphores.at[0])
            store_rows(branch_ref, branch_hbm, out_semaphores.at[1])

        w = fetch_piece(parts, buffer, semaphores)
        heads_ref[0] = nt(branch_ref[...], w).astype(BF)

        @pl.when(pl.program_id(0) == n - 1)
        def _():
            for source, target, at in ((grad_ref, grad_hbm, 0), (branch_ref, branch_hbm, 1)):
                rows = tok // 4
                for i in range(4):
                    cut = pl.ds(i * rows, rows)
                    pltpu.make_async_copy(source.at[cut], target.at[cut], out_semaphores.at[at, i]).wait()

    whole = lambda s, order: (0, 0)
    return pl.pallas_call(
        kernel,
        grid_spec=pltpu.PrefetchScalarGridSpec(
            num_scalar_prefetch=1,
            grid=(n,),
            in_specs=[
                pl.BlockSpec((tok, D), whole),
                pl.BlockSpec((tok, D), whole),
                pl.BlockSpec((tok, D), whole),
            ]
            + any_specs(pieces),
            out_specs=[
                pl.BlockSpec(memory_space=pltpu.HBM),
                pl.BlockSpec(memory_space=pltpu.HBM),
                pl.BlockSpec((1, tok, width), lambda s, order: (order[s], 0, 0)),
            ],
            scratch_shapes=[
                pltpu.VMEM((n, width, D), BF),
                pltpu.SemaphoreType.DMA((n,)),
                pltpu.VMEM((tok, D), F32),
                pltpu.VMEM((tok, D), BF),
                pltpu.SemaphoreType.DMA((2, 4)),
            ],
        ),
        out_shape=[
            jax.ShapeDtypeStruct((tok, D), F32),
            jax.ShapeDtypeStruct((tok, D), BF),
            jax.ShapeDtypeStruct((n, tok, width), BF),
        ],
        compiler_params=pltpu.CompilerParams(vmem_limit_bytes=VMEM_LIMIT),
        cost_estimate=SHORT,
        name="branch_back",
    )(order, d_two, state, out_grad, *pieces)


def split_columns(weight, gain, n_ctx, n_dp, ff_rows):
    rows = weight.shape[0]
    ff = ff_rows * n_dp

    def kernel(w_ref, gain_ref, out_ref):
        gains = gain_ref[...]
        for part in range(2):
            for d in range(n_dp):
                for c in range(n_ctx):
                    at = part * FF + (d * n_ctx + c) * ff_rows
                    to = part * ff + d * ff_rows
                    values = w_ref[:, at : at + ff_rows].astype(F32) * gains
                    out_ref[c, :, to : to + ff_rows] = values.astype(BF)

    return pl.pallas_call(
        kernel,
        in_specs=[pl.BlockSpec(memory_space=pltpu.VMEM)] * 2,
        out_specs=pl.BlockSpec(memory_space=pltpu.VMEM),
        out_shape=jax.ShapeDtypeStruct((n_ctx, rows, 2 * ff), BF),
        compiler_params=pltpu.CompilerParams(vmem_limit_bytes=VMEM_LIMIT),
        cost_estimate=LONG,
        name="split_columns",
    )(weight, gain)


def join_columns(sums, weight, gain, n_dp, ff_rows):
    n_ctx, rows, both = sums.shape
    ff = both // 2

    def kernel(s_ref, w_ref, gain_ref, out_ref, gain_out_ref):
        gains = gain_ref[...]
        total = jnp.zeros((rows, ff_rows), F32)
        for part in range(2):
            for d in range(n_dp):
                for c in range(n_ctx):
                    at = part * ff + d * ff_rows
                    to = part * FF + (d * n_ctx + c) * ff_rows
                    values = s_ref[c, :, at : at + ff_rows].astype(F32)
                    total = total + values * w_ref[:, to : to + ff_rows].astype(F32)
                    out_ref[:, to : to + ff_rows] = values * gains
        gain_out_ref[...] = jnp.sum(total, axis=1, keepdims=True)

    return pl.pallas_call(
        kernel,
        in_specs=[pl.BlockSpec(memory_space=pltpu.VMEM)] * 3,
        out_specs=[pl.BlockSpec(memory_space=pltpu.VMEM)] * 2,
        out_shape=[
            jax.ShapeDtypeStruct((rows, 2 * FF), F32),
            jax.ShapeDtypeStruct((rows, 1), F32),
        ],
        compiler_params=pltpu.CompilerParams(vmem_limit_bytes=VMEM_LIMIT),
        cost_estimate=LONG,
        name="join_columns",
    )(sums, weight, gain)


def lane_heads(rows, width):
    lane = lax.broadcasted_iota(jnp.int32, (rows, width), 1)
    return (lane % (width // 2)) // HALF


def attend_forward(slot_of, starts, queries, keys, values_t, heads, tok, first, count, before):
    seq, width = queries.shape
    blocks = seq // tok
    span = 2 * tok

    def kernel(slot_ref, start_ref, q_ref, k_ref, v_ref, *refs):
        attn_ref, slot_attn_ref, full_ref, lse_ref, scores = refs[len(before) :]
        block = first + pl.program_id(0)
        steps = (block + 2) // 2
        start = start_ref[...]
        here = block * tok + lax.broadcasted_iota(jnp.int32, (1, tok), 1)
        head_of = lane_heads(tok, width)
        q = q_ref[...]
        q_heads = [jnp.where(head_of == h, q, jnp.zeros_like(q)) for h in range(heads)]

        def score(i, peaks):
            rows = pl.ds(pl.multiple_of(i * span, span), span)
            k = k_ref[rows, :]
            there = i * span + lax.broadcasted_iota(jnp.int32, (span, tok), 0)
            visible = (there >= start) & (there <= here)
            out = []
            for h in range(heads):
                s = jnp.where(visible, nt(k, q_heads[h]), MASKED)
                scores[h, rows, :] = s
                out.append(jnp.maximum(peaks[h], jnp.max(s.reshape(span // 8, 8, tok), axis=0)))
            return tuple(out)

        peaks = lax.fori_loop(
            0, steps, score, tuple(jnp.full((8, tok), MASKED, F32) for _ in range(heads))
        )
        peaks = [jnp.max(peak, axis=0, keepdims=True) for peak in peaks]

        def weigh(i, running):
            rows = pl.ds(pl.multiple_of(i * span, span), span)
            v = v_ref[:, rows]
            out = []
            for h in range(heads):
                total, acc = running[h]
                p = jnp.exp(scores[h, rows, :] - peaks[h])
                total = total + jnp.sum(p.reshape(span // 8, 8, tok), axis=0)
                out.append((total, acc + nn(v, p.astype(BF))))
            return tuple(out)

        result = lax.fori_loop(
            0,
            steps,
            weigh,
            tuple((jnp.zeros((8, tok), F32), jnp.zeros((HD, tok), F32)) for _ in range(heads)),
        )
        rows = []
        for h in range(heads):
            total, acc = result[h]
            total = jnp.sum(total, axis=0, keepdims=True)
            rows.append(acc / total)
            lse_ref[0, h : h + 1, :] = peaks[h] + jnp.log(total)
        full = jnp.concatenate(rows, axis=0).T
        full_ref[...] = full
        attn_ref[...] = full.astype(BF)
        slot_attn_ref[...] = full.astype(BF)

    return pl.pallas_call(
        kernel,
        grid_spec=pltpu.PrefetchScalarGridSpec(
            num_scalar_prefetch=1,
            grid=(count,),
            in_specs=[
                pl.BlockSpec((1, tok), lambda j, slot: (0, first + j)),
                pl.BlockSpec((tok, width), lambda j, slot: (first + j, 0)),
                pl.BlockSpec((seq, width), lambda j, slot: (0, 0)),
                pl.BlockSpec((HD, seq), lambda j, slot: (0, 0)),
            ]
            + [pl.BlockSpec(memory_space=pltpu.HBM)] * len(before),
            out_specs=[
                pl.BlockSpec((tok, width), lambda j, slot: (first + j, 0)),
                pl.BlockSpec((tok, width), lambda j, slot: (slot[first + j], 0)),
                pl.BlockSpec((tok, width), lambda j, slot: (first + j, 0)),
                pl.BlockSpec((1, heads, tok), lambda j, slot: (first + j, 0, 0)),
            ],
            scratch_shapes=[pltpu.VMEM((heads, seq, tok), F32)],
        ),
        out_shape=[
            jax.ShapeDtypeStruct((seq, width), BF),
            jax.ShapeDtypeStruct((seq, width), BF),
            jax.ShapeDtypeStruct((seq, width), F32),
            jax.ShapeDtypeStruct((blocks, heads, tok), F32),
        ],
        input_output_aliases={5 + i: i for i in range(len(before))},
        compiler_params=pltpu.CompilerParams(vmem_limit_bytes=VMEM_LIMIT),
        cost_estimate=LONG,
        name="attend_forward",
    )(slot_of, starts, queries, keys, values_t, *before)


def attend_backward(
    slot_of, starts, queries, keys, keys_t, values, grads, full, lse, cosine, sine, unsplit, heads, tok
):
    seq, width = queries.shape
    blocks = seq // tok
    span = 2 * tok
    half = width // 2

    def kernel(
        slot_ref, start_ref, q_ref, k_ref, kt_ref, v_ref, g_ref, full_ref, lse_ref, cos_ref, sin_ref, unsplit_ref,
        out_ref, dk, dv,
    ):
        block = pl.program_id(0)
        steps = (block + 2) // 2

        @pl.when(block == 0)
        def _():
            dk[...] = jnp.zeros_like(dk)
            dv[...] = jnp.zeros_like(dv)

        start = start_ref[...]
        here = block * tok + lax.broadcasted_iota(jnp.int32, (1, tok), 1)
        head_of = lane_heads(tok, width)
        wide = lax.broadcasted_iota(jnp.int32, (tok, width), 1) // HD
        q = q_ref[...]
        g = g_ref[...]
        q_heads = [jnp.where(head_of == h, q, jnp.zeros_like(q)) for h in range(heads)]
        g_heads = [jnp.where(wide == h, g, jnp.zeros_like(g)) for h in range(heads)]
        q_stack = jnp.concatenate(q_heads, axis=0)
        g_stack = jnp.concatenate(g_heads, axis=0)
        picks = (
            lax.broadcasted_iota(jnp.int32, (8, width), 1) // HD
            == lax.broadcasted_iota(jnp.int32, (8, width), 0)
        ).astype(F32)
        deltas = lax.dot_general(
            picks,
            g.astype(F32) * full_ref[...],
            (((1,), (1,)), ((), ())),
            preferred_element_type=F32,
            precision=lax.Precision.HIGHEST,
        )

        def step(i, dq):
            rows = pl.ds(pl.multiple_of(i * span, span), span)
            k = k_ref[rows, :]
            v = v_ref[rows, :]
            kt = kt_ref[:, rows]
            there = i * span + lax.broadcasted_iota(jnp.int32, (span, tok), 0)
            visible = (there >= start) & (there <= here)
            probs, grad_scores, out = [], [], []
            for h in range(heads):
                s = jnp.where(visible, nt(k, q_heads[h]), MASKED)
                p = jnp.exp(s - lse_ref[0, h : h + 1, :])
                ds = (p * (nt(v, g_heads[h]) - deltas[h : h + 1, :])).astype(BF)
                probs.append(p.astype(BF))
                grad_scores.append(ds)
                out.append(dq[h] + nn(kt, ds))
            dv[rows, :] += nn(jnp.concatenate(probs, axis=1), g_stack)
            dk[rows, :] += nn(jnp.concatenate(grad_scores, axis=1), q_stack)
            return tuple(out)

        dq = lax.fori_loop(
            0, steps, step, tuple(jnp.zeros((HD, tok), F32) for _ in range(heads))
        )
        dq = jnp.concatenate([x[:HALF] for x in dq] + [x[HALF:] for x in dq], axis=0).T
        here_rows = pl.ds(pl.multiple_of(block * tok, tok), tok)
        cos, sin = turn_tables(cos_ref[here_rows, :], sin_ref[here_rows, :], width)
        dq = (dq * cos - swap_halves(dq) * sin) * (HD**-0.5)
        slot_rows = pl.ds(pl.multiple_of(slot_ref[block] * tok, tok), tok)
        out_ref[slot_rows, :width] = nn(dq.astype(BF), unsplit_ref[...]).astype(BF)

        @pl.when(block == blocks - 1)
        def _():
            lane = lax.broadcasted_iota(jnp.int32, (width, 128), 0)
            column = lax.broadcasted_iota(jnp.int32, (width, 128), 1)
            fold_k = ((lane // half) * HALF + lane % HALF == column).astype(BF)
            fold_v = (lane % HD + HD == column).astype(BF)

            def fold(i, unused):
                rows = pl.ds(pl.multiple_of(i * tok, tok), tok)
                cos, sin = turn_tables(cos_ref[rows, :], sin_ref[rows, :], width)
                a = dk[rows, :]
                a = a * cos - swap_halves(a) * sin
                b = dv[rows, :]
                a_high = a.astype(BF)
                b_high = b.astype(BF)
                terms = (
                    nn(a_high, fold_k)
                    + nn((a - a_high.astype(F32)).astype(BF), fold_k)
                    + nn(b_high, fold_v)
                    + nn((b - b_high.astype(F32)).astype(BF), fold_v)
                )
                slot_rows = pl.ds(pl.multiple_of(slot_ref[i] * tok, tok), tok)
                out_ref[slot_rows, width:] = terms.astype(BF)
                return unused

            lax.fori_loop(0, blocks, fold, 0)

    whole = lambda shape: pl.BlockSpec(shape, lambda j, *_: (0, 0))
    return pl.pallas_call(
        kernel,
        grid_spec=pltpu.PrefetchScalarGridSpec(
            num_scalar_prefetch=1,
            grid=(blocks,),
            in_specs=[
                pl.BlockSpec((1, tok), lambda j, *_: (0, j)),
                pl.BlockSpec((tok, width), lambda j, *_: (j, 0)),
                whole((seq, width)),
                whole((HD, seq)),
                whole((seq, width)),
                pl.BlockSpec((tok, width), lambda j, *_: (j, 0)),
                pl.BlockSpec((tok, width), lambda j, *_: (j, 0)),
                pl.BlockSpec((1, heads, tok), lambda j, *_: (j, 0, 0)),
                whole((seq, 128)),
                whole((seq, 128)),
                whole((width, width)),
            ],
            out_specs=whole((seq, width + 128)),
            scratch_shapes=[pltpu.VMEM((seq, width), F32), pltpu.VMEM((seq, width), F32)],
        ),
        out_shape=jax.ShapeDtypeStruct((seq, width + 128), BF),
        compiler_params=pltpu.CompilerParams(vmem_limit_bytes=VMEM_LIMIT),
        cost_estimate=MEDIUM,
        name="attend_backward",
    )(slot_of, starts, queries, keys, keys_t, values, grads, full, lse, cosine, sine, unsplit)


def outer_rows(activations, gradients):
    return lax.dot_general(
        activations, gradients, (((0,), (0,)), ((), ())), preferred_element_type=F32
    ).astype(BF)


def split_source(width):
    lane = np.arange(width)
    half = lane // (width // 2)
    head = (lane % (width // 2)) // HALF
    return head * HD + half * HALF + lane % HALF


def spread_matrix(width):
    matrix = np.zeros((width + 2 * HD, width + 256), np.float32)
    lane = np.arange(width)
    matrix[split_source(width), lane] = 1
    lane = np.arange(2 * HD)
    matrix[width + lane, width + lane] = 1
    lane = np.arange(HD)
    matrix[width + (lane + HALF) % HD, width + 128 + lane] = 1
    return jnp.asarray(matrix, BF)


def widen_matrix(width):
    matrix = np.zeros((2 * HD, 2 * width), np.float32)
    lane = np.arange(width)
    matrix[(lane // (width // 2)) * HALF + lane % HALF, lane] = 1
    matrix[HD + lane % HD, width + lane] = 1
    return jnp.asarray(matrix, BF)


def unsplit_matrix(width):
    matrix = np.zeros((width, width), np.float32)
    matrix[np.arange(width), split_source(width)] = 1
    return jnp.asarray(matrix, BF)


def on_device(
    block_in,
    gain_attn,
    qkv_weight,
    out_weight,
    gain_ffn,
    gate_up_weight,
    down_weight,
    doc_lengths,
    out_grad,
):
    n_ctx = lax.axis_size("ctx")
    n_dp = lax.axis_size("dp")
    me = lax.axis_index("ctx")
    tok = block_in.shape[0]
    seq = tok * n_ctx
    heads = H // n_ctx
    width = heads * HD
    sharers = n_ctx // KVH
    rows = qkv_weight.shape[0]
    ff_rows = down_weight.shape[0]
    ff = ff_rows * n_dp
    columns = width + 2 * HD

    order = me ^ jnp.where(me % 2 == 0, *[jnp.asarray(t) for t in slot_table(n_ctx)])
    slots = jnp.arange(n_ctx, dtype=jnp.int32)
    slot_of = jnp.sum(jnp.where(order[None, :] == slots[:, None], slots[None, :], 0), axis=1)
    index = jnp.arange(seq, dtype=jnp.int32)
    lengths = doc_lengths[0]
    ends = jnp.cumsum(lengths)
    starts = jnp.sum((index[:, None] >= ends[None, :]).astype(jnp.int32) * lengths[None, :], axis=1)
    lane = jnp.arange(128, dtype=F32) % HALF
    frequency = 10000.0 ** (-lane * 2.0 / HD)
    angles = (index - starts).astype(F32)[:, None] * frequency[None, :]
    cosine = jnp.cos(angles)
    sine = jnp.sin(angles)
    starts_row = starts[None, :]

    gain_one = gain_attn.astype(F32)[:, None]
    gain_two = gain_ffn.astype(F32)[:, None]
    qkv = (qkv_weight.astype(F32) * gain_one).astype(BF)
    q_cols = qkv[:, : H * HD].reshape(rows, n_ctx, width).transpose(1, 0, 2)
    k_cols = qkv[:, H * HD : (H + KVH) * HD].reshape(rows, KVH, HD).transpose(1, 0, 2)
    v_cols = qkv[:, (H + KVH) * HD :].reshape(rows, KVH, HD).transpose(1, 0, 2)
    kv_cols = jnp.repeat(jnp.concatenate([k_cols, v_cols], axis=2), sharers, axis=0)
    qkv_own = exchange(jnp.concatenate([q_cols, kv_cols], axis=2)).reshape(n_ctx * rows, columns)
    qkv_part = gather_dp(qkv_own)

    hidden_in = block_in.astype(F32)
    rms_one = lax.rsqrt(jnp.mean(hidden_in * hidden_in, axis=-1, keepdims=True) + EPS)
    one_pieces = gather_slots(after((hidden_in * rms_one).astype(BF), qkv_own), n_ctx)

    owner_pairs = [(b, b % n_dp * n_ctx + b // n_dp) for b in range(n_dp * n_ctx)]
    out_own = lax.ppermute(after(out_weight, one_pieces[1]), ("dp", "ctx"), owner_pairs)
    out_part = gather_dp(after(out_own, qkv_part))
    gate_up_cols = split_columns(gate_up_weight, gain_two, n_ctx, n_dp, ff_rows)
    gate_up_own = exchange(after(gate_up_cols, *one_pieces[: n_ctx // 2])).reshape(
        n_ctx * rows, 2 * ff
    )
    gate_up_part = gather_dp(gate_up_own)
    down_part = gather_dp(after(down_weight, gate_up_own))

    queries, keys, values, keys_t, values_t, all_one = project_qkv(
        order, one_pieces, qkv_part, spread_matrix(width), widen_matrix(width), cosine, sine, width, tok
    )
    queries = after(queries, gate_up_own)
    part = n_ctx * 5 // 8
    begun = attend_forward(slot_of, starts_row, queries, keys, values_t, heads, tok, 0, part, ())
    out_direct = gather_direct(after(out_part, begun[2]), n_ctx)
    attn, slot_attn, attended, lse = attend_forward(
        slot_of,
        starts_row,
        queries,
        keys,
        values_t,
        heads,
        tok,
        part,
        n_ctx - part,
        tuple(begun),
    )
    attn_tokens = exchange(after(attn, *out_direct).reshape(n_ctx, tok, width))
    out_pieces = gather_rest(out_direct, n_ctx, attn, attn_tokens)
    state, norm_two = project_out(order, attn_tokens, out_pieces, block_in)

    two_pieces = gather_slots(norm_two, n_ctx)
    grad_direct = gather_direct(after(out_grad, *two_pieces), n_ctx)
    hidden, factors, all_two = feed_forward(two_pieces, gate_up_part)
    grad_pieces = gather_rest(grad_direct, n_ctx, hidden)
    all_grad = lay_out(grad_pieces)
    down_terms = outer_rows(hidden, all_grad)
    down_sums = scatter_dp(down_terms)
    grad_gate_up = feed_backward(after(factors, down_terms), all_grad, down_part)

    def rows_of(x, lo, hi):
        return lax.slice_in_dim(x, lo * tok, hi * tok, axis=0)

    d_upper, d_lower = scatter_pairs(
        lambda lo, hi: nt(rows_of(grad_gate_up, lo, hi), gate_up_part), tok, n_ctx
    )
    stages = tuple(reversed(range(len(walk(n_ctx, 0)))))
    d_arrived = swap_stage(d_upper.astype(BF), n_ctx, stages[0])
    d_two, all_two = scatter_rest(d_lower, d_arrived, stages, n_ctx, all_two)
    gate_up_terms = outer_rows(all_two, grad_gate_up)
    gate_up_sums = scatter_dp(gate_up_terms)
    hidden_pairs = scatter_pairs(
        lambda lo, hi: nn(rows_of(after(hidden, d_upper, d_lower), lo, hi), down_part), tok, n_ctx
    )

    grad_state, grad_branch, grad_heads = branch_back(
        order, after(d_two, gate_up_terms, *hidden_pairs), state, out_grad, out_pieces
    )
    grad_attn = exchange(grad_heads).reshape(seq, width)
    branch_here, branch_there = gather_at_once(after(grad_branch, grad_attn), n_ctx)
    hidden_upper, hidden_lower = hidden_pairs
    hidden_arrived = swap_stage(after(hidden_upper.astype(BF), grad_attn), n_ctx, stages[0])
    grad_mixed = attend_backward(
        slot_of,
        starts_row,
        queries,
        keys,
        keys_t,
        values,
        grad_attn,
        attended,
        lse,
        cosine,
        sine,
        unsplit_matrix(width),
        heads,
        tok,
    )
    grad_mixed = after(grad_mixed, *branch_here, hidden_arrived)
    qkv_terms = outer_rows(all_one, grad_mixed)
    qkv_sums = scatter_dp(after(qkv_terms, gate_up_sums))
    d_one = scatter_chips(
        *scatter_pairs(lambda lo, hi: nt(rows_of(after(grad_mixed, qkv_terms), lo, hi), qkv_part), tok, n_ctx),
        stages,
        n_ctx,
        qkv_sums,
    )
    hidden_sums, _ = scatter_rest(hidden_lower, hidden_arrived, stages, n_ctx)
    block_out = (state + hidden_sums).astype(BF)
    out_terms = outer_rows(slot_attn, after(lay_out(branch_here + branch_there), qkv_terms))
    out_sums = scatter_dp(after(out_terms, qkv_sums))
    norm_one = hidden_in * rms_one
    input_grad = grad_state + rms_one * (
        d_one - norm_one * jnp.mean(d_one * norm_one, axis=-1, keepdims=True)
    )

    down_weight_grad = after(down_sums, grad_mixed).astype(F32)
    out_weight_grad = lax.ppermute(
        out_sums, ("dp", "ctx"), [(b, a) for a, b in owner_pairs]
    ).astype(F32)
    gate_up_weight_grad, gain_ffn_grad = join_columns(
        exchange(after(gate_up_sums, grad_mixed).reshape(n_ctx, rows, 2 * ff)), gate_up_weight, gain_two, n_dp, ff_rows
    )
    qkv_back = exchange(qkv_sums.reshape(n_ctx, rows, columns)).astype(F32)
    q_back = qkv_back[:, :, :width].transpose(1, 0, 2).reshape(rows, H * HD)
    kv_back = jnp.sum(qkv_back[:, :, width:].reshape(KVH, sharers, rows, 2 * HD), axis=1)
    k_back = kv_back[:, :, :HD].transpose(1, 0, 2).reshape(rows, KVH * HD)
    v_back = kv_back[:, :, HD:].transpose(1, 0, 2).reshape(rows, KVH * HD)
    qkv_back = jnp.concatenate([q_back, k_back, v_back], axis=1)
    qkv_weight_grad = qkv_back * gain_one
    gain_attn_grad = jnp.sum(qkv_back * qkv_weight.astype(F32), axis=1)
    return (
        block_out,
        input_grad,
        gain_attn_grad,
        qkv_weight_grad,
        out_weight_grad,
        gain_ffn_grad[:, 0],
        gate_up_weight_grad,
        down_weight_grad,
    )


def solution(mesh):
    rows = P(("dp", "ctx"), None)
    entries = P(("dp", "ctx"))
    return jax.shard_map(
        on_device,
        mesh=mesh,
        in_specs=(rows, entries, rows, rows, entries, rows, rows, P("dp", None), rows),
        out_specs=(rows, rows, entries, rows, rows, entries, rows, rows),
        check_vma=False,
    )
```

```python
import jax
import jax.numpy as jnp
import numpy as np
from jax import lax
from jax.experimental import pallas as pl
from jax.experimental.pallas import tpu as pltpu
from jax.sharding import PartitionSpec as P

D = 2048
H = 32
KVH = 4
HD = 64
FF = 5632
HALF = HD // 2

EPS = 1e-05
MASKED = -1e30
BF = jnp.bfloat16
F32 = jnp.float32
VMEM_LIMIT = 60 << 20
SHORT = pl.CostEstimate(flops=1 << 20, bytes_accessed=1 << 20, transcendentals=0)
MEDIUM = pl.CostEstimate(flops=2 * 10**10, bytes_accessed=1 << 20, transcendentals=0)
LONG = pl.CostEstimate(flops=10**11, bytes_accessed=1 << 20, transcendentals=0)


def nt(a, b):
    return lax.dot_general(a, b, (((1,), (1,)), ((), ())), preferred_element_type=F32)


def nn(a, b):
    return jnp.dot(a, b, preferred_element_type=F32)


def after(x, *earlier):
    return lax.optimization_barrier((x, *earlier))[0]


def after_each(values, *earlier):
    count = len(values)
    return lax.optimization_barrier((*values, *earlier))[:count]


def walk(n_ctx, parity):
    bits = []
    bit = 2
    while bit < n_ctx:
        bits.append(bit)
        bit *= 2
    return bits if parity == 0 else bits[::-1]


def swap_stage(x, n_ctx, stage):
    pairs = [(c, c ^ walk(n_ctx, c % 2)[stage]) for c in range(n_ctx)]
    return lax.ppermute(x, "ctx", pairs)


def swap_core(x, n_ctx):
    return lax.ppermute(x, "ctx", [(c, c ^ 1) for c in range(n_ctx)])


def slot_table(n_ctx):
    lists = []
    for parity in (0, 1):
        row = [0]
        for bit in walk(n_ctx, parity):
            row = row + [v ^ bit for v in row]
        lists.append(row)
    return np.array(
        [lists[p] + [v ^ 1 for v in lists[1 - p]] for p in (0, 1)], dtype=np.int32
    )


def gather_direct(x, n_ctx):
    return [x] + [swap_stage(x, n_ctx, stage) for stage in range(len(walk(n_ctx, 0)))]


def gather_rest(direct, n_ctx, earlier=(), last=()):
    have = direct[:1]
    for stage in range(len(walk(n_ctx, 0))):
        passed = [after(block, *earlier) if earlier else block for block in have[1:]]
        have = have + [direct[stage + 1]] + [swap_stage(block, n_ctx, stage) for block in passed]
    return have + [swap_core(after(block, *last) if last else block, n_ctx) for block in have]


def gather_at_once(x, n_ctx):
    have = [x]
    table = slot_table(n_ctx)
    for slot in range(1, n_ctx // 2):
        pairs = [(c, c ^ int(table[c % 2][slot])) for c in range(n_ctx)]
        have.append(lax.ppermute(x, "ctx", pairs))
    return have, [swap_core(block, n_ctx) for block in have]


def gather_slots(x, n_ctx):
    return gather_rest(gather_direct(x, n_ctx), n_ctx)


def scatter_pairs(term, tok, n_ctx):
    mine = n_ctx // 2
    cut = mine // 2
    sums = []
    for lo, hi in ((cut, mine), (0, cut)):
        arrived = swap_core(term(mine + lo, mine + hi).astype(BF), n_ctx)
        sums.append(term(lo, hi) + arrived.astype(F32))
    return sums


def scatter_chips(upper, lower, stages, n_ctx, *earlier):
    for stage in stages:
        if earlier and stage == 0:
            upper = after(upper.astype(BF), *earlier)
        lower = lower + swap_stage(upper.astype(BF), n_ctx, stage).astype(F32)
        if stage:
            half = lower.shape[0] // 2
            upper, lower = lower[half:], lower[:half]
    return lower if stages[-1] == 0 else (upper, lower)


def scatter_rest(lower, arrived, stages, n_ctx):
    sums = lower + arrived.astype(F32)
    if len(stages) == 1:
        return sums
    half = sums.shape[0] // 2
    return scatter_chips(sums[half:], sums[:half], stages[1:], n_ctx)


def exchange(x):
    return lax.all_to_all(x, "ctx", split_axis=0, concat_axis=0, tiled=False)


def gather_dp(x):
    return lax.all_gather(x, "dp", axis=0, tiled=True)


def scatter_dp(x):
    return lax.psum_scatter(x, "dp", scatter_dimension=0, tiled=True)


def fetch_piece(pieces, buffer, semaphores, count=1):
    step = pl.program_id(0)

    @pl.when(step == 0)
    def _():
        for i, piece in enumerate(pieces):
            pltpu.make_async_copy(piece, buffer.at[i], semaphores.at[i]).start()

    for i in range(count):
        at = step * count + i
        pltpu.make_async_copy(pieces[0], buffer.at[at], semaphores.at[at]).wait()
    if count == 1:
        return buffer[step]
    return buffer[pl.ds(step * count, count)].reshape(count * buffer.shape[1], buffer.shape[2])


def keep_pieces(buffer, target, semaphores, count=1):
    step = pl.program_id(0)
    total, tok = buffer.shape[0], buffer.shape[1]

    def copy(at):
        rows = pl.ds(pl.multiple_of(at * tok, tok), tok)
        return pltpu.make_async_copy(buffer.at[at], target.at[rows], semaphores.at[at])

    for i in range(count):
        copy(step * count + i).start()

    @pl.when(step == total // count - 1)
    def _():
        for i in range(total):
            copy(i).wait()


def store_rows(source, target, semaphores):
    count = semaphores.shape[0]
    rows = source.shape[0] // count
    copies = [
        pltpu.make_async_copy(
            source.at[pl.ds(i * rows, rows)], target.at[pl.ds(i * rows, rows)], semaphores.at[i]
        )
        for i in range(count)
    ]
    for copy in copies:
        copy.start()
    return copies


def chunks(rows):
    return next(count for count in (8, 4, 2, 1) if rows % (16 * count) == 0)


def fetch_rows(source, buffer, semaphores):
    count = semaphores.shape[0]
    rows = source.shape[0] // count

    @pl.when(pl.program_id(0) == 0)
    def _():
        copies = [
            pltpu.make_async_copy(
                source.at[pl.ds(i * rows, rows)], buffer.at[pl.ds(i * rows, rows)], semaphores.at[i]
            )
            for i in range(count)
        ]
        for copy in copies:
            copy.start()
        for copy in copies:
            copy.wait()


def swap_halves(x):
    return pltpu.roll(x, x.shape[1] // 2, axis=1)


def turn_tables(cosine, sine, width):
    times = width // 128
    cosine = jnp.concatenate([cosine] * times, axis=1) if times > 1 else cosine
    sine = jnp.concatenate([sine] * times, axis=1) if times > 1 else sine
    lane = lax.broadcasted_iota(jnp.int32, sine.shape, 1)
    return cosine, jnp.where(lane < width // 2, -sine, sine)


def any_specs(pieces):
    return [pl.BlockSpec(memory_space=pltpu.HBM) for _ in pieces]


def project_qkv(order, pieces, weight, spread, widen, cosine, sine, width, tok):
    n = len(pieces)
    seq = n * tok

    def kernel(order_ref, *refs):
        parts = refs[:n]
        w_hbm, spread_ref, widen_ref, cos_ref, sin_ref = refs[n : n + 5]
        (
            q_ref, k_ref, v_ref, kt_ref, vt_ref, all_hbm, wide, buffer, semaphores, keep_semaphores, w_ref, w_semaphores
        ) = refs[n + 5 :]
        fetch_rows(w_hbm, w_ref, w_semaphores)

        @pl.when(pl.program_id(0) == 0)
        def _():
            wide[...] = nn(w_ref[...], spread_ref[...]).astype(BF)

        x = fetch_piece(parts, buffer, semaphores)
        keep_pieces(buffer, all_hbm, keep_semaphores)
        mixed = nn(x, wide[...])
        cos, sin = turn_tables(cos_ref[...], sin_ref[...], width)
        q = mixed[:, :width]
        q_ref[...] = (q * cos + swap_halves(q) * sin).astype(BF) * (HD**-0.5)
        lane = lax.broadcasted_iota(jnp.int32, (tok, 128), 1)
        key_sine = jnp.where(lane < HALF, -sin_ref[...], sin_ref[...])
        both = jnp.where(
            lane < HD,
            mixed[:, width : width + 128] * cos_ref[...] + mixed[:, width + 128 :] * key_sine,
            mixed[:, width : width + 128],
        ).astype(BF)
        repeated = nn(both, widen_ref[...]).astype(BF)
        k_ref[...] = repeated[:, :width]
        v_ref[...] = repeated[:, width:]
        turned = both.T
        kt_ref[...] = turned[:HD]
        vt_ref[...] = turned[HD:]

    rows = lambda s, order: (order[s], 0)
    lanes = lambda s, order: (0, order[s])
    whole = lambda s, order: (0, 0)
    return pl.pallas_call(
        kernel,
        grid_spec=pltpu.PrefetchScalarGridSpec(
            num_scalar_prefetch=1,
            grid=(n,),
            in_specs=any_specs(pieces)
            + [
                pl.BlockSpec(memory_space=pltpu.HBM),
                pl.BlockSpec(spread.shape, whole),
                pl.BlockSpec(widen.shape, whole),
                pl.BlockSpec((tok, 128), rows),
                pl.BlockSpec((tok, 128), rows),
            ],
            out_specs=[
                pl.BlockSpec((tok, width), rows),
                pl.BlockSpec((tok, width), rows),
                pl.BlockSpec((tok, width), rows),
                pl.BlockSpec((HD, tok), lanes),
                pl.BlockSpec((HD, tok), lanes),
                pl.BlockSpec(memory_space=pltpu.HBM),
            ],
            scratch_shapes=[
                pltpu.VMEM((D, width + 256), BF),
                pltpu.VMEM((n, tok, D), BF),
                pltpu.SemaphoreType.DMA((n,)),
                pltpu.SemaphoreType.DMA((n,)),
                pltpu.VMEM(weight.shape, BF),
                pltpu.SemaphoreType.DMA((chunks(D),)),
            ],
        ),
        out_shape=[
            jax.ShapeDtypeStruct((seq, width), BF),
            jax.ShapeDtypeStruct((seq, width), BF),
            jax.ShapeDtypeStruct((seq, width), BF),
            jax.ShapeDtypeStruct((HD, seq), BF),
            jax.ShapeDtypeStruct((HD, seq), BF),
            jax.ShapeDtypeStruct((seq, D), BF),
        ],
        compiler_params=pltpu.CompilerParams(vmem_limit_bytes=VMEM_LIMIT),
        cost_estimate=LONG,
        name="project_qkv",
    )(order, *pieces, weight, spread, widen, cosine, sine)


def project_out(order, heads_in, pieces, residual):
    n, tok, width = heads_in.shape

    def kernel(order_ref, a_ref, *refs):
        parts = refs[:n]
        x_ref, state_hbm, norm_hbm, buffer, semaphores, state_ref, norm_ref, out_semaphores = refs[n:]
        step = pl.program_id(0)
        w = fetch_piece(parts, buffer, semaphores)

        @pl.when(step == 0)
        def _():
            state_ref[...] = x_ref[...].astype(F32)

        state_ref[...] += nn(a_ref[0], w)

        @pl.when(step == n - 1)
        def _():
            state = state_ref[...]
            scale = lax.rsqrt(jnp.mean(state * state, axis=-1, keepdims=True) + EPS)
            copies = store_rows(state_ref, state_hbm, out_semaphores.at[0])
            norm_ref[...] = (state * scale).astype(BF)
            copies += store_rows(norm_ref, norm_hbm, out_semaphores.at[1])
            for copy in copies:
                copy.wait()

    whole = lambda s, order: (0, 0)
    return pl.pallas_call(
        kernel,
        grid_spec=pltpu.PrefetchScalarGridSpec(
            num_scalar_prefetch=1,
            grid=(n,),
            in_specs=[pl.BlockSpec((1, tok, width), lambda s, order: (order[s], 0, 0))]
            + any_specs(pieces)
            + [pl.BlockSpec((tok, D), whole)],
            out_specs=[pl.BlockSpec(memory_space=pltpu.HBM)] * 2,
            scratch_shapes=[
                pltpu.VMEM((n, width, D), BF),
                pltpu.SemaphoreType.DMA((n,)),
                pltpu.VMEM((tok, D), F32),
                pltpu.VMEM((tok, D), BF),
                pltpu.SemaphoreType.DMA((2, 4)),
            ],
        ),
        out_shape=[
            jax.ShapeDtypeStruct((tok, D), F32),
            jax.ShapeDtypeStruct((tok, D), BF),
        ],
        compiler_params=pltpu.CompilerParams(vmem_limit_bytes=VMEM_LIMIT),
        cost_estimate=SHORT,
        name="project_out",
    )(order, heads_in, *pieces, residual)


def feed_forward(pieces, weight):
    n = len(pieces)
    tok = 2 * pieces[0].shape[0]
    seq = n * tok // 2
    ff = weight.shape[1] // 2

    def kernel(*refs):
        parts = refs[:n]
        w_hbm, hidden_ref, factor_ref, all_hbm, buffer, semaphores, keep_semaphores, w_ref, w_semaphores = refs[n:]
        fetch_rows(w_hbm, w_ref, w_semaphores)
        x = fetch_piece(parts, buffer, semaphores, 2)
        keep_pieces(buffer, all_hbm, keep_semaphores, 2)
        both = nn(x, w_ref[...])
        gate = both[:, :ff]
        up = both[:, ff:]
        sig = jax.nn.sigmoid(gate)
        silu = gate * sig
        hidden_ref[...] = (silu * up).astype(BF)
        factor_ref[:, :ff] = (up * sig * (1.0 + gate * (1.0 - sig))).astype(BF)
        factor_ref[:, ff:] = silu.astype(BF)

    rows = lambda s: (s, 0)
    return pl.pallas_call(
        kernel,
        grid=(n // 2,),
        in_specs=any_specs(pieces) + [pl.BlockSpec(memory_space=pltpu.HBM)],
        out_specs=[
            pl.BlockSpec((tok, ff), rows),
            pl.BlockSpec((tok, 2 * ff), rows),
            pl.BlockSpec(memory_space=pltpu.HBM),
        ],
        scratch_shapes=[
            pltpu.VMEM((n, tok // 2, D), BF),
            pltpu.SemaphoreType.DMA((n,)),
            pltpu.SemaphoreType.DMA((n,)),
            pltpu.VMEM(weight.shape, BF),
            pltpu.SemaphoreType.DMA((chunks(D),)),
        ],
        out_shape=[
            jax.ShapeDtypeStruct((seq, ff), BF),
            jax.ShapeDtypeStruct((seq, 2 * ff), BF),
            jax.ShapeDtypeStruct((seq, D), BF),
        ],
        compiler_params=pltpu.CompilerParams(vmem_limit_bytes=VMEM_LIMIT),
        cost_estimate=LONG,
        name="feed_forward",
    )(*pieces, weight)


def feed_backward(factors, grads, weight):
    seq = factors.shape[0]
    ff = weight.shape[0]
    tok = 512

    def kernel(factor_ref, g_ref, w_hbm, out_ref, w_ref, w_semaphores, turned):
        fetch_rows(w_hbm, w_ref, w_semaphores)

        @pl.when(pl.program_id(0) == 0)
        def _():
            turned[...] = w_ref[...].T

        grad_hidden = nn(g_ref[...], turned[...])
        factor = factor_ref[...].astype(F32)
        out_ref[:, :ff] = (grad_hidden * factor[:, :ff]).astype(BF)
        out_ref[:, ff:] = (grad_hidden * factor[:, ff:]).astype(BF)

    rows = lambda s: (s, 0)
    return pl.pallas_call(
        kernel,
        grid=(seq // tok,),
        in_specs=[
            pl.BlockSpec((tok, 2 * ff), rows),
            pl.BlockSpec((tok, D), rows),
            pl.BlockSpec(memory_space=pltpu.HBM),
        ],
        out_specs=pl.BlockSpec((tok, 2 * ff), rows),
        scratch_shapes=[
            pltpu.VMEM(weight.shape, BF),
            pltpu.SemaphoreType.DMA((chunks(ff),)),
            pltpu.VMEM((D, ff), BF),
        ],
        out_shape=jax.ShapeDtypeStruct((seq, 2 * ff), BF),
        compiler_params=pltpu.CompilerParams(vmem_limit_bytes=VMEM_LIMIT),
        cost_estimate=LONG,
        name="feed_backward",
    )(factors, grads, weight)


def lay_out(pieces):
    n = len(pieces)
    tok = pieces[0].shape[0]

    def kernel(*refs):
        parts = refs[:n]
        out_ref, buffer, in_semaphores, out_semaphores = refs[n:]
        arrive = [
            pltpu.make_async_copy(part, buffer.at[i], in_semaphores.at[i])
            for i, part in enumerate(parts)
        ]
        leave = [
            pltpu.make_async_copy(buffer.at[i], out_ref.at[pl.ds(i * tok, tok)], out_semaphores.at[i])
            for i in range(n)
        ]
        for copy in arrive:
            copy.start()
        for i in range(n):
            arrive[i].wait()
            leave[i].start()
        for copy in leave:
            copy.wait()

    return pl.pallas_call(
        kernel,
        in_specs=any_specs(pieces),
        out_specs=pl.BlockSpec(memory_space=pltpu.HBM),
        scratch_shapes=[
            pltpu.VMEM((n, tok, D), BF),
            pltpu.SemaphoreType.DMA((n,)),
            pltpu.SemaphoreType.DMA((n,)),
        ],
        out_shape=jax.ShapeDtypeStruct((n * tok, D), BF),
        compiler_params=pltpu.CompilerParams(vmem_limit_bytes=VMEM_LIMIT),
        cost_estimate=SHORT,
        name="lay_out",
    )(*pieces)


def branch_back(order, d_two, state, out_grad, pieces):
    n = len(pieces)
    tok = d_two.shape[0]
    width = pieces[0].shape[0]

    def kernel(order_ref, d_ref, state_ref, g_ref, *refs):
        parts = refs[:n]
        grad_hbm, branch_hbm, heads_ref, buffer, semaphores, grad_ref, branch_ref, out_semaphores = refs[n:]

        @pl.when(pl.program_id(0) == 0)
        def _():
            state = state_ref[...]
            scale = lax.rsqrt(jnp.mean(state * state, axis=-1, keepdims=True) + EPS)
            norm = state * scale
            d = d_ref[...]
            grad = g_ref[...].astype(F32) + scale * (
                d - norm * jnp.mean(d * norm, axis=-1, keepdims=True)
            )
            grad_ref[...] = grad
            branch_ref[...] = grad.astype(BF)
            store_rows(grad_ref, grad_hbm, out_semaphores.at[0])
            store_rows(branch_ref, branch_hbm, out_semaphores.at[1])

        w = fetch_piece(parts, buffer, semaphores)
        heads_ref[0] = nt(branch_ref[...], w).astype(BF)

        @pl.when(pl.program_id(0) == n - 1)
        def _():
            for source, target, at in ((grad_ref, grad_hbm, 0), (branch_ref, branch_hbm, 1)):
                rows = tok // 4
                for i in range(4):
                    cut = pl.ds(i * rows, rows)
                    pltpu.make_async_copy(source.at[cut], target.at[cut], out_semaphores.at[at, i]).wait()

    whole = lambda s, order: (0, 0)
    return pl.pallas_call(
        kernel,
        grid_spec=pltpu.PrefetchScalarGridSpec(
            num_scalar_prefetch=1,
            grid=(n,),
            in_specs=[
                pl.BlockSpec((tok, D), whole),
                pl.BlockSpec((tok, D), whole),
                pl.BlockSpec((tok, D), whole),
            ]
            + any_specs(pieces),
            out_specs=[
                pl.BlockSpec(memory_space=pltpu.HBM),
                pl.BlockSpec(memory_space=pltpu.HBM),
                pl.BlockSpec((1, tok, width), lambda s, order: (order[s], 0, 0)),
            ],
            scratch_shapes=[
                pltpu.VMEM((n, width, D), BF),
                pltpu.SemaphoreType.DMA((n,)),
                pltpu.VMEM((tok, D), F32),
                pltpu.VMEM((tok, D), BF),
                pltpu.SemaphoreType.DMA((2, 4)),
            ],
        ),
        out_shape=[
            jax.ShapeDtypeStruct((tok, D), F32),
            jax.ShapeDtypeStruct((tok, D), BF),
            jax.ShapeDtypeStruct((n, tok, width), BF),
        ],
        compiler_params=pltpu.CompilerParams(vmem_limit_bytes=VMEM_LIMIT),
        cost_estimate=SHORT,
        name="branch_back",
    )(order, d_two, state, out_grad, *pieces)


def split_columns(weight, gain, n_ctx, n_dp, ff_rows):
    rows = weight.shape[0]
    ff = ff_rows * n_dp

    def kernel(w_ref, gain_ref, out_ref):
        gains = gain_ref[...]
        for part in range(2):
            for d in range(n_dp):
                for c in range(n_ctx):
                    at = part * FF + (d * n_ctx + c) * ff_rows
                    to = part * ff + d * ff_rows
                    values = w_ref[:, at : at + ff_rows].astype(F32) * gains
                    out_ref[c, :, to : to + ff_rows] = values.astype(BF)

    return pl.pallas_call(
        kernel,
        in_specs=[pl.BlockSpec(memory_space=pltpu.VMEM)] * 2,
        out_specs=pl.BlockSpec(memory_space=pltpu.VMEM),
        out_shape=jax.ShapeDtypeStruct((n_ctx, rows, 2 * ff), BF),
        compiler_params=pltpu.CompilerParams(vmem_limit_bytes=VMEM_LIMIT),
        cost_estimate=LONG,
        name="split_columns",
    )(weight, gain)


def join_columns(sums, weight, gain, n_dp, ff_rows):
    n_ctx, rows, both = sums.shape
    ff = both // 2

    def kernel(s_ref, w_ref, gain_ref, out_ref, gain_out_ref):
        gains = gain_ref[...]
        total = jnp.zeros((rows, ff_rows), F32)
        for part in range(2):
            for d in range(n_dp):
                for c in range(n_ctx):
                    at = part * ff + d * ff_rows
                    to = part * FF + (d * n_ctx + c) * ff_rows
                    values = s_ref[c, :, at : at + ff_rows].astype(F32)
                    total = total + values * w_ref[:, to : to + ff_rows].astype(F32)
                    out_ref[:, to : to + ff_rows] = values * gains
        gain_out_ref[...] = jnp.sum(total, axis=1, keepdims=True)

    return pl.pallas_call(
        kernel,
        in_specs=[pl.BlockSpec(memory_space=pltpu.VMEM)] * 3,
        out_specs=[pl.BlockSpec(memory_space=pltpu.VMEM)] * 2,
        out_shape=[
            jax.ShapeDtypeStruct((rows, 2 * FF), F32),
            jax.ShapeDtypeStruct((rows, 1), F32),
        ],
        compiler_params=pltpu.CompilerParams(vmem_limit_bytes=VMEM_LIMIT),
        cost_estimate=LONG,
        name="join_columns",
    )(sums, weight, gain)


def lane_heads(rows, width):
    lane = lax.broadcasted_iota(jnp.int32, (rows, width), 1)
    return (lane % (width // 2)) // HALF


def attend_forward(slot_of, starts, queries, keys, values_t, heads, tok, first, count, before):
    seq, width = queries.shape
    blocks = seq // tok
    span = 2 * tok

    def kernel(slot_ref, start_ref, q_ref, k_ref, v_ref, *refs):
        attn_ref, slot_attn_ref, full_ref, lse_ref, scores = refs[len(before) :]
        block = first + pl.program_id(0)
        steps = (block + 2) // 2
        start = start_ref[...]
        here = block * tok + lax.broadcasted_iota(jnp.int32, (1, tok), 1)
        head_of = lane_heads(tok, width)
        q = q_ref[...]
        q_heads = [jnp.where(head_of == h, q, jnp.zeros_like(q)) for h in range(heads)]

        def score(i, peaks):
            rows = pl.ds(pl.multiple_of(i * span, span), span)
            k = k_ref[rows, :]
            there = i * span + lax.broadcasted_iota(jnp.int32, (span, tok), 0)
            visible = (there >= start) & (there <= here)
            out = []
            for h in range(heads):
                s = jnp.where(visible, nt(k, q_heads[h]), MASKED)
                scores[h, rows, :] = s
                out.append(jnp.maximum(peaks[h], jnp.max(s.reshape(span // 8, 8, tok), axis=0)))
            return tuple(out)

        peaks = lax.fori_loop(
            0, steps, score, tuple(jnp.full((8, tok), MASKED, F32) for _ in range(heads))
        )
        peaks = [jnp.max(peak, axis=0, keepdims=True) for peak in peaks]

        def weigh(i, running):
            rows = pl.ds(pl.multiple_of(i * span, span), span)
            v = v_ref[:, rows]
            out = []
            for h in range(heads):
                total, acc = running[h]
                p = jnp.exp(scores[h, rows, :] - peaks[h])
                total = total + jnp.sum(p.reshape(span // 8, 8, tok), axis=0)
                out.append((total, acc + nn(v, p.astype(BF))))
            return tuple(out)

        result = lax.fori_loop(
            0,
            steps,
            weigh,
            tuple((jnp.zeros((8, tok), F32), jnp.zeros((HD, tok), F32)) for _ in range(heads)),
        )
        rows = []
        for h in range(heads):
            total, acc = result[h]
            total = jnp.sum(total, axis=0, keepdims=True)
            rows.append(acc / total)
            lse_ref[0, h : h + 1, :] = peaks[h] + jnp.log(total)
        full = jnp.concatenate(rows, axis=0).T
        full_ref[...] = full
        attn_ref[...] = full.astype(BF)
        slot_attn_ref[...] = full.astype(BF)

    return pl.pallas_call(
        kernel,
        grid_spec=pltpu.PrefetchScalarGridSpec(
            num_scalar_prefetch=1,
            grid=(count,),
            in_specs=[
                pl.BlockSpec((1, tok), lambda j, slot: (0, first + j)),
                pl.BlockSpec((tok, width), lambda j, slot: (first + j, 0)),
                pl.BlockSpec((seq, width), lambda j, slot: (0, 0)),
                pl.BlockSpec((HD, seq), lambda j, slot: (0, 0)),
            ]
            + [pl.BlockSpec(memory_space=pltpu.HBM)] * len(before),
            out_specs=[
                pl.BlockSpec((tok, width), lambda j, slot: (first + j, 0)),
                pl.BlockSpec((tok, width), lambda j, slot: (slot[first + j], 0)),
                pl.BlockSpec((tok, width), lambda j, slot: (first + j, 0)),
                pl.BlockSpec((1, heads, tok), lambda j, slot: (first + j, 0, 0)),
            ],
            scratch_shapes=[pltpu.VMEM((heads, seq, tok), F32)],
        ),
        out_shape=[
            jax.ShapeDtypeStruct((seq, width), BF),
            jax.ShapeDtypeStruct((seq, width), BF),
            jax.ShapeDtypeStruct((seq, width), F32),
            jax.ShapeDtypeStruct((blocks, heads, tok), F32),
        ],
        input_output_aliases={5 + i: i for i in range(len(before))},
        compiler_params=pltpu.CompilerParams(vmem_limit_bytes=VMEM_LIMIT),
        cost_estimate=LONG,
        name="attend_forward",
    )(slot_of, starts, queries, keys, values_t, *before)


def attend_backward(
    slot_of, starts, queries, keys, keys_t, values, grads, full, lse, cosine, sine, unsplit, heads, tok
):
    seq, width = queries.shape
    blocks = seq // tok
    span = 2 * tok
    half = width // 2

    def kernel(
        slot_ref, start_ref, q_ref, k_ref, kt_ref, v_ref, g_ref, full_ref, lse_ref, cos_ref, sin_ref, unsplit_ref,
        out_ref, dk, dv,
    ):
        block = pl.program_id(0)
        steps = (block + 2) // 2

        @pl.when(block == 0)
        def _():
            dk[...] = jnp.zeros_like(dk)
            dv[...] = jnp.zeros_like(dv)

        start = start_ref[...]
        here = block * tok + lax.broadcasted_iota(jnp.int32, (1, tok), 1)
        head_of = lane_heads(tok, width)
        wide = lax.broadcasted_iota(jnp.int32, (tok, width), 1) // HD
        q = q_ref[...]
        g = g_ref[...]
        q_heads = [jnp.where(head_of == h, q, jnp.zeros_like(q)) for h in range(heads)]
        g_heads = [jnp.where(wide == h, g, jnp.zeros_like(g)) for h in range(heads)]
        q_stack = jnp.concatenate(q_heads, axis=0)
        g_stack = jnp.concatenate(g_heads, axis=0)
        picks = (
            lax.broadcasted_iota(jnp.int32, (8, width), 1) // HD
            == lax.broadcasted_iota(jnp.int32, (8, width), 0)
        ).astype(F32)
        deltas = lax.dot_general(
            picks,
            g.astype(F32) * full_ref[...],
            (((1,), (1,)), ((), ())),
            preferred_element_type=F32,
            precision=lax.Precision.HIGHEST,
        )

        def step(i, dq):
            rows = pl.ds(pl.multiple_of(i * span, span), span)
            k = k_ref[rows, :]
            v = v_ref[rows, :]
            kt = kt_ref[:, rows]
            there = i * span + lax.broadcasted_iota(jnp.int32, (span, tok), 0)
            visible = (there >= start) & (there <= here)
            probs, grad_scores, out = [], [], []
            for h in range(heads):
                s = jnp.where(visible, nt(k, q_heads[h]), MASKED)
                p = jnp.exp(s - lse_ref[0, h : h + 1, :])
                ds = (p * (nt(v, g_heads[h]) - deltas[h : h + 1, :])).astype(BF)
                probs.append(p.astype(BF))
                grad_scores.append(ds)
                out.append(dq[h] + nn(kt, ds))
            dv[rows, :] += nn(jnp.concatenate(probs, axis=1), g_stack)
            dk[rows, :] += nn(jnp.concatenate(grad_scores, axis=1), q_stack)
            return tuple(out)

        dq = lax.fori_loop(
            0, steps, step, tuple(jnp.zeros((HD, tok), F32) for _ in range(heads))
        )
        dq = jnp.concatenate([x[:HALF] for x in dq] + [x[HALF:] for x in dq], axis=0).T
        here_rows = pl.ds(pl.multiple_of(block * tok, tok), tok)
        cos, sin = turn_tables(cos_ref[here_rows, :], sin_ref[here_rows, :], width)
        dq = (dq * cos - swap_halves(dq) * sin) * (HD**-0.5)
        slot_rows = pl.ds(pl.multiple_of(slot_ref[block] * tok, tok), tok)
        out_ref[slot_rows, :width] = nn(dq.astype(BF), unsplit_ref[...]).astype(BF)

        @pl.when(block == blocks - 1)
        def _():
            lane = lax.broadcasted_iota(jnp.int32, (width, 128), 0)
            column = lax.broadcasted_iota(jnp.int32, (width, 128), 1)
            fold_k = ((lane // half) * HALF + lane % HALF == column).astype(BF)
            fold_v = (lane % HD + HD == column).astype(BF)

            def fold(i, unused):
                rows = pl.ds(pl.multiple_of(i * tok, tok), tok)
                cos, sin = turn_tables(cos_ref[rows, :], sin_ref[rows, :], width)
                a = dk[rows, :]
                a = a * cos - swap_halves(a) * sin
                b = dv[rows, :]
                a_high = a.astype(BF)
                b_high = b.astype(BF)
                terms = (
                    nn(a_high, fold_k)
                    + nn((a - a_high.astype(F32)).astype(BF), fold_k)
                    + nn(b_high, fold_v)
                    + nn((b - b_high.astype(F32)).astype(BF), fold_v)
                )
                slot_rows = pl.ds(pl.multiple_of(slot_ref[i] * tok, tok), tok)
                out_ref[slot_rows, width:] = terms.astype(BF)
                return unused

            lax.fori_loop(0, blocks, fold, 0)

    whole = lambda shape: pl.BlockSpec(shape, lambda j, *_: (0, 0))
    return pl.pallas_call(
        kernel,
        grid_spec=pltpu.PrefetchScalarGridSpec(
            num_scalar_prefetch=1,
            grid=(blocks,),
            in_specs=[
                pl.BlockSpec((1, tok), lambda j, *_: (0, j)),
                pl.BlockSpec((tok, width), lambda j, *_: (j, 0)),
                whole((seq, width)),
                whole((HD, seq)),
                whole((seq, width)),
                pl.BlockSpec((tok, width), lambda j, *_: (j, 0)),
                pl.BlockSpec((tok, width), lambda j, *_: (j, 0)),
                pl.BlockSpec((1, heads, tok), lambda j, *_: (j, 0, 0)),
                whole((seq, 128)),
                whole((seq, 128)),
                whole((width, width)),
            ],
            out_specs=whole((seq, width + 128)),
            scratch_shapes=[pltpu.VMEM((seq, width), F32), pltpu.VMEM((seq, width), F32)],
        ),
        out_shape=jax.ShapeDtypeStruct((seq, width + 128), BF),
        compiler_params=pltpu.CompilerParams(vmem_limit_bytes=VMEM_LIMIT),
        cost_estimate=MEDIUM,
        name="attend_backward",
    )(slot_of, starts, queries, keys, keys_t, values, grads, full, lse, cosine, sine, unsplit)


def outer_rows(activations, gradients):
    return lax.dot_general(
        activations, gradients, (((0,), (0,)), ((), ())), preferred_element_type=F32
    ).astype(BF)


def split_source(width):
    lane = np.arange(width)
    half = lane // (width // 2)
    head = (lane % (width // 2)) // HALF
    return head * HD + half * HALF + lane % HALF


def spread_matrix(width):
    matrix = np.zeros((width + 2 * HD, width + 256), np.float32)
    lane = np.arange(width)
    matrix[split_source(width), lane] = 1
    lane = np.arange(2 * HD)
    matrix[width + lane, width + lane] = 1
    lane = np.arange(HD)
    matrix[width + (lane + HALF) % HD, width + 128 + lane] = 1
    return jnp.asarray(matrix, BF)


def widen_matrix(width):
    matrix = np.zeros((2 * HD, 2 * width), np.float32)
    lane = np.arange(width)
    matrix[(lane // (width // 2)) * HALF + lane % HALF, lane] = 1
    matrix[HD + lane % HD, width + lane] = 1
    return jnp.asarray(matrix, BF)


def unsplit_matrix(width):
    matrix = np.zeros((width, width), np.float32)
    matrix[np.arange(width), split_source(width)] = 1
    return jnp.asarray(matrix, BF)


def on_device(
    block_in,
    gain_attn,
    qkv_weight,
    out_weight,
    gain_ffn,
    gate_up_weight,
    down_weight,
    doc_lengths,
    out_grad,
):
    n_ctx = lax.axis_size("ctx")
    n_dp = lax.axis_size("dp")
    me = lax.axis_index("ctx")
    tok = block_in.shape[0]
    seq = tok * n_ctx
    heads = H // n_ctx
    width = heads * HD
    sharers = n_ctx // KVH
    rows = qkv_weight.shape[0]
    ff_rows = down_weight.shape[0]
    ff = ff_rows * n_dp
    columns = width + 2 * HD

    order = me ^ jnp.where(me % 2 == 0, *[jnp.asarray(t) for t in slot_table(n_ctx)])
    slots = jnp.arange(n_ctx, dtype=jnp.int32)
    slot_of = jnp.sum(jnp.where(order[None, :] == slots[:, None], slots[None, :], 0), axis=1)
    index = jnp.arange(seq, dtype=jnp.int32)
    lengths = doc_lengths[0]
    ends = jnp.cumsum(lengths)
    starts = jnp.sum((index[:, None] >= ends[None, :]).astype(jnp.int32) * lengths[None, :], axis=1)
    lane = jnp.arange(128, dtype=F32) % HALF
    frequency = 10000.0 ** (-lane * 2.0 / HD)
    angles = (index - starts).astype(F32)[:, None] * frequency[None, :]
    cosine = jnp.cos(angles)
    sine = jnp.sin(angles)
    starts_row = starts[None, :]

    gain_one = gain_attn.astype(F32)[:, None]
    gain_two = gain_ffn.astype(F32)[:, None]
    qkv = (qkv_weight.astype(F32) * gain_one).astype(BF)
    q_cols = qkv[:, : H * HD].reshape(rows, n_ctx, width).transpose(1, 0, 2)
    k_cols = qkv[:, H * HD : (H + KVH) * HD].reshape(rows, KVH, HD).transpose(1, 0, 2)
    v_cols = qkv[:, (H + KVH) * HD :].reshape(rows, KVH, HD).transpose(1, 0, 2)
    kv_cols = jnp.repeat(jnp.concatenate([k_cols, v_cols], axis=2), sharers, axis=0)
    qkv_own = exchange(jnp.concatenate([q_cols, kv_cols], axis=2)).reshape(n_ctx * rows, columns)
    qkv_part = gather_dp(qkv_own)

    hidden_in = block_in.astype(F32)
    rms_one = lax.rsqrt(jnp.mean(hidden_in * hidden_in, axis=-1, keepdims=True) + EPS)
    gate_up_cols = split_columns(
        gate_up_weight, after(gain_two, cosine, sine), n_ctx, n_dp, ff_rows
    )
    one_direct = gather_direct(after((hidden_in * rms_one).astype(BF), qkv_own), n_ctx)
    owner_pairs = [(b, b % n_dp * n_ctx + b // n_dp) for b in range(n_dp * n_ctx)]
    out_own = lax.ppermute(after(out_weight, one_direct[1]), ("dp", "ctx"), owner_pairs)
    out_part = gather_dp(after(out_own, qkv_part))
    one_pieces = gather_rest(one_direct, n_ctx, (), (qkv_part, out_own, gate_up_cols))
    gate_up_own = exchange(after(gate_up_cols, qkv_part, *one_pieces[: n_ctx // 2])).reshape(
        n_ctx * rows, 2 * ff
    )
    gate_up_part = gather_dp(gate_up_own)
    down_part = gather_dp(after(down_weight, gate_up_own))

    queries, keys, values, keys_t, values_t, all_one = project_qkv(
        order, one_pieces, qkv_part, spread_matrix(width), widen_matrix(width), cosine, sine, width, tok
    )
    queries = after(queries, gate_up_own)
    part = n_ctx * 5 // 8
    out_direct = gather_direct(after(out_part, queries), n_ctx)
    begun = attend_forward(slot_of, starts_row, queries, keys, values_t, heads, tok, 0, part, ())
    out_pieces = gather_rest(out_direct, n_ctx, (begun[2],), (begun[2],))
    attn, slot_attn, attended, lse = attend_forward(
        slot_of,
        starts_row,
        after(queries, *out_direct),
        keys,
        values_t,
        heads,
        tok,
        part,
        n_ctx - part,
        tuple(begun),
    )
    attn_tokens = exchange(after(attn, *out_pieces[: n_ctx // 2]).reshape(n_ctx, tok, width))
    state, norm_two = project_out(order, attn_tokens, out_pieces, block_in)

    two_pieces = gather_slots(norm_two, n_ctx)
    grad_direct = gather_direct(after(out_grad, *two_pieces), n_ctx)
    hidden, factors, all_two = feed_forward(two_pieces, gate_up_part)
    grad_pieces = gather_rest(grad_direct, n_ctx, (hidden,))
    all_grad = lay_out(grad_pieces)
    down_terms = outer_rows(hidden, all_grad)
    down_sums = scatter_dp(down_terms)
    grad_gate_up = feed_backward(after(factors, down_terms), all_grad, down_part)

    def rows_of(x, lo, hi):
        return lax.slice_in_dim(x, lo * tok, hi * tok, axis=0)

    d_pairs = scatter_pairs(
        lambda lo, hi: nt(rows_of(grad_gate_up, lo, hi), gate_up_part), tok, n_ctx
    )
    stages = tuple(reversed(range(len(walk(n_ctx, 0)))))
    d_arrived = swap_stage(d_pairs[0].astype(BF), n_ctx, stages[0])
    d_two = scatter_rest(d_pairs[1], d_arrived, stages, n_ctx)
    gate_up_terms = outer_rows(after(all_two, *d_pairs), grad_gate_up)
    gate_up_sums = scatter_dp(gate_up_terms)
    hidden_pairs = scatter_pairs(
        lambda lo, hi: nn(rows_of(after(hidden, d_arrived), lo, hi), down_part), tok, n_ctx
    )

    grad_state, grad_branch, grad_heads = branch_back(
        order, after(d_two, gate_up_terms, *hidden_pairs), state, out_grad, out_pieces
    )
    grad_attn = exchange(grad_heads).reshape(seq, width)
    branch_here, branch_there = gather_at_once(after(grad_branch, grad_attn), n_ctx)
    hidden_upper, hidden_lower = hidden_pairs
    hidden_arrived = swap_stage(after(hidden_upper.astype(BF), grad_attn), n_ctx, stages[0])
    grad_mixed = attend_backward(
        slot_of,
        starts_row,
        queries,
        keys,
        keys_t,
        values,
        grad_attn,
        attended,
        lse,
        cosine,
        sine,
        unsplit_matrix(width),
        heads,
        tok,
    )
    qkv_terms = outer_rows(all_one, grad_mixed)
    qkv_sums = scatter_dp(after(qkv_terms, gate_up_sums))
    d_one = scatter_chips(
        *scatter_pairs(lambda lo, hi: nt(rows_of(after(grad_mixed, qkv_terms, hidden_arrived, *branch_here), lo, hi), qkv_part), tok, n_ctx),
        stages,
        n_ctx,
        qkv_sums,
    )
    hidden_sums = scatter_rest(hidden_lower, hidden_arrived, stages, n_ctx)
    block_out = (state + hidden_sums).astype(BF)
    out_terms = outer_rows(slot_attn, after(lay_out(branch_here + branch_there), qkv_terms))
    out_sums = scatter_dp(after(out_terms, qkv_sums))
    norm_one = hidden_in * rms_one
    input_grad = grad_state + rms_one * (
        d_one - norm_one * jnp.mean(d_one * norm_one, axis=-1, keepdims=True)
    )

    down_weight_grad = after(down_sums, grad_mixed).astype(F32)
    out_weight_grad = lax.ppermute(
        out_sums, ("dp", "ctx"), [(b, a) for a, b in owner_pairs]
    ).astype(F32)
    gate_up_weight_grad, gain_ffn_grad = join_columns(
        exchange(after(gate_up_sums, grad_mixed).reshape(n_ctx, rows, 2 * ff)), gate_up_weight, gain_two, n_dp, ff_rows
    )
    qkv_back = exchange(qkv_sums.reshape(n_ctx, rows, columns)).astype(F32)
    q_back = qkv_back[:, :, :width].transpose(1, 0, 2).reshape(rows, H * HD)
    kv_back = jnp.sum(qkv_back[:, :, width:].reshape(KVH, sharers, rows, 2 * HD), axis=1)
    k_back = kv_back[:, :, :HD].transpose(1, 0, 2).reshape(rows, KVH * HD)
    v_back = kv_back[:, :, HD:].transpose(1, 0, 2).reshape(rows, KVH * HD)
    qkv_back = jnp.concatenate([q_back, k_back, v_back], axis=1)
    qkv_weight_grad = qkv_back * gain_one
    gain_attn_grad = jnp.sum(qkv_back * qkv_weight.astype(F32), axis=1)
    return (
        block_out,
        input_grad,
        gain_attn_grad,
        qkv_weight_grad,
        out_weight_grad,
        gain_ffn_grad[:, 0],
        gate_up_weight_grad,
        down_weight_grad,
    )


def solution(mesh):
    rows = P(("dp", "ctx"), None)
    entries = P(("dp", "ctx"))
    return jax.shard_map(
        on_device,
        mesh=mesh,
        in_specs=(rows, entries, rows, rows, entries, rows, rows, P("dp", None), rows),
        out_specs=(rows, rows, entries, rows, rows, entries, rows, rows),
        check_vma=False,
    )
```

```python
import jax
import jax.numpy as jnp
import numpy as np
from jax import lax
from jax.experimental import pallas as pl
from jax.experimental.pallas import tpu as pltpu
from jax.sharding import PartitionSpec as P

D = 2048
H = 32
KVH = 4
HD = 64
FF = 5632
HALF = HD // 2

EPS = 1e-05
MASKED = -1e30
BF = jnp.bfloat16
F32 = jnp.float32
VMEM_LIMIT = 60 << 20
SHORT = pl.CostEstimate(flops=1 << 20, bytes_accessed=1 << 20, transcendentals=0)
MEDIUM = pl.CostEstimate(flops=2 * 10**10, bytes_accessed=1 << 20, transcendentals=0)
LONG = pl.CostEstimate(flops=10**11, bytes_accessed=1 << 20, transcendentals=0)


def nt(a, b):
    return lax.dot_general(a, b, (((1,), (1,)), ((), ())), preferred_element_type=F32)


def nn(a, b):
    return jnp.dot(a, b, preferred_element_type=F32)


def after(x, *earlier):
    return lax.optimization_barrier((x, *earlier))[0]


def after_each(values, *earlier):
    count = len(values)
    return lax.optimization_barrier((*values, *earlier))[:count]


def walk(n_ctx, parity):
    bits = []
    bit = 2
    while bit < n_ctx:
        bits.append(bit)
        bit *= 2
    return bits if parity == 0 else bits[::-1]


def swap_stage(x, n_ctx, stage):
    pairs = [(c, c ^ walk(n_ctx, c % 2)[stage]) for c in range(n_ctx)]
    return lax.ppermute(x, "ctx", pairs)


def swap_core(x, n_ctx):
    return lax.ppermute(x, "ctx", [(c, c ^ 1) for c in range(n_ctx)])


def slot_table(n_ctx):
    lists = []
    for parity in (0, 1):
        row = [0]
        for bit in walk(n_ctx, parity):
            row = row + [v ^ bit for v in row]
        lists.append(row)
    return np.array(
        [lists[p] + [v ^ 1 for v in lists[1 - p]] for p in (0, 1)], dtype=np.int32
    )


def gather_direct(x, n_ctx):
    return [x] + [swap_stage(x, n_ctx, stage) for stage in range(len(walk(n_ctx, 0)))]


def gather_rest(direct, n_ctx, earlier=(), last=()):
    have = direct[:1]
    for stage in range(len(walk(n_ctx, 0))):
        passed = [after(block, *earlier) if earlier else block for block in have[1:]]
        have = have + [direct[stage + 1]] + [swap_stage(block, n_ctx, stage) for block in passed]
    return have + [swap_core(after(block, *last) if last else block, n_ctx) for block in have]


def gather_at_once(x, n_ctx):
    have = [x]
    table = slot_table(n_ctx)
    for slot in range(1, n_ctx // 2):
        pairs = [(c, c ^ int(table[c % 2][slot])) for c in range(n_ctx)]
        have.append(lax.ppermute(x, "ctx", pairs))
    return have, [swap_core(block, n_ctx) for block in have]


def gather_slots(x, n_ctx):
    return gather_rest(gather_direct(x, n_ctx), n_ctx)


def scatter_pairs(term, tok, n_ctx):
    mine = n_ctx // 2
    cut = mine // 2
    sums, arrivals = [], []
    for lo, hi in ((cut, mine), (0, cut)):
        arrivals.append(swap_core(term(mine + lo, mine + hi).astype(BF), n_ctx))
        sums.append(term(lo, hi) + arrivals[-1].astype(F32))
    return sums, arrivals


def scatter_chips(upper, lower, stages, n_ctx, *earlier):
    for stage in stages:
        if earlier and stage == 0:
            upper = after(upper.astype(BF), *earlier)
        lower = lower + swap_stage(upper.astype(BF), n_ctx, stage).astype(F32)
        if stage:
            half = lower.shape[0] // 2
            upper, lower = lower[half:], lower[:half]
    return lower if stages[-1] == 0 else (upper, lower)


def scatter_rest(lower, arrived, stages, n_ctx):
    sums = lower + arrived.astype(F32)
    if len(stages) == 1:
        return sums
    half = sums.shape[0] // 2
    return scatter_chips(sums[half:], sums[:half], stages[1:], n_ctx)


def exchange(x):
    return lax.all_to_all(x, "ctx", split_axis=0, concat_axis=0, tiled=False)


def gather_dp(x):
    return lax.all_gather(x, "dp", axis=0, tiled=True)


def scatter_dp(x):
    return lax.psum_scatter(x, "dp", scatter_dimension=0, tiled=True)


def fetch_piece(pieces, buffer, semaphores, count=1):
    step = pl.program_id(0)

    @pl.when(step == 0)
    def _():
        for i, piece in enumerate(pieces):
            pltpu.make_async_copy(piece, buffer.at[i], semaphores.at[i]).start()

    for i in range(count):
        at = step * count + i
        pltpu.make_async_copy(pieces[0], buffer.at[at], semaphores.at[at]).wait()
    if count == 1:
        return buffer[step]
    return buffer[pl.ds(step * count, count)].reshape(count * buffer.shape[1], buffer.shape[2])


def keep_pieces(buffer, target, semaphores, count=1):
    step = pl.program_id(0)
    total, tok = buffer.shape[0], buffer.shape[1]

    def copy(at):
        rows = pl.ds(pl.multiple_of(at * tok, tok), tok)
        return pltpu.make_async_copy(buffer.at[at], target.at[rows], semaphores.at[at])

    for i in range(count):
        copy(step * count + i).start()

    @pl.when(step == total // count - 1)
    def _():
        for i in range(total):
            copy(i).wait()


def store_rows(source, target, semaphores):
    count = semaphores.shape[0]
    rows = source.shape[0] // count
    copies = [
        pltpu.make_async_copy(
            source.at[pl.ds(i * rows, rows)], target.at[pl.ds(i * rows, rows)], semaphores.at[i]
        )
        for i in range(count)
    ]
    for copy in copies:
        copy.start()
    return copies


def chunks(rows):
    return next(count for count in (8, 4, 2, 1) if rows % (16 * count) == 0)


def fetch_rows(source, buffer, semaphores):
    count = semaphores.shape[0]
    rows = source.shape[0] // count

    @pl.when(pl.program_id(0) == 0)
    def _():
        copies = [
            pltpu.make_async_copy(
                source.at[pl.ds(i * rows, rows)], buffer.at[pl.ds(i * rows, rows)], semaphores.at[i]
            )
            for i in range(count)
        ]
        for copy in copies:
            copy.start()
        for copy in copies:
            copy.wait()


def swap_halves(x):
    return pltpu.roll(x, x.shape[1] // 2, axis=1)


def turn_tables(cosine, sine, width):
    times = width // 128
    cosine = jnp.concatenate([cosine] * times, axis=1) if times > 1 else cosine
    sine = jnp.concatenate([sine] * times, axis=1) if times > 1 else sine
    lane = lax.broadcasted_iota(jnp.int32, sine.shape, 1)
    return cosine, jnp.where(lane < width // 2, -sine, sine)


def any_specs(pieces):
    return [pl.BlockSpec(memory_space=pltpu.HBM) for _ in pieces]


def project_qkv(order, pieces, weight, spread, widen, cosine, sine, width, tok):
    n = len(pieces)
    seq = n * tok

    def kernel(order_ref, *refs):
        parts = refs[:n]
        w_hbm, spread_ref, widen_ref, cos_ref, sin_ref = refs[n : n + 5]
        (
            q_ref, k_ref, v_ref, kt_ref, vt_ref, all_hbm, wide, buffer, semaphores, keep_semaphores, w_ref, w_semaphores
        ) = refs[n + 5 :]
        fetch_rows(w_hbm, w_ref, w_semaphores)

        @pl.when(pl.program_id(0) == 0)
        def _():
            wide[...] = nn(w_ref[...], spread_ref[...]).astype(BF)

        x = fetch_piece(parts, buffer, semaphores)
        keep_pieces(buffer, all_hbm, keep_semaphores)
        mixed = nn(x, wide[...])
        cos, sin = turn_tables(cos_ref[...], sin_ref[...], width)
        q = mixed[:, :width]
        q_ref[...] = (q * cos + swap_halves(q) * sin).astype(BF) * (HD**-0.5)
        lane = lax.broadcasted_iota(jnp.int32, (tok, 128), 1)
        key_sine = jnp.where(lane < HALF, -sin_ref[...], sin_ref[...])
        both = jnp.where(
            lane < HD,
            mixed[:, width : width + 128] * cos_ref[...] + mixed[:, width + 128 :] * key_sine,
            mixed[:, width : width + 128],
        ).astype(BF)
        repeated = nn(both, widen_ref[...]).astype(BF)
        k_ref[...] = repeated[:, :width]
        v_ref[...] = repeated[:, width:]
        turned = both.T
        kt_ref[...] = turned[:HD]
        vt_ref[...] = turned[HD:]

    rows = lambda s, order: (order[s], 0)
    lanes = lambda s, order: (0, order[s])
    whole = lambda s, order: (0, 0)
    return pl.pallas_call(
        kernel,
        grid_spec=pltpu.PrefetchScalarGridSpec(
            num_scalar_prefetch=1,
            grid=(n,),
            in_specs=any_specs(pieces)
            + [
                pl.BlockSpec(memory_space=pltpu.HBM),
                pl.BlockSpec(spread.shape, whole),
                pl.BlockSpec(widen.shape, whole),
                pl.BlockSpec((tok, 128), rows),
                pl.BlockSpec((tok, 128), rows),
            ],
            out_specs=[
                pl.BlockSpec((tok, width), rows),
                pl.BlockSpec((tok, width), rows),
                pl.BlockSpec((tok, width), rows),
                pl.BlockSpec((HD, tok), lanes),
                pl.BlockSpec((HD, tok), lanes),
                pl.BlockSpec(memory_space=pltpu.HBM),
            ],
            scratch_shapes=[
                pltpu.VMEM((D, width + 256), BF),
                pltpu.VMEM((n, tok, D), BF),
                pltpu.SemaphoreType.DMA((n,)),
                pltpu.SemaphoreType.DMA((n,)),
                pltpu.VMEM(weight.shape, BF),
                pltpu.SemaphoreType.DMA((chunks(D),)),
            ],
        ),
        out_shape=[
            jax.ShapeDtypeStruct((seq, width), BF),
            jax.ShapeDtypeStruct((seq, width), BF),
            jax.ShapeDtypeStruct((seq, width), BF),
            jax.ShapeDtypeStruct((HD, seq), BF),
            jax.ShapeDtypeStruct((HD, seq), BF),
            jax.ShapeDtypeStruct((seq, D), BF),
        ],
        compiler_params=pltpu.CompilerParams(vmem_limit_bytes=VMEM_LIMIT),
        cost_estimate=LONG,
        name="project_qkv",
    )(order, *pieces, weight, spread, widen, cosine, sine)


def project_out(order, heads_in, pieces, residual):
    n, tok, width = heads_in.shape

    def kernel(order_ref, a_ref, *refs):
        parts = refs[:n]
        x_ref, state_hbm, norm_hbm, buffer, semaphores, state_ref, norm_ref, out_semaphores = refs[n:]
        step = pl.program_id(0)
        w = fetch_piece(parts, buffer, semaphores)

        @pl.when(step == 0)
        def _():
            state_ref[...] = x_ref[...].astype(F32)

        state_ref[...] += nn(a_ref[0], w)

        @pl.when(step == n - 1)
        def _():
            state = state_ref[...]
            scale = lax.rsqrt(jnp.mean(state * state, axis=-1, keepdims=True) + EPS)
            copies = store_rows(state_ref, state_hbm, out_semaphores.at[0])
            norm_ref[...] = (state * scale).astype(BF)
            copies += store_rows(norm_ref, norm_hbm, out_semaphores.at[1])
            for copy in copies:
                copy.wait()

    whole = lambda s, order: (0, 0)
    return pl.pallas_call(
        kernel,
        grid_spec=pltpu.PrefetchScalarGridSpec(
            num_scalar_prefetch=1,
            grid=(n,),
            in_specs=[pl.BlockSpec((1, tok, width), lambda s, order: (order[s], 0, 0))]
            + any_specs(pieces)
            + [pl.BlockSpec((tok, D), whole)],
            out_specs=[pl.BlockSpec(memory_space=pltpu.HBM)] * 2,
            scratch_shapes=[
                pltpu.VMEM((n, width, D), BF),
                pltpu.SemaphoreType.DMA((n,)),
                pltpu.VMEM((tok, D), F32),
                pltpu.VMEM((tok, D), BF),
                pltpu.SemaphoreType.DMA((2, 4)),
            ],
        ),
        out_shape=[
            jax.ShapeDtypeStruct((tok, D), F32),
            jax.ShapeDtypeStruct((tok, D), BF),
        ],
        compiler_params=pltpu.CompilerParams(vmem_limit_bytes=VMEM_LIMIT),
        cost_estimate=SHORT,
        name="project_out",
    )(order, heads_in, *pieces, residual)


def feed_forward(pieces, weight):
    n = len(pieces)
    tok = 2 * pieces[0].shape[0]
    seq = n * tok // 2
    ff = weight.shape[1] // 2

    def kernel(*refs):
        parts = refs[:n]
        w_hbm, hidden_ref, factor_ref, all_hbm, buffer, semaphores, keep_semaphores, w_ref, w_semaphores = refs[n:]
        fetch_rows(w_hbm, w_ref, w_semaphores)
        x = fetch_piece(parts, buffer, semaphores, 2)
        keep_pieces(buffer, all_hbm, keep_semaphores, 2)
        both = nn(x, w_ref[...])
        gate = both[:, :ff]
        up = both[:, ff:]
        sig = jax.nn.sigmoid(gate)
        silu = gate * sig
        hidden_ref[...] = (silu * up).astype(BF)
        factor_ref[:, :ff] = (up * sig * (1.0 + gate * (1.0 - sig))).astype(BF)
        factor_ref[:, ff:] = silu.astype(BF)

    rows = lambda s: (s, 0)
    return pl.pallas_call(
        kernel,
        grid=(n // 2,),
        in_specs=any_specs(pieces) + [pl.BlockSpec(memory_space=pltpu.HBM)],
        out_specs=[
            pl.BlockSpec((tok, ff), rows),
            pl.BlockSpec((tok, 2 * ff), rows),
            pl.BlockSpec(memory_space=pltpu.HBM),
        ],
        scratch_shapes=[
            pltpu.VMEM((n, tok // 2, D), BF),
            pltpu.SemaphoreType.DMA((n,)),
            pltpu.SemaphoreType.DMA((n,)),
            pltpu.VMEM(weight.shape, BF),
            pltpu.SemaphoreType.DMA((chunks(D),)),
        ],
        out_shape=[
            jax.ShapeDtypeStruct((seq, ff), BF),
            jax.ShapeDtypeStruct((seq, 2 * ff), BF),
            jax.ShapeDtypeStruct((seq, D), BF),
        ],
        compiler_params=pltpu.CompilerParams(vmem_limit_bytes=VMEM_LIMIT),
        cost_estimate=LONG,
        name="feed_forward",
    )(*pieces, weight)


def feed_backward(factors, grads, weight):
    seq = factors.shape[0]
    ff = weight.shape[0]
    tok = 512

    def kernel(factor_ref, g_ref, w_hbm, out_ref, w_ref, w_semaphores, turned):
        fetch_rows(w_hbm, w_ref, w_semaphores)

        @pl.when(pl.program_id(0) == 0)
        def _():
            turned[...] = w_ref[...].T

        grad_hidden = nn(g_ref[...], turned[...])
        factor = factor_ref[...].astype(F32)
        out_ref[:, :ff] = (grad_hidden * factor[:, :ff]).astype(BF)
        out_ref[:, ff:] = (grad_hidden * factor[:, ff:]).astype(BF)

    rows = lambda s: (s, 0)
    return pl.pallas_call(
        kernel,
        grid=(seq // tok,),
        in_specs=[
            pl.BlockSpec((tok, 2 * ff), rows),
            pl.BlockSpec((tok, D), rows),
            pl.BlockSpec(memory_space=pltpu.HBM),
        ],
        out_specs=pl.BlockSpec((tok, 2 * ff), rows),
        scratch_shapes=[
            pltpu.VMEM(weight.shape, BF),
            pltpu.SemaphoreType.DMA((chunks(ff),)),
            pltpu.VMEM((D, ff), BF),
        ],
        out_shape=jax.ShapeDtypeStruct((seq, 2 * ff), BF),
        compiler_params=pltpu.CompilerParams(vmem_limit_bytes=VMEM_LIMIT),
        cost_estimate=LONG,
        name="feed_backward",
    )(factors, grads, weight)


def lay_out(pieces):
    n = len(pieces)
    tok = pieces[0].shape[0]

    def kernel(*refs):
        parts = refs[:n]
        out_ref, buffer, in_semaphores, out_semaphores = refs[n:]
        arrive = [
            pltpu.make_async_copy(part, buffer.at[i], in_semaphores.at[i])
            for i, part in enumerate(parts)
        ]
        leave = [
            pltpu.make_async_copy(buffer.at[i], out_ref.at[pl.ds(i * tok, tok)], out_semaphores.at[i])
            for i in range(n)
        ]
        for copy in arrive:
            copy.start()
        for i in range(n):
            arrive[i].wait()
            leave[i].start()
        for copy in leave:
            copy.wait()

    return pl.pallas_call(
        kernel,
        in_specs=any_specs(pieces),
        out_specs=pl.BlockSpec(memory_space=pltpu.HBM),
        scratch_shapes=[
            pltpu.VMEM((n, tok, D), BF),
            pltpu.SemaphoreType.DMA((n,)),
            pltpu.SemaphoreType.DMA((n,)),
        ],
        out_shape=jax.ShapeDtypeStruct((n * tok, D), BF),
        compiler_params=pltpu.CompilerParams(vmem_limit_bytes=VMEM_LIMIT),
        cost_estimate=SHORT,
        name="lay_out",
    )(*pieces)


def branch_back(order, d_two, state, out_grad, pieces):
    n = len(pieces)
    tok = d_two.shape[0]
    width = pieces[0].shape[0]

    def kernel(order_ref, d_ref, state_ref, g_ref, *refs):
        parts = refs[:n]
        grad_hbm, branch_hbm, heads_ref, buffer, semaphores, grad_ref, branch_ref, out_semaphores = refs[n:]

        @pl.when(pl.program_id(0) == 0)
        def _():
            state = state_ref[...]
            scale = lax.rsqrt(jnp.mean(state * state, axis=-1, keepdims=True) + EPS)
            norm = state * scale
            d = d_ref[...]
            grad = g_ref[...].astype(F32) + scale * (
                d - norm * jnp.mean(d * norm, axis=-1, keepdims=True)
            )
            grad_ref[...] = grad
            branch_ref[...] = grad.astype(BF)
            store_rows(grad_ref, grad_hbm, out_semaphores.at[0])
            store_rows(branch_ref, branch_hbm, out_semaphores.at[1])

        w = fetch_piece(parts, buffer, semaphores)
        heads_ref[0] = nt(branch_ref[...], w).astype(BF)

        @pl.when(pl.program_id(0) == n - 1)
        def _():
            for source, target, at in ((grad_ref, grad_hbm, 0), (branch_ref, branch_hbm, 1)):
                rows = tok // 4
                for i in range(4):
                    cut = pl.ds(i * rows, rows)
                    pltpu.make_async_copy(source.at[cut], target.at[cut], out_semaphores.at[at, i]).wait()

    whole = lambda s, order: (0, 0)
    return pl.pallas_call(
        kernel,
        grid_spec=pltpu.PrefetchScalarGridSpec(
            num_scalar_prefetch=1,
            grid=(n,),
            in_specs=[
                pl.BlockSpec((tok, D), whole),
                pl.BlockSpec((tok, D), whole),
                pl.BlockSpec((tok, D), whole),
            ]
            + any_specs(pieces),
            out_specs=[
                pl.BlockSpec(memory_space=pltpu.HBM),
                pl.BlockSpec(memory_space=pltpu.HBM),
                pl.BlockSpec((1, tok, width), lambda s, order: (order[s], 0, 0)),
            ],
            scratch_shapes=[
                pltpu.VMEM((n, width, D), BF),
                pltpu.SemaphoreType.DMA((n,)),
                pltpu.VMEM((tok, D), F32),
                pltpu.VMEM((tok, D), BF),
                pltpu.SemaphoreType.DMA((2, 4)),
            ],
        ),
        out_shape=[
            jax.ShapeDtypeStruct((tok, D), F32),
            jax.ShapeDtypeStruct((tok, D), BF),
            jax.ShapeDtypeStruct((n, tok, width), BF),
        ],
        compiler_params=pltpu.CompilerParams(vmem_limit_bytes=VMEM_LIMIT),
        cost_estimate=SHORT,
        name="branch_back",
    )(order, d_two, state, out_grad, *pieces)


def split_columns(weight, gain, n_ctx, n_dp, ff_rows):
    rows = weight.shape[0]
    ff = ff_rows * n_dp

    def kernel(w_ref, gain_ref, out_ref):
        gains = gain_ref[...]
        for part in range(2):
            for d in range(n_dp):
                for c in range(n_ctx):
                    at = part * FF + (d * n_ctx + c) * ff_rows
                    to = part * ff + d * ff_rows
                    values = w_ref[:, at : at + ff_rows].astype(F32) * gains
                    out_ref[c, :, to : to + ff_rows] = values.astype(BF)

    return pl.pallas_call(
        kernel,
        in_specs=[pl.BlockSpec(memory_space=pltpu.VMEM)] * 2,
        out_specs=pl.BlockSpec(memory_space=pltpu.VMEM),
        out_shape=jax.ShapeDtypeStruct((n_ctx, rows, 2 * ff), BF),
        compiler_params=pltpu.CompilerParams(vmem_limit_bytes=VMEM_LIMIT),
        cost_estimate=LONG,
        name="split_columns",
    )(weight, gain)


def join_columns(sums, weight, gain, n_dp, ff_rows):
    n_ctx, rows, both = sums.shape
    ff = both // 2

    def kernel(s_ref, w_ref, gain_ref, out_ref, gain_out_ref):
        gains = gain_ref[...]
        total = jnp.zeros((rows, ff_rows), F32)
        for part in range(2):
            for d in range(n_dp):
                for c in range(n_ctx):
                    at = part * ff + d * ff_rows
                    to = part * FF + (d * n_ctx + c) * ff_rows
                    values = s_ref[c, :, at : at + ff_rows].astype(F32)
                    total = total + values * w_ref[:, to : to + ff_rows].astype(F32)
                    out_ref[:, to : to + ff_rows] = values * gains
        gain_out_ref[...] = jnp.sum(total, axis=1, keepdims=True)

    return pl.pallas_call(
        kernel,
        in_specs=[pl.BlockSpec(memory_space=pltpu.VMEM)] * 3,
        out_specs=[pl.BlockSpec(memory_space=pltpu.VMEM)] * 2,
        out_shape=[
            jax.ShapeDtypeStruct((rows, 2 * FF), F32),
            jax.ShapeDtypeStruct((rows, 1), F32),
        ],
        compiler_params=pltpu.CompilerParams(vmem_limit_bytes=VMEM_LIMIT),
        cost_estimate=LONG,
        name="join_columns",
    )(sums, weight, gain)


def lane_heads(rows, width):
    lane = lax.broadcasted_iota(jnp.int32, (rows, width), 1)
    return (lane % (width // 2)) // HALF


def attend_forward(slot_of, starts, queries, keys, values_t, heads, tok, first, count, before):
    seq, width = queries.shape
    blocks = seq // tok
    span = 2 * tok

    def kernel(slot_ref, start_ref, q_ref, k_ref, v_ref, *refs):
        attn_ref, slot_attn_ref, full_ref, lse_ref, scores = refs[len(before) :]
        block = first + pl.program_id(0)
        steps = (block + 2) // 2
        start = start_ref[...]
        here = block * tok + lax.broadcasted_iota(jnp.int32, (1, tok), 1)
        head_of = lane_heads(tok, width)
        q = q_ref[...]
        q_heads = [jnp.where(head_of == h, q, jnp.zeros_like(q)) for h in range(heads)]

        def score(i, peaks):
            rows = pl.ds(pl.multiple_of(i * span, span), span)
            k = k_ref[rows, :]
            there = i * span + lax.broadcasted_iota(jnp.int32, (span, tok), 0)
            visible = (there >= start) & (there <= here)
            out = []
            for h in range(heads):
                s = jnp.where(visible, nt(k, q_heads[h]), MASKED)
                scores[h, rows, :] = s
                out.append(jnp.maximum(peaks[h], jnp.max(s.reshape(span // 8, 8, tok), axis=0)))
            return tuple(out)

        peaks = lax.fori_loop(
            0, steps, score, tuple(jnp.full((8, tok), MASKED, F32) for _ in range(heads))
        )
        peaks = [jnp.max(peak, axis=0, keepdims=True) for peak in peaks]

        def weigh(i, running):
            rows = pl.ds(pl.multiple_of(i * span, span), span)
            v = v_ref[:, rows]
            out = []
            for h in range(heads):
                total, acc = running[h]
                p = jnp.exp(scores[h, rows, :] - peaks[h])
                total = total + jnp.sum(p.reshape(span // 8, 8, tok), axis=0)
                out.append((total, acc + nn(v, p.astype(BF))))
            return tuple(out)

        result = lax.fori_loop(
            0,
            steps,
            weigh,
            tuple((jnp.zeros((8, tok), F32), jnp.zeros((HD, tok), F32)) for _ in range(heads)),
        )
        rows = []
        for h in range(heads):
            total, acc = result[h]
            total = jnp.sum(total, axis=0, keepdims=True)
            rows.append(acc / total)
            lse_ref[0, h : h + 1, :] = peaks[h] + jnp.log(total)
        full = jnp.concatenate(rows, axis=0).T
        full_ref[...] = full
        attn_ref[...] = full.astype(BF)
        slot_attn_ref[...] = full.astype(BF)

    return pl.pallas_call(
        kernel,
        grid_spec=pltpu.PrefetchScalarGridSpec(
            num_scalar_prefetch=1,
            grid=(count,),
            in_specs=[
                pl.BlockSpec((1, tok), lambda j, slot: (0, first + j)),
                pl.BlockSpec((tok, width), lambda j, slot: (first + j, 0)),
                pl.BlockSpec((seq, width), lambda j, slot: (0, 0)),
                pl.BlockSpec((HD, seq), lambda j, slot: (0, 0)),
            ]
            + [pl.BlockSpec(memory_space=pltpu.HBM)] * len(before),
            out_specs=[
                pl.BlockSpec((tok, width), lambda j, slot: (first + j, 0)),
                pl.BlockSpec((tok, width), lambda j, slot: (slot[first + j], 0)),
                pl.BlockSpec((tok, width), lambda j, slot: (first + j, 0)),
                pl.BlockSpec((1, heads, tok), lambda j, slot: (first + j, 0, 0)),
            ],
            scratch_shapes=[pltpu.VMEM((heads, seq, tok), F32)],
        ),
        out_shape=[
            jax.ShapeDtypeStruct((seq, width), BF),
            jax.ShapeDtypeStruct((seq, width), BF),
            jax.ShapeDtypeStruct((seq, width), F32),
            jax.ShapeDtypeStruct((blocks, heads, tok), F32),
        ],
        input_output_aliases={5 + i: i for i in range(len(before))},
        compiler_params=pltpu.CompilerParams(vmem_limit_bytes=VMEM_LIMIT),
        cost_estimate=LONG,
        name="attend_forward",
    )(slot_of, starts, queries, keys, values_t, *before)


def attend_backward(
    slot_of, starts, queries, keys, keys_t, values, grads, full, lse, cosine, sine, unsplit, heads, tok
):
    seq, width = queries.shape
    blocks = seq // tok
    span = 2 * tok
    half = width // 2

    def kernel(
        slot_ref, start_ref, q_ref, k_ref, kt_ref, v_ref, g_ref, full_ref, lse_ref, cos_ref, sin_ref, unsplit_ref,
        out_ref, dk, dv,
    ):
        block = pl.program_id(0)
        steps = (block + 2) // 2

        @pl.when(block == 0)
        def _():
            dk[...] = jnp.zeros_like(dk)
            dv[...] = jnp.zeros_like(dv)

        start = start_ref[...]
        here = block * tok + lax.broadcasted_iota(jnp.int32, (1, tok), 1)
        head_of = lane_heads(tok, width)
        wide = lax.broadcasted_iota(jnp.int32, (tok, width), 1) // HD
        q = q_ref[...]
        g = g_ref[...]
        q_heads = [jnp.where(head_of == h, q, jnp.zeros_like(q)) for h in range(heads)]
        g_heads = [jnp.where(wide == h, g, jnp.zeros_like(g)) for h in range(heads)]
        q_stack = jnp.concatenate(q_heads, axis=0)
        g_stack = jnp.concatenate(g_heads, axis=0)
        picks = (
            lax.broadcasted_iota(jnp.int32, (8, width), 1) // HD
            == lax.broadcasted_iota(jnp.int32, (8, width), 0)
        ).astype(F32)
        deltas = lax.dot_general(
            picks,
            g.astype(F32) * full_ref[...],
            (((1,), (1,)), ((), ())),
            preferred_element_type=F32,
            precision=lax.Precision.HIGHEST,
        )

        def step(i, dq):
            rows = pl.ds(pl.multiple_of(i * span, span), span)
            k = k_ref[rows, :]
            v = v_ref[rows, :]
            kt = kt_ref[:, rows]
            there = i * span + lax.broadcasted_iota(jnp.int32, (span, tok), 0)
            visible = (there >= start) & (there <= here)
            probs, grad_scores, out = [], [], []
            for h in range(heads):
                s = jnp.where(visible, nt(k, q_heads[h]), MASKED)
                p = jnp.exp(s - lse_ref[0, h : h + 1, :])
                ds = (p * (nt(v, g_heads[h]) - deltas[h : h + 1, :])).astype(BF)
                probs.append(p.astype(BF))
                grad_scores.append(ds)
                out.append(dq[h] + nn(kt, ds))
            dv[rows, :] += nn(jnp.concatenate(probs, axis=1), g_stack)
            dk[rows, :] += nn(jnp.concatenate(grad_scores, axis=1), q_stack)
            return tuple(out)

        dq = lax.fori_loop(
            0, steps, step, tuple(jnp.zeros((HD, tok), F32) for _ in range(heads))
        )
        dq = jnp.concatenate([x[:HALF] for x in dq] + [x[HALF:] for x in dq], axis=0).T
        here_rows = pl.ds(pl.multiple_of(block * tok, tok), tok)
        cos, sin = turn_tables(cos_ref[here_rows, :], sin_ref[here_rows, :], width)
        dq = (dq * cos - swap_halves(dq) * sin) * (HD**-0.5)
        slot_rows = pl.ds(pl.multiple_of(slot_ref[block] * tok, tok), tok)
        out_ref[slot_rows, :width] = nn(dq.astype(BF), unsplit_ref[...]).astype(BF)

        @pl.when(block == blocks - 1)
        def _():
            lane = lax.broadcasted_iota(jnp.int32, (width, 128), 0)
            column = lax.broadcasted_iota(jnp.int32, (width, 128), 1)
            fold_k = ((lane // half) * HALF + lane % HALF == column).astype(BF)
            fold_v = (lane % HD + HD == column).astype(BF)

            def fold(i, unused):
                rows = pl.ds(pl.multiple_of(i * tok, tok), tok)
                cos, sin = turn_tables(cos_ref[rows, :], sin_ref[rows, :], width)
                a = dk[rows, :]
                a = a * cos - swap_halves(a) * sin
                b = dv[rows, :]
                a_high = a.astype(BF)
                b_high = b.astype(BF)
                terms = (
                    nn(a_high, fold_k)
                    + nn((a - a_high.astype(F32)).astype(BF), fold_k)
                    + nn(b_high, fold_v)
                    + nn((b - b_high.astype(F32)).astype(BF), fold_v)
                )
                slot_rows = pl.ds(pl.multiple_of(slot_ref[i] * tok, tok), tok)
                out_ref[slot_rows, width:] = terms.astype(BF)
                return unused

            lax.fori_loop(0, blocks, fold, 0)

    whole = lambda shape: pl.BlockSpec(shape, lambda j, *_: (0, 0))
    return pl.pallas_call(
        kernel,
        grid_spec=pltpu.PrefetchScalarGridSpec(
            num_scalar_prefetch=1,
            grid=(blocks,),
            in_specs=[
                pl.BlockSpec((1, tok), lambda j, *_: (0, j)),
                pl.BlockSpec((tok, width), lambda j, *_: (j, 0)),
                whole((seq, width)),
                whole((HD, seq)),
                whole((seq, width)),
                pl.BlockSpec((tok, width), lambda j, *_: (j, 0)),
                pl.BlockSpec((tok, width), lambda j, *_: (j, 0)),
                pl.BlockSpec((1, heads, tok), lambda j, *_: (j, 0, 0)),
                whole((seq, 128)),
                whole((seq, 128)),
                whole((width, width)),
            ],
            out_specs=whole((seq, width + 128)),
            scratch_shapes=[pltpu.VMEM((seq, width), F32), pltpu.VMEM((seq, width), F32)],
        ),
        out_shape=jax.ShapeDtypeStruct((seq, width + 128), BF),
        compiler_params=pltpu.CompilerParams(vmem_limit_bytes=VMEM_LIMIT),
        cost_estimate=MEDIUM,
        name="attend_backward",
    )(slot_of, starts, queries, keys, keys_t, values, grads, full, lse, cosine, sine, unsplit)


def outer_rows(activations, gradients):
    return lax.dot_general(
        activations, gradients, (((0,), (0,)), ((), ())), preferred_element_type=F32
    ).astype(BF)


def split_source(width):
    lane = np.arange(width)
    half = lane // (width // 2)
    head = (lane % (width // 2)) // HALF
    return head * HD + half * HALF + lane % HALF


def spread_matrix(width):
    matrix = np.zeros((width + 2 * HD, width + 256), np.float32)
    lane = np.arange(width)
    matrix[split_source(width), lane] = 1
    lane = np.arange(2 * HD)
    matrix[width + lane, width + lane] = 1
    lane = np.arange(HD)
    matrix[width + (lane + HALF) % HD, width + 128 + lane] = 1
    return jnp.asarray(matrix, BF)


def widen_matrix(width):
    matrix = np.zeros((2 * HD, 2 * width), np.float32)
    lane = np.arange(width)
    matrix[(lane // (width // 2)) * HALF + lane % HALF, lane] = 1
    matrix[HD + lane % HD, width + lane] = 1
    return jnp.asarray(matrix, BF)


def unsplit_matrix(width):
    matrix = np.zeros((width, width), np.float32)
    matrix[np.arange(width), split_source(width)] = 1
    return jnp.asarray(matrix, BF)


def on_device(
    block_in,
    gain_attn,
    qkv_weight,
    out_weight,
    gain_ffn,
    gate_up_weight,
    down_weight,
    doc_lengths,
    out_grad,
):
    n_ctx = lax.axis_size("ctx")
    n_dp = lax.axis_size("dp")
    me = lax.axis_index("ctx")
    tok = block_in.shape[0]
    seq = tok * n_ctx
    heads = H // n_ctx
    width = heads * HD
    sharers = n_ctx // KVH
    rows = qkv_weight.shape[0]
    ff_rows = down_weight.shape[0]
    ff = ff_rows * n_dp
    columns = width + 2 * HD

    order = me ^ jnp.where(me % 2 == 0, *[jnp.asarray(t) for t in slot_table(n_ctx)])
    slots = jnp.arange(n_ctx, dtype=jnp.int32)
    slot_of = jnp.sum(jnp.where(order[None, :] == slots[:, None], slots[None, :], 0), axis=1)
    index = jnp.arange(seq, dtype=jnp.int32)
    lengths = doc_lengths[0]
    ends = jnp.cumsum(lengths)
    starts = jnp.sum((index[:, None] >= ends[None, :]).astype(jnp.int32) * lengths[None, :], axis=1)
    lane = jnp.arange(128, dtype=F32) % HALF
    frequency = 10000.0 ** (-lane * 2.0 / HD)
    angles = (index - starts).astype(F32)[:, None] * frequency[None, :]
    cosine = jnp.cos(angles)
    sine = jnp.sin(angles)
    starts_row = starts[None, :]

    gain_one = gain_attn.astype(F32)[:, None]
    gain_two = gain_ffn.astype(F32)[:, None]
    qkv = (qkv_weight.astype(F32) * gain_one).astype(BF)
    q_cols = qkv[:, : H * HD].reshape(rows, n_ctx, width).transpose(1, 0, 2)
    k_cols = qkv[:, H * HD : (H + KVH) * HD].reshape(rows, KVH, HD).transpose(1, 0, 2)
    v_cols = qkv[:, (H + KVH) * HD :].reshape(rows, KVH, HD).transpose(1, 0, 2)
    kv_cols = jnp.repeat(jnp.concatenate([k_cols, v_cols], axis=2), sharers, axis=0)
    owner_pairs = [(b, b % n_dp * n_ctx + b // n_dp) for b in range(n_dp * n_ctx)]
    out_own = lax.ppermute(out_weight, ("dp", "ctx"), owner_pairs)
    out_part = gather_dp(out_own)
    qkv_own = exchange(after(jnp.concatenate([q_cols, kv_cols], axis=2), out_own)).reshape(
        n_ctx * rows, columns
    )
    qkv_part = gather_dp(qkv_own)

    hidden_in = block_in.astype(F32)
    rms_one = lax.rsqrt(jnp.mean(hidden_in * hidden_in, axis=-1, keepdims=True) + EPS)
    one_pieces = gather_slots(after((hidden_in * rms_one).astype(BF), qkv_own), n_ctx)

    gate_up_cols = split_columns(
        gate_up_weight, after(gain_two, cosine, sine), n_ctx, n_dp, ff_rows
    )
    gate_up_own = exchange(after(gate_up_cols, *one_pieces[: n_ctx // 2])).reshape(
        n_ctx * rows, 2 * ff
    )
    gate_up_part = gather_dp(gate_up_own)
    down_part = gather_dp(after(down_weight, gate_up_own))

    queries, keys, values, keys_t, values_t, all_one = project_qkv(
        order, one_pieces, qkv_part, spread_matrix(width), widen_matrix(width), cosine, sine, width, tok
    )
    out_pieces = gather_slots(out_part, n_ctx)
    attn, slot_attn, attended, lse = attend_forward(
        slot_of, starts_row, after(queries, gate_up_own), keys, values_t, heads, tok, 0, n_ctx, ()
    )
    attn_tokens = exchange(attn.reshape(n_ctx, tok, width))
    state, norm_two = project_out(order, attn_tokens, out_pieces, block_in)

    two_pieces = gather_slots(norm_two, n_ctx)
    grad_direct = gather_direct(after(out_grad, *two_pieces), n_ctx)
    hidden, factors, all_two = feed_forward(two_pieces, gate_up_part)
    grad_pieces = gather_rest(grad_direct, n_ctx, (hidden,))
    all_grad = lay_out(grad_pieces)
    down_terms = outer_rows(hidden, all_grad)
    down_sums = scatter_dp(down_terms)
    grad_gate_up = feed_backward(after(factors, down_terms), all_grad, down_part)

    def rows_of(x, lo, hi):
        return lax.slice_in_dim(x, lo * tok, hi * tok, axis=0)

    d_pairs, _ = scatter_pairs(
        lambda lo, hi: nt(rows_of(grad_gate_up, lo, hi), gate_up_part), tok, n_ctx
    )
    stages = tuple(reversed(range(len(walk(n_ctx, 0)))))
    d_two = scatter_chips(*d_pairs, stages, n_ctx)
    hidden_pairs, _ = scatter_pairs(
        lambda lo, hi: nn(rows_of(after(hidden, *d_pairs), lo, hi), down_part), tok, n_ctx
    )
    gate_up_terms = outer_rows(after(all_two, *d_pairs), grad_gate_up)
    gate_up_sums = scatter_dp(gate_up_terms)

    grad_state, grad_branch, grad_heads = branch_back(
        order, after(d_two, gate_up_terms, *hidden_pairs), state, out_grad, out_pieces
    )
    grad_attn = exchange(grad_heads).reshape(seq, width)
    branch_here, branch_there = gather_at_once(after(grad_branch, grad_attn), n_ctx)
    hidden_upper, hidden_lower = hidden_pairs
    hidden_arrived = swap_stage(after(hidden_upper.astype(BF), grad_attn), n_ctx, stages[0])
    grad_mixed = attend_backward(
        slot_of,
        starts_row,
        queries,
        keys,
        keys_t,
        values,
        grad_attn,
        attended,
        lse,
        cosine,
        sine,
        unsplit_matrix(width),
        heads,
        tok,
    )
    qkv_terms = outer_rows(all_one, grad_mixed)
    qkv_sums = scatter_dp(after(qkv_terms, gate_up_sums))
    one_pairs, _ = scatter_pairs(
        lambda lo, hi: nt(
            rows_of(after(grad_mixed, qkv_terms, hidden_arrived, *branch_here), lo, hi), qkv_part
        ),
        tok,
        n_ctx,
    )
    d_one = scatter_chips(*one_pairs, stages, n_ctx)
    hidden_sums = scatter_rest(hidden_lower, hidden_arrived, stages, n_ctx)
    block_out = (state + hidden_sums).astype(BF)
    out_terms = outer_rows(slot_attn, after(lay_out(branch_here + branch_there), qkv_terms))
    out_sums = scatter_dp(after(out_terms, qkv_sums))
    norm_one = hidden_in * rms_one
    input_grad = grad_state + rms_one * (
        d_one - norm_one * jnp.mean(d_one * norm_one, axis=-1, keepdims=True)
    )

    down_weight_grad = after(down_sums, grad_mixed).astype(F32)
    out_weight_grad = lax.ppermute(
        out_sums, ("dp", "ctx"), [(b, a) for a, b in owner_pairs]
    ).astype(F32)
    gate_up_weight_grad, gain_ffn_grad = join_columns(
        exchange(after(gate_up_sums, grad_mixed).reshape(n_ctx, rows, 2 * ff)), gate_up_weight, gain_two, n_dp, ff_rows
    )
    qkv_back = exchange(qkv_sums.reshape(n_ctx, rows, columns)).astype(F32)
    q_back = qkv_back[:, :, :width].transpose(1, 0, 2).reshape(rows, H * HD)
    kv_back = jnp.sum(qkv_back[:, :, width:].reshape(KVH, sharers, rows, 2 * HD), axis=1)
    k_back = kv_back[:, :, :HD].transpose(1, 0, 2).reshape(rows, KVH * HD)
    v_back = kv_back[:, :, HD:].transpose(1, 0, 2).reshape(rows, KVH * HD)
    qkv_back = jnp.concatenate([q_back, k_back, v_back], axis=1)
    qkv_weight_grad = qkv_back * gain_one
    gain_attn_grad = jnp.sum(qkv_back * qkv_weight.astype(F32), axis=1)
    return (
        block_out,
        input_grad,
        gain_attn_grad,
        qkv_weight_grad,
        out_weight_grad,
        gain_ffn_grad[:, 0],
        gate_up_weight_grad,
        down_weight_grad,
    )


def solution(mesh):
    rows = P(("dp", "ctx"), None)
    entries = P(("dp", "ctx"))
    return jax.shard_map(
        on_device,
        mesh=mesh,
        in_specs=(rows, entries, rows, rows, entries, rows, rows, P("dp", None), rows),
        out_specs=(rows, rows, entries, rows, rows, entries, rows, rows),
        check_vma=False,
    )
```

```python
import jax
import jax.numpy as jnp
import numpy as np
from jax import lax
from jax.experimental import pallas as pl
from jax.experimental.pallas import tpu as pltpu
from jax.sharding import PartitionSpec as P

D = 2048
H = 32
KVH = 4
HD = 64
FF = 5632
HALF = HD // 2

EPS = 1e-05
MASKED = -1e30
BF = jnp.bfloat16
F32 = jnp.float32
VMEM_LIMIT = 60 << 20
SHORT = pl.CostEstimate(flops=1 << 20, bytes_accessed=1 << 20, transcendentals=0)
MEDIUM = pl.CostEstimate(flops=2 * 10**10, bytes_accessed=1 << 20, transcendentals=0)
LONG = pl.CostEstimate(flops=10**11, bytes_accessed=1 << 20, transcendentals=0)


def nt(a, b):
    return lax.dot_general(a, b, (((1,), (1,)), ((), ())), preferred_element_type=F32)


def nn(a, b):
    return jnp.dot(a, b, preferred_element_type=F32)


def after(x, *earlier):
    return lax.optimization_barrier((x, *earlier))[0]


def after_each(values, *earlier):
    count = len(values)
    return lax.optimization_barrier((*values, *earlier))[:count]


def walk(n_ctx, parity):
    bits = []
    bit = 2
    while bit < n_ctx:
        bits.append(bit)
        bit *= 2
    return bits if parity == 0 else bits[::-1]


def swap_stage(x, n_ctx, stage):
    pairs = [(c, c ^ walk(n_ctx, c % 2)[stage]) for c in range(n_ctx)]
    return lax.ppermute(x, "ctx", pairs)


def swap_core(x, n_ctx):
    return lax.ppermute(x, "ctx", [(c, c ^ 1) for c in range(n_ctx)])


def slot_table(n_ctx):
    lists = []
    for parity in (0, 1):
        row = [0]
        for bit in walk(n_ctx, parity):
            row = row + [v ^ bit for v in row]
        lists.append(row)
    return np.array(
        [lists[p] + [v ^ 1 for v in lists[1 - p]] for p in (0, 1)], dtype=np.int32
    )


def gather_direct(x, n_ctx):
    return [x] + [swap_stage(x, n_ctx, stage) for stage in range(len(walk(n_ctx, 0)))]


def gather_rest(direct, n_ctx, earlier=(), last=()):
    have = direct[:1]
    for stage in range(len(walk(n_ctx, 0))):
        passed = [after(block, *earlier) if earlier else block for block in have[1:]]
        have = have + [direct[stage + 1]] + [swap_stage(block, n_ctx, stage) for block in passed]
    return have + [swap_core(after(block, *last) if last else block, n_ctx) for block in have]


def gather_at_once(x, n_ctx):
    have = [x]
    table = slot_table(n_ctx)
    for slot in range(1, n_ctx // 2):
        pairs = [(c, c ^ int(table[c % 2][slot])) for c in range(n_ctx)]
        have.append(lax.ppermute(x, "ctx", pairs))
    return have, [swap_core(block, n_ctx) for block in have]


def gather_slots(x, n_ctx):
    return gather_rest(gather_direct(x, n_ctx), n_ctx)


def scatter_pairs(term, tok, n_ctx):
    mine = n_ctx // 2
    cut = mine // 2
    sums, arrivals = [], []
    for lo, hi in ((cut, mine), (0, cut)):
        arrivals.append(swap_core(term(mine + lo, mine + hi).astype(BF), n_ctx))
        sums.append(term(lo, hi) + arrivals[-1].astype(F32))
    return sums, arrivals


def scatter_chips(upper, lower, stages, n_ctx, *earlier):
    for stage in stages:
        if earlier and stage == 0:
            upper = after(upper.astype(BF), *earlier)
        lower = lower + swap_stage(upper.astype(BF), n_ctx, stage).astype(F32)
        if stage:
            half = lower.shape[0] // 2
            upper, lower = lower[half:], lower[:half]
    return lower if stages[-1] == 0 else (upper, lower)


def scatter_rest(lower, arrived, stages, n_ctx):
    sums = lower + arrived.astype(F32)
    if len(stages) == 1:
        return sums
    half = sums.shape[0] // 2
    return scatter_chips(sums[half:], sums[:half], stages[1:], n_ctx)


def exchange(x):
    return lax.all_to_all(x, "ctx", split_axis=0, concat_axis=0, tiled=False)


def gather_dp(x):
    return lax.all_gather(x, "dp", axis=0, tiled=True)


def scatter_dp(x):
    return lax.psum_scatter(x, "dp", scatter_dimension=0, tiled=True)


def fetch_piece(pieces, buffer, semaphores, count=1):
    step = pl.program_id(0)

    @pl.when(step == 0)
    def _():
        for i, piece in enumerate(pieces):
            pltpu.make_async_copy(piece, buffer.at[i], semaphores.at[i]).start()

    for i in range(count):
        at = step * count + i
        pltpu.make_async_copy(pieces[0], buffer.at[at], semaphores.at[at]).wait()
    if count == 1:
        return buffer[step]
    return buffer[pl.ds(step * count, count)].reshape(count * buffer.shape[1], buffer.shape[2])


def keep_pieces(buffer, target, semaphores, count=1):
    step = pl.program_id(0)
    total, tok = buffer.shape[0], buffer.shape[1]

    def copy(at):
        rows = pl.ds(pl.multiple_of(at * tok, tok), tok)
        return pltpu.make_async_copy(buffer.at[at], target.at[rows], semaphores.at[at])

    for i in range(count):
        copy(step * count + i).start()

    @pl.when(step == total // count - 1)
    def _():
        for i in range(total):
            copy(i).wait()


def store_rows(source, target, semaphores):
    count = semaphores.shape[0]
    rows = source.shape[0] // count
    copies = [
        pltpu.make_async_copy(
            source.at[pl.ds(i * rows, rows)], target.at[pl.ds(i * rows, rows)], semaphores.at[i]
        )
        for i in range(count)
    ]
    for copy in copies:
        copy.start()
    return copies


def chunks(rows):
    return next(count for count in (8, 4, 2, 1) if rows % (16 * count) == 0)


def fetch_rows(source, buffer, semaphores):
    count = semaphores.shape[0]
    rows = source.shape[0] // count

    @pl.when(pl.program_id(0) == 0)
    def _():
        copies = [
            pltpu.make_async_copy(
                source.at[pl.ds(i * rows, rows)], buffer.at[pl.ds(i * rows, rows)], semaphores.at[i]
            )
            for i in range(count)
        ]
        for copy in copies:
            copy.start()
        for copy in copies:
            copy.wait()


def swap_halves(x):
    return pltpu.roll(x, x.shape[1] // 2, axis=1)


def turn_tables(cosine, sine, width):
    times = width // 128
    cosine = jnp.concatenate([cosine] * times, axis=1) if times > 1 else cosine
    sine = jnp.concatenate([sine] * times, axis=1) if times > 1 else sine
    lane = lax.broadcasted_iota(jnp.int32, sine.shape, 1)
    return cosine, jnp.where(lane < width // 2, -sine, sine)


def any_specs(pieces):
    return [pl.BlockSpec(memory_space=pltpu.HBM) for _ in pieces]


def project_qkv(order, pieces, weight, spread, widen, cosine, sine, width, tok):
    n = len(pieces)
    seq = n * tok

    def kernel(order_ref, *refs):
        parts = refs[:n]
        w_hbm, spread_ref, widen_ref, cos_ref, sin_ref = refs[n : n + 5]
        (
            q_ref, k_ref, v_ref, kt_ref, vt_ref, all_hbm, wide, buffer, semaphores, keep_semaphores, w_ref, w_semaphores
        ) = refs[n + 5 :]
        fetch_rows(w_hbm, w_ref, w_semaphores)

        @pl.when(pl.program_id(0) == 0)
        def _():
            wide[...] = nn(w_ref[...], spread_ref[...]).astype(BF)

        x = fetch_piece(parts, buffer, semaphores)
        keep_pieces(buffer, all_hbm, keep_semaphores)
        mixed = nn(x, wide[...])
        cos, sin = turn_tables(cos_ref[...], sin_ref[...], width)
        q = mixed[:, :width]
        q_ref[...] = (q * cos + swap_halves(q) * sin).astype(BF) * (HD**-0.5)
        lane = lax.broadcasted_iota(jnp.int32, (tok, 128), 1)
        key_sine = jnp.where(lane < HALF, -sin_ref[...], sin_ref[...])
        both = jnp.where(
            lane < HD,
            mixed[:, width : width + 128] * cos_ref[...] + mixed[:, width + 128 :] * key_sine,
            mixed[:, width : width + 128],
        ).astype(BF)
        repeated = nn(both, widen_ref[...]).astype(BF)
        k_ref[...] = repeated[:, :width]
        v_ref[...] = repeated[:, width:]
        turned = both.T
        kt_ref[...] = turned[:HD]
        vt_ref[...] = turned[HD:]

    rows = lambda s, order: (order[s], 0)
    lanes = lambda s, order: (0, order[s])
    whole = lambda s, order: (0, 0)
    return pl.pallas_call(
        kernel,
        grid_spec=pltpu.PrefetchScalarGridSpec(
            num_scalar_prefetch=1,
            grid=(n,),
            in_specs=any_specs(pieces)
            + [
                pl.BlockSpec(memory_space=pltpu.HBM),
                pl.BlockSpec(spread.shape, whole),
                pl.BlockSpec(widen.shape, whole),
                pl.BlockSpec((tok, 128), rows),
                pl.BlockSpec((tok, 128), rows),
            ],
            out_specs=[
                pl.BlockSpec((tok, width), rows),
                pl.BlockSpec((tok, width), rows),
                pl.BlockSpec((tok, width), rows),
                pl.BlockSpec((HD, tok), lanes),
                pl.BlockSpec((HD, tok), lanes),
                pl.BlockSpec(memory_space=pltpu.HBM),
            ],
            scratch_shapes=[
                pltpu.VMEM((D, width + 256), BF),
                pltpu.VMEM((n, tok, D), BF),
                pltpu.SemaphoreType.DMA((n,)),
                pltpu.SemaphoreType.DMA((n,)),
                pltpu.VMEM(weight.shape, BF),
                pltpu.SemaphoreType.DMA((chunks(D),)),
            ],
        ),
        out_shape=[
            jax.ShapeDtypeStruct((seq, width), BF),
            jax.ShapeDtypeStruct((seq, width), BF),
            jax.ShapeDtypeStruct((seq, width), BF),
            jax.ShapeDtypeStruct((HD, seq), BF),
            jax.ShapeDtypeStruct((HD, seq), BF),
            jax.ShapeDtypeStruct((seq, D), BF),
        ],
        compiler_params=pltpu.CompilerParams(vmem_limit_bytes=VMEM_LIMIT),
        cost_estimate=LONG,
        name="project_qkv",
    )(order, *pieces, weight, spread, widen, cosine, sine)


def feed_forward(pieces, weight):
    n = len(pieces)
    tok = 2 * pieces[0].shape[0]
    seq = n * tok // 2
    ff = weight.shape[1] // 2

    def kernel(*refs):
        parts = refs[:n]
        w_hbm, hidden_ref, factor_ref, all_hbm, buffer, semaphores, keep_semaphores, w_ref, w_semaphores = refs[n:]
        fetch_rows(w_hbm, w_ref, w_semaphores)
        x = fetch_piece(parts, buffer, semaphores, 2)
        keep_pieces(buffer, all_hbm, keep_semaphores, 2)
        both = nn(x, w_ref[...])
        gate = both[:, :ff]
        up = both[:, ff:]
        sig = jax.nn.sigmoid(gate)
        silu = gate * sig
        hidden_ref[...] = (silu * up).astype(BF)
        factor_ref[:, :ff] = (up * sig * (1.0 + gate * (1.0 - sig))).astype(BF)
        factor_ref[:, ff:] = silu.astype(BF)

    rows = lambda s: (s, 0)
    return pl.pallas_call(
        kernel,
        grid=(n // 2,),
        in_specs=any_specs(pieces) + [pl.BlockSpec(memory_space=pltpu.HBM)],
        out_specs=[
            pl.BlockSpec((tok, ff), rows),
            pl.BlockSpec((tok, 2 * ff), rows),
            pl.BlockSpec(memory_space=pltpu.HBM),
        ],
        scratch_shapes=[
            pltpu.VMEM((n, tok // 2, D), BF),
            pltpu.SemaphoreType.DMA((n,)),
            pltpu.SemaphoreType.DMA((n,)),
            pltpu.VMEM(weight.shape, BF),
            pltpu.SemaphoreType.DMA((chunks(D),)),
        ],
        out_shape=[
            jax.ShapeDtypeStruct((seq, ff), BF),
            jax.ShapeDtypeStruct((seq, 2 * ff), BF),
            jax.ShapeDtypeStruct((seq, D), BF),
        ],
        compiler_params=pltpu.CompilerParams(vmem_limit_bytes=VMEM_LIMIT),
        cost_estimate=LONG,
        name="feed_forward",
    )(*pieces, weight)


def feed_backward(factors, grads, weight):
    seq = factors.shape[0]
    ff = weight.shape[0]
    tok = 512

    def kernel(factor_ref, g_ref, w_hbm, out_ref, w_ref, w_semaphores, turned):
        fetch_rows(w_hbm, w_ref, w_semaphores)

        @pl.when(pl.program_id(0) == 0)
        def _():
            turned[...] = w_ref[...].T

        grad_hidden = nn(g_ref[...], turned[...])
        factor = factor_ref[...].astype(F32)
        out_ref[:, :ff] = (grad_hidden * factor[:, :ff]).astype(BF)
        out_ref[:, ff:] = (grad_hidden * factor[:, ff:]).astype(BF)

    rows = lambda s: (s, 0)
    return pl.pallas_call(
        kernel,
        grid=(seq // tok,),
        in_specs=[
            pl.BlockSpec((tok, 2 * ff), rows),
            pl.BlockSpec((tok, D), rows),
            pl.BlockSpec(memory_space=pltpu.HBM),
        ],
        out_specs=pl.BlockSpec((tok, 2 * ff), rows),
        scratch_shapes=[
            pltpu.VMEM(weight.shape, BF),
            pltpu.SemaphoreType.DMA((chunks(ff),)),
            pltpu.VMEM((D, ff), BF),
        ],
        out_shape=jax.ShapeDtypeStruct((seq, 2 * ff), BF),
        compiler_params=pltpu.CompilerParams(vmem_limit_bytes=VMEM_LIMIT),
        cost_estimate=LONG,
        name="feed_backward",
    )(factors, grads, weight)


def lay_out(pieces):
    n = len(pieces)
    tok = pieces[0].shape[0]

    def kernel(*refs):
        parts = refs[:n]
        out_ref, buffer, in_semaphores, out_semaphores = refs[n:]
        arrive = [
            pltpu.make_async_copy(part, buffer.at[i], in_semaphores.at[i])
            for i, part in enumerate(parts)
        ]
        leave = [
            pltpu.make_async_copy(buffer.at[i], out_ref.at[pl.ds(i * tok, tok)], out_semaphores.at[i])
            for i in range(n)
        ]
        for copy in arrive:
            copy.start()
        for i in range(n):
            arrive[i].wait()
            leave[i].start()
        for copy in leave:
            copy.wait()

    return pl.pallas_call(
        kernel,
        in_specs=any_specs(pieces),
        out_specs=pl.BlockSpec(memory_space=pltpu.HBM),
        scratch_shapes=[
            pltpu.VMEM((n, tok, D), BF),
            pltpu.SemaphoreType.DMA((n,)),
            pltpu.SemaphoreType.DMA((n,)),
        ],
        out_shape=jax.ShapeDtypeStruct((n * tok, D), BF),
        compiler_params=pltpu.CompilerParams(vmem_limit_bytes=VMEM_LIMIT),
        cost_estimate=SHORT,
        name="lay_out",
    )(*pieces)


def branch_back(order, d_two, state, out_grad, pieces):
    n = len(pieces)
    tok = d_two.shape[0]
    width = pieces[0].shape[0]

    def kernel(order_ref, d_ref, state_ref, g_ref, *refs):
        parts = refs[:n]
        grad_hbm, branch_hbm, heads_ref, buffer, semaphores, grad_ref, branch_ref, out_semaphores = refs[n:]

        @pl.when(pl.program_id(0) == 0)
        def _():
            state = state_ref[...]
            scale = lax.rsqrt(jnp.mean(state * state, axis=-1, keepdims=True) + EPS)
            norm = state * scale
            d = d_ref[...]
            grad = g_ref[...].astype(F32) + scale * (
                d - norm * jnp.mean(d * norm, axis=-1, keepdims=True)
            )
            grad_ref[...] = grad
            branch_ref[...] = grad.astype(BF)
            store_rows(grad_ref, grad_hbm, out_semaphores.at[0])
            store_rows(branch_ref, branch_hbm, out_semaphores.at[1])

        w = fetch_piece(parts, buffer, semaphores)
        heads_ref[0] = nt(branch_ref[...], w).astype(BF)

        @pl.when(pl.program_id(0) == n - 1)
        def _():
            for source, target, at in ((grad_ref, grad_hbm, 0), (branch_ref, branch_hbm, 1)):
                rows = tok // 4
                for i in range(4):
                    cut = pl.ds(i * rows, rows)
                    pltpu.make_async_copy(source.at[cut], target.at[cut], out_semaphores.at[at, i]).wait()

    whole = lambda s, order: (0, 0)
    return pl.pallas_call(
        kernel,
        grid_spec=pltpu.PrefetchScalarGridSpec(
            num_scalar_prefetch=1,
            grid=(n,),
            in_specs=[
                pl.BlockSpec((tok, D), whole),
                pl.BlockSpec((tok, D), whole),
                pl.BlockSpec((tok, D), whole),
            ]
            + any_specs(pieces),
            out_specs=[
                pl.BlockSpec(memory_space=pltpu.HBM),
                pl.BlockSpec(memory_space=pltpu.HBM),
                pl.BlockSpec((1, tok, width), lambda s, order: (order[s], 0, 0)),
            ],
            scratch_shapes=[
                pltpu.VMEM((n, width, D), BF),
                pltpu.SemaphoreType.DMA((n,)),
                pltpu.VMEM((tok, D), F32),
                pltpu.VMEM((tok, D), BF),
                pltpu.SemaphoreType.DMA((2, 4)),
            ],
        ),
        out_shape=[
            jax.ShapeDtypeStruct((tok, D), F32),
            jax.ShapeDtypeStruct((tok, D), BF),
            jax.ShapeDtypeStruct((n, tok, width), BF),
        ],
        compiler_params=pltpu.CompilerParams(vmem_limit_bytes=VMEM_LIMIT),
        cost_estimate=SHORT,
        name="branch_back",
    )(order, d_two, state, out_grad, *pieces)


def split_columns(weight, gain, n_ctx, n_dp, ff_rows):
    rows = weight.shape[0]
    ff = ff_rows * n_dp

    def kernel(w_ref, gain_ref, out_ref):
        gains = gain_ref[...]
        for part in range(2):
            for d in range(n_dp):
                for c in range(n_ctx):
                    at = part * FF + (d * n_ctx + c) * ff_rows
                    to = part * ff + d * ff_rows
                    values = w_ref[:, at : at + ff_rows].astype(F32) * gains
                    out_ref[c, :, to : to + ff_rows] = values.astype(BF)

    return pl.pallas_call(
        kernel,
        in_specs=[pl.BlockSpec(memory_space=pltpu.VMEM)] * 2,
        out_specs=pl.BlockSpec(memory_space=pltpu.VMEM),
        out_shape=jax.ShapeDtypeStruct((n_ctx, rows, 2 * ff), BF),
        compiler_params=pltpu.CompilerParams(vmem_limit_bytes=VMEM_LIMIT),
        cost_estimate=LONG,
        name="split_columns",
    )(weight, gain)


def join_columns(sums, weight, gain, n_dp, ff_rows):
    n_ctx, rows, both = sums.shape
    ff = both // 2

    def kernel(s_ref, w_ref, gain_ref, out_ref, gain_out_ref):
        gains = gain_ref[...]
        total = jnp.zeros((rows, ff_rows), F32)
        for part in range(2):
            for d in range(n_dp):
                for c in range(n_ctx):
                    at = part * ff + d * ff_rows
                    to = part * FF + (d * n_ctx + c) * ff_rows
                    values = s_ref[c, :, at : at + ff_rows].astype(F32)
                    total = total + values * w_ref[:, to : to + ff_rows].astype(F32)
                    out_ref[:, to : to + ff_rows] = values * gains
        gain_out_ref[...] = jnp.sum(total, axis=1, keepdims=True)

    return pl.pallas_call(
        kernel,
        in_specs=[pl.BlockSpec(memory_space=pltpu.VMEM)] * 3,
        out_specs=[pl.BlockSpec(memory_space=pltpu.VMEM)] * 2,
        out_shape=[
            jax.ShapeDtypeStruct((rows, 2 * FF), F32),
            jax.ShapeDtypeStruct((rows, 1), F32),
        ],
        compiler_params=pltpu.CompilerParams(vmem_limit_bytes=VMEM_LIMIT),
        cost_estimate=LONG,
        name="join_columns",
    )(sums, weight, gain)


def lane_heads(rows, width):
    lane = lax.broadcasted_iota(jnp.int32, (rows, width), 1)
    return (lane % (width // 2)) // HALF


def attend_forward(slot_of, starts, queries, keys, values_t, heads, tok):
    seq, width = queries.shape
    blocks = seq // tok
    span = 2 * tok

    def kernel(slot_ref, start_ref, q_ref, k_ref, v_ref, slot_attn_ref, full_ref, lse_ref, scores):
        block = pl.program_id(0)
        steps = (block + 2) // 2
        start = start_ref[...]
        here = block * tok + lax.broadcasted_iota(jnp.int32, (1, tok), 1)
        head_of = lane_heads(tok, width)
        q = q_ref[...]
        q_heads = [jnp.where(head_of == h, q, jnp.zeros_like(q)) for h in range(heads)]

        def score(i, peaks):
            rows = pl.ds(pl.multiple_of(i * span, span), span)
            k = k_ref[rows, :]
            there = i * span + lax.broadcasted_iota(jnp.int32, (span, tok), 0)
            visible = (there >= start) & (there <= here)
            out = []
            for h in range(heads):
                s = jnp.where(visible, nt(k, q_heads[h]), MASKED)
                scores[h, rows, :] = s
                out.append(jnp.maximum(peaks[h], jnp.max(s.reshape(span // 8, 8, tok), axis=0)))
            return tuple(out)

        peaks = lax.fori_loop(
            0, steps, score, tuple(jnp.full((8, tok), MASKED, F32) for _ in range(heads))
        )
        peaks = [jnp.max(peak, axis=0, keepdims=True) for peak in peaks]

        def weigh(i, running):
            rows = pl.ds(pl.multiple_of(i * span, span), span)
            v = v_ref[:, rows]
            out = []
            for h in range(heads):
                total, acc = running[h]
                p = jnp.exp(scores[h, rows, :] - peaks[h])
                total = total + jnp.sum(p.reshape(span // 8, 8, tok), axis=0)
                out.append((total, acc + nn(v, p.astype(BF))))
            return tuple(out)

        result = lax.fori_loop(
            0,
            steps,
            weigh,
            tuple((jnp.zeros((8, tok), F32), jnp.zeros((HD, tok), F32)) for _ in range(heads)),
        )
        rows = []
        for h in range(heads):
            total, acc = result[h]
            total = jnp.sum(total, axis=0, keepdims=True)
            rows.append(acc / total)
            lse_ref[0, h : h + 1, :] = peaks[h] + jnp.log(total)
        full = jnp.concatenate(rows, axis=0).T
        full_ref[...] = full
        slot_attn_ref[...] = full.astype(BF)

    return pl.pallas_call(
        kernel,
        grid_spec=pltpu.PrefetchScalarGridSpec(
            num_scalar_prefetch=1,
            grid=(blocks,),
            in_specs=[
                pl.BlockSpec((1, tok), lambda j, slot: (0, j)),
                pl.BlockSpec((tok, width), lambda j, slot: (j, 0)),
                pl.BlockSpec((seq, width), lambda j, slot: (0, 0)),
                pl.BlockSpec((HD, seq), lambda j, slot: (0, 0)),
            ],
            out_specs=[
                pl.BlockSpec((tok, width), lambda j, slot: (slot[j], 0)),
                pl.BlockSpec((tok, width), lambda j, slot: (j, 0)),
                pl.BlockSpec((1, heads, tok), lambda j, slot: (j, 0, 0)),
            ],
            scratch_shapes=[pltpu.VMEM((heads, seq, tok), F32)],
        ),
        out_shape=[
            jax.ShapeDtypeStruct((seq, width), BF),
            jax.ShapeDtypeStruct((seq, width), F32),
            jax.ShapeDtypeStruct((blocks, heads, tok), F32),
        ],
        compiler_params=pltpu.CompilerParams(vmem_limit_bytes=VMEM_LIMIT),
        cost_estimate=SHORT,
        name="attend_forward",
    )(slot_of, starts, queries, keys, values_t)


def attend_backward(
    slot_of, starts, queries, keys, keys_t, values, grads, full, lse, cosine, sine, unsplit, heads, tok
):
    seq, width = queries.shape
    blocks = seq // tok
    span = 2 * tok
    half = width // 2

    def kernel(
        slot_ref, start_ref, q_ref, k_ref, kt_ref, v_ref, g_ref, full_ref, lse_ref, cos_ref, sin_ref, unsplit_ref,
        out_ref, dk, dv,
    ):
        block = pl.program_id(0)
        steps = (block + 2) // 2

        @pl.when(block == 0)
        def _():
            dk[...] = jnp.zeros_like(dk)
            dv[...] = jnp.zeros_like(dv)

        start = start_ref[...]
        here = block * tok + lax.broadcasted_iota(jnp.int32, (1, tok), 1)
        head_of = lane_heads(tok, width)
        wide = lax.broadcasted_iota(jnp.int32, (tok, width), 1) // HD
        q = q_ref[...]
        g = g_ref[...]
        q_heads = [jnp.where(head_of == h, q, jnp.zeros_like(q)) for h in range(heads)]
        g_heads = [jnp.where(wide == h, g, jnp.zeros_like(g)) for h in range(heads)]
        q_stack = jnp.concatenate(q_heads, axis=0)
        g_stack = jnp.concatenate(g_heads, axis=0)
        picks = (
            lax.broadcasted_iota(jnp.int32, (8, width), 1) // HD
            == lax.broadcasted_iota(jnp.int32, (8, width), 0)
        ).astype(F32)
        deltas = lax.dot_general(
            picks,
            g.astype(F32) * full_ref[...],
            (((1,), (1,)), ((), ())),
            preferred_element_type=F32,
            precision=lax.Precision.HIGHEST,
        )

        def step(i, dq):
            rows = pl.ds(pl.multiple_of(i * span, span), span)
            k = k_ref[rows, :]
            v = v_ref[rows, :]
            kt = kt_ref[:, rows]
            there = i * span + lax.broadcasted_iota(jnp.int32, (span, tok), 0)
            visible = (there >= start) & (there <= here)
            probs, grad_scores, out = [], [], []
            for h in range(heads):
                s = jnp.where(visible, nt(k, q_heads[h]), MASKED)
                p = jnp.exp(s - lse_ref[0, h : h + 1, :])
                ds = (p * (nt(v, g_heads[h]) - deltas[h : h + 1, :])).astype(BF)
                probs.append(p.astype(BF))
                grad_scores.append(ds)
                out.append(dq[h] + nn(kt, ds))
            dv[rows, :] += nn(jnp.concatenate(probs, axis=1), g_stack)
            dk[rows, :] += nn(jnp.concatenate(grad_scores, axis=1), q_stack)
            return tuple(out)

        dq = lax.fori_loop(
            0, steps, step, tuple(jnp.zeros((HD, tok), F32) for _ in range(heads))
        )
        dq = jnp.concatenate([x[:HALF] for x in dq] + [x[HALF:] for x in dq], axis=0).T
        here_rows = pl.ds(pl.multiple_of(block * tok, tok), tok)
        cos, sin = turn_tables(cos_ref[here_rows, :], sin_ref[here_rows, :], width)
        dq = (dq * cos - swap_halves(dq) * sin) * (HD**-0.5)
        slot_rows = pl.ds(pl.multiple_of(slot_ref[block] * tok, tok), tok)
        out_ref[slot_rows, :width] = nn(dq.astype(BF), unsplit_ref[...]).astype(BF)

        @pl.when(block == blocks - 1)
        def _():
            lane = lax.broadcasted_iota(jnp.int32, (width, 128), 0)
            column = lax.broadcasted_iota(jnp.int32, (width, 128), 1)
            fold_k = ((lane // half) * HALF + lane % HALF == column).astype(BF)
            fold_v = (lane % HD + HD == column).astype(BF)

            def fold(i, unused):
                rows = pl.ds(pl.multiple_of(i * tok, tok), tok)
                cos, sin = turn_tables(cos_ref[rows, :], sin_ref[rows, :], width)
                a = dk[rows, :]
                a = a * cos - swap_halves(a) * sin
                b = dv[rows, :]
                a_high = a.astype(BF)
                b_high = b.astype(BF)
                terms = (
                    nn(a_high, fold_k)
                    + nn((a - a_high.astype(F32)).astype(BF), fold_k)
                    + nn(b_high, fold_v)
                    + nn((b - b_high.astype(F32)).astype(BF), fold_v)
                )
                slot_rows = pl.ds(pl.multiple_of(slot_ref[i] * tok, tok), tok)
                out_ref[slot_rows, width:] = terms.astype(BF)
                return unused

            lax.fori_loop(0, blocks, fold, 0)

    whole = lambda shape: pl.BlockSpec(shape, lambda j, *_: (0, 0))
    return pl.pallas_call(
        kernel,
        grid_spec=pltpu.PrefetchScalarGridSpec(
            num_scalar_prefetch=1,
            grid=(blocks,),
            in_specs=[
                pl.BlockSpec((1, tok), lambda j, *_: (0, j)),
                pl.BlockSpec((tok, width), lambda j, *_: (j, 0)),
                whole((seq, width)),
                whole((HD, seq)),
                whole((seq, width)),
                pl.BlockSpec((tok, width), lambda j, *_: (j, 0)),
                pl.BlockSpec((tok, width), lambda j, *_: (j, 0)),
                pl.BlockSpec((1, heads, tok), lambda j, *_: (j, 0, 0)),
                whole((seq, 128)),
                whole((seq, 128)),
                whole((width, width)),
            ],
            out_specs=whole((seq, width + 128)),
            scratch_shapes=[pltpu.VMEM((seq, width), F32), pltpu.VMEM((seq, width), F32)],
        ),
        out_shape=jax.ShapeDtypeStruct((seq, width + 128), BF),
        compiler_params=pltpu.CompilerParams(vmem_limit_bytes=VMEM_LIMIT),
        cost_estimate=MEDIUM,
        name="attend_backward",
    )(slot_of, starts, queries, keys, keys_t, values, grads, full, lse, cosine, sine, unsplit)


def outer_rows(activations, gradients):
    return lax.dot_general(
        activations, gradients, (((0,), (0,)), ((), ())), preferred_element_type=F32
    ).astype(BF)


def split_source(width):
    lane = np.arange(width)
    half = lane // (width // 2)
    head = (lane % (width // 2)) // HALF
    return head * HD + half * HALF + lane % HALF


def spread_matrix(width):
    matrix = np.zeros((width + 2 * HD, width + 256), np.float32)
    lane = np.arange(width)
    matrix[split_source(width), lane] = 1
    lane = np.arange(2 * HD)
    matrix[width + lane, width + lane] = 1
    lane = np.arange(HD)
    matrix[width + (lane + HALF) % HD, width + 128 + lane] = 1
    return jnp.asarray(matrix, BF)


def widen_matrix(width):
    matrix = np.zeros((2 * HD, 2 * width), np.float32)
    lane = np.arange(width)
    matrix[(lane // (width // 2)) * HALF + lane % HALF, lane] = 1
    matrix[HD + lane % HD, width + lane] = 1
    return jnp.asarray(matrix, BF)


def unsplit_matrix(width):
    matrix = np.zeros((width, width), np.float32)
    matrix[np.arange(width), split_source(width)] = 1
    return jnp.asarray(matrix, BF)


def on_device(
    block_in,
    gain_attn,
    qkv_weight,
    out_weight,
    gain_ffn,
    gate_up_weight,
    down_weight,
    doc_lengths,
    out_grad,
):
    n_ctx = lax.axis_size("ctx")
    n_dp = lax.axis_size("dp")
    me = lax.axis_index("ctx")
    tok = block_in.shape[0]
    seq = tok * n_ctx
    heads = H // n_ctx
    width = heads * HD
    sharers = n_ctx // KVH
    rows = qkv_weight.shape[0]
    ff_rows = down_weight.shape[0]
    ff = ff_rows * n_dp
    columns = width + 2 * HD

    order = me ^ jnp.where(me % 2 == 0, *[jnp.asarray(t) for t in slot_table(n_ctx)])
    slots = jnp.arange(n_ctx, dtype=jnp.int32)
    slot_of = jnp.sum(jnp.where(order[None, :] == slots[:, None], slots[None, :], 0), axis=1)
    index = jnp.arange(seq, dtype=jnp.int32)
    lengths = doc_lengths[0]
    ends = jnp.cumsum(lengths)
    starts = jnp.sum((index[:, None] >= ends[None, :]).astype(jnp.int32) * lengths[None, :], axis=1)
    lane = jnp.arange(128, dtype=F32) % HALF
    frequency = 10000.0 ** (-lane * 2.0 / HD)
    angles = (index - starts).astype(F32)[:, None] * frequency[None, :]
    cosine = jnp.cos(angles)
    sine = jnp.sin(angles)
    starts_row = starts[None, :]

    gain_one = gain_attn.astype(F32)[:, None]
    gain_two = gain_ffn.astype(F32)[:, None]
    qkv = (qkv_weight.astype(F32) * gain_one).astype(BF)
    q_cols = qkv[:, : H * HD].reshape(rows, n_ctx, width).transpose(1, 0, 2)
    k_cols = qkv[:, H * HD : (H + KVH) * HD].reshape(rows, KVH, HD).transpose(1, 0, 2)
    v_cols = qkv[:, (H + KVH) * HD :].reshape(rows, KVH, HD).transpose(1, 0, 2)
    kv_cols = jnp.repeat(jnp.concatenate([k_cols, v_cols], axis=2), sharers, axis=0)
    qkv_own = exchange(jnp.concatenate([q_cols, kv_cols], axis=2)).reshape(n_ctx * rows, columns)
    qkv_part = gather_dp(qkv_own)

    hidden_in = block_in.astype(F32)
    rms_one = lax.rsqrt(jnp.mean(hidden_in * hidden_in, axis=-1, keepdims=True) + EPS)
    one_direct = gather_direct(after((hidden_in * rms_one).astype(BF), qkv_own), n_ctx)
    gate_up_cols = split_columns(
        gate_up_weight, after(gain_two, cosine, sine), n_ctx, n_dp, ff_rows
    )
    one_pieces = gather_rest(one_direct, n_ctx, (), (qkv_part, gate_up_cols))
    owner_pairs = [(b, b % n_dp * n_ctx + b // n_dp) for b in range(n_dp * n_ctx)]
    out_own = lax.ppermute(after(out_weight, qkv_part), ("dp", "ctx"), owner_pairs)
    out_part = gather_dp(out_own)

    gate_up_own = exchange(after(gate_up_cols, *one_pieces[: n_ctx // 2])).reshape(
        n_ctx * rows, 2 * ff
    )
    gate_up_part = gather_dp(gate_up_own)
    down_part = gather_dp(after(down_weight, gate_up_own))

    queries, keys, values, keys_t, values_t, all_one = project_qkv(
        order, one_pieces, qkv_part, spread_matrix(width), widen_matrix(width), cosine, sine, width, tok
    )
    slot_attn, attended, lse = attend_forward(
        slot_of, starts_row, after(queries, gate_up_own), keys, values_t, heads, tok
    )
    stages = tuple(reversed(range(len(walk(n_ctx, 0)))))

    def rows_of(x, lo, hi):
        return lax.slice_in_dim(x, lo * tok, hi * tok, axis=0)

    attn_pairs, _ = scatter_pairs(
        lambda lo, hi: nn(rows_of(slot_attn, lo, hi), out_part), tok, n_ctx
    )
    state = hidden_in + scatter_chips(*attn_pairs, stages, n_ctx)
    rms_two = lax.rsqrt(jnp.mean(state * state, axis=-1, keepdims=True) + EPS)
    norm_two = (state * rms_two).astype(BF)

    two_pieces = gather_slots(norm_two, n_ctx)
    grad_direct = gather_direct(after(out_grad, *two_pieces), n_ctx)
    hidden, factors, all_two = feed_forward(two_pieces, gate_up_part)
    grad_pieces = gather_rest(grad_direct, n_ctx, (hidden,))
    all_grad = lay_out(grad_pieces)
    out_direct = gather_direct(after(out_part, *grad_pieces[: n_ctx // 2]), n_ctx)
    out_pieces = gather_rest(out_direct, n_ctx)
    down_terms = outer_rows(hidden, all_grad)
    down_sums = scatter_dp(down_terms)
    grad_gate_up = feed_backward(
        after(factors, down_terms, *out_direct), all_grad, down_part
    )

    grad_gate_up = after(grad_gate_up, *out_pieces[: n_ctx // 2])
    d_pairs, _ = scatter_pairs(
        lambda lo, hi: nt(rows_of(grad_gate_up, lo, hi), gate_up_part), tok, n_ctx
    )
    d_two = scatter_chips(*d_pairs, stages, n_ctx)
    hidden_pairs, _ = scatter_pairs(
        lambda lo, hi: nn(rows_of(after(hidden, *d_pairs), lo, hi), down_part), tok, n_ctx
    )
    gate_up_terms = outer_rows(after(all_two, *d_pairs), grad_gate_up)
    gate_up_sums = scatter_dp(gate_up_terms)

    grad_state, grad_branch, grad_heads = branch_back(
        order, after(d_two, gate_up_terms, *hidden_pairs), state, out_grad, out_pieces
    )
    grad_attn = exchange(grad_heads).reshape(seq, width)
    branch_here, branch_there = gather_at_once(after(grad_branch, grad_attn), n_ctx)
    hidden_upper, hidden_lower = hidden_pairs
    hidden_arrived = swap_stage(after(hidden_upper.astype(BF), grad_attn), n_ctx, stages[0])
    grad_mixed = attend_backward(
        slot_of,
        starts_row,
        queries,
        keys,
        keys_t,
        values,
        grad_attn,
        attended,
        lse,
        cosine,
        sine,
        unsplit_matrix(width),
        heads,
        tok,
    )
    qkv_terms = outer_rows(all_one, grad_mixed)
    qkv_sums = scatter_dp(after(qkv_terms, gate_up_sums))
    one_pairs, _ = scatter_pairs(
        lambda lo, hi: nt(
            rows_of(after(grad_mixed, qkv_terms, hidden_arrived, *branch_here), lo, hi), qkv_part
        ),
        tok,
        n_ctx,
    )
    d_one = scatter_chips(*one_pairs, stages, n_ctx)
    hidden_sums = scatter_rest(hidden_lower, hidden_arrived, stages, n_ctx)
    block_out = (state + hidden_sums).astype(BF)
    out_terms = outer_rows(slot_attn, after(lay_out(branch_here + branch_there), qkv_terms))
    out_sums = scatter_dp(after(out_terms, qkv_sums))
    norm_one = hidden_in * rms_one
    input_grad = grad_state + rms_one * (
        d_one - norm_one * jnp.mean(d_one * norm_one, axis=-1, keepdims=True)
    )

    down_weight_grad = after(down_sums, grad_mixed).astype(F32)
    out_weight_grad = lax.ppermute(
        out_sums, ("dp", "ctx"), [(b, a) for a, b in owner_pairs]
    ).astype(F32)
    gate_up_weight_grad, gain_ffn_grad = join_columns(
        exchange(after(gate_up_sums, grad_mixed).reshape(n_ctx, rows, 2 * ff)), gate_up_weight, gain_two, n_dp, ff_rows
    )
    qkv_back = exchange(qkv_sums.reshape(n_ctx, rows, columns)).astype(F32)
    q_back = qkv_back[:, :, :width].transpose(1, 0, 2).reshape(rows, H * HD)
    kv_back = jnp.sum(qkv_back[:, :, width:].reshape(KVH, sharers, rows, 2 * HD), axis=1)
    k_back = kv_back[:, :, :HD].transpose(1, 0, 2).reshape(rows, KVH * HD)
    v_back = kv_back[:, :, HD:].transpose(1, 0, 2).reshape(rows, KVH * HD)
    qkv_back = jnp.concatenate([q_back, k_back, v_back], axis=1)
    qkv_weight_grad = qkv_back * gain_one
    gain_attn_grad = jnp.sum(qkv_back * qkv_weight.astype(F32), axis=1)
    return (
        block_out,
        input_grad,
        gain_attn_grad,
        qkv_weight_grad,
        out_weight_grad,
        gain_ffn_grad[:, 0],
        gate_up_weight_grad,
        down_weight_grad,
    )


def solution(mesh):
    rows = P(("dp", "ctx"), None)
    entries = P(("dp", "ctx"))
    return jax.shard_map(
        on_device,
        mesh=mesh,
        in_specs=(rows, entries, rows, rows, entries, rows, rows, P("dp", None), rows),
        out_specs=(rows, rows, entries, rows, rows, entries, rows, rows),
        check_vma=False,
    )
```

```python
import jax
import jax.numpy as jnp
import numpy as np
from jax import lax
from jax.experimental import pallas as pl
from jax.experimental.pallas import tpu as pltpu
from jax.sharding import PartitionSpec as P

D = 2048
H = 32
KVH = 4
HD = 64
FF = 5632
HALF = HD // 2

EPS = 1e-05
MASKED = -1e30
BF = jnp.bfloat16
F32 = jnp.float32
VMEM_LIMIT = 60 << 20
SHORT = pl.CostEstimate(flops=1 << 20, bytes_accessed=1 << 20, transcendentals=0)
MEDIUM = pl.CostEstimate(flops=2 * 10**10, bytes_accessed=1 << 20, transcendentals=0)
LONG = pl.CostEstimate(flops=10**11, bytes_accessed=1 << 20, transcendentals=0)


def nt(a, b):
    return lax.dot_general(a, b, (((1,), (1,)), ((), ())), preferred_element_type=F32)


def nn(a, b):
    return jnp.dot(a, b, preferred_element_type=F32)


def after(x, *earlier):
    return lax.optimization_barrier((x, *earlier))[0]


def after_each(values, *earlier):
    count = len(values)
    return lax.optimization_barrier((*values, *earlier))[:count]


def walk(n_ctx, parity):
    bits = []
    bit = 2
    while bit < n_ctx:
        bits.append(bit)
        bit *= 2
    return bits if parity == 0 else bits[::-1]


def swap_stage(x, n_ctx, stage):
    pairs = [(c, c ^ walk(n_ctx, c % 2)[stage]) for c in range(n_ctx)]
    return lax.ppermute(x, "ctx", pairs)


def swap_core(x, n_ctx):
    return lax.ppermute(x, "ctx", [(c, c ^ 1) for c in range(n_ctx)])


def slot_table(n_ctx):
    lists = []
    for parity in (0, 1):
        row = [0]
        for bit in walk(n_ctx, parity):
            row = row + [v ^ bit for v in row]
        lists.append(row)
    return np.array(
        [lists[p] + [v ^ 1 for v in lists[1 - p]] for p in (0, 1)], dtype=np.int32
    )


def gather_direct(x, n_ctx):
    return [x] + [swap_stage(x, n_ctx, stage) for stage in range(len(walk(n_ctx, 0)))]


def gather_rest(direct, n_ctx, earlier=(), last=()):
    have = direct[:1]
    for stage in range(len(walk(n_ctx, 0))):
        passed = [after(block, *earlier) if earlier else block for block in have[1:]]
        have = have + [direct[stage + 1]] + [swap_stage(block, n_ctx, stage) for block in passed]
    return have + [swap_core(after(block, *last) if last else block, n_ctx) for block in have]


def gather_at_once(x, n_ctx):
    have = [x]
    table = slot_table(n_ctx)
    for slot in range(1, n_ctx // 2):
        pairs = [(c, c ^ int(table[c % 2][slot])) for c in range(n_ctx)]
        have.append(lax.ppermute(x, "ctx", pairs))
    return have, [swap_core(block, n_ctx) for block in have]


def gather_slots(x, n_ctx):
    return gather_rest(gather_direct(x, n_ctx), n_ctx)


def scatter_pairs(term, tok, n_ctx):
    mine = n_ctx // 2
    cut = mine // 2
    sums, arrivals = [], []
    for lo, hi in ((cut, mine), (0, cut)):
        arrivals.append(swap_core(term(mine + lo, mine + hi).astype(BF), n_ctx))
        sums.append(term(lo, hi) + arrivals[-1].astype(F32))
    return sums, arrivals


def scatter_chips(upper, lower, stages, n_ctx, *earlier):
    for stage in stages:
        if earlier and stage == 0:
            upper = after(upper.astype(BF), *earlier)
        lower = lower + swap_stage(upper.astype(BF), n_ctx, stage).astype(F32)
        if stage:
            half = lower.shape[0] // 2
            upper, lower = lower[half:], lower[:half]
    return lower if stages[-1] == 0 else (upper, lower)


def scatter_rest(lower, arrived, stages, n_ctx):
    sums = lower + arrived.astype(F32)
    if len(stages) == 1:
        return sums
    half = sums.shape[0] // 2
    return scatter_chips(sums[half:], sums[:half], stages[1:], n_ctx)


def exchange(x):
    return lax.all_to_all(x, "ctx", split_axis=0, concat_axis=0, tiled=False)


def gather_dp(x):
    return lax.all_gather(x, "dp", axis=0, tiled=True)


def scatter_dp(x):
    return lax.psum_scatter(x, "dp", scatter_dimension=0, tiled=True)


def fetch_piece(pieces, buffer, semaphores, count=1):
    step = pl.program_id(0)

    @pl.when(step == 0)
    def _():
        for i, piece in enumerate(pieces):
            pltpu.make_async_copy(piece, buffer.at[i], semaphores.at[i]).start()

    for i in range(count):
        at = step * count + i
        pltpu.make_async_copy(pieces[0], buffer.at[at], semaphores.at[at]).wait()
    if count == 1:
        return buffer[step]
    return buffer[pl.ds(step * count, count)].reshape(count * buffer.shape[1], buffer.shape[2])


def keep_pieces(buffer, target, semaphores, count=1):
    step = pl.program_id(0)
    total, tok = buffer.shape[0], buffer.shape[1]

    def copy(at):
        rows = pl.ds(pl.multiple_of(at * tok, tok), tok)
        return pltpu.make_async_copy(buffer.at[at], target.at[rows], semaphores.at[at])

    for i in range(count):
        copy(step * count + i).start()

    @pl.when(step == total // count - 1)
    def _():
        for i in range(total):
            copy(i).wait()


def store_rows(source, target, semaphores):
    count = semaphores.shape[0]
    rows = source.shape[0] // count
    copies = [
        pltpu.make_async_copy(
            source.at[pl.ds(i * rows, rows)], target.at[pl.ds(i * rows, rows)], semaphores.at[i]
        )
        for i in range(count)
    ]
    for copy in copies:
        copy.start()
    return copies


def chunks(rows):
    return next(count for count in (8, 4, 2, 1) if rows % (16 * count) == 0)


def fetch_rows(source, buffer, semaphores):
    count = semaphores.shape[0]
    rows = source.shape[0] // count

    @pl.when(pl.program_id(0) == 0)
    def _():
        copies = [
            pltpu.make_async_copy(
                source.at[pl.ds(i * rows, rows), pl.ds(0, buffer.shape[1])],
                buffer.at[pl.ds(i * rows, rows)],
                semaphores.at[i],
            )
            for i in range(count)
        ]
        for copy in copies:
            copy.start()
        for copy in copies:
            copy.wait()


def swap_halves(x):
    return pltpu.roll(x, x.shape[1] // 2, axis=1)


def turn_tables(cosine, sine, width):
    times = width // 128
    cosine = jnp.concatenate([cosine] * times, axis=1) if times > 1 else cosine
    sine = jnp.concatenate([sine] * times, axis=1) if times > 1 else sine
    lane = lax.broadcasted_iota(jnp.int32, sine.shape, 1)
    return cosine, jnp.where(lane < width // 2, -sine, sine)


def any_specs(pieces):
    return [pl.BlockSpec(memory_space=pltpu.HBM) for _ in pieces]


def project_qkv(order, pieces, weight, spread, widen, cosine, sine, width, tok):
    n = len(pieces)
    seq = n * tok

    def kernel(order_ref, *refs):
        parts = refs[:n]
        w_hbm, spread_ref, widen_ref, cos_ref, sin_ref = refs[n : n + 5]
        (
            q_ref, k_ref, v_ref, kt_ref, vt_ref, all_hbm, wide, buffer, semaphores, keep_semaphores, w_ref, w_semaphores
        ) = refs[n + 5 :]
        fetch_rows(w_hbm, w_ref, w_semaphores)

        @pl.when(pl.program_id(0) == 0)
        def _():
            wide[...] = nn(w_ref[...], spread_ref[...]).astype(BF)

        x = fetch_piece(parts, buffer, semaphores)
        keep_pieces(buffer, all_hbm, keep_semaphores)
        mixed = nn(x, wide[...])
        cos, sin = turn_tables(cos_ref[...], sin_ref[...], width)
        q = mixed[:, :width]
        q_ref[...] = (q * cos + swap_halves(q) * sin).astype(BF) * (HD**-0.5)
        lane = lax.broadcasted_iota(jnp.int32, (tok, 128), 1)
        key_sine = jnp.where(lane < HALF, -sin_ref[...], sin_ref[...])
        both = jnp.where(
            lane < HD,
            mixed[:, width : width + 128] * cos_ref[...] + mixed[:, width + 128 :] * key_sine,
            mixed[:, width : width + 128],
        ).astype(BF)
        repeated = nn(both, widen_ref[...]).astype(BF)
        k_ref[...] = repeated[:, :width]
        v_ref[...] = repeated[:, width:]
        turned = both.T
        kt_ref[...] = turned[:HD]
        vt_ref[...] = turned[HD:]

    rows = lambda s, order: (order[s], 0)
    lanes = lambda s, order: (0, order[s])
    whole = lambda s, order: (0, 0)
    return pl.pallas_call(
        kernel,
        grid_spec=pltpu.PrefetchScalarGridSpec(
            num_scalar_prefetch=1,
            grid=(n,),
            in_specs=any_specs(pieces)
            + [
                pl.BlockSpec(memory_space=pltpu.HBM),
                pl.BlockSpec(spread.shape, whole),
                pl.BlockSpec(widen.shape, whole),
                pl.BlockSpec((tok, 128), rows),
                pl.BlockSpec((tok, 128), rows),
            ],
            out_specs=[
                pl.BlockSpec((tok, width), rows),
                pl.BlockSpec((tok, width), rows),
                pl.BlockSpec((tok, width), rows),
                pl.BlockSpec((HD, tok), lanes),
                pl.BlockSpec((HD, tok), lanes),
                pl.BlockSpec(memory_space=pltpu.HBM),
            ],
            scratch_shapes=[
                pltpu.VMEM((D, width + 256), BF),
                pltpu.VMEM((n, tok, D), BF),
                pltpu.SemaphoreType.DMA((n,)),
                pltpu.SemaphoreType.DMA((n,)),
                pltpu.VMEM((D, width + 2 * HD), BF),
                pltpu.SemaphoreType.DMA((chunks(D),)),
            ],
        ),
        out_shape=[
            jax.ShapeDtypeStruct((seq, width), BF),
            jax.ShapeDtypeStruct((seq, width), BF),
            jax.ShapeDtypeStruct((seq, width), BF),
            jax.ShapeDtypeStruct((HD, seq), BF),
            jax.ShapeDtypeStruct((HD, seq), BF),
            jax.ShapeDtypeStruct((seq, D), BF),
        ],
        compiler_params=pltpu.CompilerParams(vmem_limit_bytes=VMEM_LIMIT),
        cost_estimate=LONG,
        name="project_qkv",
    )(order, *pieces, weight, spread, widen, cosine, sine)


def project_out(order, heads_in, pieces, residual):
    n, tok, width = heads_in.shape

    def kernel(order_ref, a_ref, *refs):
        parts = refs[:n]
        x_ref, state_hbm, norm_hbm, buffer, semaphores, state_ref, norm_ref, out_semaphores = refs[n:]
        step = pl.program_id(0)
        w = fetch_piece(parts, buffer, semaphores)

        @pl.when(step == 0)
        def _():
            state_ref[...] = x_ref[...].astype(F32)

        state_ref[...] += nn(a_ref[0], w)

        @pl.when(step == n - 1)
        def _():
            state = state_ref[...]
            scale = lax.rsqrt(jnp.mean(state * state, axis=-1, keepdims=True) + EPS)
            copies = store_rows(state_ref, state_hbm, out_semaphores.at[0])
            norm_ref[...] = (state * scale).astype(BF)
            copies += store_rows(norm_ref, norm_hbm, out_semaphores.at[1])
            for copy in copies:
                copy.wait()

    whole = lambda s, order: (0, 0)
    return pl.pallas_call(
        kernel,
        grid_spec=pltpu.PrefetchScalarGridSpec(
            num_scalar_prefetch=1,
            grid=(n,),
            in_specs=[pl.BlockSpec((1, tok, width), lambda s, order: (order[s], 0, 0))]
            + any_specs(pieces)
            + [pl.BlockSpec((tok, D), whole)],
            out_specs=[pl.BlockSpec(memory_space=pltpu.HBM)] * 2,
            scratch_shapes=[
                pltpu.VMEM((n, width, D), BF),
                pltpu.SemaphoreType.DMA((n,)),
                pltpu.VMEM((tok, D), F32),
                pltpu.VMEM((tok, D), BF),
                pltpu.SemaphoreType.DMA((2, 4)),
            ],
        ),
        out_shape=[
            jax.ShapeDtypeStruct((tok, D), F32),
            jax.ShapeDtypeStruct((tok, D), BF),
        ],
        compiler_params=pltpu.CompilerParams(vmem_limit_bytes=VMEM_LIMIT),
        cost_estimate=SHORT,
        name="project_out",
    )(order, heads_in, *pieces, residual)


def feed_forward(pieces, weight):
    n = len(pieces)
    tok = 2 * pieces[0].shape[0]
    seq = n * tok // 2
    ff = weight.shape[1] // 2

    def kernel(*refs):
        parts = refs[:n]
        w_hbm, hidden_ref, factor_ref, all_hbm, buffer, semaphores, keep_semaphores, w_ref, w_semaphores = refs[n:]
        fetch_rows(w_hbm, w_ref, w_semaphores)
        x = fetch_piece(parts, buffer, semaphores, 2)
        keep_pieces(buffer, all_hbm, keep_semaphores, 2)
        both = nn(x, w_ref[...])
        gate = both[:, :ff]
        up = both[:, ff:]
        sig = jax.nn.sigmoid(gate)
        silu = gate * sig
        hidden_ref[...] = (silu * up).astype(BF)
        factor_ref[:, :ff] = (up * sig * (1.0 + gate * (1.0 - sig))).astype(BF)
        factor_ref[:, ff:] = silu.astype(BF)

    rows = lambda s: (s, 0)
    return pl.pallas_call(
        kernel,
        grid=(n // 2,),
        in_specs=any_specs(pieces) + [pl.BlockSpec(memory_space=pltpu.HBM)],
        out_specs=[
            pl.BlockSpec((tok, ff), rows),
            pl.BlockSpec((tok, 2 * ff), rows),
            pl.BlockSpec(memory_space=pltpu.HBM),
        ],
        scratch_shapes=[
            pltpu.VMEM((n, tok // 2, D), BF),
            pltpu.SemaphoreType.DMA((n,)),
            pltpu.SemaphoreType.DMA((n,)),
            pltpu.VMEM(weight.shape, BF),
            pltpu.SemaphoreType.DMA((chunks(D),)),
        ],
        out_shape=[
            jax.ShapeDtypeStruct((seq, ff), BF),
            jax.ShapeDtypeStruct((seq, 2 * ff), BF),
            jax.ShapeDtypeStruct((seq, D), BF),
        ],
        compiler_params=pltpu.CompilerParams(vmem_limit_bytes=VMEM_LIMIT),
        cost_estimate=LONG,
        name="feed_forward",
    )(*pieces, weight)


def feed_backward(factors, grads, weight):
    seq = factors.shape[0]
    ff = weight.shape[0]
    tok = 512

    def kernel(factor_ref, g_ref, w_hbm, out_ref, w_ref, w_semaphores, turned):
        fetch_rows(w_hbm, w_ref, w_semaphores)

        @pl.when(pl.program_id(0) == 0)
        def _():
            turned[...] = w_ref[...].T

        grad_hidden = nn(g_ref[...], turned[...])
        factor = factor_ref[...].astype(F32)
        out_ref[:, :ff] = (grad_hidden * factor[:, :ff]).astype(BF)
        out_ref[:, ff:] = (grad_hidden * factor[:, ff:]).astype(BF)

    rows = lambda s: (s, 0)
    return pl.pallas_call(
        kernel,
        grid=(seq // tok,),
        in_specs=[
            pl.BlockSpec((tok, 2 * ff), rows),
            pl.BlockSpec((tok, D), rows),
            pl.BlockSpec(memory_space=pltpu.HBM),
        ],
        out_specs=pl.BlockSpec((tok, 2 * ff), rows),
        scratch_shapes=[
            pltpu.VMEM(weight.shape, BF),
            pltpu.SemaphoreType.DMA((chunks(ff),)),
            pltpu.VMEM((D, ff), BF),
        ],
        out_shape=jax.ShapeDtypeStruct((seq, 2 * ff), BF),
        compiler_params=pltpu.CompilerParams(vmem_limit_bytes=VMEM_LIMIT),
        cost_estimate=LONG,
        name="feed_backward",
    )(factors, grads, weight)


def lay_out(pieces):
    n = len(pieces)
    tok = pieces[0].shape[0]

    def kernel(*refs):
        parts = refs[:n]
        out_ref, buffer, in_semaphores, out_semaphores = refs[n:]
        arrive = [
            pltpu.make_async_copy(part, buffer.at[i], in_semaphores.at[i])
            for i, part in enumerate(parts)
        ]
        leave = [
            pltpu.make_async_copy(buffer.at[i], out_ref.at[pl.ds(i * tok, tok)], out_semaphores.at[i])
            for i in range(n)
        ]
        for copy in arrive:
            copy.start()
        for i in range(n):
            arrive[i].wait()
            leave[i].start()
        for copy in leave:
            copy.wait()

    return pl.pallas_call(
        kernel,
        in_specs=any_specs(pieces),
        out_specs=pl.BlockSpec(memory_space=pltpu.HBM),
        scratch_shapes=[
            pltpu.VMEM((n, tok, D), BF),
            pltpu.SemaphoreType.DMA((n,)),
            pltpu.SemaphoreType.DMA((n,)),
        ],
        out_shape=jax.ShapeDtypeStruct((n * tok, D), BF),
        compiler_params=pltpu.CompilerParams(vmem_limit_bytes=VMEM_LIMIT),
        cost_estimate=SHORT,
        name="lay_out",
    )(*pieces)


def branch_back(order, d_two, state, out_grad, pieces):
    n = len(pieces)
    tok = d_two.shape[0]
    width = pieces[0].shape[0]

    def kernel(order_ref, d_ref, state_ref, g_ref, *refs):
        parts = refs[:n]
        grad_hbm, branch_hbm, heads_ref, buffer, semaphores, grad_ref, branch_ref, out_semaphores = refs[n:]

        @pl.when(pl.program_id(0) == 0)
        def _():
            state = state_ref[...]
            scale = lax.rsqrt(jnp.mean(state * state, axis=-1, keepdims=True) + EPS)
            norm = state * scale
            d = d_ref[...]
            grad = g_ref[...].astype(F32) + scale * (
                d - norm * jnp.mean(d * norm, axis=-1, keepdims=True)
            )
            grad_ref[...] = grad
            branch_ref[...] = grad.astype(BF)
            store_rows(grad_ref, grad_hbm, out_semaphores.at[0])
            store_rows(branch_ref, branch_hbm, out_semaphores.at[1])

        w = fetch_piece(parts, buffer, semaphores)
        heads_ref[0] = nt(branch_ref[...], w).astype(BF)

        @pl.when(pl.program_id(0) == n - 1)
        def _():
            for source, target, at in ((grad_ref, grad_hbm, 0), (branch_ref, branch_hbm, 1)):
                rows = tok // 4
                for i in range(4):
                    cut = pl.ds(i * rows, rows)
                    pltpu.make_async_copy(source.at[cut], target.at[cut], out_semaphores.at[at, i]).wait()

    whole = lambda s, order: (0, 0)
    return pl.pallas_call(
        kernel,
        grid_spec=pltpu.PrefetchScalarGridSpec(
            num_scalar_prefetch=1,
            grid=(n,),
            in_specs=[
                pl.BlockSpec((tok, D), whole),
                pl.BlockSpec((tok, D), whole),
                pl.BlockSpec((tok, D), whole),
            ]
            + any_specs(pieces),
            out_specs=[
                pl.BlockSpec(memory_space=pltpu.HBM),
                pl.BlockSpec(memory_space=pltpu.HBM),
                pl.BlockSpec((1, tok, width), lambda s, order: (order[s], 0, 0)),
            ],
            scratch_shapes=[
                pltpu.VMEM((n, width, D), BF),
                pltpu.SemaphoreType.DMA((n,)),
                pltpu.VMEM((tok, D), F32),
                pltpu.VMEM((tok, D), BF),
                pltpu.SemaphoreType.DMA((2, 4)),
            ],
        ),
        out_shape=[
            jax.ShapeDtypeStruct((tok, D), F32),
            jax.ShapeDtypeStruct((tok, D), BF),
            jax.ShapeDtypeStruct((n, tok, width), BF),
        ],
        compiler_params=pltpu.CompilerParams(vmem_limit_bytes=VMEM_LIMIT),
        cost_estimate=SHORT,
        name="branch_back",
    )(order, d_two, state, out_grad, *pieces)


def split_columns(weight, gain, n_ctx, n_dp, ff_rows):
    rows = weight.shape[0]
    ff = ff_rows * n_dp

    def kernel(w_ref, gain_ref, out_ref):
        gains = gain_ref[...]
        for part in range(2):
            for d in range(n_dp):
                for c in range(n_ctx):
                    at = part * FF + (d * n_ctx + c) * ff_rows
                    to = part * ff + d * ff_rows
                    values = w_ref[:, at : at + ff_rows].astype(F32) * gains
                    out_ref[c, :, to : to + ff_rows] = values.astype(BF)

    return pl.pallas_call(
        kernel,
        in_specs=[pl.BlockSpec(memory_space=pltpu.VMEM)] * 2,
        out_specs=pl.BlockSpec(memory_space=pltpu.VMEM),
        out_shape=jax.ShapeDtypeStruct((n_ctx, rows, 2 * ff), BF),
        compiler_params=pltpu.CompilerParams(vmem_limit_bytes=VMEM_LIMIT),
        cost_estimate=LONG,
        name="split_columns",
    )(weight, gain)


def join_columns(sums, weight, gain, n_dp, ff_rows):
    n_ctx, rows, both = sums.shape
    ff = both // 2

    def kernel(s_ref, w_ref, gain_ref, out_ref, gain_out_ref):
        gains = gain_ref[...]
        total = jnp.zeros((rows, ff_rows), F32)
        for part in range(2):
            for d in range(n_dp):
                for c in range(n_ctx):
                    at = part * ff + d * ff_rows
                    to = part * FF + (d * n_ctx + c) * ff_rows
                    values = s_ref[c, :, at : at + ff_rows].astype(F32)
                    total = total + values * w_ref[:, to : to + ff_rows].astype(F32)
                    out_ref[:, to : to + ff_rows] = values * gains
        gain_out_ref[...] = jnp.sum(total, axis=1, keepdims=True)

    return pl.pallas_call(
        kernel,
        in_specs=[pl.BlockSpec(memory_space=pltpu.VMEM)] * 3,
        out_specs=[pl.BlockSpec(memory_space=pltpu.VMEM)] * 2,
        out_shape=[
            jax.ShapeDtypeStruct((rows, 2 * FF), F32),
            jax.ShapeDtypeStruct((rows, 1), F32),
        ],
        compiler_params=pltpu.CompilerParams(vmem_limit_bytes=VMEM_LIMIT),
        cost_estimate=LONG,
        name="join_columns",
    )(sums, weight, gain)


def lane_heads(rows, width):
    lane = lax.broadcasted_iota(jnp.int32, (rows, width), 1)
    return (lane % (width // 2)) // HALF


def attend_forward(slot_of, starts, queries, keys, values_t, heads, tok, first, count, before):
    seq, width = queries.shape
    blocks = seq // tok
    span = 2 * tok

    def kernel(slot_ref, start_ref, q_ref, k_ref, v_ref, *refs):
        attn_ref, slot_attn_ref, full_ref, lse_ref, scores = refs[len(before) :]
        block = first + pl.program_id(0)
        steps = (block + 2) // 2
        start = start_ref[...]
        here = block * tok + lax.broadcasted_iota(jnp.int32, (1, tok), 1)
        head_of = lane_heads(tok, width)
        q = q_ref[...]
        q_heads = [jnp.where(head_of == h, q, jnp.zeros_like(q)) for h in range(heads)]

        def score(i, peaks):
            rows = pl.ds(pl.multiple_of(i * span, span), span)
            k = k_ref[rows, :]
            there = i * span + lax.broadcasted_iota(jnp.int32, (span, tok), 0)
            visible = (there >= start) & (there <= here)
            out = []
            for h in range(heads):
                s = jnp.where(visible, nt(k, q_heads[h]), MASKED)
                scores[h, rows, :] = s
                out.append(jnp.maximum(peaks[h], jnp.max(s.reshape(span // 8, 8, tok), axis=0)))
            return tuple(out)

        peaks = lax.fori_loop(
            0, steps, score, tuple(jnp.full((8, tok), MASKED, F32) for _ in range(heads))
        )
        peaks = [jnp.max(peak, axis=0, keepdims=True) for peak in peaks]

        def weigh(i, running):
            rows = pl.ds(pl.multiple_of(i * span, span), span)
            v = v_ref[:, rows]
            out = []
            for h in range(heads):
                total, acc = running[h]
                p = jnp.exp(scores[h, rows, :] - peaks[h])
                total = total + jnp.sum(p.reshape(span // 8, 8, tok), axis=0)
                out.append((total, acc + nn(v, p.astype(BF))))
            return tuple(out)

        result = lax.fori_loop(
            0,
            steps,
            weigh,
            tuple((jnp.zeros((8, tok), F32), jnp.zeros((HD, tok), F32)) for _ in range(heads)),
        )
        rows = []
        for h in range(heads):
            total, acc = result[h]
            total = jnp.sum(total, axis=0, keepdims=True)
            rows.append(acc / total)
            lse_ref[0, h : h + 1, :] = peaks[h] + jnp.log(total)
        full = jnp.concatenate(rows, axis=0).T
        full_ref[...] = full
        attn_ref[...] = full.astype(BF)
        slot_attn_ref[...] = full.astype(BF)

    return pl.pallas_call(
        kernel,
        grid_spec=pltpu.PrefetchScalarGridSpec(
            num_scalar_prefetch=1,
            grid=(count,),
            in_specs=[
                pl.BlockSpec((1, tok), lambda j, slot: (0, first + j)),
                pl.BlockSpec((tok, width), lambda j, slot: (first + j, 0)),
                pl.BlockSpec((seq, width), lambda j, slot: (0, 0)),
                pl.BlockSpec((HD, seq), lambda j, slot: (0, 0)),
            ]
            + [pl.BlockSpec(memory_space=pltpu.HBM)] * len(before),
            out_specs=[
                pl.BlockSpec((tok, width), lambda j, slot: (first + j, 0)),
                pl.BlockSpec((tok, width), lambda j, slot: (slot[first + j], 0)),
                pl.BlockSpec((tok, width), lambda j, slot: (first + j, 0)),
                pl.BlockSpec((1, heads, tok), lambda j, slot: (first + j, 0, 0)),
            ],
            scratch_shapes=[pltpu.VMEM((heads, seq, tok), F32)],
        ),
        out_shape=[
            jax.ShapeDtypeStruct((seq, width), BF),
            jax.ShapeDtypeStruct((seq, width), BF),
            jax.ShapeDtypeStruct((seq, width), F32),
            jax.ShapeDtypeStruct((blocks, heads, tok), F32),
        ],
        input_output_aliases={5 + i: i for i in range(len(before))},
        compiler_params=pltpu.CompilerParams(vmem_limit_bytes=VMEM_LIMIT),
        cost_estimate=LONG,
        name="attend_forward",
    )(slot_of, starts, queries, keys, values_t, *before)


def attend_backward(
    slot_of, starts, queries, keys, keys_t, values, grads, full, lse, cosine, sine, unsplit, heads, tok
):
    seq, width = queries.shape
    blocks = seq // tok
    span = 2 * tok
    half = width // 2

    def kernel(
        slot_ref, start_ref, q_ref, k_ref, kt_ref, v_ref, g_ref, full_ref, lse_ref, cos_ref, sin_ref, unsplit_ref,
        out_ref, dk, dv,
    ):
        block = pl.program_id(0)
        steps = (block + 2) // 2

        @pl.when(block == 0)
        def _():
            dk[...] = jnp.zeros_like(dk)
            dv[...] = jnp.zeros_like(dv)

        start = start_ref[...]
        here = block * tok + lax.broadcasted_iota(jnp.int32, (1, tok), 1)
        head_of = lane_heads(tok, width)
        wide = lax.broadcasted_iota(jnp.int32, (tok, width), 1) // HD
        q = q_ref[...]
        g = g_ref[...]
        q_heads = [jnp.where(head_of == h, q, jnp.zeros_like(q)) for h in range(heads)]
        g_heads = [jnp.where(wide == h, g, jnp.zeros_like(g)) for h in range(heads)]
        q_stack = jnp.concatenate(q_heads, axis=0)
        g_stack = jnp.concatenate(g_heads, axis=0)
        picks = (
            lax.broadcasted_iota(jnp.int32, (8, width), 1) // HD
            == lax.broadcasted_iota(jnp.int32, (8, width), 0)
        ).astype(F32)
        deltas = lax.dot_general(
            picks,
            g.astype(F32) * full_ref[...],
            (((1,), (1,)), ((), ())),
            preferred_element_type=F32,
            precision=lax.Precision.HIGHEST,
        )

        def step(i, dq):
            rows = pl.ds(pl.multiple_of(i * span, span), span)
            k = k_ref[rows, :]
            v = v_ref[rows, :]
            kt = kt_ref[:, rows]
            there = i * span + lax.broadcasted_iota(jnp.int32, (span, tok), 0)
            visible = (there >= start) & (there <= here)
            probs, grad_scores, out = [], [], []
            for h in range(heads):
                s = jnp.where(visible, nt(k, q_heads[h]), MASKED)
                p = jnp.exp(s - lse_ref[0, h : h + 1, :])
                ds = (p * (nt(v, g_heads[h]) - deltas[h : h + 1, :])).astype(BF)
                probs.append(p.astype(BF))
                grad_scores.append(ds)
                out.append(dq[h] + nn(kt, ds))
            dv[rows, :] += nn(jnp.concatenate(probs, axis=1), g_stack)
            dk[rows, :] += nn(jnp.concatenate(grad_scores, axis=1), q_stack)
            return tuple(out)

        dq = lax.fori_loop(
            0, steps, step, tuple(jnp.zeros((HD, tok), F32) for _ in range(heads))
        )
        dq = jnp.concatenate([x[:HALF] for x in dq] + [x[HALF:] for x in dq], axis=0).T
        here_rows = pl.ds(pl.multiple_of(block * tok, tok), tok)
        cos, sin = turn_tables(cos_ref[here_rows, :], sin_ref[here_rows, :], width)
        dq = (dq * cos - swap_halves(dq) * sin) * (HD**-0.5)
        slot_rows = pl.ds(pl.multiple_of(slot_ref[block] * tok, tok), tok)
        out_ref[slot_rows, :width] = nn(dq.astype(BF), unsplit_ref[...]).astype(BF)

        @pl.when(block == blocks - 1)
        def _():
            lane = lax.broadcasted_iota(jnp.int32, (width, 128), 0)
            column = lax.broadcasted_iota(jnp.int32, (width, 128), 1)
            fold_k = ((lane // half) * HALF + lane % HALF == column).astype(BF)
            fold_v = (lane % HD + HD == column).astype(BF)

            def fold(i, unused):
                rows = pl.ds(pl.multiple_of(i * tok, tok), tok)
                cos, sin = turn_tables(cos_ref[rows, :], sin_ref[rows, :], width)
                a = dk[rows, :]
                a = a * cos - swap_halves(a) * sin
                b = dv[rows, :]
                a_high = a.astype(BF)
                b_high = b.astype(BF)
                terms = (
                    nn(a_high, fold_k)
                    + nn((a - a_high.astype(F32)).astype(BF), fold_k)
                    + nn(b_high, fold_v)
                    + nn((b - b_high.astype(F32)).astype(BF), fold_v)
                )
                slot_rows = pl.ds(pl.multiple_of(slot_ref[i] * tok, tok), tok)
                out_ref[slot_rows, width:] = terms.astype(BF)
                return unused

            lax.fori_loop(0, blocks, fold, 0)

    whole = lambda shape: pl.BlockSpec(shape, lambda j, *_: (0, 0))
    return pl.pallas_call(
        kernel,
        grid_spec=pltpu.PrefetchScalarGridSpec(
            num_scalar_prefetch=1,
            grid=(blocks,),
            in_specs=[
                pl.BlockSpec((1, tok), lambda j, *_: (0, j)),
                pl.BlockSpec((tok, width), lambda j, *_: (j, 0)),
                whole((seq, width)),
                whole((HD, seq)),
                whole((seq, width)),
                pl.BlockSpec((tok, width), lambda j, *_: (j, 0)),
                pl.BlockSpec((tok, width), lambda j, *_: (j, 0)),
                pl.BlockSpec((1, heads, tok), lambda j, *_: (j, 0, 0)),
                whole((seq, 128)),
                whole((seq, 128)),
                whole((width, width)),
            ],
            out_specs=whole((seq, width + 128)),
            scratch_shapes=[pltpu.VMEM((seq, width), F32), pltpu.VMEM((seq, width), F32)],
        ),
        out_shape=jax.ShapeDtypeStruct((seq, width + 128), BF),
        compiler_params=pltpu.CompilerParams(vmem_limit_bytes=VMEM_LIMIT),
        cost_estimate=MEDIUM,
        name="attend_backward",
    )(slot_of, starts, queries, keys, keys_t, values, grads, full, lse, cosine, sine, unsplit)


def outer_rows(activations, gradients):
    return lax.dot_general(
        activations, gradients, (((0,), (0,)), ((), ())), preferred_element_type=F32
    ).astype(BF)


def split_source(width):
    lane = np.arange(width)
    half = lane // (width // 2)
    head = (lane % (width // 2)) // HALF
    return head * HD + half * HALF + lane % HALF


def spread_matrix(width):
    matrix = np.zeros((width + 2 * HD, width + 256), np.float32)
    lane = np.arange(width)
    matrix[split_source(width), lane] = 1
    lane = np.arange(2 * HD)
    matrix[width + lane, width + lane] = 1
    lane = np.arange(HD)
    matrix[width + (lane + HALF) % HD, width + 128 + lane] = 1
    return jnp.asarray(matrix, BF)


def widen_matrix(width):
    matrix = np.zeros((2 * HD, 2 * width), np.float32)
    lane = np.arange(width)
    matrix[(lane // (width // 2)) * HALF + lane % HALF, lane] = 1
    matrix[HD + lane % HD, width + lane] = 1
    return jnp.asarray(matrix, BF)


def unsplit_matrix(width):
    matrix = np.zeros((width, width), np.float32)
    matrix[np.arange(width), split_source(width)] = 1
    return jnp.asarray(matrix, BF)


def on_device(
    block_in,
    gain_attn,
    qkv_weight,
    out_weight,
    gain_ffn,
    gate_up_weight,
    down_weight,
    doc_lengths,
    out_grad,
):
    n_ctx = lax.axis_size("ctx")
    n_dp = lax.axis_size("dp")
    me = lax.axis_index("ctx")
    tok = block_in.shape[0]
    seq = tok * n_ctx
    heads = H // n_ctx
    width = heads * HD
    sharers = n_ctx // KVH
    rows = qkv_weight.shape[0]
    ff_rows = down_weight.shape[0]
    ff = ff_rows * n_dp
    columns = width + 2 * HD

    order = me ^ jnp.where(me % 2 == 0, *[jnp.asarray(t) for t in slot_table(n_ctx)])
    slots = jnp.arange(n_ctx, dtype=jnp.int32)
    slot_of = jnp.sum(jnp.where(order[None, :] == slots[:, None], slots[None, :], 0), axis=1)
    index = jnp.arange(seq, dtype=jnp.int32)
    gain_one = gain_attn.astype(F32)[:, None]
    gain_two = gain_ffn.astype(F32)[:, None]
    qkv = (qkv_weight.astype(F32) * gain_one).astype(BF)
    q_cols = qkv[:, : H * HD].reshape(rows, n_ctx, width).transpose(1, 0, 2)
    k_cols = qkv[:, H * HD : (H + KVH) * HD].reshape(rows, KVH, HD).transpose(1, 0, 2)
    v_cols = qkv[:, (H + KVH) * HD :].reshape(rows, KVH, HD).transpose(1, 0, 2)
    kv_cols = jnp.repeat(jnp.concatenate([k_cols, v_cols], axis=2), sharers, axis=0)
    owner_pairs = [(b, b % n_dp * n_ctx + b // n_dp) for b in range(n_dp * n_ctx)]
    out_own = lax.ppermute(out_weight, ("dp", "ctx"), owner_pairs)
    qkv_own = exchange(jnp.concatenate([q_cols, kv_cols], axis=2)).reshape(n_ctx * rows, columns)
    attn_part = gather_dp(
        jnp.concatenate([qkv_own, out_own.reshape(n_ctx * rows, width)], axis=1)
    )
    qkv_part = attn_part[:, :columns]
    out_part = attn_part[:, columns:].reshape(width, D)

    hidden_in = block_in.astype(F32)
    rms_one = lax.rsqrt(jnp.mean(hidden_in * hidden_in, axis=-1, keepdims=True) + EPS)
    one_direct = gather_direct(after((hidden_in * rms_one).astype(BF), qkv_own, out_own), n_ctx)
    lengths = after(doc_lengths[0], one_direct[1])
    ends = jnp.cumsum(lengths)
    starts = jnp.sum((index[:, None] >= ends[None, :]).astype(jnp.int32) * lengths[None, :], axis=1)
    lane = jnp.arange(128, dtype=F32) % HALF
    frequency = 10000.0 ** (-lane * 2.0 / HD)
    angles = (index - starts).astype(F32)[:, None] * frequency[None, :]
    cosine = jnp.cos(angles)
    sine = jnp.sin(angles)
    starts_row = starts[None, :]
    gate_up_cols = split_columns(
        gate_up_weight, after(gain_two, cosine, sine), n_ctx, n_dp, ff_rows
    )
    one_pieces = gather_rest(one_direct, n_ctx, (), (attn_part, gate_up_cols))
    gate_up_own = exchange(after(gate_up_cols, *one_pieces[: n_ctx // 2])).reshape(
        n_ctx * rows, 2 * ff
    )
    gate_up_part = gather_dp(gate_up_own)
    down_part = gather_dp(after(down_weight, gate_up_own))

    queries, keys, values, keys_t, values_t, all_one = project_qkv(
        order, one_pieces, attn_part, spread_matrix(width), widen_matrix(width), cosine, sine, width, tok
    )
    out_direct = gather_direct(out_part, n_ctx)
    attn, slot_attn, attended, lse = attend_forward(
        slot_of, starts_row, after(queries, gate_up_own, *out_direct), keys, values_t, heads, tok, 0, n_ctx, ()
    )
    attn_tokens = exchange(attn.reshape(n_ctx, tok, width))
    out_pieces = gather_rest(out_direct, n_ctx, (queries,), (attn,))
    state, norm_two = project_out(order, attn_tokens, out_pieces, block_in)

    two_pieces = gather_slots(norm_two, n_ctx)
    grad_direct = gather_direct(after(out_grad, *two_pieces), n_ctx)
    hidden, factors, all_two = feed_forward(two_pieces, gate_up_part)
    grad_pieces = gather_rest(grad_direct, n_ctx, (hidden,))
    all_grad = lay_out(grad_pieces)
    down_terms = outer_rows(hidden, all_grad)
    down_sums = scatter_dp(down_terms)
    grad_gate_up = feed_backward(after(factors, down_terms), all_grad, down_part)

    def rows_of(x, lo, hi):
        return lax.slice_in_dim(x, lo * tok, hi * tok, axis=0)

    d_pairs, _ = scatter_pairs(
        lambda lo, hi: nt(rows_of(grad_gate_up, lo, hi), gate_up_part), tok, n_ctx
    )
    stages = tuple(reversed(range(len(walk(n_ctx, 0)))))
    d_two = scatter_chips(*d_pairs, stages, n_ctx)
    hidden_pairs, _ = scatter_pairs(
        lambda lo, hi: nn(rows_of(after(hidden, *d_pairs), lo, hi), down_part), tok, n_ctx
    )
    gate_up_terms = outer_rows(after(all_two, *d_pairs), grad_gate_up)
    gate_up_sums = scatter_dp(gate_up_terms)

    grad_state, grad_branch, grad_heads = branch_back(
        order, after(d_two, gate_up_terms, *hidden_pairs), state, out_grad, out_pieces
    )
    grad_attn = exchange(grad_heads).reshape(seq, width)
    branch_here, branch_there = gather_at_once(after(grad_branch, grad_attn), n_ctx)
    hidden_upper, hidden_lower = hidden_pairs
    hidden_arrived = swap_stage(after(hidden_upper.astype(BF), grad_attn), n_ctx, stages[0])
    grad_mixed = attend_backward(
        slot_of,
        starts_row,
        queries,
        keys,
        keys_t,
        values,
        grad_attn,
        attended,
        lse,
        cosine,
        sine,
        unsplit_matrix(width),
        heads,
        tok,
    )
    qkv_terms = outer_rows(all_one, grad_mixed)
    qkv_sums = scatter_dp(after(qkv_terms, gate_up_sums))
    one_pairs, _ = scatter_pairs(
        lambda lo, hi: nt(
            rows_of(after(grad_mixed, qkv_terms, hidden_arrived, *branch_here), lo, hi), qkv_part
        ),
        tok,
        n_ctx,
    )
    d_one = scatter_chips(*one_pairs, stages, n_ctx)
    hidden_sums = scatter_rest(hidden_lower, hidden_arrived, stages, n_ctx)
    block_out = (state + hidden_sums).astype(BF)
    out_terms = outer_rows(slot_attn, after(lay_out(branch_here + branch_there), qkv_terms))
    out_sums = scatter_dp(after(out_terms, qkv_sums))
    norm_one = hidden_in * rms_one
    input_grad = grad_state + rms_one * (
        d_one - norm_one * jnp.mean(d_one * norm_one, axis=-1, keepdims=True)
    )

    down_weight_grad = after(down_sums, grad_mixed).astype(F32)
    out_weight_grad = lax.ppermute(
        out_sums, ("dp", "ctx"), [(b, a) for a, b in owner_pairs]
    ).astype(F32)
    gate_up_weight_grad, gain_ffn_grad = join_columns(
        exchange(after(gate_up_sums, grad_mixed).reshape(n_ctx, rows, 2 * ff)), gate_up_weight, gain_two, n_dp, ff_rows
    )
    qkv_back = exchange(qkv_sums.reshape(n_ctx, rows, columns)).astype(F32)
    q_back = qkv_back[:, :, :width].transpose(1, 0, 2).reshape(rows, H * HD)
    kv_back = jnp.sum(qkv_back[:, :, width:].reshape(KVH, sharers, rows, 2 * HD), axis=1)
    k_back = kv_back[:, :, :HD].transpose(1, 0, 2).reshape(rows, KVH * HD)
    v_back = kv_back[:, :, HD:].transpose(1, 0, 2).reshape(rows, KVH * HD)
    qkv_back = jnp.concatenate([q_back, k_back, v_back], axis=1)
    qkv_weight_grad = qkv_back * gain_one
    gain_attn_grad = jnp.sum(qkv_back * qkv_weight.astype(F32), axis=1)
    return (
        block_out,
        input_grad,
        gain_attn_grad,
        qkv_weight_grad,
        out_weight_grad,
        gain_ffn_grad[:, 0],
        gate_up_weight_grad,
        down_weight_grad,
    )


def solution(mesh):
    rows = P(("dp", "ctx"), None)
    entries = P(("dp", "ctx"))
    return jax.shard_map(
        on_device,
        mesh=mesh,
        in_specs=(rows, entries, rows, rows, entries, rows, rows, P("dp", None), rows),
        out_specs=(rows, rows, entries, rows, rows, entries, rows, rows),
        check_vma=False,
    )
```

```python
import jax
import jax.numpy as jnp
import numpy as np
from jax import lax
from jax.experimental import pallas as pl
from jax.experimental.pallas import tpu as pltpu
from jax.sharding import PartitionSpec as P

D = 2048
H = 32
KVH = 4
HD = 64
FF = 5632
HALF = HD // 2

EPS = 1e-05
MASKED = -1e30
BF = jnp.bfloat16
F32 = jnp.float32
VMEM_LIMIT = 60 << 20
SHORT = pl.CostEstimate(flops=1 << 20, bytes_accessed=1 << 20, transcendentals=0)
MEDIUM = pl.CostEstimate(flops=2 * 10**10, bytes_accessed=1 << 20, transcendentals=0)
LONG = pl.CostEstimate(flops=10**11, bytes_accessed=1 << 20, transcendentals=0)


def nt(a, b):
    return lax.dot_general(a, b, (((1,), (1,)), ((), ())), preferred_element_type=F32)


def nn(a, b):
    return jnp.dot(a, b, preferred_element_type=F32)


def after(x, *earlier):
    return lax.optimization_barrier((x, *earlier))[0]


def after_each(values, *earlier):
    count = len(values)
    return lax.optimization_barrier((*values, *earlier))[:count]


def walk(n_ctx, parity):
    bits = []
    bit = 2
    while bit < n_ctx:
        bits.append(bit)
        bit *= 2
    return bits if parity == 0 else bits[::-1]


def swap_stage(x, n_ctx, stage):
    pairs = [(c, c ^ walk(n_ctx, c % 2)[stage]) for c in range(n_ctx)]
    return lax.ppermute(x, "ctx", pairs)


def swap_core(x, n_ctx):
    return lax.ppermute(x, "ctx", [(c, c ^ 1) for c in range(n_ctx)])


def slot_table(n_ctx):
    lists = []
    for parity in (0, 1):
        row = [0]
        for bit in walk(n_ctx, parity):
            row = row + [v ^ bit for v in row]
        lists.append(row)
    return np.array(
        [lists[p] + [v ^ 1 for v in lists[1 - p]] for p in (0, 1)], dtype=np.int32
    )


def gather_direct(x, n_ctx):
    return [x] + [swap_stage(x, n_ctx, stage) for stage in range(len(walk(n_ctx, 0)))]


def gather_rest(direct, n_ctx, earlier=(), last=()):
    have = direct[:1]
    for stage in range(len(walk(n_ctx, 0))):
        passed = [after(block, *earlier) if earlier else block for block in have[1:]]
        have = have + [direct[stage + 1]] + [swap_stage(block, n_ctx, stage) for block in passed]
    return have + [swap_core(after(block, *last) if last else block, n_ctx) for block in have]


def gather_at_once(x, n_ctx):
    have = [x]
    table = slot_table(n_ctx)
    for slot in range(1, n_ctx // 2):
        pairs = [(c, c ^ int(table[c % 2][slot])) for c in range(n_ctx)]
        have.append(lax.ppermute(x, "ctx", pairs))
    return have, [swap_core(block, n_ctx) for block in have]


def gather_slots(x, n_ctx):
    return gather_rest(gather_direct(x, n_ctx), n_ctx)


def scatter_pairs(term, tok, n_ctx):
    mine = n_ctx // 2
    cut = mine // 2
    sums, arrivals = [], []
    for lo, hi in ((cut, mine), (0, cut)):
        arrivals.append(swap_core(term(mine + lo, mine + hi).astype(BF), n_ctx))
        sums.append(term(lo, hi) + arrivals[-1].astype(F32))
    return sums, arrivals


def scatter_chips(upper, lower, stages, n_ctx, *earlier):
    for stage in stages:
        if earlier and stage == 0:
            upper = after(upper.astype(BF), *earlier)
        lower = lower + swap_stage(upper.astype(BF), n_ctx, stage).astype(F32)
        if stage:
            half = lower.shape[0] // 2
            upper, lower = lower[half:], lower[:half]
    return lower if stages[-1] == 0 else (upper, lower)


def scatter_rest(lower, arrived, stages, n_ctx):
    sums = lower + arrived.astype(F32)
    if len(stages) == 1:
        return sums
    half = sums.shape[0] // 2
    return scatter_chips(sums[half:], sums[:half], stages[1:], n_ctx)


def exchange(x):
    return lax.all_to_all(x, "ctx", split_axis=0, concat_axis=0, tiled=False)


def gather_dp(x):
    return lax.all_gather(x, "dp", axis=0, tiled=True)


def scatter_dp(x):
    return lax.psum_scatter(x, "dp", scatter_dimension=0, tiled=True)


def fetch_piece(pieces, buffer, semaphores, count=1):
    step = pl.program_id(0)

    @pl.when(step == 0)
    def _():
        for i, piece in enumerate(pieces):
            pltpu.make_async_copy(piece, buffer.at[i], semaphores.at[i]).start()

    for i in range(count):
        at = step * count + i
        pltpu.make_async_copy(pieces[0], buffer.at[at], semaphores.at[at]).wait()
    if count == 1:
        return buffer[step]
    return buffer[pl.ds(step * count, count)].reshape(count * buffer.shape[1], buffer.shape[2])


def keep_pieces(buffer, target, semaphores, count=1):
    step = pl.program_id(0)
    total, tok = buffer.shape[0], buffer.shape[1]

    def copy(at):
        rows = pl.ds(pl.multiple_of(at * tok, tok), tok)
        return pltpu.make_async_copy(buffer.at[at], target.at[rows], semaphores.at[at])

    for i in range(count):
        copy(step * count + i).start()

    @pl.when(step == total // count - 1)
    def _():
        for i in range(total):
            copy(i).wait()


def store_rows(source, target, semaphores):
    count = semaphores.shape[0]
    rows = source.shape[0] // count
    copies = [
        pltpu.make_async_copy(
            source.at[pl.ds(i * rows, rows)], target.at[pl.ds(i * rows, rows)], semaphores.at[i]
        )
        for i in range(count)
    ]
    for copy in copies:
        copy.start()
    return copies


def chunks(rows):
    return next(count for count in (8, 4, 2, 1) if rows % (16 * count) == 0)


def fetch_rows(source, buffer, semaphores):
    count = semaphores.shape[0]
    rows = source.shape[0] // count

    @pl.when(pl.program_id(0) == 0)
    def _():
        copies = [
            pltpu.make_async_copy(
                source.at[pl.ds(i * rows, rows)], buffer.at[pl.ds(i * rows, rows)], semaphores.at[i]
            )
            for i in range(count)
        ]
        for copy in copies:
            copy.start()
        for copy in copies:
            copy.wait()


def swap_halves(x):
    return pltpu.roll(x, x.shape[1] // 2, axis=1)


def turn_tables(cosine, sine, width):
    times = width // 128
    cosine = jnp.concatenate([cosine] * times, axis=1) if times > 1 else cosine
    sine = jnp.concatenate([sine] * times, axis=1) if times > 1 else sine
    lane = lax.broadcasted_iota(jnp.int32, sine.shape, 1)
    return cosine, jnp.where(lane < width // 2, -sine, sine)


def any_specs(pieces):
    return [pl.BlockSpec(memory_space=pltpu.HBM) for _ in pieces]


def project_qkv(order, pieces, weight, spread, widen, cosine, sine, width, tok):
    n = len(pieces)
    seq = n * tok

    def kernel(order_ref, *refs):
        parts = refs[:n]
        w_hbm, spread_ref, widen_ref, cos_ref, sin_ref = refs[n : n + 5]
        (
            q_ref, k_ref, v_ref, kt_ref, vt_ref, all_hbm, wide, buffer, semaphores, keep_semaphores, w_ref, w_semaphores
        ) = refs[n + 5 :]
        fetch_rows(w_hbm, w_ref, w_semaphores)

        @pl.when(pl.program_id(0) == 0)
        def _():
            wide[...] = nn(w_ref[...], spread_ref[...]).astype(BF)

        x = fetch_piece(parts, buffer, semaphores)
        keep_pieces(buffer, all_hbm, keep_semaphores)
        mixed = nn(x, wide[...])
        cos, sin = turn_tables(cos_ref[...], sin_ref[...], width)
        q = mixed[:, :width]
        q_ref[...] = (q * cos + swap_halves(q) * sin).astype(BF) * (HD**-0.5)
        lane = lax.broadcasted_iota(jnp.int32, (tok, 128), 1)
        key_sine = jnp.where(lane < HALF, -sin_ref[...], sin_ref[...])
        both = jnp.where(
            lane < HD,
            mixed[:, width : width + 128] * cos_ref[...] + mixed[:, width + 128 :] * key_sine,
            mixed[:, width : width + 128],
        ).astype(BF)
        repeated = nn(both, widen_ref[...]).astype(BF)
        k_ref[...] = repeated[:, :width]
        v_ref[...] = repeated[:, width:]
        turned = both.T
        kt_ref[...] = turned[:HD]
        vt_ref[...] = turned[HD:]

    rows = lambda s, order: (order[s], 0)
    lanes = lambda s, order: (0, order[s])
    whole = lambda s, order: (0, 0)
    return pl.pallas_call(
        kernel,
        grid_spec=pltpu.PrefetchScalarGridSpec(
            num_scalar_prefetch=1,
            grid=(n,),
            in_specs=any_specs(pieces)
            + [
                pl.BlockSpec(memory_space=pltpu.HBM),
                pl.BlockSpec(spread.shape, whole),
                pl.BlockSpec(widen.shape, whole),
                pl.BlockSpec((tok, 128), rows),
                pl.BlockSpec((tok, 128), rows),
            ],
            out_specs=[
                pl.BlockSpec((tok, width), rows),
                pl.BlockSpec((tok, width), rows),
                pl.BlockSpec((tok, width), rows),
                pl.BlockSpec((HD, tok), lanes),
                pl.BlockSpec((HD, tok), lanes),
                pl.BlockSpec(memory_space=pltpu.HBM),
            ],
            scratch_shapes=[
                pltpu.VMEM((D, width + 256), BF),
                pltpu.VMEM((n, tok, D), BF),
                pltpu.SemaphoreType.DMA((n,)),
                pltpu.SemaphoreType.DMA((n,)),
                pltpu.VMEM(weight.shape, BF),
                pltpu.SemaphoreType.DMA((chunks(D),)),
            ],
        ),
        out_shape=[
            jax.ShapeDtypeStruct((seq, width), BF),
            jax.ShapeDtypeStruct((seq, width), BF),
            jax.ShapeDtypeStruct((seq, width), BF),
            jax.ShapeDtypeStruct((HD, seq), BF),
            jax.ShapeDtypeStruct((HD, seq), BF),
            jax.ShapeDtypeStruct((seq, D), BF),
        ],
        compiler_params=pltpu.CompilerParams(vmem_limit_bytes=VMEM_LIMIT),
        cost_estimate=LONG,
        name="project_qkv",
    )(order, *pieces, weight, spread, widen, cosine, sine)


def project_out(order, heads_in, pieces, residual):
    n, tok, width = heads_in.shape

    def kernel(order_ref, a_ref, *refs):
        parts = refs[:n]
        x_ref, state_hbm, norm_hbm, buffer, semaphores, state_ref, norm_ref, out_semaphores = refs[n:]
        step = pl.program_id(0)
        w = fetch_piece(parts, buffer, semaphores)

        @pl.when(step == 0)
        def _():
            state_ref[...] = x_ref[...].astype(F32)

        state_ref[...] += nn(a_ref[0], w)

        @pl.when(step == n - 1)
        def _():
            state = state_ref[...]
            scale = lax.rsqrt(jnp.mean(state * state, axis=-1, keepdims=True) + EPS)
            copies = store_rows(state_ref, state_hbm, out_semaphores.at[0])
            norm_ref[...] = (state * scale).astype(BF)
            copies += store_rows(norm_ref, norm_hbm, out_semaphores.at[1])
            for copy in copies:
                copy.wait()

    whole = lambda s, order: (0, 0)
    return pl.pallas_call(
        kernel,
        grid_spec=pltpu.PrefetchScalarGridSpec(
            num_scalar_prefetch=1,
            grid=(n,),
            in_specs=[pl.BlockSpec((1, tok, width), lambda s, order: (order[s], 0, 0))]
            + any_specs(pieces)
            + [pl.BlockSpec((tok, D), whole)],
            out_specs=[pl.BlockSpec(memory_space=pltpu.HBM)] * 2,
            scratch_shapes=[
                pltpu.VMEM((n, width, D), BF),
                pltpu.SemaphoreType.DMA((n,)),
                pltpu.VMEM((tok, D), F32),
                pltpu.VMEM((tok, D), BF),
                pltpu.SemaphoreType.DMA((2, 4)),
            ],
        ),
        out_shape=[
            jax.ShapeDtypeStruct((tok, D), F32),
            jax.ShapeDtypeStruct((tok, D), BF),
        ],
        compiler_params=pltpu.CompilerParams(vmem_limit_bytes=VMEM_LIMIT),
        cost_estimate=SHORT,
        name="project_out",
    )(order, heads_in, *pieces, residual)


def feed_forward(pieces, weight):
    n = len(pieces)
    tok = 2 * pieces[0].shape[0]
    seq = n * tok // 2
    ff = weight.shape[1] // 2

    def kernel(*refs):
        parts = refs[:n]
        w_hbm, hidden_ref, factor_ref, all_hbm, buffer, semaphores, keep_semaphores, w_ref, w_semaphores = refs[n:]
        fetch_rows(w_hbm, w_ref, w_semaphores)
        x = fetch_piece(parts, buffer, semaphores, 2)
        keep_pieces(buffer, all_hbm, keep_semaphores, 2)
        both = nn(x, w_ref[...])
        gate = both[:, :ff]
        up = both[:, ff:]
        sig = jax.nn.sigmoid(gate)
        silu = gate * sig
        hidden_ref[...] = (silu * up).astype(BF)
        factor_ref[:, :ff] = (up * sig * (1.0 + gate * (1.0 - sig))).astype(BF)
        factor_ref[:, ff:] = silu.astype(BF)

    rows = lambda s: (s, 0)
    return pl.pallas_call(
        kernel,
        grid=(n // 2,),
        in_specs=any_specs(pieces) + [pl.BlockSpec(memory_space=pltpu.HBM)],
        out_specs=[
            pl.BlockSpec((tok, ff), rows),
            pl.BlockSpec((tok, 2 * ff), rows),
            pl.BlockSpec(memory_space=pltpu.HBM),
        ],
        scratch_shapes=[
            pltpu.VMEM((n, tok // 2, D), BF),
            pltpu.SemaphoreType.DMA((n,)),
            pltpu.SemaphoreType.DMA((n,)),
            pltpu.VMEM(weight.shape, BF),
            pltpu.SemaphoreType.DMA((chunks(D),)),
        ],
        out_shape=[
            jax.ShapeDtypeStruct((seq, ff), BF),
            jax.ShapeDtypeStruct((seq, 2 * ff), BF),
            jax.ShapeDtypeStruct((seq, D), BF),
        ],
        compiler_params=pltpu.CompilerParams(vmem_limit_bytes=VMEM_LIMIT),
        cost_estimate=LONG,
        name="feed_forward",
    )(*pieces, weight)


def feed_backward(factors, grads, weight):
    seq = factors.shape[0]
    ff = weight.shape[0]
    tok = 512

    def kernel(factor_ref, g_ref, w_hbm, out_ref, w_ref, w_semaphores, turned):
        fetch_rows(w_hbm, w_ref, w_semaphores)

        @pl.when(pl.program_id(0) == 0)
        def _():
            turned[...] = w_ref[...].T

        grad_hidden = nn(g_ref[...], turned[...])
        factor = factor_ref[...].astype(F32)
        out_ref[:, :ff] = (grad_hidden * factor[:, :ff]).astype(BF)
        out_ref[:, ff:] = (grad_hidden * factor[:, ff:]).astype(BF)

    rows = lambda s: (s, 0)
    return pl.pallas_call(
        kernel,
        grid=(seq // tok,),
        in_specs=[
            pl.BlockSpec((tok, 2 * ff), rows),
            pl.BlockSpec((tok, D), rows),
            pl.BlockSpec(memory_space=pltpu.HBM),
        ],
        out_specs=pl.BlockSpec((tok, 2 * ff), rows),
        scratch_shapes=[
            pltpu.VMEM(weight.shape, BF),
            pltpu.SemaphoreType.DMA((chunks(ff),)),
            pltpu.VMEM((D, ff), BF),
        ],
        out_shape=jax.ShapeDtypeStruct((seq, 2 * ff), BF),
        compiler_params=pltpu.CompilerParams(vmem_limit_bytes=VMEM_LIMIT),
        cost_estimate=LONG,
        name="feed_backward",
    )(factors, grads, weight)


def lay_out(pieces):
    n = len(pieces)
    tok = pieces[0].shape[0]

    def kernel(*refs):
        parts = refs[:n]
        out_ref, buffer, in_semaphores, out_semaphores = refs[n:]
        arrive = [
            pltpu.make_async_copy(part, buffer.at[i], in_semaphores.at[i])
            for i, part in enumerate(parts)
        ]
        leave = [
            pltpu.make_async_copy(buffer.at[i], out_ref.at[pl.ds(i * tok, tok)], out_semaphores.at[i])
            for i in range(n)
        ]
        for copy in arrive:
            copy.start()
        for i in range(n):
            arrive[i].wait()
            leave[i].start()
        for copy in leave:
            copy.wait()

    return pl.pallas_call(
        kernel,
        in_specs=any_specs(pieces),
        out_specs=pl.BlockSpec(memory_space=pltpu.HBM),
        scratch_shapes=[
            pltpu.VMEM((n, tok, D), BF),
            pltpu.SemaphoreType.DMA((n,)),
            pltpu.SemaphoreType.DMA((n,)),
        ],
        out_shape=jax.ShapeDtypeStruct((n * tok, D), BF),
        compiler_params=pltpu.CompilerParams(vmem_limit_bytes=VMEM_LIMIT),
        cost_estimate=SHORT,
        name="lay_out",
    )(*pieces)


def branch_back(order, d_two, state, out_grad, pieces):
    n = len(pieces)
    tok = d_two.shape[0]
    width = pieces[0].shape[0]

    def kernel(order_ref, d_ref, state_ref, g_ref, *refs):
        parts = refs[:n]
        grad_hbm, branch_hbm, heads_ref, buffer, semaphores, grad_ref, branch_ref, out_semaphores = refs[n:]

        @pl.when(pl.program_id(0) == 0)
        def _():
            state = state_ref[...]
            scale = lax.rsqrt(jnp.mean(state * state, axis=-1, keepdims=True) + EPS)
            norm = state * scale
            d = d_ref[...]
            grad = g_ref[...].astype(F32) + scale * (
                d - norm * jnp.mean(d * norm, axis=-1, keepdims=True)
            )
            grad_ref[...] = grad
            branch_ref[...] = grad.astype(BF)
            store_rows(grad_ref, grad_hbm, out_semaphores.at[0])
            store_rows(branch_ref, branch_hbm, out_semaphores.at[1])

        w = fetch_piece(parts, buffer, semaphores)
        heads_ref[0] = nt(branch_ref[...], w).astype(BF)

        @pl.when(pl.program_id(0) == n - 1)
        def _():
            for source, target, at in ((grad_ref, grad_hbm, 0), (branch_ref, branch_hbm, 1)):
                rows = tok // 4
                for i in range(4):
                    cut = pl.ds(i * rows, rows)
                    pltpu.make_async_copy(source.at[cut], target.at[cut], out_semaphores.at[at, i]).wait()

    whole = lambda s, order: (0, 0)
    return pl.pallas_call(
        kernel,
        grid_spec=pltpu.PrefetchScalarGridSpec(
            num_scalar_prefetch=1,
            grid=(n,),
            in_specs=[
                pl.BlockSpec((tok, D), whole),
                pl.BlockSpec((tok, D), whole),
                pl.BlockSpec((tok, D), whole),
            ]
            + any_specs(pieces),
            out_specs=[
                pl.BlockSpec(memory_space=pltpu.HBM),
                pl.BlockSpec(memory_space=pltpu.HBM),
                pl.BlockSpec((1, tok, width), lambda s, order: (order[s], 0, 0)),
            ],
            scratch_shapes=[
                pltpu.VMEM((n, width, D), BF),
                pltpu.SemaphoreType.DMA((n,)),
                pltpu.VMEM((tok, D), F32),
                pltpu.VMEM((tok, D), BF),
                pltpu.SemaphoreType.DMA((2, 4)),
            ],
        ),
        out_shape=[
            jax.ShapeDtypeStruct((tok, D), F32),
            jax.ShapeDtypeStruct((tok, D), BF),
            jax.ShapeDtypeStruct((n, tok, width), BF),
        ],
        compiler_params=pltpu.CompilerParams(vmem_limit_bytes=VMEM_LIMIT),
        cost_estimate=SHORT,
        name="branch_back",
    )(order, d_two, state, out_grad, *pieces)


def split_columns(weight, gain, n_ctx, n_dp, ff_rows):
    rows = weight.shape[0]
    ff = ff_rows * n_dp

    def kernel(w_ref, gain_ref, out_ref):
        gains = gain_ref[...]
        for part in range(2):
            for d in range(n_dp):
                for c in range(n_ctx):
                    at = part * FF + (d * n_ctx + c) * ff_rows
                    to = part * ff + d * ff_rows
                    values = w_ref[:, at : at + ff_rows].astype(F32) * gains
                    out_ref[c, :, to : to + ff_rows] = values.astype(BF)

    return pl.pallas_call(
        kernel,
        in_specs=[pl.BlockSpec(memory_space=pltpu.VMEM)] * 2,
        out_specs=pl.BlockSpec(memory_space=pltpu.VMEM),
        out_shape=jax.ShapeDtypeStruct((n_ctx, rows, 2 * ff), BF),
        compiler_params=pltpu.CompilerParams(vmem_limit_bytes=VMEM_LIMIT),
        cost_estimate=LONG,
        name="split_columns",
    )(weight, gain)


def join_columns(sums, weight, gain, n_dp, ff_rows):
    n_ctx, rows, both = sums.shape
    ff = both // 2

    def kernel(s_ref, w_ref, gain_ref, out_ref, gain_out_ref):
        gains = gain_ref[...]
        total = jnp.zeros((rows, ff_rows), F32)
        for part in range(2):
            for d in range(n_dp):
                for c in range(n_ctx):
                    at = part * ff + d * ff_rows
                    to = part * FF + (d * n_ctx + c) * ff_rows
                    values = s_ref[c, :, at : at + ff_rows].astype(F32)
                    total = total + values * w_ref[:, to : to + ff_rows].astype(F32)
                    out_ref[:, to : to + ff_rows] = values * gains
        gain_out_ref[...] = jnp.sum(total, axis=1, keepdims=True)

    return pl.pallas_call(
        kernel,
        in_specs=[pl.BlockSpec(memory_space=pltpu.VMEM)] * 3,
        out_specs=[pl.BlockSpec(memory_space=pltpu.VMEM)] * 2,
        out_shape=[
            jax.ShapeDtypeStruct((rows, 2 * FF), F32),
            jax.ShapeDtypeStruct((rows, 1), F32),
        ],
        compiler_params=pltpu.CompilerParams(vmem_limit_bytes=VMEM_LIMIT),
        cost_estimate=LONG,
        name="join_columns",
    )(sums, weight, gain)


def lane_heads(rows, width):
    lane = lax.broadcasted_iota(jnp.int32, (rows, width), 1)
    return (lane % (width // 2)) // HALF


def attend_forward(slot_of, starts, queries, keys, values_t, heads, tok, first, count, before):
    seq, width = queries.shape
    blocks = seq // tok
    span = 2 * tok

    def kernel(slot_ref, start_ref, q_ref, k_ref, v_ref, *refs):
        attn_ref, slot_attn_ref, full_ref, lse_ref, scores = refs[len(before) :]
        block = first + pl.program_id(0)
        steps = (block + 2) // 2
        start = start_ref[...]
        here = block * tok + lax.broadcasted_iota(jnp.int32, (1, tok), 1)
        head_of = lane_heads(tok, width)
        q = q_ref[...]
        q_heads = [jnp.where(head_of == h, q, jnp.zeros_like(q)) for h in range(heads)]

        def score(i, peaks):
            rows = pl.ds(pl.multiple_of(i * span, span), span)
            k = k_ref[rows, :]
            there = i * span + lax.broadcasted_iota(jnp.int32, (span, tok), 0)
            visible = (there >= start) & (there <= here)
            out = []
            for h in range(heads):
                s = jnp.where(visible, nt(k, q_heads[h]), MASKED)
                scores[h, rows, :] = s
                out.append(jnp.maximum(peaks[h], jnp.max(s.reshape(span // 8, 8, tok), axis=0)))
            return tuple(out)

        peaks = lax.fori_loop(
            0, steps, score, tuple(jnp.full((8, tok), MASKED, F32) for _ in range(heads))
        )
        peaks = [jnp.max(peak, axis=0, keepdims=True) for peak in peaks]

        def weigh(i, running):
            rows = pl.ds(pl.multiple_of(i * span, span), span)
            v = v_ref[:, rows]
            out = []
            for h in range(heads):
                total, acc = running[h]
                p = jnp.exp(scores[h, rows, :] - peaks[h])
                total = total + jnp.sum(p.reshape(span // 8, 8, tok), axis=0)
                out.append((total, acc + nn(v, p.astype(BF))))
            return tuple(out)

        result = lax.fori_loop(
            0,
            steps,
            weigh,
            tuple((jnp.zeros((8, tok), F32), jnp.zeros((HD, tok), F32)) for _ in range(heads)),
        )
        rows = []
        for h in range(heads):
            total, acc = result[h]
            total = jnp.sum(total, axis=0, keepdims=True)
            rows.append(acc / total)
            lse_ref[0, h : h + 1, :] = peaks[h] + jnp.log(total)
        full = jnp.concatenate(rows, axis=0).T
        full_ref[...] = full
        attn_ref[...] = full.astype(BF)
        slot_attn_ref[...] = full.astype(BF)

    return pl.pallas_call(
        kernel,
        grid_spec=pltpu.PrefetchScalarGridSpec(
            num_scalar_prefetch=1,
            grid=(count,),
            in_specs=[
                pl.BlockSpec((1, tok), lambda j, slot: (0, first + j)),
                pl.BlockSpec((tok, width), lambda j, slot: (first + j, 0)),
                pl.BlockSpec((seq, width), lambda j, slot: (0, 0)),
                pl.BlockSpec((HD, seq), lambda j, slot: (0, 0)),
            ]
            + [pl.BlockSpec(memory_space=pltpu.HBM)] * len(before),
            out_specs=[
                pl.BlockSpec((tok, width), lambda j, slot: (first + j, 0)),
                pl.BlockSpec((tok, width), lambda j, slot: (slot[first + j], 0)),
                pl.BlockSpec((tok, width), lambda j, slot: (first + j, 0)),
                pl.BlockSpec((1, heads, tok), lambda j, slot: (first + j, 0, 0)),
            ],
            scratch_shapes=[pltpu.VMEM((heads, seq, tok), F32)],
        ),
        out_shape=[
            jax.ShapeDtypeStruct((seq, width), BF),
            jax.ShapeDtypeStruct((seq, width), BF),
            jax.ShapeDtypeStruct((seq, width), F32),
            jax.ShapeDtypeStruct((blocks, heads, tok), F32),
        ],
        input_output_aliases={5 + i: i for i in range(len(before))},
        compiler_params=pltpu.CompilerParams(vmem_limit_bytes=VMEM_LIMIT),
        cost_estimate=LONG,
        name="attend_forward",
    )(slot_of, starts, queries, keys, values_t, *before)


def attend_backward(
    slot_of, starts, queries, keys, keys_t, values, grads, full, lse, cosine, sine, unsplit, heads, tok
):
    seq, width = queries.shape
    blocks = seq // tok
    span = 2 * tok
    half = width // 2

    def kernel(
        slot_ref, start_ref, q_ref, k_ref, kt_ref, v_ref, g_ref, full_ref, lse_ref, cos_ref, sin_ref, unsplit_ref,
        out_ref, dk, dv,
    ):
        block = pl.program_id(0)
        steps = (block + 2) // 2

        @pl.when(block == 0)
        def _():
            dk[...] = jnp.zeros_like(dk)
            dv[...] = jnp.zeros_like(dv)

        start = start_ref[...]
        here = block * tok + lax.broadcasted_iota(jnp.int32, (1, tok), 1)
        head_of = lane_heads(tok, width)
        wide = lax.broadcasted_iota(jnp.int32, (tok, width), 1) // HD
        q = q_ref[...]
        g = g_ref[...]
        q_heads = [jnp.where(head_of == h, q, jnp.zeros_like(q)) for h in range(heads)]
        g_heads = [jnp.where(wide == h, g, jnp.zeros_like(g)) for h in range(heads)]
        q_stack = jnp.concatenate(q_heads, axis=0)
        g_stack = jnp.concatenate(g_heads, axis=0)
        picks = (
            lax.broadcasted_iota(jnp.int32, (8, width), 1) // HD
            == lax.broadcasted_iota(jnp.int32, (8, width), 0)
        ).astype(F32)
        deltas = lax.dot_general(
            picks,
            g.astype(F32) * full_ref[...],
            (((1,), (1,)), ((), ())),
            preferred_element_type=F32,
            precision=lax.Precision.HIGHEST,
        )

        def step(i, dq):
            rows = pl.ds(pl.multiple_of(i * span, span), span)
            k = k_ref[rows, :]
            v = v_ref[rows, :]
            kt = kt_ref[:, rows]
            there = i * span + lax.broadcasted_iota(jnp.int32, (span, tok), 0)
            visible = (there >= start) & (there <= here)
            probs, grad_scores, out = [], [], []
            for h in range(heads):
                s = jnp.where(visible, nt(k, q_heads[h]), MASKED)
                p = jnp.exp(s - lse_ref[0, h : h + 1, :])
                ds = (p * (nt(v, g_heads[h]) - deltas[h : h + 1, :])).astype(BF)
                probs.append(p.astype(BF))
                grad_scores.append(ds)
                out.append(dq[h] + nn(kt, ds))
            dv[rows, :] += nn(jnp.concatenate(probs, axis=1), g_stack)
            dk[rows, :] += nn(jnp.concatenate(grad_scores, axis=1), q_stack)
            return tuple(out)

        dq = lax.fori_loop(
            0, steps, step, tuple(jnp.zeros((HD, tok), F32) for _ in range(heads))
        )
        dq = jnp.concatenate([x[:HALF] for x in dq] + [x[HALF:] for x in dq], axis=0).T
        here_rows = pl.ds(pl.multiple_of(block * tok, tok), tok)
        cos, sin = turn_tables(cos_ref[here_rows, :], sin_ref[here_rows, :], width)
        dq = (dq * cos - swap_halves(dq) * sin) * (HD**-0.5)
        slot_rows = pl.ds(pl.multiple_of(slot_ref[block] * tok, tok), tok)
        out_ref[slot_rows, :width] = nn(dq.astype(BF), unsplit_ref[...]).astype(BF)

        @pl.when(block == blocks - 1)
        def _():
            lane = lax.broadcasted_iota(jnp.int32, (width, 128), 0)
            column = lax.broadcasted_iota(jnp.int32, (width, 128), 1)
            fold_k = ((lane // half) * HALF + lane % HALF == column).astype(BF)
            fold_v = (lane % HD + HD == column).astype(BF)

            def fold(i, unused):
                rows = pl.ds(pl.multiple_of(i * tok, tok), tok)
                cos, sin = turn_tables(cos_ref[rows, :], sin_ref[rows, :], width)
                a = dk[rows, :]
                a = a * cos - swap_halves(a) * sin
                b = dv[rows, :]
                a_high = a.astype(BF)
                b_high = b.astype(BF)
                terms = (
                    nn(a_high, fold_k)
                    + nn((a - a_high.astype(F32)).astype(BF), fold_k)
                    + nn(b_high, fold_v)
                    + nn((b - b_high.astype(F32)).astype(BF), fold_v)
                )
                slot_rows = pl.ds(pl.multiple_of(slot_ref[i] * tok, tok), tok)
                out_ref[slot_rows, width:] = terms.astype(BF)
                return unused

            lax.fori_loop(0, blocks, fold, 0)

    whole = lambda shape: pl.BlockSpec(shape, lambda j, *_: (0, 0))
    return pl.pallas_call(
        kernel,
        grid_spec=pltpu.PrefetchScalarGridSpec(
            num_scalar_prefetch=1,
            grid=(blocks,),
            in_specs=[
                pl.BlockSpec((1, tok), lambda j, *_: (0, j)),
                pl.BlockSpec((tok, width), lambda j, *_: (j, 0)),
                whole((seq, width)),
                whole((HD, seq)),
                whole((seq, width)),
                pl.BlockSpec((tok, width), lambda j, *_: (j, 0)),
                pl.BlockSpec((tok, width), lambda j, *_: (j, 0)),
                pl.BlockSpec((1, heads, tok), lambda j, *_: (j, 0, 0)),
                whole((seq, 128)),
                whole((seq, 128)),
                whole((width, width)),
            ],
            out_specs=whole((seq, width + 128)),
            scratch_shapes=[pltpu.VMEM((seq, width), F32), pltpu.VMEM((seq, width), F32)],
        ),
        out_shape=jax.ShapeDtypeStruct((seq, width + 128), BF),
        compiler_params=pltpu.CompilerParams(vmem_limit_bytes=VMEM_LIMIT),
        cost_estimate=MEDIUM,
        name="attend_backward",
    )(slot_of, starts, queries, keys, keys_t, values, grads, full, lse, cosine, sine, unsplit)


def outer_rows(activations, gradients):
    return lax.dot_general(
        activations, gradients, (((0,), (0,)), ((), ())), preferred_element_type=F32
    ).astype(BF)


def split_source(width):
    lane = np.arange(width)
    half = lane // (width // 2)
    head = (lane % (width // 2)) // HALF
    return head * HD + half * HALF + lane % HALF


def spread_matrix(width):
    matrix = np.zeros((width + 2 * HD, width + 256), np.float32)
    lane = np.arange(width)
    matrix[split_source(width), lane] = 1
    lane = np.arange(2 * HD)
    matrix[width + lane, width + lane] = 1
    lane = np.arange(HD)
    matrix[width + (lane + HALF) % HD, width + 128 + lane] = 1
    return jnp.asarray(matrix, BF)


def widen_matrix(width):
    matrix = np.zeros((2 * HD, 2 * width), np.float32)
    lane = np.arange(width)
    matrix[(lane // (width // 2)) * HALF + lane % HALF, lane] = 1
    matrix[HD + lane % HD, width + lane] = 1
    return jnp.asarray(matrix, BF)


def unsplit_matrix(width):
    matrix = np.zeros((width, width), np.float32)
    matrix[np.arange(width), split_source(width)] = 1
    return jnp.asarray(matrix, BF)


def on_device(
    block_in,
    gain_attn,
    qkv_weight,
    out_weight,
    gain_ffn,
    gate_up_weight,
    down_weight,
    doc_lengths,
    out_grad,
):
    n_ctx = lax.axis_size("ctx")
    n_dp = lax.axis_size("dp")
    me = lax.axis_index("ctx")
    tok = block_in.shape[0]
    seq = tok * n_ctx
    heads = H // n_ctx
    width = heads * HD
    sharers = n_ctx // KVH
    rows = qkv_weight.shape[0]
    ff_rows = down_weight.shape[0]
    ff = ff_rows * n_dp
    columns = width + 2 * HD

    order = me ^ jnp.where(me % 2 == 0, *[jnp.asarray(t) for t in slot_table(n_ctx)])
    slots = jnp.arange(n_ctx, dtype=jnp.int32)
    slot_of = jnp.sum(jnp.where(order[None, :] == slots[:, None], slots[None, :], 0), axis=1)
    index = jnp.arange(seq, dtype=jnp.int32)
    lengths = doc_lengths[0]
    ends = jnp.cumsum(lengths)
    starts = jnp.sum((index[:, None] >= ends[None, :]).astype(jnp.int32) * lengths[None, :], axis=1)
    lane = jnp.arange(128, dtype=F32) % HALF
    frequency = 10000.0 ** (-lane * 2.0 / HD)
    angles = (index - starts).astype(F32)[:, None] * frequency[None, :]
    cosine = jnp.cos(angles)
    sine = jnp.sin(angles)
    starts_row = starts[None, :]

    gain_one = gain_attn.astype(F32)[:, None]
    gain_two = gain_ffn.astype(F32)[:, None]
    qkv = (qkv_weight.astype(F32) * gain_one).astype(BF)
    q_cols = qkv[:, : H * HD].reshape(rows, n_ctx, width).transpose(1, 0, 2)
    k_cols = qkv[:, H * HD : (H + KVH) * HD].reshape(rows, KVH, HD).transpose(1, 0, 2)
    v_cols = qkv[:, (H + KVH) * HD :].reshape(rows, KVH, HD).transpose(1, 0, 2)
    kv_cols = jnp.repeat(jnp.concatenate([k_cols, v_cols], axis=2), sharers, axis=0)
    owner_pairs = [(b, b % n_dp * n_ctx + b // n_dp) for b in range(n_dp * n_ctx)]
    out_own = lax.ppermute(out_weight, ("dp", "ctx"), owner_pairs)
    out_part = gather_dp(out_own)
    qkv_own = exchange(jnp.concatenate([q_cols, kv_cols], axis=2)).reshape(n_ctx * rows, columns)
    qkv_part = gather_dp(qkv_own)

    hidden_in = block_in.astype(F32)
    rms_one = lax.rsqrt(jnp.mean(hidden_in * hidden_in, axis=-1, keepdims=True) + EPS)
    one_pieces = gather_slots(after((hidden_in * rms_one).astype(BF), qkv_own, out_own), n_ctx)

    gate_up_cols = split_columns(
        gate_up_weight, after(gain_two, cosine, sine), n_ctx, n_dp, ff_rows
    )
    gate_up_own = exchange(after(gate_up_cols, *one_pieces[: n_ctx // 2])).reshape(
        n_ctx * rows, 2 * ff
    )
    gate_up_part = gather_dp(gate_up_own)
    down_part = gather_dp(after(down_weight, gate_up_own))

    queries, keys, values, keys_t, values_t, all_one = project_qkv(
        order, one_pieces, qkv_part, spread_matrix(width), widen_matrix(width), cosine, sine, width, tok
    )
    out_direct = gather_direct(out_part, n_ctx)
    attn, slot_attn, attended, lse = attend_forward(
        slot_of, starts_row, after(queries, gate_up_own, *out_direct), keys, values_t, heads, tok, 0, n_ctx, ()
    )
    attn_tokens = exchange(attn.reshape(n_ctx, tok, width))
    out_pieces = gather_rest(out_direct, n_ctx, (queries,), (attn,))
    state, norm_two = project_out(order, attn_tokens, out_pieces, block_in)

    two_pieces = gather_slots(norm_two, n_ctx)
    grad_direct = gather_direct(after(out_grad, *two_pieces), n_ctx)
    hidden, factors, all_two = feed_forward(two_pieces, gate_up_part)
    grad_pieces = gather_rest(grad_direct, n_ctx, (hidden,))
    all_grad = lay_out(grad_pieces)
    down_terms = outer_rows(hidden, all_grad)
    down_sums = scatter_dp(down_terms)
    grad_gate_up = feed_backward(after(factors, down_terms), all_grad, down_part)

    def rows_of(x, lo, hi):
        return lax.slice_in_dim(x, lo * tok, hi * tok, axis=0)

    d_pairs, _ = scatter_pairs(
        lambda lo, hi: nt(rows_of(grad_gate_up, lo, hi), gate_up_part), tok, n_ctx
    )
    stages = tuple(reversed(range(len(walk(n_ctx, 0)))))
    d_two = scatter_chips(*d_pairs, stages, n_ctx)
    hidden_pairs, _ = scatter_pairs(
        lambda lo, hi: nn(rows_of(after(hidden, *d_pairs), lo, hi), down_part), tok, n_ctx
    )
    gate_up_terms = outer_rows(after(all_two, *d_pairs), grad_gate_up)
    gate_up_sums = scatter_dp(gate_up_terms)

    grad_state, grad_branch, grad_heads = branch_back(
        order, after(d_two, gate_up_terms, *hidden_pairs), state, out_grad, out_pieces
    )
    grad_attn = exchange(grad_heads).reshape(seq, width)
    branch_here, branch_there = gather_at_once(after(grad_branch, grad_attn), n_ctx)
    hidden_upper, hidden_lower = hidden_pairs
    hidden_arrived = swap_stage(after(hidden_upper.astype(BF), grad_attn), n_ctx, stages[0])
    grad_mixed = attend_backward(
        slot_of,
        starts_row,
        queries,
        keys,
        keys_t,
        values,
        grad_attn,
        attended,
        lse,
        cosine,
        sine,
        unsplit_matrix(width),
        heads,
        tok,
    )
    qkv_terms = outer_rows(all_one, grad_mixed)
    qkv_sums = scatter_dp(after(qkv_terms, gate_up_sums))
    one_pairs, _ = scatter_pairs(
        lambda lo, hi: nt(
            rows_of(after(grad_mixed, qkv_terms, hidden_arrived, *branch_here), lo, hi), qkv_part
        ),
        tok,
        n_ctx,
    )
    d_one = scatter_chips(*one_pairs, stages, n_ctx)
    hidden_sums = scatter_rest(hidden_lower, hidden_arrived, stages, n_ctx)
    block_out = (state + hidden_sums).astype(BF)
    out_terms = outer_rows(slot_attn, after(lay_out(branch_here + branch_there), qkv_terms))
    out_sums = scatter_dp(after(out_terms, qkv_sums))
    norm_one = hidden_in * rms_one
    input_grad = grad_state + rms_one * (
        d_one - norm_one * jnp.mean(d_one * norm_one, axis=-1, keepdims=True)
    )

    down_weight_grad = after(down_sums, grad_mixed).astype(F32)
    out_weight_grad = lax.ppermute(
        out_sums, ("dp", "ctx"), [(b, a) for a, b in owner_pairs]
    ).astype(F32)
    gate_up_weight_grad, gain_ffn_grad = join_columns(
        exchange(after(gate_up_sums, grad_mixed).reshape(n_ctx, rows, 2 * ff)), gate_up_weight, gain_two, n_dp, ff_rows
    )
    qkv_back = exchange(qkv_sums.reshape(n_ctx, rows, columns)).astype(F32)
    q_back = qkv_back[:, :, :width].transpose(1, 0, 2).reshape(rows, H * HD)
    kv_back = jnp.sum(qkv_back[:, :, width:].reshape(KVH, sharers, rows, 2 * HD), axis=1)
    k_back = kv_back[:, :, :HD].transpose(1, 0, 2).reshape(rows, KVH * HD)
    v_back = kv_back[:, :, HD:].transpose(1, 0, 2).reshape(rows, KVH * HD)
    qkv_back = jnp.concatenate([q_back, k_back, v_back], axis=1)
    qkv_weight_grad = qkv_back * gain_one
    gain_attn_grad = jnp.sum(qkv_back * qkv_weight.astype(F32), axis=1)
    return (
        block_out,
        input_grad,
        gain_attn_grad,
        qkv_weight_grad,
        out_weight_grad,
        gain_ffn_grad[:, 0],
        gate_up_weight_grad,
        down_weight_grad,
    )


def solution(mesh):
    rows = P(("dp", "ctx"), None)
    entries = P(("dp", "ctx"))
    return jax.shard_map(
        on_device,
        mesh=mesh,
        in_specs=(rows, entries, rows, rows, entries, rows, rows, P("dp", None), rows),
        out_specs=(rows, rows, entries, rows, rows, entries, rows, rows),
        check_vma=False,
    )
```

```python
import jax
import jax.numpy as jnp
import numpy as np
from jax import lax
from jax.experimental import pallas as pl
from jax.experimental.pallas import tpu as pltpu
from jax.sharding import PartitionSpec as P

D = 2048
H = 32
KVH = 4
HD = 64
FF = 5632
HALF = HD // 2

EPS = 1e-05
MASKED = -1e30
BF = jnp.bfloat16
F32 = jnp.float32
VMEM_LIMIT = 60 << 20
SHORT = pl.CostEstimate(flops=1 << 20, bytes_accessed=1 << 20, transcendentals=0)
MEDIUM = pl.CostEstimate(flops=2 * 10**10, bytes_accessed=1 << 20, transcendentals=0)
LONG = pl.CostEstimate(flops=10**11, bytes_accessed=1 << 20, transcendentals=0)


def nt(a, b):
    return lax.dot_general(a, b, (((1,), (1,)), ((), ())), preferred_element_type=F32)


def nn(a, b):
    return jnp.dot(a, b, preferred_element_type=F32)


def after(x, *earlier):
    return lax.optimization_barrier((x, *earlier))[0]


def after_each(values, *earlier):
    count = len(values)
    return lax.optimization_barrier((*values, *earlier))[:count]


def walk(n_ctx, parity):
    bits = []
    bit = 2
    while bit < n_ctx:
        bits.append(bit)
        bit *= 2
    return bits if parity == 0 else bits[::-1]


def swap_stage(x, n_ctx, stage):
    pairs = [(c, c ^ walk(n_ctx, c % 2)[stage]) for c in range(n_ctx)]
    return lax.ppermute(x, "ctx", pairs)


def swap_core(x, n_ctx):
    return lax.ppermute(x, "ctx", [(c, c ^ 1) for c in range(n_ctx)])


def slot_table(n_ctx):
    lists = []
    for parity in (0, 1):
        row = [0]
        for bit in walk(n_ctx, parity):
            row = row + [v ^ bit for v in row]
        lists.append(row)
    return np.array(
        [lists[p] + [v ^ 1 for v in lists[1 - p]] for p in (0, 1)], dtype=np.int32
    )


def gather_direct(x, n_ctx):
    return [x] + [swap_stage(x, n_ctx, stage) for stage in range(len(walk(n_ctx, 0)))]


def gather_rest(direct, n_ctx, earlier=(), last=()):
    have = direct[:1]
    for stage in range(len(walk(n_ctx, 0))):
        passed = [after(block, *earlier) if earlier else block for block in have[1:]]
        have = have + [direct[stage + 1]] + [swap_stage(block, n_ctx, stage) for block in passed]
    return have + [swap_core(after(block, *last) if last else block, n_ctx) for block in have]


def gather_at_once(x, n_ctx):
    have = [x]
    table = slot_table(n_ctx)
    for slot in range(1, n_ctx // 2):
        pairs = [(c, c ^ int(table[c % 2][slot])) for c in range(n_ctx)]
        have.append(lax.ppermute(x, "ctx", pairs))
    return have, [swap_core(block, n_ctx) for block in have]


def gather_slots(x, n_ctx):
    return gather_rest(gather_direct(x, n_ctx), n_ctx)


def scatter_pairs(term, tok, n_ctx):
    mine = n_ctx // 2
    cut = mine // 2
    sums, arrivals = [], []
    for lo, hi in ((cut, mine), (0, cut)):
        arrivals.append(swap_core(term(mine + lo, mine + hi).astype(BF), n_ctx))
        sums.append(term(lo, hi) + arrivals[-1].astype(F32))
    return sums, arrivals


def scatter_chips(upper, lower, stages, n_ctx, *earlier):
    for stage in stages:
        if earlier and stage == 0:
            upper = after(upper.astype(BF), *earlier)
        lower = lower + swap_stage(upper.astype(BF), n_ctx, stage).astype(F32)
        if stage:
            half = lower.shape[0] // 2
            upper, lower = lower[half:], lower[:half]
    return lower if stages[-1] == 0 else (upper, lower)


def scatter_rest(lower, arrived, stages, n_ctx):
    sums = lower + arrived.astype(F32)
    if len(stages) == 1:
        return sums
    half = sums.shape[0] // 2
    return scatter_chips(sums[half:], sums[:half], stages[1:], n_ctx)


def exchange(x):
    return lax.all_to_all(x, "ctx", split_axis=0, concat_axis=0, tiled=False)


def gather_dp(x):
    return lax.all_gather(x, "dp", axis=0, tiled=True)


def scatter_dp(x):
    return lax.psum_scatter(x, "dp", scatter_dimension=0, tiled=True)


def fetch_piece(pieces, buffer, semaphores, count=1):
    step = pl.program_id(0)

    @pl.when(step == 0)
    def _():
        for i, piece in enumerate(pieces):
            pltpu.make_async_copy(piece, buffer.at[i], semaphores.at[i]).start()

    for i in range(count):
        at = step * count + i
        pltpu.make_async_copy(pieces[0], buffer.at[at], semaphores.at[at]).wait()
    if count == 1:
        return buffer[step]
    return buffer[pl.ds(step * count, count)].reshape(count * buffer.shape[1], buffer.shape[2])


def keep_pieces(buffer, target, semaphores):
    step = pl.program_id(0)
    total, tok = buffer.shape[0], buffer.shape[1]

    def copy(at):
        rows = pl.ds(pl.multiple_of(at * tok, tok), tok)
        return pltpu.make_async_copy(buffer.at[at], target.at[rows], semaphores.at[at])

    copy(step).start()

    @pl.when(step == total - 1)
    def _():
        for i in range(total):
            copy(i).wait()


def store_rows(source, target, semaphores):
    count = semaphores.shape[0]
    rows = source.shape[0] // count
    copies = [
        pltpu.make_async_copy(
            source.at[pl.ds(i * rows, rows)], target.at[pl.ds(i * rows, rows)], semaphores.at[i]
        )
        for i in range(count)
    ]
    for copy in copies:
        copy.start()
    return copies


def chunks(rows):
    return next(count for count in (8, 4, 2, 1) if rows % (16 * count) == 0)


def fetch_rows(source, buffer, semaphores):
    count = semaphores.shape[0]
    rows = source.shape[0] // count

    @pl.when(pl.program_id(0) == 0)
    def _():
        copies = [
            pltpu.make_async_copy(
                source.at[pl.ds(i * rows, rows)], buffer.at[pl.ds(i * rows, rows)], semaphores.at[i]
            )
            for i in range(count)
        ]
        for copy in copies:
            copy.start()
        for copy in copies:
            copy.wait()


def swap_halves(x):
    return pltpu.roll(x, x.shape[1] // 2, axis=1)


def turn_tables(cosine, sine, width):
    times = width // 128
    cosine = jnp.concatenate([cosine] * times, axis=1) if times > 1 else cosine
    sine = jnp.concatenate([sine] * times, axis=1) if times > 1 else sine
    lane = lax.broadcasted_iota(jnp.int32, sine.shape, 1)
    return cosine, jnp.where(lane < width // 2, -sine, sine)


def any_specs(pieces):
    return [pl.BlockSpec(memory_space=pltpu.HBM) for _ in pieces]


def project_qkv(order, pieces, weight, spread, widen, cosine, sine, width, tok):
    n = len(pieces)
    seq = n * tok

    def kernel(order_ref, *refs):
        parts = refs[:n]
        w_hbm, spread_ref, widen_ref, cos_ref, sin_ref = refs[n : n + 5]
        (
            q_ref, k_ref, v_ref, kt_ref, vt_ref, all_hbm, wide, buffer, semaphores, keep_semaphores, w_ref, w_semaphores
        ) = refs[n + 5 :]
        fetch_rows(w_hbm, w_ref, w_semaphores)

        @pl.when(pl.program_id(0) == 0)
        def _():
            wide[...] = nn(w_ref[...], spread_ref[...]).astype(BF)

        x = fetch_piece(parts, buffer, semaphores)
        keep_pieces(buffer, all_hbm, keep_semaphores)
        mixed = nn(x, wide[...])
        cos, sin = turn_tables(cos_ref[...], sin_ref[...], width)
        q = mixed[:, :width]
        q_ref[...] = (q * cos + swap_halves(q) * sin).astype(BF) * (HD**-0.5)
        lane = lax.broadcasted_iota(jnp.int32, (tok, 128), 1)
        key_sine = jnp.where(lane < HALF, -sin_ref[...], sin_ref[...])
        both = jnp.where(
            lane < HD,
            mixed[:, width : width + 128] * cos_ref[...] + mixed[:, width + 128 :] * key_sine,
            mixed[:, width : width + 128],
        ).astype(BF)
        repeated = nn(both, widen_ref[...]).astype(BF)
        k_ref[...] = repeated[:, :width]
        v_ref[...] = repeated[:, width:]
        turned = both.T
        kt_ref[...] = turned[:HD]
        vt_ref[...] = turned[HD:]

    rows = lambda s, order: (order[s], 0)
    lanes = lambda s, order: (0, order[s])
    whole = lambda s, order: (0, 0)
    return pl.pallas_call(
        kernel,
        grid_spec=pltpu.PrefetchScalarGridSpec(
            num_scalar_prefetch=1,
            grid=(n,),
            in_specs=any_specs(pieces)
            + [
                pl.BlockSpec(memory_space=pltpu.HBM),
                pl.BlockSpec(spread.shape, whole),
                pl.BlockSpec(widen.shape, whole),
                pl.BlockSpec((tok, 128), rows),
                pl.BlockSpec((tok, 128), rows),
            ],
            out_specs=[
                pl.BlockSpec((tok, width), rows),
                pl.BlockSpec((tok, width), rows),
                pl.BlockSpec((tok, width), rows),
                pl.BlockSpec((HD, tok), lanes),
                pl.BlockSpec((HD, tok), lanes),
                pl.BlockSpec(memory_space=pltpu.HBM),
            ],
            scratch_shapes=[
                pltpu.VMEM((D, width + 256), BF),
                pltpu.VMEM((n, tok, D), BF),
                pltpu.SemaphoreType.DMA((n,)),
                pltpu.SemaphoreType.DMA((n,)),
                pltpu.VMEM(weight.shape, BF),
                pltpu.SemaphoreType.DMA((chunks(D),)),
            ],
        ),
        out_shape=[
            jax.ShapeDtypeStruct((seq, width), BF),
            jax.ShapeDtypeStruct((seq, width), BF),
            jax.ShapeDtypeStruct((seq, width), BF),
            jax.ShapeDtypeStruct((HD, seq), BF),
            jax.ShapeDtypeStruct((HD, seq), BF),
            jax.ShapeDtypeStruct((seq, D), BF),
        ],
        compiler_params=pltpu.CompilerParams(vmem_limit_bytes=VMEM_LIMIT),
        cost_estimate=LONG,
        name="project_qkv",
    )(order, *pieces, weight, spread, widen, cosine, sine)


def project_out(order, heads_in, pieces, residual):
    n, tok, width = heads_in.shape

    def kernel(order_ref, a_ref, *refs):
        parts = refs[:n]
        x_ref, state_hbm, norm_hbm, buffer, semaphores, state_ref, norm_ref, out_semaphores = refs[n:]
        step = pl.program_id(0)
        w = fetch_piece(parts, buffer, semaphores)

        @pl.when(step == 0)
        def _():
            state_ref[...] = x_ref[...].astype(F32)

        state_ref[...] += nn(a_ref[0], w)

        @pl.when(step == n - 1)
        def _():
            state = state_ref[...]
            scale = lax.rsqrt(jnp.mean(state * state, axis=-1, keepdims=True) + EPS)
            copies = store_rows(state_ref, state_hbm, out_semaphores.at[0])
            norm_ref[...] = (state * scale).astype(BF)
            copies += store_rows(norm_ref, norm_hbm, out_semaphores.at[1])
            for copy in copies:
                copy.wait()

    whole = lambda s, order: (0, 0)
    return pl.pallas_call(
        kernel,
        grid_spec=pltpu.PrefetchScalarGridSpec(
            num_scalar_prefetch=1,
            grid=(n,),
            in_specs=[pl.BlockSpec((1, tok, width), lambda s, order: (order[s], 0, 0))]
            + any_specs(pieces)
            + [pl.BlockSpec((tok, D), whole)],
            out_specs=[pl.BlockSpec(memory_space=pltpu.HBM)] * 2,
            scratch_shapes=[
                pltpu.VMEM((n, width, D), BF),
                pltpu.SemaphoreType.DMA((n,)),
                pltpu.VMEM((tok, D), F32),
                pltpu.VMEM((tok, D), BF),
                pltpu.SemaphoreType.DMA((2, 4)),
            ],
        ),
        out_shape=[
            jax.ShapeDtypeStruct((tok, D), F32),
            jax.ShapeDtypeStruct((tok, D), BF),
        ],
        compiler_params=pltpu.CompilerParams(vmem_limit_bytes=VMEM_LIMIT),
        cost_estimate=SHORT,
        name="project_out",
    )(order, heads_in, *pieces, residual)


def feed_forward(pieces, weight):
    n = len(pieces)
    tok = 2 * pieces[0].shape[0]
    seq = n * tok // 2
    ff = weight.shape[1] // 2

    def kernel(*refs):
        parts = refs[:n]
        w_hbm, hidden_ref, factor_ref, all_ref, buffer, semaphores, w_ref, w_semaphores = refs[n:]
        fetch_rows(w_hbm, w_ref, w_semaphores)
        x = fetch_piece(parts, buffer, semaphores, 2)
        all_ref[...] = x
        both = nn(x, w_ref[...])
        gate = both[:, :ff]
        up = both[:, ff:]
        sig = jax.nn.sigmoid(gate)
        silu = gate * sig
        hidden_ref[...] = (silu * up).astype(BF)
        factor_ref[:, :ff] = (up * sig * (1.0 + gate * (1.0 - sig))).astype(BF)
        factor_ref[:, ff:] = silu.astype(BF)

    rows = lambda s: (s, 0)
    return pl.pallas_call(
        kernel,
        grid=(n // 2,),
        in_specs=any_specs(pieces) + [pl.BlockSpec(memory_space=pltpu.HBM)],
        out_specs=[
            pl.BlockSpec((tok, ff), rows),
            pl.BlockSpec((tok, 2 * ff), rows),
            pl.BlockSpec((tok, D), rows),
        ],
        scratch_shapes=[
            pltpu.VMEM((n, tok // 2, D), BF),
            pltpu.SemaphoreType.DMA((n,)),
            pltpu.VMEM(weight.shape, BF),
            pltpu.SemaphoreType.DMA((chunks(D),)),
        ],
        out_shape=[
            jax.ShapeDtypeStruct((seq, ff), BF),
            jax.ShapeDtypeStruct((seq, 2 * ff), BF),
            jax.ShapeDtypeStruct((seq, D), BF),
        ],
        compiler_params=pltpu.CompilerParams(vmem_limit_bytes=VMEM_LIMIT),
        cost_estimate=LONG,
        name="feed_forward",
    )(*pieces, weight)


def feed_backward(factors, grads, weight):
    seq = factors.shape[0]
    ff = weight.shape[0]
    tok = 512

    def kernel(factor_ref, g_ref, w_hbm, out_ref, w_ref, w_semaphores, turned):
        fetch_rows(w_hbm, w_ref, w_semaphores)

        @pl.when(pl.program_id(0) == 0)
        def _():
            turned[...] = w_ref[...].T

        grad_hidden = nn(g_ref[...], turned[...])
        factor = factor_ref[...].astype(F32)
        out_ref[:, :ff] = (grad_hidden * factor[:, :ff]).astype(BF)
        out_ref[:, ff:] = (grad_hidden * factor[:, ff:]).astype(BF)

    rows = lambda s: (s, 0)
    return pl.pallas_call(
        kernel,
        grid=(seq // tok,),
        in_specs=[
            pl.BlockSpec((tok, 2 * ff), rows),
            pl.BlockSpec((tok, D), rows),
            pl.BlockSpec(memory_space=pltpu.HBM),
        ],
        out_specs=pl.BlockSpec((tok, 2 * ff), rows),
        scratch_shapes=[
            pltpu.VMEM(weight.shape, BF),
            pltpu.SemaphoreType.DMA((chunks(ff),)),
            pltpu.VMEM((D, ff), BF),
        ],
        out_shape=jax.ShapeDtypeStruct((seq, 2 * ff), BF),
        compiler_params=pltpu.CompilerParams(vmem_limit_bytes=VMEM_LIMIT),
        cost_estimate=LONG,
        name="feed_backward",
    )(factors, grads, weight)


def lay_out(pieces):
    n = len(pieces)
    tok = pieces[0].shape[0]

    def kernel(*refs):
        parts = refs[:n]
        out_ref, buffer, in_semaphores, out_semaphores = refs[n:]
        arrive = [
            pltpu.make_async_copy(part, buffer.at[i], in_semaphores.at[i])
            for i, part in enumerate(parts)
        ]
        leave = [
            pltpu.make_async_copy(buffer.at[i], out_ref.at[pl.ds(i * tok, tok)], out_semaphores.at[i])
            for i in range(n)
        ]
        for copy in arrive:
            copy.start()
        for i in range(n):
            arrive[i].wait()
            leave[i].start()
        for copy in leave:
            copy.wait()

    return pl.pallas_call(
        kernel,
        in_specs=any_specs(pieces),
        out_specs=pl.BlockSpec(memory_space=pltpu.HBM),
        scratch_shapes=[
            pltpu.VMEM((n, tok, D), BF),
            pltpu.SemaphoreType.DMA((n,)),
            pltpu.SemaphoreType.DMA((n,)),
        ],
        out_shape=jax.ShapeDtypeStruct((n * tok, D), BF),
        compiler_params=pltpu.CompilerParams(vmem_limit_bytes=VMEM_LIMIT),
        cost_estimate=SHORT,
        name="lay_out",
    )(*pieces)


def branch_back(order, d_two, state, out_grad, pieces):
    n = len(pieces)
    tok = d_two.shape[0]
    width = pieces[0].shape[0]

    def kernel(order_ref, d_ref, state_ref, g_ref, *refs):
        parts = refs[:n]
        grad_hbm, branch_hbm, heads_ref, buffer, semaphores, grad_ref, branch_ref, out_semaphores = refs[n:]

        @pl.when(pl.program_id(0) == 0)
        def _():
            state = state_ref[...]
            scale = lax.rsqrt(jnp.mean(state * state, axis=-1, keepdims=True) + EPS)
            norm = state * scale
            d = d_ref[...]
            grad = g_ref[...].astype(F32) + scale * (
                d - norm * jnp.mean(d * norm, axis=-1, keepdims=True)
            )
            grad_ref[...] = grad
            branch_ref[...] = grad.astype(BF)
            store_rows(grad_ref, grad_hbm, out_semaphores.at[0])
            store_rows(branch_ref, branch_hbm, out_semaphores.at[1])

        w = fetch_piece(parts, buffer, semaphores)
        heads_ref[0] = nt(branch_ref[...], w).astype(BF)

        @pl.when(pl.program_id(0) == n - 1)
        def _():
            for source, target, at in ((grad_ref, grad_hbm, 0), (branch_ref, branch_hbm, 1)):
                rows = tok // 4
                for i in range(4):
                    cut = pl.ds(i * rows, rows)
                    pltpu.make_async_copy(source.at[cut], target.at[cut], out_semaphores.at[at, i]).wait()

    whole = lambda s, order: (0, 0)
    return pl.pallas_call(
        kernel,
        grid_spec=pltpu.PrefetchScalarGridSpec(
            num_scalar_prefetch=1,
            grid=(n,),
            in_specs=[
                pl.BlockSpec((tok, D), whole),
                pl.BlockSpec((tok, D), whole),
                pl.BlockSpec((tok, D), whole),
            ]
            + any_specs(pieces),
            out_specs=[
                pl.BlockSpec(memory_space=pltpu.HBM),
                pl.BlockSpec(memory_space=pltpu.HBM),
                pl.BlockSpec((1, tok, width), lambda s, order: (order[s], 0, 0)),
            ],
            scratch_shapes=[
                pltpu.VMEM((n, width, D), BF),
                pltpu.SemaphoreType.DMA((n,)),
                pltpu.VMEM((tok, D), F32),
                pltpu.VMEM((tok, D), BF),
                pltpu.SemaphoreType.DMA((2, 4)),
            ],
        ),
        out_shape=[
            jax.ShapeDtypeStruct((tok, D), F32),
            jax.ShapeDtypeStruct((tok, D), BF),
            jax.ShapeDtypeStruct((n, tok, width), BF),
        ],
        compiler_params=pltpu.CompilerParams(vmem_limit_bytes=VMEM_LIMIT),
        cost_estimate=SHORT,
        name="branch_back",
    )(order, d_two, state, out_grad, *pieces)


def split_columns(weight, gain, n_ctx, n_dp, ff_rows):
    rows = weight.shape[0]
    ff = ff_rows * n_dp

    def kernel(w_ref, gain_ref, out_ref):
        gains = gain_ref[...]
        for part in range(2):
            for d in range(n_dp):
                for c in range(n_ctx):
                    at = part * FF + (d * n_ctx + c) * ff_rows
                    to = part * ff + d * ff_rows
                    values = w_ref[:, at : at + ff_rows].astype(F32) * gains
                    out_ref[c, :, to : to + ff_rows] = values.astype(BF)

    return pl.pallas_call(
        kernel,
        in_specs=[pl.BlockSpec(memory_space=pltpu.VMEM)] * 2,
        out_specs=pl.BlockSpec(memory_space=pltpu.VMEM),
        out_shape=jax.ShapeDtypeStruct((n_ctx, rows, 2 * ff), BF),
        compiler_params=pltpu.CompilerParams(vmem_limit_bytes=VMEM_LIMIT),
        cost_estimate=LONG,
        name="split_columns",
    )(weight, gain)


def join_columns(sums, weight, gain, n_dp, ff_rows):
    n_ctx, rows, both = sums.shape
    ff = both // 2

    def kernel(s_ref, w_ref, gain_ref, out_ref, gain_out_ref):
        gains = gain_ref[...]
        total = jnp.zeros((rows, ff_rows), F32)
        for part in range(2):
            for d in range(n_dp):
                for c in range(n_ctx):
                    at = part * ff + d * ff_rows
                    to = part * FF + (d * n_ctx + c) * ff_rows
                    values = s_ref[c, :, at : at + ff_rows].astype(F32)
                    total = total + values * w_ref[:, to : to + ff_rows].astype(F32)
                    out_ref[:, to : to + ff_rows] = values * gains
        gain_out_ref[...] = jnp.sum(total, axis=1, keepdims=True)

    return pl.pallas_call(
        kernel,
        in_specs=[pl.BlockSpec(memory_space=pltpu.VMEM)] * 3,
        out_specs=[pl.BlockSpec(memory_space=pltpu.VMEM)] * 2,
        out_shape=[
            jax.ShapeDtypeStruct((rows, 2 * FF), F32),
            jax.ShapeDtypeStruct((rows, 1), F32),
        ],
        compiler_params=pltpu.CompilerParams(vmem_limit_bytes=VMEM_LIMIT),
        cost_estimate=LONG,
        name="join_columns",
    )(sums, weight, gain)


def lane_heads(rows, width):
    lane = lax.broadcasted_iota(jnp.int32, (rows, width), 1)
    return (lane % (width // 2)) // HALF


def attend_forward(slot_of, starts, queries, keys, values_t, heads, tok, first, count, before):
    seq, width = queries.shape
    blocks = seq // tok
    span = 2 * tok

    def kernel(slot_ref, start_ref, q_ref, k_ref, v_ref, *refs):
        attn_ref, slot_attn_ref, full_ref, lse_ref, scores = refs[len(before) :]
        block = first + pl.program_id(0)
        steps = (block + 2) // 2
        start = start_ref[...]
        here = block * tok + lax.broadcasted_iota(jnp.int32, (1, tok), 1)
        head_of = lane_heads(tok, width)
        q = q_ref[...]
        q_heads = [jnp.where(head_of == h, q, jnp.zeros_like(q)) for h in range(heads)]

        def score(i, peaks):
            rows = pl.ds(pl.multiple_of(i * span, span), span)
            k = k_ref[rows, :]
            there = i * span + lax.broadcasted_iota(jnp.int32, (span, tok), 0)
            visible = (there >= start) & (there <= here)
            out = []
            for h in range(heads):
                s = jnp.where(visible, nt(k, q_heads[h]), MASKED)
                scores[h, rows, :] = s
                out.append(jnp.maximum(peaks[h], jnp.max(s.reshape(span // 8, 8, tok), axis=0)))
            return tuple(out)

        peaks = lax.fori_loop(
            0, steps, score, tuple(jnp.full((8, tok), MASKED, F32) for _ in range(heads))
        )
        peaks = [jnp.max(peak, axis=0, keepdims=True) for peak in peaks]

        def weigh(i, running):
            rows = pl.ds(pl.multiple_of(i * span, span), span)
            v = v_ref[:, rows]
            out = []
            for h in range(heads):
                total, acc = running[h]
                p = jnp.exp(scores[h, rows, :] - peaks[h])
                total = total + jnp.sum(p.reshape(span // 8, 8, tok), axis=0)
                out.append((total, acc + nn(v, p.astype(BF))))
            return tuple(out)

        result = lax.fori_loop(
            0,
            steps,
            weigh,
            tuple((jnp.zeros((8, tok), F32), jnp.zeros((HD, tok), F32)) for _ in range(heads)),
        )
        rows = []
        for h in range(heads):
            total, acc = result[h]
            total = jnp.sum(total, axis=0, keepdims=True)
            rows.append(acc / total)
            lse_ref[0, h : h + 1, :] = peaks[h] + jnp.log(total)
        full = jnp.concatenate(rows, axis=0).T
        full_ref[...] = full
        attn_ref[...] = full.astype(BF)
        slot_attn_ref[...] = full.astype(BF)

    return pl.pallas_call(
        kernel,
        grid_spec=pltpu.PrefetchScalarGridSpec(
            num_scalar_prefetch=1,
            grid=(count,),
            in_specs=[
                pl.BlockSpec((1, tok), lambda j, slot: (0, first + j)),
                pl.BlockSpec((tok, width), lambda j, slot: (first + j, 0)),
                pl.BlockSpec((seq, width), lambda j, slot: (0, 0)),
                pl.BlockSpec((HD, seq), lambda j, slot: (0, 0)),
            ]
            + [pl.BlockSpec(memory_space=pltpu.HBM)] * len(before),
            out_specs=[
                pl.BlockSpec((tok, width), lambda j, slot: (first + j, 0)),
                pl.BlockSpec((tok, width), lambda j, slot: (slot[first + j], 0)),
                pl.BlockSpec((tok, width), lambda j, slot: (first + j, 0)),
                pl.BlockSpec((1, heads, tok), lambda j, slot: (first + j, 0, 0)),
            ],
            scratch_shapes=[pltpu.VMEM((heads, seq, tok), F32)],
        ),
        out_shape=[
            jax.ShapeDtypeStruct((seq, width), BF),
            jax.ShapeDtypeStruct((seq, width), BF),
            jax.ShapeDtypeStruct((seq, width), F32),
            jax.ShapeDtypeStruct((blocks, heads, tok), F32),
        ],
        input_output_aliases={5 + i: i for i in range(len(before))},
        compiler_params=pltpu.CompilerParams(vmem_limit_bytes=VMEM_LIMIT),
        cost_estimate=LONG,
        name="attend_forward",
    )(slot_of, starts, queries, keys, values_t, *before)


def attend_backward(
    slot_of, starts, queries, keys, keys_t, values, grads, full, lse, cosine, sine, unsplit, heads, tok
):
    seq, width = queries.shape
    blocks = seq // tok
    span = 2 * tok
    half = width // 2

    def kernel(
        slot_ref, start_ref, q_ref, k_ref, kt_ref, v_ref, g_ref, full_ref, lse_ref, cos_ref, sin_ref, unsplit_ref,
        out_ref, dk, dv,
    ):
        block = pl.program_id(0)
        steps = (block + 2) // 2

        @pl.when(block == 0)
        def _():
            dk[...] = jnp.zeros_like(dk)
            dv[...] = jnp.zeros_like(dv)

        start = start_ref[...]
        here = block * tok + lax.broadcasted_iota(jnp.int32, (1, tok), 1)
        head_of = lane_heads(tok, width)
        wide = lax.broadcasted_iota(jnp.int32, (tok, width), 1) // HD
        q = q_ref[...]
        g = g_ref[...]
        q_heads = [jnp.where(head_of == h, q, jnp.zeros_like(q)) for h in range(heads)]
        g_heads = [jnp.where(wide == h, g, jnp.zeros_like(g)) for h in range(heads)]
        q_stack = jnp.concatenate(q_heads, axis=0)
        g_stack = jnp.concatenate(g_heads, axis=0)
        picks = (
            lax.broadcasted_iota(jnp.int32, (8, width), 1) // HD
            == lax.broadcasted_iota(jnp.int32, (8, width), 0)
        ).astype(F32)
        deltas = lax.dot_general(
            picks,
            g.astype(F32) * full_ref[...],
            (((1,), (1,)), ((), ())),
            preferred_element_type=F32,
            precision=lax.Precision.HIGHEST,
        )

        def step(i, dq):
            rows = pl.ds(pl.multiple_of(i * span, span), span)
            k = k_ref[rows, :]
            v = v_ref[rows, :]
            kt = kt_ref[:, rows]
            there = i * span + lax.broadcasted_iota(jnp.int32, (span, tok), 0)
            visible = (there >= start) & (there <= here)
            probs, grad_scores, out = [], [], []
            for h in range(heads):
                s = jnp.where(visible, nt(k, q_heads[h]), MASKED)
                p = jnp.exp(s - lse_ref[0, h : h + 1, :])
                ds = (p * (nt(v, g_heads[h]) - deltas[h : h + 1, :])).astype(BF)
                probs.append(p.astype(BF))
                grad_scores.append(ds)
                out.append(dq[h] + nn(kt, ds))
            dv[rows, :] += nn(jnp.concatenate(probs, axis=1), g_stack)
            dk[rows, :] += nn(jnp.concatenate(grad_scores, axis=1), q_stack)
            return tuple(out)

        dq = lax.fori_loop(
            0, steps, step, tuple(jnp.zeros((HD, tok), F32) for _ in range(heads))
        )
        dq = jnp.concatenate([x[:HALF] for x in dq] + [x[HALF:] for x in dq], axis=0).T
        here_rows = pl.ds(pl.multiple_of(block * tok, tok), tok)
        cos, sin = turn_tables(cos_ref[here_rows, :], sin_ref[here_rows, :], width)
        dq = (dq * cos - swap_halves(dq) * sin) * (HD**-0.5)
        slot_rows = pl.ds(pl.multiple_of(slot_ref[block] * tok, tok), tok)
        out_ref[slot_rows, :width] = nn(dq.astype(BF), unsplit_ref[...]).astype(BF)

        @pl.when(block == blocks - 1)
        def _():
            lane = lax.broadcasted_iota(jnp.int32, (width, 128), 0)
            column = lax.broadcasted_iota(jnp.int32, (width, 128), 1)
            fold_k = ((lane // half) * HALF + lane % HALF == column).astype(BF)
            fold_v = (lane % HD + HD == column).astype(BF)

            def fold(i, unused):
                rows = pl.ds(pl.multiple_of(i * tok, tok), tok)
                cos, sin = turn_tables(cos_ref[rows, :], sin_ref[rows, :], width)
                a = dk[rows, :]
                a = a * cos - swap_halves(a) * sin
                b = dv[rows, :]
                a_high = a.astype(BF)
                b_high = b.astype(BF)
                terms = (
                    nn(a_high, fold_k)
                    + nn((a - a_high.astype(F32)).astype(BF), fold_k)
                    + nn(b_high, fold_v)
                    + nn((b - b_high.astype(F32)).astype(BF), fold_v)
                )
                slot_rows = pl.ds(pl.multiple_of(slot_ref[i] * tok, tok), tok)
                out_ref[slot_rows, width:] = terms.astype(BF)
                return unused

            lax.fori_loop(0, blocks, fold, 0)

    whole = lambda shape: pl.BlockSpec(shape, lambda j, *_: (0, 0))
    return pl.pallas_call(
        kernel,
        grid_spec=pltpu.PrefetchScalarGridSpec(
            num_scalar_prefetch=1,
            grid=(blocks,),
            in_specs=[
                pl.BlockSpec((1, tok), lambda j, *_: (0, j)),
                pl.BlockSpec((tok, width), lambda j, *_: (j, 0)),
                whole((seq, width)),
                whole((HD, seq)),
                whole((seq, width)),
                pl.BlockSpec((tok, width), lambda j, *_: (j, 0)),
                pl.BlockSpec((tok, width), lambda j, *_: (j, 0)),
                pl.BlockSpec((1, heads, tok), lambda j, *_: (j, 0, 0)),
                whole((seq, 128)),
                whole((seq, 128)),
                whole((width, width)),
            ],
            out_specs=whole((seq, width + 128)),
            scratch_shapes=[pltpu.VMEM((seq, width), F32), pltpu.VMEM((seq, width), F32)],
        ),
        out_shape=jax.ShapeDtypeStruct((seq, width + 128), BF),
        compiler_params=pltpu.CompilerParams(vmem_limit_bytes=VMEM_LIMIT),
        cost_estimate=MEDIUM,
        name="attend_backward",
    )(slot_of, starts, queries, keys, keys_t, values, grads, full, lse, cosine, sine, unsplit)


def outer_rows(activations, gradients):
    return lax.dot_general(
        activations, gradients, (((0,), (0,)), ((), ())), preferred_element_type=F32
    ).astype(BF)


def split_source(width):
    lane = np.arange(width)
    half = lane // (width // 2)
    head = (lane % (width // 2)) // HALF
    return head * HD + half * HALF + lane % HALF


def spread_matrix(width):
    matrix = np.zeros((width + 2 * HD, width + 256), np.float32)
    lane = np.arange(width)
    matrix[split_source(width), lane] = 1
    lane = np.arange(2 * HD)
    matrix[width + lane, width + lane] = 1
    lane = np.arange(HD)
    matrix[width + (lane + HALF) % HD, width + 128 + lane] = 1
    return jnp.asarray(matrix, BF)


def widen_matrix(width):
    matrix = np.zeros((2 * HD, 2 * width), np.float32)
    lane = np.arange(width)
    matrix[(lane // (width // 2)) * HALF + lane % HALF, lane] = 1
    matrix[HD + lane % HD, width + lane] = 1
    return jnp.asarray(matrix, BF)


def unsplit_matrix(width):
    matrix = np.zeros((width, width), np.float32)
    matrix[np.arange(width), split_source(width)] = 1
    return jnp.asarray(matrix, BF)


def on_device(
    block_in,
    gain_attn,
    qkv_weight,
    out_weight,
    gain_ffn,
    gate_up_weight,
    down_weight,
    doc_lengths,
    out_grad,
):
    n_ctx = lax.axis_size("ctx")
    n_dp = lax.axis_size("dp")
    me = lax.axis_index("ctx")
    tok = block_in.shape[0]
    seq = tok * n_ctx
    heads = H // n_ctx
    width = heads * HD
    sharers = n_ctx // KVH
    rows = qkv_weight.shape[0]
    ff_rows = down_weight.shape[0]
    ff = ff_rows * n_dp
    columns = width + 2 * HD

    order = me ^ jnp.where(me % 2 == 0, *[jnp.asarray(t) for t in slot_table(n_ctx)])
    slots = jnp.arange(n_ctx, dtype=jnp.int32)
    slot_of = jnp.sum(jnp.where(order[None, :] == slots[:, None], slots[None, :], 0), axis=1)
    index = jnp.arange(seq, dtype=jnp.int32)
    lengths = doc_lengths[0]
    ends = jnp.cumsum(lengths)
    starts = jnp.sum((index[:, None] >= ends[None, :]).astype(jnp.int32) * lengths[None, :], axis=1)
    lane = jnp.arange(128, dtype=F32) % HALF
    frequency = 10000.0 ** (-lane * 2.0 / HD)
    angles = (index - starts).astype(F32)[:, None] * frequency[None, :]
    cosine = jnp.cos(angles)
    sine = jnp.sin(angles)
    starts_row = starts[None, :]

    gain_one = gain_attn.astype(F32)[:, None]
    gain_two = gain_ffn.astype(F32)[:, None]
    qkv = (qkv_weight.astype(F32) * gain_one).astype(BF)
    q_cols = qkv[:, : H * HD].reshape(rows, n_ctx, width).transpose(1, 0, 2)
    k_cols = qkv[:, H * HD : (H + KVH) * HD].reshape(rows, KVH, HD).transpose(1, 0, 2)
    v_cols = qkv[:, (H + KVH) * HD :].reshape(rows, KVH, HD).transpose(1, 0, 2)
    kv_cols = jnp.repeat(jnp.concatenate([k_cols, v_cols], axis=2), sharers, axis=0)
    owner_pairs = [(b, b % n_dp * n_ctx + b // n_dp) for b in range(n_dp * n_ctx)]
    out_own = lax.ppermute(out_weight, ("dp", "ctx"), owner_pairs)
    out_part = gather_dp(out_own)
    qkv_own = exchange(jnp.concatenate([q_cols, kv_cols], axis=2)).reshape(n_ctx * rows, columns)
    qkv_part = gather_dp(qkv_own)

    hidden_in = block_in.astype(F32)
    rms_one = lax.rsqrt(jnp.mean(hidden_in * hidden_in, axis=-1, keepdims=True) + EPS)
    one_pieces = gather_slots(after((hidden_in * rms_one).astype(BF), qkv_own, out_own), n_ctx)

    gate_up_cols = split_columns(
        gate_up_weight, after(gain_two, cosine, sine), n_ctx, n_dp, ff_rows
    )
    gate_up_own = exchange(after(gate_up_cols, *one_pieces[: n_ctx // 2])).reshape(
        n_ctx * rows, 2 * ff
    )
    gate_up_part = gather_dp(gate_up_own)
    down_part = gather_dp(after(down_weight, gate_up_own))

    queries, keys, values, keys_t, values_t, all_one = project_qkv(
        order, one_pieces, qkv_part, spread_matrix(width), widen_matrix(width), cosine, sine, width, tok
    )
    out_direct = gather_direct(out_part, n_ctx)
    attn, slot_attn, attended, lse = attend_forward(
        slot_of, starts_row, after(queries, gate_up_own, *out_direct), keys, values_t, heads, tok, 0, n_ctx, ()
    )
    attn_tokens = exchange(attn.reshape(n_ctx, tok, width))
    out_pieces = gather_rest(out_direct, n_ctx, (queries,), (attn,))
    state, norm_two = project_out(order, attn_tokens, out_pieces, block_in)

    two_pieces = gather_slots(norm_two, n_ctx)
    grad_direct = gather_direct(after(out_grad, *two_pieces), n_ctx)
    hidden, factors, all_two = feed_forward(two_pieces, gate_up_part)
    grad_pieces = gather_rest(grad_direct, n_ctx, (hidden,))
    all_grad = lay_out(grad_pieces)
    down_terms = outer_rows(hidden, all_grad)
    down_sums = scatter_dp(down_terms)
    grad_gate_up = feed_backward(after(factors, down_terms), all_grad, down_part)

    def rows_of(x, lo, hi):
        return lax.slice_in_dim(x, lo * tok, hi * tok, axis=0)

    d_pairs, _ = scatter_pairs(
        lambda lo, hi: nt(rows_of(grad_gate_up, lo, hi), gate_up_part), tok, n_ctx
    )
    stages = tuple(reversed(range(len(walk(n_ctx, 0)))))
    d_two = scatter_chips(*d_pairs, stages, n_ctx)
    hidden_pairs, _ = scatter_pairs(
        lambda lo, hi: nn(rows_of(after(hidden, *d_pairs), lo, hi), down_part), tok, n_ctx
    )
    gate_up_terms = outer_rows(after(all_two, *d_pairs), grad_gate_up)
    gate_up_sums = scatter_dp(gate_up_terms)

    grad_state, grad_branch, grad_heads = branch_back(
        order, after(d_two, gate_up_terms, *hidden_pairs), state, out_grad, out_pieces
    )
    grad_attn = exchange(grad_heads).reshape(seq, width)
    branch_here, branch_there = gather_at_once(after(grad_branch, grad_attn), n_ctx)
    hidden_upper, hidden_lower = hidden_pairs
    hidden_arrived = swap_stage(after(hidden_upper.astype(BF), grad_attn), n_ctx, stages[0])
    grad_mixed = attend_backward(
        slot_of,
        starts_row,
        queries,
        keys,
        keys_t,
        values,
        after(grad_attn, down_sums),
        attended,
        lse,
        cosine,
        sine,
        unsplit_matrix(width),
        heads,
        tok,
    )
    qkv_terms = outer_rows(all_one, after(grad_mixed, gate_up_sums))
    qkv_sums = scatter_dp(qkv_terms)
    one_pairs, _ = scatter_pairs(
        lambda lo, hi: nt(
            rows_of(after(grad_mixed, qkv_terms, hidden_arrived, *branch_here), lo, hi), qkv_part
        ),
        tok,
        n_ctx,
    )
    d_one = scatter_chips(*one_pairs, stages, n_ctx)
    hidden_sums = scatter_rest(hidden_lower, hidden_arrived, stages, n_ctx)
    block_out = (state + hidden_sums).astype(BF)
    out_terms = outer_rows(slot_attn, after(lay_out(branch_here + branch_there), qkv_terms))
    out_sums = scatter_dp(after(out_terms, qkv_sums))
    norm_one = hidden_in * rms_one
    input_grad = grad_state + rms_one * (
        d_one - norm_one * jnp.mean(d_one * norm_one, axis=-1, keepdims=True)
    )

    down_weight_grad = after(down_sums, grad_mixed).astype(F32)
    out_weight_grad = lax.ppermute(
        out_sums, ("dp", "ctx"), [(b, a) for a, b in owner_pairs]
    ).astype(F32)
    gate_up_weight_grad, gain_ffn_grad = join_columns(
        exchange(after(gate_up_sums, grad_mixed).reshape(n_ctx, rows, 2 * ff)), gate_up_weight, gain_two, n_dp, ff_rows
    )
    qkv_back = exchange(qkv_sums.reshape(n_ctx, rows, columns)).astype(F32)
    q_back = qkv_back[:, :, :width].transpose(1, 0, 2).reshape(rows, H * HD)
    kv_back = jnp.sum(qkv_back[:, :, width:].reshape(KVH, sharers, rows, 2 * HD), axis=1)
    k_back = kv_back[:, :, :HD].transpose(1, 0, 2).reshape(rows, KVH * HD)
    v_back = kv_back[:, :, HD:].transpose(1, 0, 2).reshape(rows, KVH * HD)
    qkv_back = jnp.concatenate([q_back, k_back, v_back], axis=1)
    qkv_weight_grad = qkv_back * gain_one
    gain_attn_grad = jnp.sum(qkv_back * qkv_weight.astype(F32), axis=1)
    return (
        block_out,
        input_grad,
        gain_attn_grad,
        qkv_weight_grad,
        out_weight_grad,
        gain_ffn_grad[:, 0],
        gate_up_weight_grad,
        down_weight_grad,
    )


def solution(mesh):
    rows = P(("dp", "ctx"), None)
    entries = P(("dp", "ctx"))
    return jax.shard_map(
        on_device,
        mesh=mesh,
        in_specs=(rows, entries, rows, rows, entries, rows, rows, P("dp", None), rows),
        out_specs=(rows, rows, entries, rows, rows, entries, rows, rows),
        check_vma=False,
    )
```

```python
import jax
import jax.numpy as jnp
import numpy as np
from jax import lax
from jax.experimental import pallas as pl
from jax.experimental.pallas import tpu as pltpu
from jax.sharding import PartitionSpec as P

D = 2048
H = 32
KVH = 4
HD = 64
FF = 5632
HALF = HD // 2

EPS = 1e-05
MASKED = -1e30
BF = jnp.bfloat16
F32 = jnp.float32
VMEM_LIMIT = 60 << 20
SHORT = pl.CostEstimate(flops=1 << 20, bytes_accessed=1 << 20, transcendentals=0)
MEDIUM = pl.CostEstimate(flops=2 * 10**10, bytes_accessed=1 << 20, transcendentals=0)
LONG = pl.CostEstimate(flops=10**11, bytes_accessed=1 << 20, transcendentals=0)


def nt(a, b):
    return lax.dot_general(a, b, (((1,), (1,)), ((), ())), preferred_element_type=F32)


def nn(a, b):
    return jnp.dot(a, b, preferred_element_type=F32)


def after(x, *earlier):
    return lax.optimization_barrier((x, *earlier))[0]


def after_each(values, *earlier):
    count = len(values)
    return lax.optimization_barrier((*values, *earlier))[:count]


def walk(n_ctx, parity):
    bits = []
    bit = 2
    while bit < n_ctx:
        bits.append(bit)
        bit *= 2
    return bits if parity == 0 else bits[::-1]


def swap_stage(x, n_ctx, stage):
    pairs = [(c, c ^ walk(n_ctx, c % 2)[stage]) for c in range(n_ctx)]
    return lax.ppermute(x, "ctx", pairs)


def swap_core(x, n_ctx):
    return lax.ppermute(x, "ctx", [(c, c ^ 1) for c in range(n_ctx)])


def slot_table(n_ctx):
    lists = []
    for parity in (0, 1):
        row = [0]
        for bit in walk(n_ctx, parity):
            row = row + [v ^ bit for v in row]
        lists.append(row)
    return np.array(
        [lists[p] + [v ^ 1 for v in lists[1 - p]] for p in (0, 1)], dtype=np.int32
    )


def gather_direct(x, n_ctx):
    return [x] + [swap_stage(x, n_ctx, stage) for stage in range(len(walk(n_ctx, 0)))]


def gather_rest(direct, n_ctx, earlier=(), last=()):
    have = direct[:1]
    for stage in range(len(walk(n_ctx, 0))):
        passed = [after(block, *earlier) if earlier else block for block in have[1:]]
        have = have + [direct[stage + 1]] + [swap_stage(block, n_ctx, stage) for block in passed]
    return have + [swap_core(after(block, *last) if last else block, n_ctx) for block in have]


def gather_at_once(x, n_ctx):
    have = [x]
    table = slot_table(n_ctx)
    for slot in range(1, n_ctx // 2):
        pairs = [(c, c ^ int(table[c % 2][slot])) for c in range(n_ctx)]
        have.append(lax.ppermute(x, "ctx", pairs))
    return have, [swap_core(block, n_ctx) for block in have]


def gather_slots(x, n_ctx):
    return gather_rest(gather_direct(x, n_ctx), n_ctx)


def scatter_pairs(term, tok, n_ctx):
    mine = n_ctx // 2
    cut = mine // 2
    sums, arrivals = [], []
    for lo, hi in ((cut, mine), (0, cut)):
        arrivals.append(swap_core(term(mine + lo, mine + hi).astype(BF), n_ctx))
        sums.append(term(lo, hi) + arrivals[-1].astype(F32))
    return sums, arrivals


def scatter_chips(upper, lower, stages, n_ctx, *earlier):
    for stage in stages:
        if earlier and stage == 0:
            upper = after(upper.astype(BF), *earlier)
        lower = lower + swap_stage(upper.astype(BF), n_ctx, stage).astype(F32)
        if stage:
            half = lower.shape[0] // 2
            upper, lower = lower[half:], lower[:half]
    return lower if stages[-1] == 0 else (upper, lower)


def scatter_rest(lower, arrived, stages, n_ctx):
    sums = lower + arrived.astype(F32)
    if len(stages) == 1:
        return sums
    half = sums.shape[0] // 2
    return scatter_chips(sums[half:], sums[:half], stages[1:], n_ctx)


def exchange(x):
    return lax.all_to_all(x, "ctx", split_axis=0, concat_axis=0, tiled=False)


def gather_dp(x):
    return lax.all_gather(x, "dp", axis=0, tiled=True)


def scatter_dp(x):
    return lax.psum_scatter(x, "dp", scatter_dimension=0, tiled=True)


def fetch_piece(pieces, buffer, semaphores, count=1):
    step = pl.program_id(0)

    @pl.when(step == 0)
    def _():
        for i, piece in enumerate(pieces):
            pltpu.make_async_copy(piece, buffer.at[i], semaphores.at[i]).start()

    for i in range(count):
        at = step * count + i
        pltpu.make_async_copy(pieces[0], buffer.at[at], semaphores.at[at]).wait()
    if count == 1:
        return buffer[step]
    return buffer[pl.ds(step * count, count)].reshape(count * buffer.shape[1], buffer.shape[2])


def keep_pieces(buffer, target, semaphores):
    step = pl.program_id(0)
    total, tok = buffer.shape[0], buffer.shape[1]

    def copy(at):
        rows = pl.ds(pl.multiple_of(at * tok, tok), tok)
        return pltpu.make_async_copy(buffer.at[at], target.at[rows], semaphores.at[at])

    copy(step).start()

    @pl.when(step == total - 1)
    def _():
        for i in range(total):
            copy(i).wait()


def store_rows(source, target, semaphores):
    count = semaphores.shape[0]
    rows = source.shape[0] // count
    copies = [
        pltpu.make_async_copy(
            source.at[pl.ds(i * rows, rows)], target.at[pl.ds(i * rows, rows)], semaphores.at[i]
        )
        for i in range(count)
    ]
    for copy in copies:
        copy.start()
    return copies


def chunks(rows):
    return next(count for count in (8, 4, 2, 1) if rows % (16 * count) == 0)


def fetch_rows(source, buffer, semaphores):
    count = semaphores.shape[0]
    rows = source.shape[0] // count

    @pl.when(pl.program_id(0) == 0)
    def _():
        copies = [
            pltpu.make_async_copy(
                source.at[pl.ds(i * rows, rows)], buffer.at[pl.ds(i * rows, rows)], semaphores.at[i]
            )
            for i in range(count)
        ]
        for copy in copies:
            copy.start()
        for copy in copies:
            copy.wait()


def swap_halves(x):
    return pltpu.roll(x, x.shape[1] // 2, axis=1)


def turn_tables(cosine, sine, width):
    times = width // 128
    cosine = jnp.concatenate([cosine] * times, axis=1) if times > 1 else cosine
    sine = jnp.concatenate([sine] * times, axis=1) if times > 1 else sine
    lane = lax.broadcasted_iota(jnp.int32, sine.shape, 1)
    return cosine, jnp.where(lane < width // 2, -sine, sine)


def any_specs(pieces):
    return [pl.BlockSpec(memory_space=pltpu.HBM) for _ in pieces]


def project_qkv(order, pieces, weight, spread, widen, cosine, sine, width, tok):
    n = len(pieces)
    seq = n * tok

    def kernel(order_ref, *refs):
        parts = refs[:n]
        w_hbm, spread_ref, widen_ref, cos_ref, sin_ref = refs[n : n + 5]
        (
            q_ref, k_ref, v_ref, kt_ref, vt_ref, all_hbm, wide, buffer, semaphores, keep_semaphores, w_ref, w_semaphores
        ) = refs[n + 5 :]
        fetch_rows(w_hbm, w_ref, w_semaphores)

        @pl.when(pl.program_id(0) == 0)
        def _():
            wide[...] = nn(w_ref[...], spread_ref[...]).astype(BF)

        x = fetch_piece(parts, buffer, semaphores)
        keep_pieces(buffer, all_hbm, keep_semaphores)
        mixed = nn(x, wide[...])
        cos, sin = turn_tables(cos_ref[...], sin_ref[...], width)
        q = mixed[:, :width]
        q_ref[...] = (q * cos + swap_halves(q) * sin).astype(BF) * (HD**-0.5)
        lane = lax.broadcasted_iota(jnp.int32, (tok, 128), 1)
        key_sine = jnp.where(lane < HALF, -sin_ref[...], sin_ref[...])
        both = jnp.where(
            lane < HD,
            mixed[:, width : width + 128] * cos_ref[...] + mixed[:, width + 128 :] * key_sine,
            mixed[:, width : width + 128],
        ).astype(BF)
        repeated = nn(both, widen_ref[...]).astype(BF)
        k_ref[...] = repeated[:, :width]
        v_ref[...] = repeated[:, width:]
        turned = both.T
        kt_ref[...] = turned[:HD]
        vt_ref[...] = turned[HD:]

    rows = lambda s, order: (order[s], 0)
    lanes = lambda s, order: (0, order[s])
    whole = lambda s, order: (0, 0)
    return pl.pallas_call(
        kernel,
        grid_spec=pltpu.PrefetchScalarGridSpec(
            num_scalar_prefetch=1,
            grid=(n,),
            in_specs=any_specs(pieces)
            + [
                pl.BlockSpec(memory_space=pltpu.HBM),
                pl.BlockSpec(spread.shape, whole),
                pl.BlockSpec(widen.shape, whole),
                pl.BlockSpec((tok, 128), rows),
                pl.BlockSpec((tok, 128), rows),
            ],
            out_specs=[
                pl.BlockSpec((tok, width), rows),
                pl.BlockSpec((tok, width), rows),
                pl.BlockSpec((tok, width), rows),
                pl.BlockSpec((HD, tok), lanes),
                pl.BlockSpec((HD, tok), lanes),
                pl.BlockSpec(memory_space=pltpu.HBM),
            ],
            scratch_shapes=[
                pltpu.VMEM((D, width + 256), BF),
                pltpu.VMEM((n, tok, D), BF),
                pltpu.SemaphoreType.DMA((n,)),
                pltpu.SemaphoreType.DMA((n,)),
                pltpu.VMEM(weight.shape, BF),
                pltpu.SemaphoreType.DMA((chunks(D),)),
            ],
        ),
        out_shape=[
            jax.ShapeDtypeStruct((seq, width), BF),
            jax.ShapeDtypeStruct((seq, width), BF),
            jax.ShapeDtypeStruct((seq, width), BF),
            jax.ShapeDtypeStruct((HD, seq), BF),
            jax.ShapeDtypeStruct((HD, seq), BF),
            jax.ShapeDtypeStruct((seq, D), BF),
        ],
        compiler_params=pltpu.CompilerParams(vmem_limit_bytes=VMEM_LIMIT),
        cost_estimate=LONG,
        name="project_qkv",
    )(order, *pieces, weight, spread, widen, cosine, sine)


def project_out(order, heads_in, pieces, residual):
    n, tok, width = heads_in.shape

    def kernel(order_ref, a_ref, *refs):
        parts = refs[:n]
        x_ref, state_hbm, norm_hbm, buffer, semaphores, state_ref, norm_ref, out_semaphores = refs[n:]
        step = pl.program_id(0)
        w = fetch_piece(parts, buffer, semaphores)

        @pl.when(step == 0)
        def _():
            state_ref[...] = x_ref[...].astype(F32)

        state_ref[...] += nn(a_ref[0], w)

        @pl.when(step == n - 1)
        def _():
            state = state_ref[...]
            scale = lax.rsqrt(jnp.mean(state * state, axis=-1, keepdims=True) + EPS)
            copies = store_rows(state_ref, state_hbm, out_semaphores.at[0])
            norm_ref[...] = (state * scale).astype(BF)
            copies += store_rows(norm_ref, norm_hbm, out_semaphores.at[1])
            for copy in copies:
                copy.wait()

    whole = lambda s, order: (0, 0)
    return pl.pallas_call(
        kernel,
        grid_spec=pltpu.PrefetchScalarGridSpec(
            num_scalar_prefetch=1,
            grid=(n,),
            in_specs=[pl.BlockSpec((1, tok, width), lambda s, order: (order[s], 0, 0))]
            + any_specs(pieces)
            + [pl.BlockSpec((tok, D), whole)],
            out_specs=[pl.BlockSpec(memory_space=pltpu.HBM)] * 2,
            scratch_shapes=[
                pltpu.VMEM((n, width, D), BF),
                pltpu.SemaphoreType.DMA((n,)),
                pltpu.VMEM((tok, D), F32),
                pltpu.VMEM((tok, D), BF),
                pltpu.SemaphoreType.DMA((2, 4)),
            ],
        ),
        out_shape=[
            jax.ShapeDtypeStruct((tok, D), F32),
            jax.ShapeDtypeStruct((tok, D), BF),
        ],
        compiler_params=pltpu.CompilerParams(vmem_limit_bytes=VMEM_LIMIT),
        cost_estimate=SHORT,
        name="project_out",
    )(order, heads_in, *pieces, residual)


def feed_forward(pieces, weight):
    n = len(pieces)
    tok = 2 * pieces[0].shape[0]
    seq = n * tok // 2
    ff = weight.shape[1] // 2

    def kernel(*refs):
        parts = refs[:n]
        w_hbm, hidden_ref, factor_ref, all_ref, buffer, semaphores, w_ref, w_semaphores = refs[n:]
        fetch_rows(w_hbm, w_ref, w_semaphores)
        x = fetch_piece(parts, buffer, semaphores, 2)
        all_ref[...] = x
        both = nn(x, w_ref[...])
        gate = both[:, :ff]
        up = both[:, ff:]
        sig = jax.nn.sigmoid(gate)
        silu = gate * sig
        hidden_ref[...] = (silu * up).astype(BF)
        factor_ref[:, :ff] = (up * sig * (1.0 + gate * (1.0 - sig))).astype(BF)
        factor_ref[:, ff:] = silu.astype(BF)

    rows = lambda s: (s, 0)
    return pl.pallas_call(
        kernel,
        grid=(n // 2,),
        in_specs=any_specs(pieces) + [pl.BlockSpec(memory_space=pltpu.HBM)],
        out_specs=[
            pl.BlockSpec((tok, ff), rows),
            pl.BlockSpec((tok, 2 * ff), rows),
            pl.BlockSpec((tok, D), rows),
        ],
        scratch_shapes=[
            pltpu.VMEM((n, tok // 2, D), BF),
            pltpu.SemaphoreType.DMA((n,)),
            pltpu.VMEM(weight.shape, BF),
            pltpu.SemaphoreType.DMA((chunks(D),)),
        ],
        out_shape=[
            jax.ShapeDtypeStruct((seq, ff), BF),
            jax.ShapeDtypeStruct((seq, 2 * ff), BF),
            jax.ShapeDtypeStruct((seq, D), BF),
        ],
        compiler_params=pltpu.CompilerParams(vmem_limit_bytes=VMEM_LIMIT),
        cost_estimate=LONG,
        name="feed_forward",
    )(*pieces, weight)


def feed_backward(factors, grads, weight):
    seq = factors.shape[0]
    ff = weight.shape[0]
    tok = 512

    def kernel(factor_ref, g_ref, w_hbm, out_ref, w_ref, w_semaphores, turned):
        fetch_rows(w_hbm, w_ref, w_semaphores)

        @pl.when(pl.program_id(0) == 0)
        def _():
            turned[...] = w_ref[...].T

        grad_hidden = nn(g_ref[...], turned[...])
        factor = factor_ref[...].astype(F32)
        out_ref[:, :ff] = (grad_hidden * factor[:, :ff]).astype(BF)
        out_ref[:, ff:] = (grad_hidden * factor[:, ff:]).astype(BF)

    rows = lambda s: (s, 0)
    return pl.pallas_call(
        kernel,
        grid=(seq // tok,),
        in_specs=[
            pl.BlockSpec((tok, 2 * ff), rows),
            pl.BlockSpec((tok, D), rows),
            pl.BlockSpec(memory_space=pltpu.HBM),
        ],
        out_specs=pl.BlockSpec((tok, 2 * ff), rows),
        scratch_shapes=[
            pltpu.VMEM(weight.shape, BF),
            pltpu.SemaphoreType.DMA((chunks(ff),)),
            pltpu.VMEM((D, ff), BF),
        ],
        out_shape=jax.ShapeDtypeStruct((seq, 2 * ff), BF),
        compiler_params=pltpu.CompilerParams(vmem_limit_bytes=VMEM_LIMIT),
        cost_estimate=LONG,
        name="feed_backward",
    )(factors, grads, weight)


def lay_out(pieces):
    n = len(pieces)
    tok = pieces[0].shape[0]

    def kernel(*refs):
        parts = refs[:n]
        out_ref, buffer, in_semaphores, out_semaphores = refs[n:]
        arrive = [
            pltpu.make_async_copy(part, buffer.at[i], in_semaphores.at[i])
            for i, part in enumerate(parts)
        ]
        leave = [
            pltpu.make_async_copy(buffer.at[i], out_ref.at[pl.ds(i * tok, tok)], out_semaphores.at[i])
            for i in range(n)
        ]
        for copy in arrive:
            copy.start()
        for i in range(n):
            arrive[i].wait()
            leave[i].start()
        for copy in leave:
            copy.wait()

    return pl.pallas_call(
        kernel,
        in_specs=any_specs(pieces),
        out_specs=pl.BlockSpec(memory_space=pltpu.HBM),
        scratch_shapes=[
            pltpu.VMEM((n, tok, D), BF),
            pltpu.SemaphoreType.DMA((n,)),
            pltpu.SemaphoreType.DMA((n,)),
        ],
        out_shape=jax.ShapeDtypeStruct((n * tok, D), BF),
        compiler_params=pltpu.CompilerParams(vmem_limit_bytes=VMEM_LIMIT),
        cost_estimate=SHORT,
        name="lay_out",
    )(*pieces)


def branch_back(order, d_two, state, out_grad, pieces):
    n = len(pieces)
    tok = d_two.shape[0]
    width = pieces[0].shape[0]

    def kernel(order_ref, d_ref, state_ref, g_ref, *refs):
        parts = refs[:n]
        grad_hbm, branch_hbm, heads_ref, buffer, semaphores, grad_ref, branch_ref, out_semaphores = refs[n:]

        @pl.when(pl.program_id(0) == 0)
        def _():
            state = state_ref[...]
            scale = lax.rsqrt(jnp.mean(state * state, axis=-1, keepdims=True) + EPS)
            norm = state * scale
            d = d_ref[...]
            grad = g_ref[...].astype(F32) + scale * (
                d - norm * jnp.mean(d * norm, axis=-1, keepdims=True)
            )
            grad_ref[...] = grad
            branch_ref[...] = grad.astype(BF)
            store_rows(grad_ref, grad_hbm, out_semaphores.at[0])
            store_rows(branch_ref, branch_hbm, out_semaphores.at[1])

        w = fetch_piece(parts, buffer, semaphores)
        heads_ref[0] = nt(branch_ref[...], w).astype(BF)

        @pl.when(pl.program_id(0) == n - 1)
        def _():
            for source, target, at in ((grad_ref, grad_hbm, 0), (branch_ref, branch_hbm, 1)):
                rows = tok // 4
                for i in range(4):
                    cut = pl.ds(i * rows, rows)
                    pltpu.make_async_copy(source.at[cut], target.at[cut], out_semaphores.at[at, i]).wait()

    whole = lambda s, order: (0, 0)
    return pl.pallas_call(
        kernel,
        grid_spec=pltpu.PrefetchScalarGridSpec(
            num_scalar_prefetch=1,
            grid=(n,),
            in_specs=[
                pl.BlockSpec((tok, D), whole),
                pl.BlockSpec((tok, D), whole),
                pl.BlockSpec((tok, D), whole),
            ]
            + any_specs(pieces),
            out_specs=[
                pl.BlockSpec(memory_space=pltpu.HBM),
                pl.BlockSpec(memory_space=pltpu.HBM),
                pl.BlockSpec((1, tok, width), lambda s, order: (order[s], 0, 0)),
            ],
            scratch_shapes=[
                pltpu.VMEM((n, width, D), BF),
                pltpu.SemaphoreType.DMA((n,)),
                pltpu.VMEM((tok, D), F32),
                pltpu.VMEM((tok, D), BF),
                pltpu.SemaphoreType.DMA((2, 4)),
            ],
        ),
        out_shape=[
            jax.ShapeDtypeStruct((tok, D), F32),
            jax.ShapeDtypeStruct((tok, D), BF),
            jax.ShapeDtypeStruct((n, tok, width), BF),
        ],
        compiler_params=pltpu.CompilerParams(vmem_limit_bytes=VMEM_LIMIT),
        cost_estimate=SHORT,
        name="branch_back",
    )(order, d_two, state, out_grad, *pieces)


def split_columns(weight, gain, n_ctx, n_dp, ff_rows):
    rows = weight.shape[0]
    ff = ff_rows * n_dp

    def kernel(w_ref, gain_ref, out_ref):
        gains = gain_ref[...]
        for part in range(2):
            for d in range(n_dp):
                for c in range(n_ctx):
                    at = part * FF + (d * n_ctx + c) * ff_rows
                    to = part * ff + d * ff_rows
                    values = w_ref[:, at : at + ff_rows].astype(F32) * gains
                    out_ref[c, :, to : to + ff_rows] = values.astype(BF)

    return pl.pallas_call(
        kernel,
        in_specs=[pl.BlockSpec(memory_space=pltpu.VMEM)] * 2,
        out_specs=pl.BlockSpec(memory_space=pltpu.VMEM),
        out_shape=jax.ShapeDtypeStruct((n_ctx, rows, 2 * ff), BF),
        compiler_params=pltpu.CompilerParams(vmem_limit_bytes=VMEM_LIMIT),
        cost_estimate=LONG,
        name="split_columns",
    )(weight, gain)


def join_columns(sums, weight, gain, n_dp, ff_rows):
    n_ctx, rows, both = sums.shape
    ff = both // 2

    def kernel(s_ref, w_ref, gain_ref, out_ref, gain_out_ref):
        gains = gain_ref[...]
        total = jnp.zeros((rows, ff_rows), F32)
        for part in range(2):
            for d in range(n_dp):
                for c in range(n_ctx):
                    at = part * ff + d * ff_rows
                    to = part * FF + (d * n_ctx + c) * ff_rows
                    values = s_ref[c, :, at : at + ff_rows].astype(F32)
                    total = total + values * w_ref[:, to : to + ff_rows].astype(F32)
                    out_ref[:, to : to + ff_rows] = values * gains
        gain_out_ref[...] = jnp.sum(total, axis=1, keepdims=True)

    return pl.pallas_call(
        kernel,
        in_specs=[pl.BlockSpec(memory_space=pltpu.VMEM)] * 3,
        out_specs=[pl.BlockSpec(memory_space=pltpu.VMEM)] * 2,
        out_shape=[
            jax.ShapeDtypeStruct((rows, 2 * FF), F32),
            jax.ShapeDtypeStruct((rows, 1), F32),
        ],
        compiler_params=pltpu.CompilerParams(vmem_limit_bytes=VMEM_LIMIT),
        cost_estimate=LONG,
        name="join_columns",
    )(sums, weight, gain)


def lane_heads(rows, width):
    lane = lax.broadcasted_iota(jnp.int32, (rows, width), 1)
    return (lane % (width // 2)) // HALF


def attend_forward(slot_of, starts, queries, keys, values_t, heads, tok, first, count, before):
    seq, width = queries.shape
    blocks = seq // tok
    span = 2 * tok

    def kernel(slot_ref, start_ref, q_ref, k_ref, v_ref, *refs):
        attn_ref, slot_attn_ref, full_ref, lse_ref, scores = refs[len(before) :]
        block = first + pl.program_id(0)
        steps = (block + 2) // 2
        start = start_ref[...]
        here = block * tok + lax.broadcasted_iota(jnp.int32, (1, tok), 1)
        head_of = lane_heads(tok, width)
        q = q_ref[...]
        q_heads = [jnp.where(head_of == h, q, jnp.zeros_like(q)) for h in range(heads)]

        def score(i, peaks):
            rows = pl.ds(pl.multiple_of(i * span, span), span)
            k = k_ref[rows, :]
            there = i * span + lax.broadcasted_iota(jnp.int32, (span, tok), 0)
            visible = (there >= start) & (there <= here)
            out = []
            for h in range(heads):
                s = jnp.where(visible, nt(k, q_heads[h]), MASKED)
                scores[h, rows, :] = s
                out.append(jnp.maximum(peaks[h], jnp.max(s.reshape(span // 8, 8, tok), axis=0)))
            return tuple(out)

        peaks = lax.fori_loop(
            0, steps, score, tuple(jnp.full((8, tok), MASKED, F32) for _ in range(heads))
        )
        peaks = [jnp.max(peak, axis=0, keepdims=True) for peak in peaks]

        def weigh(i, running):
            rows = pl.ds(pl.multiple_of(i * span, span), span)
            v = v_ref[:, rows]
            out = []
            for h in range(heads):
                total, acc = running[h]
                p = jnp.exp(scores[h, rows, :] - peaks[h])
                total = total + jnp.sum(p.reshape(span // 8, 8, tok), axis=0)
                out.append((total, acc + nn(v, p.astype(BF))))
            return tuple(out)

        result = lax.fori_loop(
            0,
            steps,
            weigh,
            tuple((jnp.zeros((8, tok), F32), jnp.zeros((HD, tok), F32)) for _ in range(heads)),
        )
        rows = []
        for h in range(heads):
            total, acc = result[h]
            total = jnp.sum(total, axis=0, keepdims=True)
            rows.append(acc / total)
            lse_ref[0, h : h + 1, :] = peaks[h] + jnp.log(total)
        full = jnp.concatenate(rows, axis=0).T
        full_ref[...] = full
        attn_ref[...] = full.astype(BF)
        slot_attn_ref[...] = full.astype(BF)

    return pl.pallas_call(
        kernel,
        grid_spec=pltpu.PrefetchScalarGridSpec(
            num_scalar_prefetch=1,
            grid=(count,),
            in_specs=[
                pl.BlockSpec((1, tok), lambda j, slot: (0, first + j)),
                pl.BlockSpec((tok, width), lambda j, slot: (first + j, 0)),
                pl.BlockSpec((seq, width), lambda j, slot: (0, 0)),
                pl.BlockSpec((HD, seq), lambda j, slot: (0, 0)),
            ]
            + [pl.BlockSpec(memory_space=pltpu.HBM)] * len(before),
            out_specs=[
                pl.BlockSpec((tok, width), lambda j, slot: (first + j, 0)),
                pl.BlockSpec((tok, width), lambda j, slot: (slot[first + j], 0)),
                pl.BlockSpec((tok, width), lambda j, slot: (first + j, 0)),
                pl.BlockSpec((1, heads, tok), lambda j, slot: (first + j, 0, 0)),
            ],
            scratch_shapes=[pltpu.VMEM((heads, seq, tok), F32)],
        ),
        out_shape=[
            jax.ShapeDtypeStruct((seq, width), BF),
            jax.ShapeDtypeStruct((seq, width), BF),
            jax.ShapeDtypeStruct((seq, width), F32),
            jax.ShapeDtypeStruct((blocks, heads, tok), F32),
        ],
        input_output_aliases={5 + i: i for i in range(len(before))},
        compiler_params=pltpu.CompilerParams(vmem_limit_bytes=VMEM_LIMIT),
        cost_estimate=LONG,
        name="attend_forward",
    )(slot_of, starts, queries, keys, values_t, *before)


def attend_backward(
    slot_of, starts, queries, keys, keys_t, values, grads, full, lse, cosine, sine, unsplit, heads, tok
):
    seq, width = queries.shape
    blocks = seq // tok
    span = 2 * tok
    half = width // 2

    def kernel(
        slot_ref, start_ref, q_ref, k_ref, kt_ref, v_ref, g_ref, full_ref, lse_ref, cos_ref, sin_ref, unsplit_ref,
        out_ref, dk, dv,
    ):
        block = pl.program_id(0)
        steps = (block + 2) // 2

        @pl.when(block == 0)
        def _():
            dk[...] = jnp.zeros_like(dk)
            dv[...] = jnp.zeros_like(dv)

        start = start_ref[...]
        here = block * tok + lax.broadcasted_iota(jnp.int32, (1, tok), 1)
        head_of = lane_heads(tok, width)
        wide = lax.broadcasted_iota(jnp.int32, (tok, width), 1) // HD
        q = q_ref[...]
        g = g_ref[...]
        q_heads = [jnp.where(head_of == h, q, jnp.zeros_like(q)) for h in range(heads)]
        g_heads = [jnp.where(wide == h, g, jnp.zeros_like(g)) for h in range(heads)]
        q_stack = jnp.concatenate(q_heads, axis=0)
        g_stack = jnp.concatenate(g_heads, axis=0)
        picks = (
            lax.broadcasted_iota(jnp.int32, (8, width), 1) // HD
            == lax.broadcasted_iota(jnp.int32, (8, width), 0)
        ).astype(F32)
        deltas = lax.dot_general(
            picks,
            g.astype(F32) * full_ref[...],
            (((1,), (1,)), ((), ())),
            preferred_element_type=F32,
            precision=lax.Precision.HIGHEST,
        )

        def step(i, dq):
            rows = pl.ds(pl.multiple_of(i * span, span), span)
            k = k_ref[rows, :]
            v = v_ref[rows, :]
            kt = kt_ref[:, rows]
            there = i * span + lax.broadcasted_iota(jnp.int32, (span, tok), 0)
            visible = (there >= start) & (there <= here)
            probs, grad_scores, out = [], [], []
            for h in range(heads):
                s = jnp.where(visible, nt(k, q_heads[h]), MASKED)
                p = jnp.exp(s - lse_ref[0, h : h + 1, :])
                ds = (p * (nt(v, g_heads[h]) - deltas[h : h + 1, :])).astype(BF)
                probs.append(p.astype(BF))
                grad_scores.append(ds)
                out.append(dq[h] + nn(kt, ds))
            dv[rows, :] += nn(jnp.concatenate(probs, axis=1), g_stack)
            dk[rows, :] += nn(jnp.concatenate(grad_scores, axis=1), q_stack)
            return tuple(out)

        dq = lax.fori_loop(
            0, steps, step, tuple(jnp.zeros((HD, tok), F32) for _ in range(heads))
        )
        dq = jnp.concatenate([x[:HALF] for x in dq] + [x[HALF:] for x in dq], axis=0).T
        here_rows = pl.ds(pl.multiple_of(block * tok, tok), tok)
        cos, sin = turn_tables(cos_ref[here_rows, :], sin_ref[here_rows, :], width)
        dq = (dq * cos - swap_halves(dq) * sin) * (HD**-0.5)
        slot_rows = pl.ds(pl.multiple_of(slot_ref[block] * tok, tok), tok)
        out_ref[slot_rows, :width] = nn(dq.astype(BF), unsplit_ref[...]).astype(BF)

        @pl.when(block == blocks - 1)
        def _():
            lane = lax.broadcasted_iota(jnp.int32, (width, 128), 0)
            column = lax.broadcasted_iota(jnp.int32, (width, 128), 1)
            fold_k = ((lane // half) * HALF + lane % HALF == column).astype(BF)
            fold_v = (lane % HD + HD == column).astype(BF)

            def fold(i, unused):
                rows = pl.ds(pl.multiple_of(i * tok, tok), tok)
                cos, sin = turn_tables(cos_ref[rows, :], sin_ref[rows, :], width)
                a = dk[rows, :]
                a = a * cos - swap_halves(a) * sin
                b = dv[rows, :]
                a_high = a.astype(BF)
                b_high = b.astype(BF)
                terms = (
                    nn(a_high, fold_k)
                    + nn((a - a_high.astype(F32)).astype(BF), fold_k)
                    + nn(b_high, fold_v)
                    + nn((b - b_high.astype(F32)).astype(BF), fold_v)
                )
                slot_rows = pl.ds(pl.multiple_of(slot_ref[i] * tok, tok), tok)
                out_ref[slot_rows, width:] = terms.astype(BF)
                return unused

            lax.fori_loop(0, blocks, fold, 0)

    whole = lambda shape: pl.BlockSpec(shape, lambda j, *_: (0, 0))
    return pl.pallas_call(
        kernel,
        grid_spec=pltpu.PrefetchScalarGridSpec(
            num_scalar_prefetch=1,
            grid=(blocks,),
            in_specs=[
                pl.BlockSpec((1, tok), lambda j, *_: (0, j)),
                pl.BlockSpec((tok, width), lambda j, *_: (j, 0)),
                whole((seq, width)),
                whole((HD, seq)),
                whole((seq, width)),
                pl.BlockSpec((tok, width), lambda j, *_: (j, 0)),
                pl.BlockSpec((tok, width), lambda j, *_: (j, 0)),
                pl.BlockSpec((1, heads, tok), lambda j, *_: (j, 0, 0)),
                whole((seq, 128)),
                whole((seq, 128)),
                whole((width, width)),
            ],
            out_specs=whole((seq, width + 128)),
            scratch_shapes=[pltpu.VMEM((seq, width), F32), pltpu.VMEM((seq, width), F32)],
        ),
        out_shape=jax.ShapeDtypeStruct((seq, width + 128), BF),
        compiler_params=pltpu.CompilerParams(vmem_limit_bytes=VMEM_LIMIT),
        cost_estimate=MEDIUM,
        name="attend_backward",
    )(slot_of, starts, queries, keys, keys_t, values, grads, full, lse, cosine, sine, unsplit)


def outer_rows(activations, gradients):
    return lax.dot_general(
        activations, gradients, (((0,), (0,)), ((), ())), preferred_element_type=F32
    ).astype(BF)


def split_source(width):
    lane = np.arange(width)
    half = lane // (width // 2)
    head = (lane % (width // 2)) // HALF
    return head * HD + half * HALF + lane % HALF


def spread_matrix(width):
    matrix = np.zeros((width + 2 * HD, width + 256), np.float32)
    lane = np.arange(width)
    matrix[split_source(width), lane] = 1
    lane = np.arange(2 * HD)
    matrix[width + lane, width + lane] = 1
    lane = np.arange(HD)
    matrix[width + (lane + HALF) % HD, width + 128 + lane] = 1
    return jnp.asarray(matrix, BF)


def widen_matrix(width):
    matrix = np.zeros((2 * HD, 2 * width), np.float32)
    lane = np.arange(width)
    matrix[(lane // (width // 2)) * HALF + lane % HALF, lane] = 1
    matrix[HD + lane % HD, width + lane] = 1
    return jnp.asarray(matrix, BF)


def unsplit_matrix(width):
    matrix = np.zeros((width, width), np.float32)
    matrix[np.arange(width), split_source(width)] = 1
    return jnp.asarray(matrix, BF)


def on_device(
    block_in,
    gain_attn,
    qkv_weight,
    out_weight,
    gain_ffn,
    gate_up_weight,
    down_weight,
    doc_lengths,
    out_grad,
):
    n_ctx = lax.axis_size("ctx")
    n_dp = lax.axis_size("dp")
    me = lax.axis_index("ctx")
    tok = block_in.shape[0]
    seq = tok * n_ctx
    heads = H // n_ctx
    width = heads * HD
    sharers = n_ctx // KVH
    rows = qkv_weight.shape[0]
    ff_rows = down_weight.shape[0]
    ff = ff_rows * n_dp
    columns = width + 2 * HD

    order = me ^ jnp.where(me % 2 == 0, *[jnp.asarray(t) for t in slot_table(n_ctx)])
    slots = jnp.arange(n_ctx, dtype=jnp.int32)
    slot_of = jnp.sum(jnp.where(order[None, :] == slots[:, None], slots[None, :], 0), axis=1)
    index = jnp.arange(seq, dtype=jnp.int32)
    lengths = doc_lengths[0]
    ends = jnp.cumsum(lengths)
    starts = jnp.sum((index[:, None] >= ends[None, :]).astype(jnp.int32) * lengths[None, :], axis=1)
    lane = jnp.arange(128, dtype=F32) % HALF
    frequency = 10000.0 ** (-lane * 2.0 / HD)
    angles = (index - starts).astype(F32)[:, None] * frequency[None, :]
    cosine = jnp.cos(angles)
    sine = jnp.sin(angles)
    starts_row = starts[None, :]

    gain_one = gain_attn.astype(F32)[:, None]
    gain_two = gain_ffn.astype(F32)[:, None]
    qkv = (qkv_weight.astype(F32) * gain_one).astype(BF)
    q_cols = qkv[:, : H * HD].reshape(rows, n_ctx, width).transpose(1, 0, 2)
    k_cols = qkv[:, H * HD : (H + KVH) * HD].reshape(rows, KVH, HD).transpose(1, 0, 2)
    v_cols = qkv[:, (H + KVH) * HD :].reshape(rows, KVH, HD).transpose(1, 0, 2)
    kv_cols = jnp.repeat(jnp.concatenate([k_cols, v_cols], axis=2), sharers, axis=0)
    owner_pairs = [(b, b % n_dp * n_ctx + b // n_dp) for b in range(n_dp * n_ctx)]
    out_own = lax.ppermute(out_weight, ("dp", "ctx"), owner_pairs)
    out_part = gather_dp(out_own)
    qkv_own = exchange(jnp.concatenate([q_cols, kv_cols], axis=2)).reshape(n_ctx * rows, columns)
    qkv_part = gather_dp(qkv_own)

    hidden_in = block_in.astype(F32)
    rms_one = lax.rsqrt(jnp.mean(hidden_in * hidden_in, axis=-1, keepdims=True) + EPS)
    one_pieces = gather_slots(after((hidden_in * rms_one).astype(BF), qkv_own, out_own), n_ctx)

    gate_up_cols = split_columns(
        gate_up_weight, after(gain_two, cosine, sine), n_ctx, n_dp, ff_rows
    )
    gate_up_own = exchange(after(gate_up_cols, *one_pieces[: n_ctx // 2])).reshape(
        n_ctx * rows, 2 * ff
    )
    gate_up_part = gather_dp(gate_up_own)
    down_part = gather_dp(after(down_weight, gate_up_own))

    queries, keys, values, keys_t, values_t, all_one = project_qkv(
        order, one_pieces, qkv_part, spread_matrix(width), widen_matrix(width), cosine, sine, width, tok
    )
    out_direct = gather_direct(out_part, n_ctx)
    attn, slot_attn, attended, lse = attend_forward(
        slot_of, starts_row, after(queries, gate_up_own, *out_direct), keys, values_t, heads, tok, 0, n_ctx, ()
    )
    attn_tokens = exchange(attn.reshape(n_ctx, tok, width))
    out_pieces = gather_rest(out_direct, n_ctx, (queries,), (attn,))
    state, norm_two = project_out(order, attn_tokens, out_pieces, block_in)

    two_pieces = gather_slots(norm_two, n_ctx)
    grad_direct = gather_direct(after(out_grad, *two_pieces), n_ctx)
    hidden, factors, all_two = feed_forward(two_pieces, gate_up_part)
    grad_pieces = gather_rest(grad_direct, n_ctx, (hidden,))
    all_grad = lay_out(grad_pieces)
    down_terms = outer_rows(hidden, all_grad)
    down_sums = scatter_dp(down_terms)
    grad_gate_up = feed_backward(after(factors, down_terms), all_grad, down_part)

    def rows_of(x, lo, hi):
        return lax.slice_in_dim(x, lo * tok, hi * tok, axis=0)

    d_pairs, _ = scatter_pairs(
        lambda lo, hi: nt(rows_of(grad_gate_up, lo, hi), gate_up_part), tok, n_ctx
    )
    stages = tuple(reversed(range(len(walk(n_ctx, 0)))))
    d_two = scatter_chips(*d_pairs, stages, n_ctx)
    hidden_pairs, _ = scatter_pairs(
        lambda lo, hi: nn(rows_of(after(hidden, *d_pairs), lo, hi), down_part), tok, n_ctx
    )
    gate_up_terms = outer_rows(after(all_two, *d_pairs), grad_gate_up)
    gate_up_sums = scatter_dp(gate_up_terms)

    grad_state, grad_branch, grad_heads = branch_back(
        order, after(d_two, gate_up_terms, *hidden_pairs), state, out_grad, out_pieces
    )
    grad_attn = exchange(grad_heads).reshape(seq, width)
    branch_here, branch_there = gather_at_once(after(grad_branch, grad_attn), n_ctx)
    hidden_upper, hidden_lower = hidden_pairs
    hidden_arrived = swap_stage(after(hidden_upper.astype(BF), grad_attn), n_ctx, stages[0])
    grad_mixed = attend_backward(
        slot_of,
        starts_row,
        queries,
        keys,
        keys_t,
        values,
        grad_attn,
        attended,
        lse,
        cosine,
        sine,
        unsplit_matrix(width),
        heads,
        tok,
    )
    qkv_terms = outer_rows(all_one, grad_mixed)
    qkv_sums = scatter_dp(after(qkv_terms, gate_up_sums))
    one_pairs, _ = scatter_pairs(
        lambda lo, hi: nt(
            rows_of(after(grad_mixed, qkv_terms, hidden_arrived, *branch_here), lo, hi), qkv_part
        ),
        tok,
        n_ctx,
    )
    d_one = scatter_chips(*one_pairs, stages, n_ctx)
    hidden_sums = scatter_rest(hidden_lower, hidden_arrived, stages, n_ctx)
    block_out = (state + hidden_sums).astype(BF)
    out_terms = outer_rows(slot_attn, after(lay_out(branch_here + branch_there), qkv_terms))
    out_sums = scatter_dp(after(out_terms, qkv_sums))
    norm_one = hidden_in * rms_one
    input_grad = grad_state + rms_one * (
        d_one - norm_one * jnp.mean(d_one * norm_one, axis=-1, keepdims=True)
    )

    down_weight_grad = after(down_sums, grad_mixed).astype(F32)
    out_weight_grad = lax.ppermute(
        out_sums, ("dp", "ctx"), [(b, a) for a, b in owner_pairs]
    ).astype(F32)
    gate_up_weight_grad, gain_ffn_grad = join_columns(
        exchange(after(gate_up_sums, grad_mixed).reshape(n_ctx, rows, 2 * ff)), gate_up_weight, gain_two, n_dp, ff_rows
    )
    qkv_back = exchange(qkv_sums.reshape(n_ctx, rows, columns)).astype(F32)
    q_back = qkv_back[:, :, :width].transpose(1, 0, 2).reshape(rows, H * HD)
    kv_back = jnp.sum(qkv_back[:, :, width:].reshape(KVH, sharers, rows, 2 * HD), axis=1)
    k_back = kv_back[:, :, :HD].transpose(1, 0, 2).reshape(rows, KVH * HD)
    v_back = kv_back[:, :, HD:].transpose(1, 0, 2).reshape(rows, KVH * HD)
    qkv_back = jnp.concatenate([q_back, k_back, v_back], axis=1)
    qkv_weight_grad = qkv_back * gain_one
    gain_attn_grad = jnp.sum(qkv_back * qkv_weight.astype(F32), axis=1)
    return (
        block_out,
        input_grad,
        gain_attn_grad,
        qkv_weight_grad,
        out_weight_grad,
        gain_ffn_grad[:, 0],
        gate_up_weight_grad,
        down_weight_grad,
    )


def solution(mesh):
    rows = P(("dp", "ctx"), None)
    entries = P(("dp", "ctx"))
    return jax.shard_map(
        on_device,
        mesh=mesh,
        in_specs=(rows, entries, rows, rows, entries, rows, rows, P("dp", None), rows),
        out_specs=(rows, rows, entries, rows, rows, entries, rows, rows),
        check_vma=False,
    )
```

```python
import jax
import jax.numpy as jnp
import numpy as np
from jax import lax
from jax.experimental import pallas as pl
from jax.experimental.pallas import tpu as pltpu
from jax.sharding import PartitionSpec as P

D = 2048
H = 32
KVH = 4
HD = 64
FF = 5632
HALF = HD // 2

EPS = 1e-05
MASKED = -1e30
BF = jnp.bfloat16
F32 = jnp.float32
VMEM_LIMIT = 60 << 20
SHORT = pl.CostEstimate(flops=1 << 20, bytes_accessed=1 << 20, transcendentals=0)
MEDIUM = pl.CostEstimate(flops=2 * 10**10, bytes_accessed=1 << 20, transcendentals=0)
LONG = pl.CostEstimate(flops=10**11, bytes_accessed=1 << 20, transcendentals=0)


def nt(a, b):
    return lax.dot_general(a, b, (((1,), (1,)), ((), ())), preferred_element_type=F32)


def nn(a, b):
    return jnp.dot(a, b, preferred_element_type=F32)


def after(x, *earlier):
    return lax.optimization_barrier((x, *earlier))[0]


def after_each(values, *earlier):
    count = len(values)
    return lax.optimization_barrier((*values, *earlier))[:count]


def walk(n_ctx, parity):
    bits = []
    bit = 2
    while bit < n_ctx:
        bits.append(bit)
        bit *= 2
    return bits if parity == 0 else bits[::-1]


def swap_stage(x, n_ctx, stage):
    pairs = [(c, c ^ walk(n_ctx, c % 2)[stage]) for c in range(n_ctx)]
    return lax.ppermute(x, "ctx", pairs)


def swap_core(x, n_ctx):
    return lax.ppermute(x, "ctx", [(c, c ^ 1) for c in range(n_ctx)])


def slot_table(n_ctx):
    lists = []
    for parity in (0, 1):
        row = [0]
        for bit in walk(n_ctx, parity):
            row = row + [v ^ bit for v in row]
        lists.append(row)
    return np.array(
        [lists[p] + [v ^ 1 for v in lists[1 - p]] for p in (0, 1)], dtype=np.int32
    )


def gather_direct(x, n_ctx):
    return [x] + [swap_stage(x, n_ctx, stage) for stage in range(len(walk(n_ctx, 0)))]


def gather_rest(direct, n_ctx, earlier=(), last=()):
    have = direct[:1]
    for stage in range(len(walk(n_ctx, 0))):
        passed = [after(block, *earlier) if earlier else block for block in have[1:]]
        have = have + [direct[stage + 1]] + [swap_stage(block, n_ctx, stage) for block in passed]
    return have + [swap_core(after(block, *last) if last else block, n_ctx) for block in have]


def gather_at_once(x, n_ctx):
    have = [x]
    table = slot_table(n_ctx)
    for slot in range(1, n_ctx // 2):
        pairs = [(c, c ^ int(table[c % 2][slot])) for c in range(n_ctx)]
        have.append(lax.ppermute(x, "ctx", pairs))
    return have, [swap_core(block, n_ctx) for block in have]


def gather_slots(x, n_ctx):
    return gather_rest(gather_direct(x, n_ctx), n_ctx)


def scatter_pairs(term, tok, n_ctx):
    mine = n_ctx // 2
    cut = mine // 2
    sums, arrivals = [], []
    for lo, hi in ((cut, mine), (0, cut)):
        arrivals.append(swap_core(term(mine + lo, mine + hi).astype(BF), n_ctx))
        sums.append(term(lo, hi) + arrivals[-1].astype(F32))
    return sums, arrivals


def scatter_chips(upper, lower, stages, n_ctx, *earlier):
    for stage in stages:
        if earlier and stage == 0:
            upper = after(upper.astype(BF), *earlier)
        lower = lower + swap_stage(upper.astype(BF), n_ctx, stage).astype(F32)
        if stage:
            half = lower.shape[0] // 2
            upper, lower = lower[half:], lower[:half]
    return lower if stages[-1] == 0 else (upper, lower)


def scatter_rest(lower, arrived, stages, n_ctx):
    sums = lower + arrived.astype(F32)
    if len(stages) == 1:
        return sums
    half = sums.shape[0] // 2
    return scatter_chips(sums[half:], sums[:half], stages[1:], n_ctx)


def exchange(x):
    return lax.all_to_all(x, "ctx", split_axis=0, concat_axis=0, tiled=False)


def gather_dp(x):
    return lax.all_gather(x, "dp", axis=0, tiled=True)


def scatter_dp(x):
    return lax.psum_scatter(x, "dp", scatter_dimension=0, tiled=True)


def fetch_piece(pieces, buffer, semaphores, count=1):
    step = pl.program_id(0)

    @pl.when(step == 0)
    def _():
        for i, piece in enumerate(pieces):
            pltpu.make_async_copy(piece, buffer.at[i], semaphores.at[i]).start()

    for i in range(count):
        at = step * count + i
        pltpu.make_async_copy(pieces[0], buffer.at[at], semaphores.at[at]).wait()
    if count == 1:
        return buffer[step]
    return buffer[pl.ds(step * count, count)].reshape(count * buffer.shape[1], buffer.shape[2])


def keep_pieces(buffer, target, semaphores):
    step = pl.program_id(0)
    total, tok = buffer.shape[0], buffer.shape[1]

    def copy(at):
        rows = pl.ds(pl.multiple_of(at * tok, tok), tok)
        return pltpu.make_async_copy(buffer.at[at], target.at[rows], semaphores.at[at])

    copy(step).start()

    @pl.when(step == total - 1)
    def _():
        for i in range(total):
            copy(i).wait()


def store_rows(source, target, semaphores):
    count = semaphores.shape[0]
    rows = source.shape[0] // count
    copies = [
        pltpu.make_async_copy(
            source.at[pl.ds(i * rows, rows)], target.at[pl.ds(i * rows, rows)], semaphores.at[i]
        )
        for i in range(count)
    ]
    for copy in copies:
        copy.start()
    return copies


def chunks(rows):
    return next(count for count in (8, 4, 2, 1) if rows % (16 * count) == 0)


def fetch_rows(source, buffer, semaphores):
    count = semaphores.shape[0]
    rows = source.shape[0] // count

    @pl.when(pl.program_id(0) == 0)
    def _():
        copies = [
            pltpu.make_async_copy(
                source.at[pl.ds(i * rows, rows)], buffer.at[pl.ds(i * rows, rows)], semaphores.at[i]
            )
            for i in range(count)
        ]
        for copy in copies:
            copy.start()
        for copy in copies:
            copy.wait()


def swap_halves(x):
    return pltpu.roll(x, x.shape[1] // 2, axis=1)


def turn_tables(cosine, sine, width):
    times = width // 128
    cosine = jnp.concatenate([cosine] * times, axis=1) if times > 1 else cosine
    sine = jnp.concatenate([sine] * times, axis=1) if times > 1 else sine
    lane = lax.broadcasted_iota(jnp.int32, sine.shape, 1)
    return cosine, jnp.where(lane < width // 2, -sine, sine)


def any_specs(pieces):
    return [pl.BlockSpec(memory_space=pltpu.HBM) for _ in pieces]


def project_qkv(order, pieces, weight, spread, widen, cosine, sine, width, tok):
    n = len(pieces)
    seq = n * tok

    def kernel(order_ref, *refs):
        parts = refs[:n]
        w_hbm, spread_ref, widen_ref, cos_ref, sin_ref = refs[n : n + 5]
        (
            q_ref, k_ref, v_ref, kt_ref, vt_ref, all_hbm, wide, buffer, semaphores, keep_semaphores, w_ref, w_semaphores
        ) = refs[n + 5 :]
        fetch_rows(w_hbm, w_ref, w_semaphores)

        @pl.when(pl.program_id(0) == 0)
        def _():
            wide[...] = nn(w_ref[...], spread_ref[...]).astype(BF)

        x = fetch_piece(parts, buffer, semaphores)
        keep_pieces(buffer, all_hbm, keep_semaphores)
        mixed = nn(x, wide[...])
        cos, sin = turn_tables(cos_ref[...], sin_ref[...], width)
        q = mixed[:, :width]
        q_ref[...] = (q * cos + swap_halves(q) * sin).astype(BF) * (HD**-0.5)
        lane = lax.broadcasted_iota(jnp.int32, (tok, 128), 1)
        key_sine = jnp.where(lane < HALF, -sin_ref[...], sin_ref[...])
        both = jnp.where(
            lane < HD,
            mixed[:, width : width + 128] * cos_ref[...] + mixed[:, width + 128 :] * key_sine,
            mixed[:, width : width + 128],
        ).astype(BF)
        repeated = nn(both, widen_ref[...]).astype(BF)
        k_ref[...] = repeated[:, :width]
        v_ref[...] = repeated[:, width:]
        turned = both.T
        kt_ref[...] = turned[:HD]
        vt_ref[...] = turned[HD:]

    rows = lambda s, order: (order[s], 0)
    lanes = lambda s, order: (0, order[s])
    whole = lambda s, order: (0, 0)
    return pl.pallas_call(
        kernel,
        grid_spec=pltpu.PrefetchScalarGridSpec(
            num_scalar_prefetch=1,
            grid=(n,),
            in_specs=any_specs(pieces)
            + [
                pl.BlockSpec(memory_space=pltpu.HBM),
                pl.BlockSpec(spread.shape, whole),
                pl.BlockSpec(widen.shape, whole),
                pl.BlockSpec((tok, 128), rows),
                pl.BlockSpec((tok, 128), rows),
            ],
            out_specs=[
                pl.BlockSpec((tok, width), rows),
                pl.BlockSpec((tok, width), rows),
                pl.BlockSpec((tok, width), rows),
                pl.BlockSpec((HD, tok), lanes),
                pl.BlockSpec((HD, tok), lanes),
                pl.BlockSpec(memory_space=pltpu.HBM),
            ],
            scratch_shapes=[
                pltpu.VMEM((D, width + 256), BF),
                pltpu.VMEM((n, tok, D), BF),
                pltpu.SemaphoreType.DMA((n,)),
                pltpu.SemaphoreType.DMA((n,)),
                pltpu.VMEM(weight.shape, BF),
                pltpu.SemaphoreType.DMA((chunks(D),)),
            ],
        ),
        out_shape=[
            jax.ShapeDtypeStruct((seq, width), BF),
            jax.ShapeDtypeStruct((seq, width), BF),
            jax.ShapeDtypeStruct((seq, width), BF),
            jax.ShapeDtypeStruct((HD, seq), BF),
            jax.ShapeDtypeStruct((HD, seq), BF),
            jax.ShapeDtypeStruct((seq, D), BF),
        ],
        compiler_params=pltpu.CompilerParams(vmem_limit_bytes=VMEM_LIMIT),
        cost_estimate=LONG,
        name="project_qkv",
    )(order, *pieces, weight, spread, widen, cosine, sine)


def project_out(order, heads_in, pieces, residual):
    n, tok, width = heads_in.shape

    def kernel(order_ref, a_ref, *refs):
        parts = refs[:n]
        x_ref, state_hbm, norm_hbm, buffer, semaphores, state_ref, norm_ref, out_semaphores = refs[n:]
        step = pl.program_id(0)
        w = fetch_piece(parts, buffer, semaphores)

        @pl.when(step == 0)
        def _():
            state_ref[...] = x_ref[...].astype(F32)

        state_ref[...] += nn(a_ref[0], w)

        @pl.when(step == n - 1)
        def _():
            state = state_ref[...]
            scale = lax.rsqrt(jnp.mean(state * state, axis=-1, keepdims=True) + EPS)
            copies = store_rows(state_ref, state_hbm, out_semaphores.at[0])
            norm_ref[...] = (state * scale).astype(BF)
            copies += store_rows(norm_ref, norm_hbm, out_semaphores.at[1])
            for copy in copies:
                copy.wait()

    whole = lambda s, order: (0, 0)
    return pl.pallas_call(
        kernel,
        grid_spec=pltpu.PrefetchScalarGridSpec(
            num_scalar_prefetch=1,
            grid=(n,),
            in_specs=[pl.BlockSpec((1, tok, width), lambda s, order: (order[s], 0, 0))]
            + any_specs(pieces)
            + [pl.BlockSpec((tok, D), whole)],
            out_specs=[pl.BlockSpec(memory_space=pltpu.HBM)] * 2,
            scratch_shapes=[
                pltpu.VMEM((n, width, D), BF),
                pltpu.SemaphoreType.DMA((n,)),
                pltpu.VMEM((tok, D), F32),
                pltpu.VMEM((tok, D), BF),
                pltpu.SemaphoreType.DMA((2, 4)),
            ],
        ),
        out_shape=[
            jax.ShapeDtypeStruct((tok, D), F32),
            jax.ShapeDtypeStruct((tok, D), BF),
        ],
        compiler_params=pltpu.CompilerParams(vmem_limit_bytes=VMEM_LIMIT),
        cost_estimate=SHORT,
        name="project_out",
    )(order, heads_in, *pieces, residual)


def feed_forward(pieces, weight):
    n = len(pieces)
    tok = 2 * pieces[0].shape[0]
    seq = n * tok // 2
    ff = weight.shape[1] // 2

    def kernel(*refs):
        parts = refs[:n]
        w_hbm, hidden_ref, factor_ref, all_ref, buffer, semaphores, w_ref, w_semaphores = refs[n:]
        fetch_rows(w_hbm, w_ref, w_semaphores)
        x = fetch_piece(parts, buffer, semaphores, 2)
        all_ref[...] = x
        both = nn(x, w_ref[...])
        gate = both[:, :ff]
        up = both[:, ff:]
        sig = jax.nn.sigmoid(gate)
        silu = gate * sig
        hidden_ref[...] = (silu * up).astype(BF)
        factor_ref[:, :ff] = (up * sig * (1.0 + gate * (1.0 - sig))).astype(BF)
        factor_ref[:, ff:] = silu.astype(BF)

    rows = lambda s: (s, 0)
    return pl.pallas_call(
        kernel,
        grid=(n // 2,),
        in_specs=any_specs(pieces) + [pl.BlockSpec(memory_space=pltpu.HBM)],
        out_specs=[
            pl.BlockSpec((tok, ff), rows),
            pl.BlockSpec((tok, 2 * ff), rows),
            pl.BlockSpec((tok, D), rows),
        ],
        scratch_shapes=[
            pltpu.VMEM((n, tok // 2, D), BF),
            pltpu.SemaphoreType.DMA((n,)),
            pltpu.VMEM(weight.shape, BF),
            pltpu.SemaphoreType.DMA((chunks(D),)),
        ],
        out_shape=[
            jax.ShapeDtypeStruct((seq, ff), BF),
            jax.ShapeDtypeStruct((seq, 2 * ff), BF),
            jax.ShapeDtypeStruct((seq, D), BF),
        ],
        compiler_params=pltpu.CompilerParams(vmem_limit_bytes=VMEM_LIMIT),
        cost_estimate=LONG,
        name="feed_forward",
    )(*pieces, weight)


def feed_backward(factors, grads, weight):
    seq = factors.shape[0]
    ff = weight.shape[0]
    tok = 512

    def kernel(factor_ref, g_ref, w_hbm, out_ref, w_ref, w_semaphores, turned):
        fetch_rows(w_hbm, w_ref, w_semaphores)

        @pl.when(pl.program_id(0) == 0)
        def _():
            turned[...] = w_ref[...].T

        grad_hidden = nn(g_ref[...], turned[...])
        factor = factor_ref[...].astype(F32)
        out_ref[:, :ff] = (grad_hidden * factor[:, :ff]).astype(BF)
        out_ref[:, ff:] = (grad_hidden * factor[:, ff:]).astype(BF)

    rows = lambda s: (s, 0)
    return pl.pallas_call(
        kernel,
        grid=(seq // tok,),
        in_specs=[
            pl.BlockSpec((tok, 2 * ff), rows),
            pl.BlockSpec((tok, D), rows),
            pl.BlockSpec(memory_space=pltpu.HBM),
        ],
        out_specs=pl.BlockSpec((tok, 2 * ff), rows),
        scratch_shapes=[
            pltpu.VMEM(weight.shape, BF),
            pltpu.SemaphoreType.DMA((chunks(ff),)),
            pltpu.VMEM((D, ff), BF),
        ],
        out_shape=jax.ShapeDtypeStruct((seq, 2 * ff), BF),
        compiler_params=pltpu.CompilerParams(vmem_limit_bytes=VMEM_LIMIT),
        cost_estimate=LONG,
        name="feed_backward",
    )(factors, grads, weight)


def lay_out(pieces):
    n = len(pieces)
    tok = pieces[0].shape[0]

    def kernel(*refs):
        parts = refs[:n]
        out_ref, buffer, in_semaphores, out_semaphores = refs[n:]
        arrive = [
            pltpu.make_async_copy(part, buffer.at[i], in_semaphores.at[i])
            for i, part in enumerate(parts)
        ]
        leave = [
            pltpu.make_async_copy(buffer.at[i], out_ref.at[pl.ds(i * tok, tok)], out_semaphores.at[i])
            for i in range(n)
        ]
        for copy in arrive:
            copy.start()
        for i in range(n):
            arrive[i].wait()
            leave[i].start()
        for copy in leave:
            copy.wait()

    return pl.pallas_call(
        kernel,
        in_specs=any_specs(pieces),
        out_specs=pl.BlockSpec(memory_space=pltpu.HBM),
        scratch_shapes=[
            pltpu.VMEM((n, tok, D), BF),
            pltpu.SemaphoreType.DMA((n,)),
            pltpu.SemaphoreType.DMA((n,)),
        ],
        out_shape=jax.ShapeDtypeStruct((n * tok, D), BF),
        compiler_params=pltpu.CompilerParams(vmem_limit_bytes=VMEM_LIMIT),
        cost_estimate=SHORT,
        name="lay_out",
    )(*pieces)


def branch_back(order, d_two, state, out_grad, pieces):
    n = len(pieces)
    tok = d_two.shape[0]
    width = pieces[0].shape[0]

    def kernel(order_ref, d_ref, state_ref, g_ref, *refs):
        parts = refs[:n]
        grad_hbm, branch_hbm, heads_ref, buffer, semaphores, grad_ref, branch_ref, out_semaphores = refs[n:]

        @pl.when(pl.program_id(0) == 0)
        def _():
            state = state_ref[...]
            scale = lax.rsqrt(jnp.mean(state * state, axis=-1, keepdims=True) + EPS)
            norm = state * scale
            d = d_ref[...]
            grad = g_ref[...].astype(F32) + scale * (
                d - norm * jnp.mean(d * norm, axis=-1, keepdims=True)
            )
            grad_ref[...] = grad
            branch_ref[...] = grad.astype(BF)
            store_rows(grad_ref, grad_hbm, out_semaphores.at[0])
            store_rows(branch_ref, branch_hbm, out_semaphores.at[1])

        w = fetch_piece(parts, buffer, semaphores)
        heads_ref[0] = nt(branch_ref[...], w).astype(BF)

        @pl.when(pl.program_id(0) == n - 1)
        def _():
            for source, target, at in ((grad_ref, grad_hbm, 0), (branch_ref, branch_hbm, 1)):
                rows = tok // 4
                for i in range(4):
                    cut = pl.ds(i * rows, rows)
                    pltpu.make_async_copy(source.at[cut], target.at[cut], out_semaphores.at[at, i]).wait()

    whole = lambda s, order: (0, 0)
    return pl.pallas_call(
        kernel,
        grid_spec=pltpu.PrefetchScalarGridSpec(
            num_scalar_prefetch=1,
            grid=(n,),
            in_specs=[
                pl.BlockSpec((tok, D), whole),
                pl.BlockSpec((tok, D), whole),
                pl.BlockSpec((tok, D), whole),
            ]
            + any_specs(pieces),
            out_specs=[
                pl.BlockSpec(memory_space=pltpu.HBM),
                pl.BlockSpec(memory_space=pltpu.HBM),
                pl.BlockSpec((1, tok, width), lambda s, order: (order[s], 0, 0)),
            ],
            scratch_shapes=[
                pltpu.VMEM((n, width, D), BF),
                pltpu.SemaphoreType.DMA((n,)),
                pltpu.VMEM((tok, D), F32),
                pltpu.VMEM((tok, D), BF),
                pltpu.SemaphoreType.DMA((2, 4)),
            ],
        ),
        out_shape=[
            jax.ShapeDtypeStruct((tok, D), F32),
            jax.ShapeDtypeStruct((tok, D), BF),
            jax.ShapeDtypeStruct((n, tok, width), BF),
        ],
        compiler_params=pltpu.CompilerParams(vmem_limit_bytes=VMEM_LIMIT),
        cost_estimate=SHORT,
        name="branch_back",
    )(order, d_two, state, out_grad, *pieces)


def split_columns(weight, gain, n_ctx, n_dp, ff_rows):
    rows = weight.shape[0]
    ff = ff_rows * n_dp

    def kernel(w_ref, gain_ref, out_ref):
        gains = gain_ref[...]
        for part in range(2):
            for d in range(n_dp):
                for c in range(n_ctx):
                    at = part * FF + (d * n_ctx + c) * ff_rows
                    to = part * ff + d * ff_rows
                    values = w_ref[:, at : at + ff_rows].astype(F32) * gains
                    out_ref[c, :, to : to + ff_rows] = values.astype(BF)

    return pl.pallas_call(
        kernel,
        in_specs=[pl.BlockSpec(memory_space=pltpu.VMEM)] * 2,
        out_specs=pl.BlockSpec(memory_space=pltpu.VMEM),
        out_shape=jax.ShapeDtypeStruct((n_ctx, rows, 2 * ff), BF),
        compiler_params=pltpu.CompilerParams(vmem_limit_bytes=VMEM_LIMIT),
        cost_estimate=LONG,
        name="split_columns",
    )(weight, gain)


def join_columns(sums, weight, gain, n_dp, ff_rows):
    n_ctx, rows, both = sums.shape
    ff = both // 2

    def kernel(s_ref, w_ref, gain_ref, out_ref, gain_out_ref):
        gains = gain_ref[...]
        total = jnp.zeros((rows, ff_rows), F32)
        for part in range(2):
            for d in range(n_dp):
                for c in range(n_ctx):
                    at = part * ff + d * ff_rows
                    to = part * FF + (d * n_ctx + c) * ff_rows
                    values = s_ref[c, :, at : at + ff_rows].astype(F32)
                    total = total + values * w_ref[:, to : to + ff_rows].astype(F32)
                    out_ref[:, to : to + ff_rows] = values * gains
        gain_out_ref[...] = jnp.sum(total, axis=1, keepdims=True)

    return pl.pallas_call(
        kernel,
        in_specs=[pl.BlockSpec(memory_space=pltpu.VMEM)] * 3,
        out_specs=[pl.BlockSpec(memory_space=pltpu.VMEM)] * 2,
        out_shape=[
            jax.ShapeDtypeStruct((rows, 2 * FF), F32),
            jax.ShapeDtypeStruct((rows, 1), F32),
        ],
        compiler_params=pltpu.CompilerParams(vmem_limit_bytes=VMEM_LIMIT),
        cost_estimate=LONG,
        name="join_columns",
    )(sums, weight, gain)


def lane_heads(rows, width):
    lane = lax.broadcasted_iota(jnp.int32, (rows, width), 1)
    return (lane % (width // 2)) // HALF


def attend_forward(slot_of, starts, queries, keys, values_t, heads, tok, first, count, before):
    seq, width = queries.shape
    blocks = seq // tok
    span = 2 * tok

    def kernel(slot_ref, start_ref, q_ref, k_ref, v_ref, *refs):
        attn_ref, slot_attn_ref, full_ref, lse_ref, scores = refs[len(before) :]
        block = first + pl.program_id(0)
        steps = (block + 2) // 2
        start = start_ref[...]
        here = block * tok + lax.broadcasted_iota(jnp.int32, (1, tok), 1)
        head_of = lane_heads(tok, width)
        q = q_ref[...]
        q_heads = [jnp.where(head_of == h, q, jnp.zeros_like(q)) for h in range(heads)]

        def score(i, peaks):
            rows = pl.ds(pl.multiple_of(i * span, span), span)
            k = k_ref[rows, :]
            there = i * span + lax.broadcasted_iota(jnp.int32, (span, tok), 0)
            visible = (there >= start) & (there <= here)
            out = []
            for h in range(heads):
                s = jnp.where(visible, nt(k, q_heads[h]), MASKED)
                scores[h, rows, :] = s
                out.append(jnp.maximum(peaks[h], jnp.max(s.reshape(span // 8, 8, tok), axis=0)))
            return tuple(out)

        peaks = lax.fori_loop(
            0, steps, score, tuple(jnp.full((8, tok), MASKED, F32) for _ in range(heads))
        )
        peaks = [jnp.max(peak, axis=0, keepdims=True) for peak in peaks]

        def weigh(i, running):
            rows = pl.ds(pl.multiple_of(i * span, span), span)
            v = v_ref[:, rows]
            out = []
            for h in range(heads):
                total, acc = running[h]
                p = jnp.exp(scores[h, rows, :] - peaks[h])
                total = total + jnp.sum(p.reshape(span // 8, 8, tok), axis=0)
                out.append((total, acc + nn(v, p.astype(BF))))
            return tuple(out)

        result = lax.fori_loop(
            0,
            steps,
            weigh,
            tuple((jnp.zeros((8, tok), F32), jnp.zeros((HD, tok), F32)) for _ in range(heads)),
        )
        rows = []
        for h in range(heads):
            total, acc = result[h]
            total = jnp.sum(total, axis=0, keepdims=True)
            rows.append(acc / total)
            lse_ref[0, h : h + 1, :] = peaks[h] + jnp.log(total)
        full = jnp.concatenate(rows, axis=0).T
        full_ref[...] = full
        attn_ref[...] = full.astype(BF)
        slot_attn_ref[...] = full.astype(BF)

    return pl.pallas_call(
        kernel,
        grid_spec=pltpu.PrefetchScalarGridSpec(
            num_scalar_prefetch=1,
            grid=(count,),
            in_specs=[
                pl.BlockSpec((1, tok), lambda j, slot: (0, first + j)),
                pl.BlockSpec((tok, width), lambda j, slot: (first + j, 0)),
                pl.BlockSpec((seq, width), lambda j, slot: (0, 0)),
                pl.BlockSpec((HD, seq), lambda j, slot: (0, 0)),
            ]
            + [pl.BlockSpec(memory_space=pltpu.HBM)] * len(before),
            out_specs=[
                pl.BlockSpec((tok, width), lambda j, slot: (first + j, 0)),
                pl.BlockSpec((tok, width), lambda j, slot: (slot[first + j], 0)),
                pl.BlockSpec((tok, width), lambda j, slot: (first + j, 0)),
                pl.BlockSpec((1, heads, tok), lambda j, slot: (first + j, 0, 0)),
            ],
            scratch_shapes=[pltpu.VMEM((heads, seq, tok), F32)],
        ),
        out_shape=[
            jax.ShapeDtypeStruct((seq, width), BF),
            jax.ShapeDtypeStruct((seq, width), BF),
            jax.ShapeDtypeStruct((seq, width), F32),
            jax.ShapeDtypeStruct((blocks, heads, tok), F32),
        ],
        input_output_aliases={5 + i: i for i in range(len(before))},
        compiler_params=pltpu.CompilerParams(vmem_limit_bytes=VMEM_LIMIT),
        cost_estimate=LONG,
        name="attend_forward",
    )(slot_of, starts, queries, keys, values_t, *before)


def attend_backward(
    slot_of, starts, queries, keys, keys_t, values, grads, full, lse, cosine, sine, unsplit, heads, tok
):
    seq, width = queries.shape
    blocks = seq // tok
    span = 2 * tok
    half = width // 2

    def kernel(
        slot_ref, start_ref, q_ref, k_ref, kt_ref, v_ref, g_ref, full_ref, lse_ref, cos_ref, sin_ref, unsplit_ref,
        out_ref, dk, dv,
    ):
        block = pl.program_id(0)
        steps = (block + 2) // 2

        @pl.when(block == 0)
        def _():
            dk[...] = jnp.zeros_like(dk)
            dv[...] = jnp.zeros_like(dv)

        start = start_ref[...]
        here = block * tok + lax.broadcasted_iota(jnp.int32, (1, tok), 1)
        head_of = lane_heads(tok, width)
        wide = lax.broadcasted_iota(jnp.int32, (tok, width), 1) // HD
        q = q_ref[...]
        g = g_ref[...]
        q_heads = [jnp.where(head_of == h, q, jnp.zeros_like(q)) for h in range(heads)]
        g_heads = [jnp.where(wide == h, g, jnp.zeros_like(g)) for h in range(heads)]
        q_stack = jnp.concatenate(q_heads, axis=0)
        g_stack = jnp.concatenate(g_heads, axis=0)
        picks = (
            lax.broadcasted_iota(jnp.int32, (8, width), 1) // HD
            == lax.broadcasted_iota(jnp.int32, (8, width), 0)
        ).astype(F32)
        deltas = lax.dot_general(
            picks,
            g.astype(F32) * full_ref[...],
            (((1,), (1,)), ((), ())),
            preferred_element_type=F32,
            precision=lax.Precision.HIGHEST,
        )

        def step(i, dq):
            rows = pl.ds(pl.multiple_of(i * span, span), span)
            k = k_ref[rows, :]
            v = v_ref[rows, :]
            kt = kt_ref[:, rows]
            there = i * span + lax.broadcasted_iota(jnp.int32, (span, tok), 0)
            visible = (there >= start) & (there <= here)
            probs, grad_scores, out = [], [], []
            for h in range(heads):
                s = jnp.where(visible, nt(k, q_heads[h]), MASKED)
                p = jnp.exp(s - lse_ref[0, h : h + 1, :])
                ds = (p * (nt(v, g_heads[h]) - deltas[h : h + 1, :])).astype(BF)
                probs.append(p.astype(BF))
                grad_scores.append(ds)
                out.append(dq[h] + nn(kt, ds))
            dv[rows, :] += nn(jnp.concatenate(probs, axis=1), g_stack)
            dk[rows, :] += nn(jnp.concatenate(grad_scores, axis=1), q_stack)
            return tuple(out)

        dq = lax.fori_loop(
            0, steps, step, tuple(jnp.zeros((HD, tok), F32) for _ in range(heads))
        )
        dq = jnp.concatenate([x[:HALF] for x in dq] + [x[HALF:] for x in dq], axis=0).T
        here_rows = pl.ds(pl.multiple_of(block * tok, tok), tok)
        cos, sin = turn_tables(cos_ref[here_rows, :], sin_ref[here_rows, :], width)
        dq = (dq * cos - swap_halves(dq) * sin) * (HD**-0.5)
        slot_rows = pl.ds(pl.multiple_of(slot_ref[block] * tok, tok), tok)
        out_ref[slot_rows, :width] = nn(dq.astype(BF), unsplit_ref[...]).astype(BF)

        @pl.when(block == blocks - 1)
        def _():
            lane = lax.broadcasted_iota(jnp.int32, (width, 128), 0)
            column = lax.broadcasted_iota(jnp.int32, (width, 128), 1)
            fold_k = ((lane // half) * HALF + lane % HALF == column).astype(BF)
            fold_v = (lane % HD + HD == column).astype(BF)

            def fold(i, unused):
                rows = pl.ds(pl.multiple_of(i * tok, tok), tok)
                cos, sin = turn_tables(cos_ref[rows, :], sin_ref[rows, :], width)
                a = dk[rows, :]
                a = a * cos - swap_halves(a) * sin
                b = dv[rows, :]
                a_high = a.astype(BF)
                b_high = b.astype(BF)
                terms = (
                    nn(a_high, fold_k)
                    + nn((a - a_high.astype(F32)).astype(BF), fold_k)
                    + nn(b_high, fold_v)
                    + nn((b - b_high.astype(F32)).astype(BF), fold_v)
                )
                slot_rows = pl.ds(pl.multiple_of(slot_ref[i] * tok, tok), tok)
                out_ref[slot_rows, width:] = terms.astype(BF)
                return unused

            lax.fori_loop(0, blocks, fold, 0)

    whole = lambda shape: pl.BlockSpec(shape, lambda j, *_: (0, 0))
    return pl.pallas_call(
        kernel,
        grid_spec=pltpu.PrefetchScalarGridSpec(
            num_scalar_prefetch=1,
            grid=(blocks,),
            in_specs=[
                pl.BlockSpec((1, tok), lambda j, *_: (0, j)),
                pl.BlockSpec((tok, width), lambda j, *_: (j, 0)),
                whole((seq, width)),
                whole((HD, seq)),
                whole((seq, width)),
                pl.BlockSpec((tok, width), lambda j, *_: (j, 0)),
                pl.BlockSpec((tok, width), lambda j, *_: (j, 0)),
                pl.BlockSpec((1, heads, tok), lambda j, *_: (j, 0, 0)),
                whole((seq, 128)),
                whole((seq, 128)),
                whole((width, width)),
            ],
            out_specs=whole((seq, width + 128)),
            scratch_shapes=[pltpu.VMEM((seq, width), F32), pltpu.VMEM((seq, width), F32)],
        ),
        out_shape=jax.ShapeDtypeStruct((seq, width + 128), BF),
        compiler_params=pltpu.CompilerParams(vmem_limit_bytes=VMEM_LIMIT),
        cost_estimate=MEDIUM,
        name="attend_backward",
    )(slot_of, starts, queries, keys, keys_t, values, grads, full, lse, cosine, sine, unsplit)


def outer_rows(activations, gradients):
    return lax.dot_general(
        activations, gradients, (((0,), (0,)), ((), ())), preferred_element_type=F32
    ).astype(BF)


def split_source(width):
    lane = np.arange(width)
    half = lane // (width // 2)
    head = (lane % (width // 2)) // HALF
    return head * HD + half * HALF + lane % HALF


def spread_matrix(width):
    matrix = np.zeros((width + 2 * HD, width + 256), np.float32)
    lane = np.arange(width)
    matrix[split_source(width), lane] = 1
    lane = np.arange(2 * HD)
    matrix[width + lane, width + lane] = 1
    lane = np.arange(HD)
    matrix[width + (lane + HALF) % HD, width + 128 + lane] = 1
    return jnp.asarray(matrix, BF)


def widen_matrix(width):
    matrix = np.zeros((2 * HD, 2 * width), np.float32)
    lane = np.arange(width)
    matrix[(lane // (width // 2)) * HALF + lane % HALF, lane] = 1
    matrix[HD + lane % HD, width + lane] = 1
    return jnp.asarray(matrix, BF)


def unsplit_matrix(width):
    matrix = np.zeros((width, width), np.float32)
    matrix[np.arange(width), split_source(width)] = 1
    return jnp.asarray(matrix, BF)


def on_device(
    block_in,
    gain_attn,
    qkv_weight,
    out_weight,
    gain_ffn,
    gate_up_weight,
    down_weight,
    doc_lengths,
    out_grad,
):
    n_ctx = lax.axis_size("ctx")
    n_dp = lax.axis_size("dp")
    me = lax.axis_index("ctx")
    tok = block_in.shape[0]
    seq = tok * n_ctx
    heads = H // n_ctx
    width = heads * HD
    sharers = n_ctx // KVH
    rows = qkv_weight.shape[0]
    ff_rows = down_weight.shape[0]
    ff = ff_rows * n_dp
    columns = width + 2 * HD

    order = me ^ jnp.where(me % 2 == 0, *[jnp.asarray(t) for t in slot_table(n_ctx)])
    slots = jnp.arange(n_ctx, dtype=jnp.int32)
    slot_of = jnp.sum(jnp.where(order[None, :] == slots[:, None], slots[None, :], 0), axis=1)
    index = jnp.arange(seq, dtype=jnp.int32)
    lengths = doc_lengths[0]
    ends = jnp.cumsum(lengths)
    starts = jnp.sum((index[:, None] >= ends[None, :]).astype(jnp.int32) * lengths[None, :], axis=1)
    lane = jnp.arange(128, dtype=F32) % HALF
    frequency = 10000.0 ** (-lane * 2.0 / HD)
    angles = (index - starts).astype(F32)[:, None] * frequency[None, :]
    cosine = jnp.cos(angles)
    sine = jnp.sin(angles)
    starts_row = starts[None, :]

    gain_one = gain_attn.astype(F32)[:, None]
    gain_two = gain_ffn.astype(F32)[:, None]
    qkv = (qkv_weight.astype(F32) * gain_one).astype(BF)
    q_cols = qkv[:, : H * HD].reshape(rows, n_ctx, width).transpose(1, 0, 2)
    k_cols = qkv[:, H * HD : (H + KVH) * HD].reshape(rows, KVH, HD).transpose(1, 0, 2)
    v_cols = qkv[:, (H + KVH) * HD :].reshape(rows, KVH, HD).transpose(1, 0, 2)
    kv_cols = jnp.repeat(jnp.concatenate([k_cols, v_cols], axis=2), sharers, axis=0)
    owner_pairs = [(b, b % n_dp * n_ctx + b // n_dp) for b in range(n_dp * n_ctx)]
    out_own = lax.ppermute(out_weight, ("dp", "ctx"), owner_pairs)
    out_part = gather_dp(out_own)
    qkv_own = exchange(jnp.concatenate([q_cols, kv_cols], axis=2)).reshape(n_ctx * rows, columns)
    qkv_part = gather_dp(qkv_own)

    hidden_in = block_in.astype(F32)
    rms_one = lax.rsqrt(jnp.mean(hidden_in * hidden_in, axis=-1, keepdims=True) + EPS)
    one_pieces = gather_slots(after((hidden_in * rms_one).astype(BF), qkv_own, out_own), n_ctx)

    gate_up_cols = split_columns(
        gate_up_weight, after(gain_two, cosine, sine), n_ctx, n_dp, ff_rows
    )
    gate_up_own = exchange(after(gate_up_cols, *one_pieces[: n_ctx // 2])).reshape(
        n_ctx * rows, 2 * ff
    )
    gate_up_part = gather_dp(gate_up_own)
    down_part = gather_dp(after(down_weight, gate_up_own))

    queries, keys, values, keys_t, values_t, all_one = project_qkv(
        order, one_pieces, qkv_part, spread_matrix(width), widen_matrix(width), cosine, sine, width, tok
    )
    out_direct = gather_direct(out_part, n_ctx)
    attn, slot_attn, attended, lse = attend_forward(
        slot_of, starts_row, after(queries, gate_up_own, *out_direct), keys, values_t, heads, tok, 0, n_ctx, ()
    )
    attn_tokens = exchange(attn.reshape(n_ctx, tok, width))
    out_pieces = gather_rest(out_direct, n_ctx, (queries,), (attn,))
    state, norm_two = project_out(order, attn_tokens, out_pieces, block_in)

    two_pieces = gather_slots(norm_two, n_ctx)
    grad_direct = gather_direct(after(out_grad, *two_pieces), n_ctx)
    hidden, factors, all_two = feed_forward(two_pieces, gate_up_part)
    grad_pieces = gather_rest(grad_direct, n_ctx, (hidden,))
    all_grad = lay_out(grad_pieces)
    down_terms = outer_rows(hidden, all_grad)
    down_sums = scatter_dp(down_terms)
    grad_gate_up = feed_backward(factors, all_grad, down_part)

    def rows_of(x, lo, hi):
        return lax.slice_in_dim(x, lo * tok, hi * tok, axis=0)

    d_pairs, _ = scatter_pairs(
        lambda lo, hi: nt(rows_of(grad_gate_up, lo, hi), gate_up_part), tok, n_ctx
    )
    stages = tuple(reversed(range(len(walk(n_ctx, 0)))))
    d_two = scatter_chips(*d_pairs, stages, n_ctx)
    hidden_pairs, _ = scatter_pairs(
        lambda lo, hi: nn(rows_of(after(hidden, *d_pairs), lo, hi), down_part), tok, n_ctx
    )
    gate_up_terms = outer_rows(after(all_two, *d_pairs), grad_gate_up)
    gate_up_sums = scatter_dp(gate_up_terms)

    grad_state, grad_branch, grad_heads = branch_back(
        order, after(d_two, gate_up_terms, *hidden_pairs), state, out_grad, out_pieces
    )
    grad_attn = exchange(grad_heads).reshape(seq, width)
    branch_here, branch_there = gather_at_once(after(grad_branch, grad_attn), n_ctx)
    hidden_upper, hidden_lower = hidden_pairs
    hidden_arrived = swap_stage(after(hidden_upper.astype(BF), grad_attn), n_ctx, stages[0])
    grad_mixed = attend_backward(
        slot_of,
        starts_row,
        queries,
        keys,
        keys_t,
        values,
        grad_attn,
        attended,
        lse,
        cosine,
        sine,
        unsplit_matrix(width),
        heads,
        tok,
    )
    qkv_terms = outer_rows(all_one, grad_mixed)
    qkv_sums = scatter_dp(after(qkv_terms, gate_up_sums))
    one_pairs, _ = scatter_pairs(
        lambda lo, hi: nt(
            rows_of(after(grad_mixed, qkv_terms, hidden_arrived, *branch_here), lo, hi), qkv_part
        ),
        tok,
        n_ctx,
    )
    d_one = scatter_chips(*one_pairs, stages, n_ctx)
    hidden_sums = scatter_rest(hidden_lower, hidden_arrived, stages, n_ctx)
    block_out = (state + hidden_sums).astype(BF)
    out_terms = outer_rows(slot_attn, after(lay_out(branch_here + branch_there), qkv_terms))
    out_sums = scatter_dp(after(out_terms, qkv_sums))
    norm_one = hidden_in * rms_one
    input_grad = grad_state + rms_one * (
        d_one - norm_one * jnp.mean(d_one * norm_one, axis=-1, keepdims=True)
    )

    down_weight_grad = after(down_sums, grad_mixed).astype(F32)
    out_weight_grad = lax.ppermute(
        out_sums, ("dp", "ctx"), [(b, a) for a, b in owner_pairs]
    ).astype(F32)
    gate_up_weight_grad, gain_ffn_grad = join_columns(
        exchange(after(gate_up_sums, grad_mixed).reshape(n_ctx, rows, 2 * ff)), gate_up_weight, gain_two, n_dp, ff_rows
    )
    qkv_back = exchange(qkv_sums.reshape(n_ctx, rows, columns)).astype(F32)
    q_back = qkv_back[:, :, :width].transpose(1, 0, 2).reshape(rows, H * HD)
    kv_back = jnp.sum(qkv_back[:, :, width:].reshape(KVH, sharers, rows, 2 * HD), axis=1)
    k_back = kv_back[:, :, :HD].transpose(1, 0, 2).reshape(rows, KVH * HD)
    v_back = kv_back[:, :, HD:].transpose(1, 0, 2).reshape(rows, KVH * HD)
    qkv_back = jnp.concatenate([q_back, k_back, v_back], axis=1)
    qkv_weight_grad = qkv_back * gain_one
    gain_attn_grad = jnp.sum(qkv_back * qkv_weight.astype(F32), axis=1)
    return (
        block_out,
        input_grad,
        gain_attn_grad,
        qkv_weight_grad,
        out_weight_grad,
        gain_ffn_grad[:, 0],
        gate_up_weight_grad,
        down_weight_grad,
    )


def solution(mesh):
    rows = P(("dp", "ctx"), None)
    entries = P(("dp", "ctx"))
    return jax.shard_map(
        on_device,
        mesh=mesh,
        in_specs=(rows, entries, rows, rows, entries, rows, rows, P("dp", None), rows),
        out_specs=(rows, rows, entries, rows, rows, entries, rows, rows),
        check_vma=False,
    )
```
